32 devices in a mesh: ctx: 8 (over y, x, core), head: 4 (over z).
Axes of the slice: x: 2, y: 2, z: 4, core: 2. Of those that a mesh axis runs over, the one named last changes fastest.
Arguments:
- hidden: bfloat16 [16384, 1024], P('ctx'), may hold values from -6 to 6
- norm_gain: float32 [1024], replicated, may hold values from 0.1 to 1.9
- w_zx: bfloat16 [1024, 2, 2048], P(None, None, 'head'), may hold values from -0.1875 to 0.1875
- w_bc: bfloat16 [1024, 256], replicated, may hold values from -0.1875 to 0.1875
- w_dt: bfloat16 [1024, 32], P(None, 'head'), may hold values from -0.1875 to 0.1875
- dt_bias: float32 [32], P('head'), may hold values from -2 to 1
- decay_rate: float32 [32], P('head'), may hold values from 1e-07 to 0.03
- skip_gain: float32 [32], P('head'), may hold values from 0.5 to 2
- conv_x: float32 [4, 2048], P(None, 'head'), may hold values from -3 to 3
- conv_bc: float32 [4, 256], replicated, may hold values from -3 to 3
- w_out: bfloat16 [2048, 1024], P('head'), may hold values from -0.125 to 0.125
Outputs:
- mixed: bfloat16 [16384, 1024], P(('ctx', 'head'))
The draws below stay inside these ranges and needn't reach their ends.
All inputs are finite; a program needn't handle non-finite values.
Results may differ from the reference program's by a relative error of at most 0.013.
Values may be sent and summed in bfloat16 or wider, within the bound.
No kernel may reach another device: no remote copies, remote signals or barrier semaphores. Data moves between devices by JAX's collectives and lax.ppermute only.
A program may use at most 128 MiB of HBM per device.

```python
import jax
import jax.numpy as jnp
from jax import lax

D = 1024
HEADS = 32
STATE = 128
CONV = 4
BLOCK = 256
INNER = 2048
LENGTH = 16384


def draw_decay_rate(key, part):
    spread = jax.random.uniform(key, (HEADS,), jnp.float32)
    return jnp.exp(jnp.log(1e-05) + spread * (jnp.log(0.03) - jnp.log(1e-05)))


def block_levels(key, dims, split, low, largest):
    level = 1.0
    for dim, shards_of in split:
        steps = jax.random.uniform(jax.random.fold_in(jax.random.fold_in(key, 6), dim), (shards_of,), jnp.float32, low / len(split), largest / len(split))
        level = level * jnp.repeat(jnp.exp(steps), dims[dim] // shards_of).reshape((-1,) + (1,) * (len(dims) - 1 - dim))
    return level


def gaussian(stream_key, shape, deviation, reach, pieces=(), dtype=jnp.bfloat16):
    array = jax.random.normal(stream_key, shape, jnp.float32) * deviation
    if len(pieces) > 0:
        array = block_levels(stream_key, shape, pieces, -0.22, 0.18) * array
    return jnp.clip(array, min=-reach, max=reach).astype(dtype)


def setup_inputs(seed: int = 0) -> dict:
    key_of = jax.random.split(jax.random.key(seed), 12)
    hidden = gaussian(key_of[0], (LENGTH, D), 1.0, 6.0, ((0, 8),))
    norm_gain = jnp.clip(1.0 + 0.18 * jax.random.normal(key_of[1], (D,), jnp.float32), 0.1, 1.9)
    w_zx = gaussian(key_of[2], (D, 2, INNER), D ** -0.5, 0.1875, ((2, 4),))
    w_bc = gaussian(key_of[3], (D, 2 * STATE), D ** -0.5, 0.1875)
    w_dt = gaussian(key_of[4], (D, HEADS), D ** -0.5, 0.1875, ((1, 4),))
    dt_bias = jnp.clip(-2.0 + 3.0 * jax.random.uniform(key_of[5], (HEADS,), jnp.float32) ** block_levels(key_of[5], (HEADS,), ((0, 4),), -0.2, 0.2), -2.0, 1.0)
    decay_rate = draw_decay_rate(jax.random.fold_in(key_of[11], 71), 0)
    skip_gain = jnp.clip(0.5 + 1.5 * jax.random.uniform(key_of[7], (HEADS,), jnp.float32) ** block_levels(key_of[7], (HEADS,), ((0, 4),), -0.2, 0.2), 0.5, 2.0)
    conv_x = gaussian(key_of[8], (CONV, INNER), 0.5, 3.0, ((1, 4),), jnp.float32)
    conv_bc = gaussian(key_of[9], (CONV, 2 * STATE), 0.5, 3.0, (), jnp.float32)
    w_out = gaussian(key_of[10], (INNER, D), INNER ** -0.5, 0.125, ((0, 4),))
    return {"hidden": hidden, "norm_gain": norm_gain, "w_zx": w_zx, "w_bc": w_bc, "w_dt": w_dt, "dt_bias": dt_bias, "decay_rate": decay_rate, "skip_gain": skip_gain, "conv_x": conv_x, "conv_bc": conv_bc, "w_out": w_out}


epsilon = 1e-05

def normed_rows(rows, norm_gain):
    values = rows.astype(jnp.float32)
    scales = lax.rsqrt(lax.optimization_barrier(jnp.mean(values * values, axis=-1, keepdims=True)) + epsilon)
    return (values * scales * norm_gain).astype(jnp.bfloat16)

def project_rows(normed, w_zx, w_bc, w_dt, dt_bias):
    widths = w_zx.shape[2]
    joined = jnp.dot(normed, w_zx.reshape(w_zx.shape[0], 2 * widths), preferred_element_type=jnp.float32).astype(jnp.bfloat16)
    maps = jnp.dot(normed, w_bc, preferred_element_type=jnp.float32).astype(jnp.bfloat16)
    gates = joined[:, :widths]
    stream = jnp.concatenate([joined[:, widths:], maps], axis=1)
    steps_dt = jax.nn.softplus(jnp.dot(normed, w_dt, preferred_element_type=jnp.float32) + dt_bias)
    return (gates, stream, steps_dt)

def conv_silu(padded, conv_weights, amount):
    summed = jnp.zeros((amount, padded.shape[1]), jnp.float32)
    for lag_index in range(conv_weights.shape[0]):
        summed = summed + conv_weights[lag_index] * padded[lag_index:lag_index + amount].astype(jnp.float32)
    return jax.nn.silu(summed).astype(jnp.bfloat16)

def block_terms(values, b_rows, c_rows, steps_dt, decay_rate):
    cumulated = jnp.cumsum(-decay_rate * steps_dt, axis=1)
    weighted = (values.astype(jnp.float32) * steps_dt[..., None]).astype(jnp.bfloat16)
    scores = jnp.einsum('bsn,brn->bsr', c_rows.astype(jnp.float32), b_rows.astype(jnp.float32))
    across = jnp.swapaxes(cumulated, 1, 2)
    length_block = values.shape[1]
    lower = jnp.arange(length_block)[:, None] >= jnp.arange(length_block)[None, :]
    decays = jnp.exp(jnp.where(lower, across[..., :, None] - across[..., None, :], -jnp.inf))
    mixing = (scores[:, None] * decays).astype(jnp.bfloat16)
    inside = jnp.einsum('bhsr,brhp->bshp', mixing.astype(jnp.float32), weighted.astype(jnp.float32))
    tails = (weighted.astype(jnp.float32) * jnp.exp(cumulated[:, -1:, :] - cumulated)[..., None]).astype(jnp.bfloat16)
    ends = jnp.einsum('brhp,brn->bhpn', tails.astype(jnp.float32), b_rows.astype(jnp.float32))
    return (inside, ends, cumulated)

def carried_part(c_rows, cumulated, entering):
    reads = jnp.einsum('bsn,bhpn->bshp', c_rows.astype(jnp.float32), entering, precision=lax.Precision.HIGHEST)
    return reads * jnp.exp(cumulated)[..., None]

def strand(stream, gates, steps_dt, conv_weights, decay_rate, skip_gain):
    amount = stream.shape[0]
    heads = steps_dt.shape[1]
    inner = gates.shape[1]
    blocks = amount // BLOCK
    padded = jnp.concatenate([jnp.zeros((conv_weights.shape[0] - 1, stream.shape[1]), jnp.bfloat16), stream], axis=0)
    active = conv_silu(padded, conv_weights, amount)
    values = active[:, :inner].reshape(blocks, BLOCK, heads, inner // heads)
    b_rows = active[:, inner:inner + STATE].reshape(blocks, BLOCK, STATE)
    c_rows = active[:, inner + STATE:].reshape(blocks, BLOCK, STATE)
    blocked_dt = steps_dt.reshape(blocks, BLOCK, heads)

    def step_block(carried, inputs):
        values_b, b_block, c_block, dt_block = inputs
        inside, ends, cumulated = block_terms(values_b[None], b_block[None], c_block[None], dt_block[None], decay_rate)
        outputs = inside + carried_part(c_block[None], cumulated, carried[None])
        renewed = jnp.exp(cumulated[0, -1])[:, None, None] * carried + ends[0]
        return (renewed, outputs[0])
    initial = jnp.zeros((heads, inner // heads, STATE), jnp.float32)
    final_state, outputs = lax.scan(step_block, initial, (values, b_rows, c_rows, blocked_dt))
    outputs = outputs.reshape(amount, heads, inner // heads)
    outputs = outputs + skip_gain[:, None] * values.reshape(amount, heads, inner // heads).astype(jnp.float32)
    gated = outputs * jax.nn.silu(gates.astype(jnp.float32)).reshape(amount, heads, inner // heads)
    normed = gated * lax.rsqrt(lax.optimization_barrier(jnp.mean(gated * gated, axis=-1, keepdims=True)) + epsilon)
    return normed.reshape(amount, inner)

def reference(hidden, norm_gain, w_zx, w_bc, w_dt, dt_bias, decay_rate, skip_gain, conv_x, conv_bc, w_out):
    conv_weights = jnp.concatenate([conv_x, conv_bc], axis=1)
    results = []
    for strand_rows in (hidden, hidden[::-1, ::-1]):
        normed = normed_rows(strand_rows, norm_gain)
        gates, stream, steps_dt = project_rows(normed, w_zx, w_bc, w_dt, dt_bias)
        results.append(strand(stream, gates, steps_dt, conv_weights, decay_rate, skip_gain))
    combined = (results[0] + results[1][::-1]).astype(jnp.bfloat16)
    mixed = hidden.astype(jnp.float32) + jnp.dot(combined, w_out, preferred_element_type=jnp.float32)
    return mixed.astype(jnp.bfloat16)
```

```python
import functools

import jax
import jax.numpy as jnp
from jax import lax
from jax.experimental import pallas as pl
from jax.experimental.pallas import tpu as pltpu
from jax.sharding import PartitionSpec as P

STATE = 128
CHUNK = 128
TILE = 256
EPS = 1e-05
RIM = 16
TAIL = 16
F32 = jnp.float32
BF16 = jnp.bfloat16
MIB = 2**20


def params(limit=58):
    return pltpu.CompilerParams(
        dimension_semantics=("arbitrary",), vmem_limit_bytes=limit * MIB
    )


def cost(flops, bytes_accessed):
    return pl.CostEstimate(flops=int(flops), bytes_accessed=int(bytes_accessed), transcendentals=0)


def whole(shape):
    return pl.BlockSpec(shape, lambda *_: (0,) * len(shape))


def silu(x):
    half = 0.5 * x
    return half + half * jnp.tanh(half)


def tri(rows, reverse):
    r = lax.broadcasted_iota(jnp.int32, (rows, rows), 0)
    c = lax.broadcasted_iota(jnp.int32, (rows, rows), 1)
    return (r <= c) if reverse else (r >= c)


def spread_matrix(first, heads, width):
    r = lax.broadcasted_iota(jnp.int32, (2 * 128, heads * width), 0) % 128
    c = lax.broadcasted_iota(jnp.int32, (2 * 128, heads * width), 1) // width
    return (r == c + first).astype(BF16)


def spread(q, matrix):
    high = q.astype(BF16)
    low = (q - high.astype(F32)).astype(BF16)
    return jnp.dot(jnp.concatenate([high, low], axis=1), matrix, preferred_element_type=F32)


def prepare_kernel(inner, heads, zx_ref, bc_ref, dt_ref, gain_ref, wf_ref, wr_ref):
    rows = zx_ref.shape[0]
    gain = gain_ref[...]
    zx = zx_ref[...].astype(F32).reshape(rows, 2 * inner)
    r = lax.broadcasted_iota(jnp.int32, (rows, rows), 0)
    c = lax.broadcasted_iota(jnp.int32, (rows, rows), 1)
    turn = (r + c == rows - 1).astype(BF16)
    at = 0
    for part in (zx[:, inner:], bc_ref[...].astype(F32), zx[:, :inner], dt_ref[...].astype(F32)):
        scaled = (part * gain).astype(BF16)
        size = scaled.shape[1]
        wf_ref[:, at : at + size] = scaled
        wr_ref[:, at : at + size] = jnp.dot(turn, scaled, preferred_element_type=F32).astype(BF16)
        at += size


def prepare(w_zx, w_bc, w_dt, gain):
    depth, _, inner = w_zx.shape
    tile = min(256, depth)
    n = depth // tile
    wide = 2 * inner + w_bc.shape[1] + 128
    return pl.pallas_call(
        functools.partial(prepare_kernel, inner, None),
        grid=(n,),
        in_specs=[pl.BlockSpec((tile, 2, inner), lambda i: (i, 0, 0)),
                  pl.BlockSpec((tile, w_bc.shape[1]), lambda i: (i, 0)),
                  pl.BlockSpec((tile, 128), lambda i: (i, 0)),
                  pl.BlockSpec((tile, 1), lambda i: (i, 0))],
        out_specs=[pl.BlockSpec((tile, wide), lambda i: (i, 0)),
                   pl.BlockSpec((tile, wide), lambda i: (n - 1 - i, 0))],
        out_shape=[jax.ShapeDtypeStruct((depth, wide), BF16)] * 2,
        compiler_params=params(),
        cost_estimate=cost(1e9, 8e6),
        name="prepare",
    )(w_zx, w_bc, w_dt, gain)


def project_kernel(heads, inner, *refs):
    (hf_ref, hr_ref, rimf_ref, rimr_ref, wf_ref, wr_ref, conv_ref, bias_ref, rate_ref, copy_ref,
     actf_ref, zf_ref, smallf_ref, cumtf_ref, enterf_ref, priorf_ref,
     actr_ref, zr_ref, smallr_ref, cumtr_ref, enterr_ref, priorr_ref,
     msg_ref, buff, bufr, statef, stater, totalf, totalr) = refs
    step = pl.program_id(0)
    last = pl.num_programs(0) - 1
    stream = inner + 2 * STATE
    blocks = stream // 128
    wide = stream + inner
    rows = hf_ref.shape[0]
    sides = (
        (False, hf_ref, rimf_ref, wf_ref, actf_ref, zf_ref, smallf_ref, cumtf_ref, enterf_ref, priorf_ref,
         buff, statef, totalf),
        (True, hr_ref, rimr_ref, wr_ref, actr_ref, zr_ref, smallr_ref, cumtr_ref, enterr_ref, priorr_ref,
         bufr, stater, totalr),
    )

    def row_scale(h):
        hf = h.astype(F32)
        return lax.rsqrt(jnp.mean(hf * hf, axis=-1, keepdims=True) + EPS)

    @pl.when(step == 0)
    def _():
        for reverse, _, rim_ref, w_ref, _, _, _, _, _, _, buf, state, total in sides:
            edge = rows if reverse else 0
            state[...] = jnp.zeros_like(state)
            total[...] = jnp.zeros_like(total)
            rim = rim_ref[...]
            out = jnp.dot(rim, w_ref[:, :stream], preferred_element_type=F32) * row_scale(rim)
            for j in range(blocks):
                part = out[:, j * 128 : (j + 1) * 128]
                buf[j, edge : edge + 8, :] = part[:8] if reverse else part[RIM - 8 :]

    lane = lax.broadcasted_iota(jnp.int32, (CHUNK, 128), 1)
    copy = copy_ref[...]
    hs = [side[1][...] for side in sides]
    scales = [row_scale(h) for h in hs]
    small = []
    for k, (reverse, _, _, w_ref, _, _, small_ref, cumt_ref, _, _, _, _, _) in enumerate(sides):
        raw = jnp.dot(hs[k], w_ref[:, wide:], preferred_element_type=F32) * scales[k] + bias_ref[...]
        dt = jnp.maximum(raw, 0.0) + jnp.log1p(jnp.exp(-jnp.abs(raw)))
        steps = -rate_ref[...] * dt
        mask = tri(CHUNK, reverse).astype(F32)
        parts = []
        for c in range(0, rows, CHUNK):
            cum = jnp.dot(mask, steps[c : c + CHUNK], preferred_element_type=F32, precision=lax.Precision.HIGHEST)
            own = dt[c : c + CHUNK]
            small_ref[c : c + CHUNK, :] = jnp.where(lane < heads, own, pltpu.roll(cum, heads, 1))
            cumt_ref[:, c : c + CHUNK] = jnp.transpose(cum)[:heads]
            parts.append((own, cum))
        small.append(parts)

    for g in range(0, stream, 256):
        for k, (reverse, _, _, w_ref, act_ref, _, _, _, _, _, buf, _, _) in enumerate(sides):
            edge = rows if reverse else 0
            body = 0 if reverse else 8
            out = jnp.dot(hs[k], w_ref[:, g : g + 256], preferred_element_type=F32) * scales[k]
            for j in range(g // 128, g // 128 + 2):
                x = out[:, j * 128 - g : (j + 1) * 128 - g]
                buf[j, body : body + rows, :] = x
                cols = slice(j * 128, (j + 1) * 128)
                total = conv_ref[3:4, cols] * x
                for d in (1, 2, 3):
                    at = body + d if reverse else body - d
                    total = total + conv_ref[3 - d : 4 - d, cols] * buf[j, at : at + rows, :]
                act_ref[:, cols] = silu(total).astype(BF16)
                buf[j, edge : edge + 8, :] = x[:8] if reverse else x[rows - 8 :]

    for g in range(0, inner, 256):
        for k, (_, _, _, w_ref, _, z_ref, _, _, _, _, _, _, _) in enumerate(sides):
            out = jnp.dot(hs[k], w_ref[:, stream + g : stream + g + 256], preferred_element_type=F32) * scales[k]
            z_ref[:, g : g + 256] = out.astype(BF16)

    count = rows // CHUNK
    for i in range(count):
        for k, (reverse, _, _, _, act_ref, _, _, _, enter_ref, prior_ref, _, state, total) in enumerate(sides):
            c = count - 1 - i if reverse else i
            at = slice(c * CHUNK, (c + 1) * CHUNK)
            dt, cum = small[k][c]
            end = cum[:1] if reverse else cum[CHUNK - 1 :]
            weights = spread(jnp.where(lane < heads, dt * jnp.exp(end - cum), 0.0), copy)
            tails = (act_ref[at, :inner].astype(F32) * weights).astype(BF16)
            ends = lax.dot_general(act_ref[at, inner : inner + STATE], tails, (((0,), (0,)), ((), ())),
                                   preferred_element_type=F32)
            before = state[...]
            enter_ref[c] = before.astype(BF16)
            prior_ref[c] = spread(jnp.exp(total[...]), copy)
            decay = spread(jnp.exp(jnp.broadcast_to(end, (8, 128))), copy)[:1]
            state[...] = before * decay + ends
            total[...] = total[...] + end

    @pl.when(step == last)
    def _():
        for k, side in enumerate(sides):
            state, total = side[-2:]
            at = k * (STATE + TAIL)
            msg_ref[at : at + STATE, :] = state[...].astype(BF16)
            t = total[...]
            high = t.astype(BF16).astype(F32)
            mid = (t - high).astype(BF16).astype(F32)
            low = t - high - mid
            row = lax.broadcasted_iota(jnp.int32, (8, 128), 0)
            packed = jnp.where(row == 0, high, jnp.where(row == 1, mid, jnp.where(row == 2, low, 0.0)))
            rows3 = spread(packed, copy)
            msg_ref[at + STATE : at + STATE + TAIL, :] = jnp.concatenate(
                [rows3, jnp.zeros_like(rows3)], axis=0).astype(BF16)


def project(hidden, rim_f, rim_r, w_f, w_r, conv, bias, rate, copy, heads, inner):
    rows, depth = hidden.shape
    stream = inner + 2 * STATE
    n = rows // TILE
    per = TILE // CHUNK
    up, down = (lambda i: i), (lambda i: n - 1 - i)
    by_rows = lambda width, at: pl.BlockSpec((TILE, width), lambda i: (at(i), 0))
    out_specs, out_shape = [], []
    for at in (up, down):
        out_specs += [by_rows(stream, at), by_rows(inner, at), by_rows(128, at),
                      pl.BlockSpec((heads, TILE), lambda i, at=at: (0, at(i))),
                      pl.BlockSpec((per, STATE, inner), lambda i, at=at: (at(i), 0, 0)),
                      pl.BlockSpec((per, 8, inner), lambda i, at=at: (at(i), 0, 0))]
        out_shape += [jax.ShapeDtypeStruct((rows, stream), BF16), jax.ShapeDtypeStruct((rows, inner), BF16),
                      jax.ShapeDtypeStruct((rows, 128), F32), jax.ShapeDtypeStruct((heads, rows), F32),
                      jax.ShapeDtypeStruct((n * per, STATE, inner), BF16),
                      jax.ShapeDtypeStruct((n * per, 8, inner), F32)]
    message = (2 * (STATE + TAIL), inner)
    buf = pltpu.VMEM((stream // 128, TILE + 8, 128), F32)
    state, total = pltpu.VMEM((STATE, inner), F32), pltpu.VMEM((8, 128), F32)
    return pl.pallas_call(
        functools.partial(project_kernel, heads, inner),
        grid=(n,),
        in_specs=[by_rows(depth, up), by_rows(depth, down), whole(rim_f.shape), whole(rim_r.shape),
                  whole(w_f.shape), whole(w_r.shape), whole(conv.shape), whole((1, 128)), whole((1, 128)),
                  whole(copy.shape)],
        out_specs=out_specs + [whole(message)],
        out_shape=out_shape + [jax.ShapeDtypeStruct(message, BF16)],
        scratch_shapes=[buf, buf, state, state, total, total],
        compiler_params=params(),
        cost_estimate=cost(22e9, 40e6),
        name="project",
    )(hidden, hidden, rim_f, rim_r, w_f, w_r, conv, bias, rate, copy)


def inside_kernel(heads, inner, actf_ref, smallf_ref, cumtf_ref, actr_ref, smallr_ref, cumtr_ref, skip_ref, copy_ref,
                  basef_ref, baser_ref):
    width = inner // heads
    per = 128 // width
    copy = copy_ref[...]
    lane = lax.broadcasted_iota(jnp.int32, (CHUNK, 128), 1)
    group = lane // width
    sides = ((False, actf_ref, smallf_ref, cumtf_ref, basef_ref), (True, actr_ref, smallr_ref, cumtr_ref, baser_ref))
    for reverse, act_ref, small_ref, cumt_ref, base_ref in sides:
        small = small_ref[...]
        values = act_ref[:, :inner].astype(F32)
        weighted = (values * spread(jnp.where(lane < heads, small, 0.0), copy)).astype(BF16)
        scores = lax.dot_general(act_ref[:, inner + STATE :], act_ref[:, inner : inner + STATE],
                                 (((1,), (1,)), ((), ())), preferred_element_type=F32)
        scores = jnp.where(tri(CHUNK, reverse), scores, 0.0)
        for p in range(inner // 128):
            cols = slice(p * 128, (p + 1) * 128)
            pair = weighted[:, cols]
            mixing, stacked = [], []
            for q in range(per):
                h = p * per + q
                gap = jnp.minimum(small[:, heads + h : heads + h + 1] - cumt_ref[h : h + 1, :], 0.0)
                mixing.append((scores * jnp.exp(gap)).astype(BF16))
                stacked.append(jnp.where(group == q, pair, jnp.zeros_like(pair)))
            out = jnp.dot(jnp.concatenate(mixing, axis=1), jnp.concatenate(stacked, axis=0),
                          preferred_element_type=F32)
            base_ref[:, cols] = (out + skip_ref[:, cols] * values[:, cols]).astype(BF16)


def inside(strands, skip, copy, heads, inner):
    rows, columns = strands[0][0].shape
    by_rows = lambda width: pl.BlockSpec((CHUNK, width), lambda i: (i, 0))
    one = [by_rows(columns), by_rows(128), pl.BlockSpec((heads, CHUNK), lambda i: (0, i))]
    return pl.pallas_call(
        functools.partial(inside_kernel, heads, inner),
        grid=(rows // CHUNK,),
        in_specs=one + one + [whole((1, inner)), whole(copy.shape)],
        out_specs=[by_rows(inner)] * 2,
        out_shape=[jax.ShapeDtypeStruct((rows, inner), BF16)] * 2,
        compiler_params=params(),
        cost_estimate=cost(14e9, 16e6),
        name="inside",
    )(*strands[0], *strands[1], skip, copy)


def finish_kernel(heads, inner, *refs):
    (cf_ref, bf_ref, zf_ref, ef_ref, pf_ref, sf_ref, cr_ref, br_ref, zr_ref, er_ref, pr_ref, sr_ref,
     in_ref, copy_ref, out_ref) = refs
    width = inner // heads
    r = lax.broadcasted_iota(jnp.int32, (256, 256), 0) // width
    c = lax.broadcasted_iota(jnp.int32, (256, 256), 1) // width
    mean = jnp.where(r == c, 1.0 / width, 0.0).astype(BF16)
    copy = copy_ref[...]
    both = None
    for k, (c_ref, b_ref, z_ref, e_ref, p_ref, s_ref) in enumerate(
            ((cf_ref, bf_ref, zf_ref, ef_ref, pf_ref, sf_ref), (cr_ref, br_ref, zr_ref, er_ref, pr_ref, sr_ref))):
        entering = (e_ref[0].astype(F32) + p_ref[0, :1, :] * in_ref[k]).astype(BF16)
        reads = jnp.dot(c_ref[...], entering, preferred_element_type=F32)
        grown = spread(jnp.exp(jnp.minimum(s_ref[...], 0.0)), copy)
        out = b_ref[...].astype(F32) + reads * grown
        gated = out * silu(z_ref[...].astype(F32))
        squares = (gated * gated).astype(BF16)
        means = jnp.concatenate(
            [jnp.dot(squares[:, g : g + 256], mean, preferred_element_type=F32) for g in range(0, inner, 256)], axis=1)
        result = gated * lax.rsqrt(means + EPS)
        both = result if both is None else both + result
    out_ref[...] = both.astype(BF16)


def finish(chunks, strands, entering, copy, heads, inner):
    count, at = chunks
    last = strands[0][0].shape[1] // STATE - 1
    by_rows = lambda width: pl.BlockSpec((CHUNK, width), lambda i: (at(i), 0))
    one = [pl.BlockSpec((CHUNK, STATE), lambda i: (at(i), last)), by_rows(inner), by_rows(inner),
           pl.BlockSpec((1, STATE, inner), lambda i: (at(i), 0, 0)),
           pl.BlockSpec((1, 8, inner), lambda i: (at(i), 0, 0)), by_rows(128)]
    return pl.pallas_call(
        functools.partial(finish_kernel, heads, inner),
        grid=(count,),
        in_specs=one + one + [whole((2, STATE, inner)), whole(copy.shape)],
        out_specs=pl.BlockSpec((CHUNK, inner), lambda i: (i, 0)),
        out_shape=jax.ShapeDtypeStruct((count * CHUNK, inner), BF16),
        compiler_params=params(),
        cost_estimate=cost(8e9 * count / 16, 10e6),
        name="finish",
    )(*strands[0], *strands[1], entering, copy)


def hop_kernel(first, final, *refs):
    upper_ref, mine_ref, other_ref = refs[:3]
    into_ref = None if first else refs[3]
    outs = refs[3:] if first else refs[4:]
    upper = upper_ref[0].astype(F32)
    for k in (0, 1):
        later = upper if k == 0 else 1.0 - upper
        at = k * (STATE + TAIL)

        def read(ref):
            tail = ref[at + STATE : at + STATE + TAIL, :].astype(F32)
            return ref[at : at + STATE, :].astype(F32), tail[0:1] + tail[1:2] + tail[2:3]

        o_state, o_log = read(other_ref)
        if first:
            new_state, new_log = later * o_state, later * o_log
        else:
            into_log = into_ref[k, STATE : STATE + 1, :]
            new_state = into_ref[k, :STATE, :] + later * jnp.exp(into_log) * o_state
            new_log = into_log + later * o_log
        if final:
            outs[0][k] = new_state
            continue
        outs[0][k, :STATE, :] = new_state
        outs[0][k, STATE:, :] = jnp.broadcast_to(new_log, (8, new_log.shape[1]))
        state, log = read(mine_ref)
        of_other = later * jnp.exp(log) + (1.0 - later)
        of_mine = later + (1.0 - later) * jnp.exp(o_log)
        outs[1][at : at + STATE, :] = (of_other * o_state + of_mine * state).astype(BF16)
        t = log + o_log
        high = t.astype(BF16).astype(F32)
        mid = (t - high).astype(BF16).astype(F32)
        low = t - high - mid
        row = lax.broadcasted_iota(jnp.int32, (TAIL, t.shape[1]), 0)
        packed = jnp.where(row == 0, high, jnp.where(row == 1, mid, jnp.where(row == 2, low, 0.0)))
        outs[1][at + STATE : at + STATE + TAIL, :] = packed.astype(BF16)


def hop(upper, mine, other, into, final):
    inner = mine.shape[1]
    first = into is None
    smem = pl.BlockSpec(memory_space=pltpu.SMEM)
    if final:
        out_shape = [jax.ShapeDtypeStruct((2, STATE, inner), F32)]
    else:
        out_shape = [jax.ShapeDtypeStruct((2, STATE + 8, inner), F32), jax.ShapeDtypeStruct(mine.shape, BF16)]
    operands = [mine, other] + ([] if first else [into])
    return pl.pallas_call(
        functools.partial(hop_kernel, first, final),
        grid=(1,),
        in_specs=[smem] + [whole(x.shape) for x in operands],
        out_specs=[whole(x.shape) for x in out_shape],
        out_shape=out_shape,
        compiler_params=params(),
        cost_estimate=cost(1e6, 1.5e6),
        name="hop",
    )(upper, *operands)


def incoming(message, axis):
    count, index = lax.axis_size(axis), lax.axis_index(axis)
    into = None
    distance = 1
    while distance < count:
        other = lax.ppermute(message, axis, [(i, i ^ distance) for i in range(count)])
        upper = ((index // distance) % 2).astype(jnp.int32).reshape(1)
        final = 2 * distance >= count
        result = hop(upper, message, other, into, final)
        if final:
            return result[0]
        into, message = result
        distance *= 2


def shifted(block, axis, distance):
    devices = range(lax.axis_size(axis))
    return lax.ppermute(block, axis, [(i - distance, i) for i in devices if i - distance in devices])


def on_device(
    hidden, norm_gain, w_zx, w_bc, w_dt, dt_bias, decay_rate, skip_gain, conv_x, conv_bc, w_out
):
    rows, depth = hidden.shape
    inner = conv_x.shape[1]
    heads = dt_bias.shape[0]
    width = inner // heads
    n_ctx, n_head = lax.axis_size("ctx"), lax.axis_size("head")
    ctx, head = lax.axis_index("ctx"), lax.axis_index("head")

    rim_f = shifted(hidden[rows - RIM :], "ctx", 1)
    rim_r = shifted(hidden[:RIM], "ctx", -1)

    part = w_out.shape[0] // n_ctx
    own = lax.dynamic_slice_in_dim(w_out, ctx * part, part, 0)
    gathered = lax.all_gather(own, ("ctx", "head"), axis=0)
    gathered = gathered.reshape(n_ctx, n_head, part, depth)

    pad = lambda v: jnp.pad(v, [(0, 0)] * (v.ndim - 1) + [(0, 128 - heads)])
    w_f, w_r = prepare(w_zx, w_bc, pad(w_dt), norm_gain[:, None])
    conv = jnp.concatenate([conv_x, conv_bc], axis=1)
    skip = jnp.repeat(skip_gain, width)[None, :]
    copy_first = spread_matrix(0, heads, width)
    copy_second = spread_matrix(heads, heads, width)
    (act_f, z_f, small_f, cumt_f, enter_f, prior_f, act_r, z_r, small_r, cumt_r, enter_r, prior_r,
     message) = project(hidden, rim_f, rim_r, w_f, w_r, conv, pad(dt_bias)[None, :], pad(decay_rate)[None, :],
                        copy_first, heads, inner)
    entering = incoming(message, "ctx")
    base_f, base_r = inside(((act_f, small_f, cumt_f), (act_r, small_r, cumt_r)), skip, copy_first, heads, inner)

    share = rows // n_head
    per_share = share // CHUNK
    pieces = 2 if per_share % 2 == 0 else 1
    per_piece = per_share // pieces
    w_groups = gathered.transpose(1, 0, 2, 3).reshape(n_head, n_ctx * part, depth)
    own_rows = lax.dynamic_slice_in_dim(hidden, head * share, share, 0)
    outs = []
    for k in range(pieces):
        chunks = (n_head * per_piece, lambda i, k=k: (i // per_piece) * per_share + k * per_piece + i % per_piece)
        combined = finish(chunks, ((act_f, base_f, z_f, enter_f, prior_f, small_f),
                                   (act_r, base_r, z_r, enter_r, prior_r, small_r)),
                          entering, copy_second, heads, inner)
        size = per_piece * CHUNK
        total = own_rows[k * size : (k + 1) * size].astype(F32)
        for d in range(n_head):
            block = lax.dynamic_slice_in_dim(combined, ((head + d) % n_head) * size, size, 0)
            if d:
                block = lax.ppermute(block, "head", [(i, (i + d) % n_head) for i in range(n_head)])
            source = (head - d) % n_head
            weights = lax.dynamic_index_in_dim(w_groups, source, 0, keepdims=False)
            total = total + jnp.dot(block, weights, preferred_element_type=F32)
        outs.append(total.astype(BF16))
    return jnp.concatenate(outs, axis=0)


def solution(mesh):
    placed = (
        P("ctx", None),
        P(),
        P(None, None, "head"),
        P(),
        P(None, "head"),
        P("head"),
        P("head"),
        P("head"),
        P(None, "head"),
        P(),
        P("head", None),
    )
    return jax.shard_map(
        on_device, mesh=mesh, in_specs=placed, out_specs=P(("ctx", "head"), None), check_vma=False
    )
```

```python
import functools

import jax
import jax.numpy as jnp
import numpy as np
from jax import lax
from jax.experimental import pallas as pl
from jax.experimental.pallas import tpu as pltpu
from jax.sharding import PartitionSpec as P

STATE = 128
CHUNK = 128
TILE = 256
EPS = 1e-05
RIM = 16
TAIL = 16
F32 = jnp.float32
BF16 = jnp.bfloat16
MIB = 2**20


def params(limit):
    return pltpu.CompilerParams(
        dimension_semantics=("arbitrary",), vmem_limit_bytes=limit * MIB
    )


def cost(flops, bytes_accessed):
    return pl.CostEstimate(flops=int(flops), bytes_accessed=int(bytes_accessed), transcendentals=0)


def whole(shape):
    return pl.BlockSpec(shape, lambda *_: (0,) * len(shape), pipeline_mode=pl.Buffered(1))


def silu(x):
    half = 0.5 * x
    return half + half * jnp.tanh(half)


def tri(rows, reverse):
    r = lax.broadcasted_iota(jnp.int32, (rows, rows), 0)
    c = lax.broadcasted_iota(jnp.int32, (rows, rows), 1)
    return (r <= c) if reverse else (r >= c)


def spread_matrix(first, heads, width):
    r = np.arange(2 * 128)[:, None] % 128
    c = np.arange(heads * width)[None, :] // width
    return jnp.asarray((r == c + first).astype(BF16))


def spread(q, matrix):
    high = q.astype(BF16)
    low = (q - high.astype(F32)).astype(BF16)
    return jnp.dot(jnp.concatenate([high, low], axis=1), matrix, preferred_element_type=F32)


def prepare_kernel(inner, zx_ref, bc_ref, dt_ref, gain_ref, wf_ref, wr_ref, gf_ref, gr_ref):
    rows = zx_ref.shape[0]
    gain = jnp.transpose(jnp.broadcast_to(gain_ref[...], (128, rows)))
    zx = zx_ref[...].astype(F32).reshape(rows, 2 * inner)
    steps = dt_ref[...].astype(F32)
    steps = jnp.transpose(jnp.concatenate([steps, jnp.zeros((128 - steps.shape[0], rows), F32)], axis=0))
    r = lax.broadcasted_iota(jnp.int32, (rows, rows), 0)
    c = lax.broadcasted_iota(jnp.int32, (rows, rows), 1)
    turn = (r + c == rows - 1).astype(BF16)

    def put(part, at, forward_ref, turned_ref):
        size = part.shape[1]
        scaled = jnp.concatenate([part[:, g : g + 128] * gain for g in range(0, size, 128)], axis=1).astype(BF16)
        forward_ref[:, at : at + size] = scaled
        turned_ref[:, at : at + size] = jnp.dot(turn, scaled, preferred_element_type=F32).astype(BF16)

    put(zx[:, inner:], 0, wf_ref, wr_ref)
    put(bc_ref[...].astype(F32), inner, wf_ref, wr_ref)
    put(steps, inner + bc_ref.shape[1], wf_ref, wr_ref)
    put(zx[:, :inner], 0, gf_ref, gr_ref)


def prepare(w_zx, w_bc, w_dt, gain):
    depth, _, inner = w_zx.shape
    tile = min(256, depth)
    n = depth // tile
    wide = inner + w_bc.shape[1] + 128
    forward, turned = (lambda i: (i, 0)), (lambda i: (n - 1 - i, 0))
    return pl.pallas_call(
        functools.partial(prepare_kernel, inner),
        grid=(n,),
        in_specs=[pl.BlockSpec((tile, 2, inner), lambda i: (i, 0, 0)),
                  pl.BlockSpec((tile, w_bc.shape[1]), forward),
                  pl.BlockSpec((w_dt.shape[1], tile), lambda i: (0, i)),
                  pl.BlockSpec((1, tile), lambda i: (0, i))],
        out_specs=[pl.BlockSpec((tile, wide), forward), pl.BlockSpec((tile, wide), turned),
                   pl.BlockSpec((tile, inner), forward), pl.BlockSpec((tile, inner), turned)],
        out_shape=[jax.ShapeDtypeStruct((depth, wide), BF16)] * 2 + [jax.ShapeDtypeStruct((depth, inner), BF16)] * 2,
        compiler_params=params(58),
        cost_estimate=cost(4e9, 8e6),
        name="prepare",
    )(w_zx, w_bc, w_dt.T, gain[None, :])


def row_scale(h):
    hf = h.astype(F32)
    return lax.rsqrt(jnp.mean(hf * hf, axis=-1, keepdims=True) + EPS)


def project_kernel(heads, inner, *refs):
    (hf_ref, hr_ref, rimf_ref, rimr_ref, wf_ref, wr_ref, convx_ref, convbc_ref, lanes_ref, copy_ref,
     actf_ref, smallf_ref, cumtf_ref, enterf_ref, priorf_ref,
     actr_ref, smallr_ref, cumtr_ref, enterr_ref, priorr_ref,
     msg_ref, buff, bufr, statef, stater, totalf, totalr) = refs
    step = pl.program_id(0)
    last = pl.num_programs(0) - 1
    stream = inner + 2 * STATE
    blocks = stream // 128
    rows = hf_ref.shape[0]
    count = rows // CHUNK
    sides = (
        (False, hf_ref, rimf_ref, wf_ref, actf_ref, smallf_ref, cumtf_ref, enterf_ref, priorf_ref, buff, statef, totalf),
        (True, hr_ref, rimr_ref, wr_ref, actr_ref, smallr_ref, cumtr_ref, enterr_ref, priorr_ref, bufr, stater, totalr),
    )

    @pl.when(step == 0)
    def _():
        for reverse, _, rim_ref, w_ref, _, _, _, _, _, buf, state, total in sides:
            edge = rows if reverse else 0
            state[...] = jnp.zeros_like(state)
            total[...] = jnp.zeros_like(total)
            rim = rim_ref[...]
            out = jnp.dot(rim, w_ref[:, :stream], preferred_element_type=F32) * row_scale(rim)
            for j in range(blocks):
                part = out[:, j * 128 : (j + 1) * 128]
                buf[j, edge : edge + 8, :] = part[:8] if reverse else part[RIM - 8 :]

    lane = lax.broadcasted_iota(jnp.int32, (rows, 128), 1)
    row8 = lax.broadcasted_iota(jnp.int32, (8, 128), 0)
    r = lax.broadcasted_iota(jnp.int32, (rows, rows), 0)
    c = lax.broadcasted_iota(jnp.int32, (rows, rows), 1)
    same = r // CHUNK == c // CHUNK
    hs = [side[1][...] for side in sides]
    scales = [row_scale(h) for h in hs]
    tail_rows, aux_rows = [], []
    for k, (reverse, _, _, w_ref, _, small_ref, cumt_ref, _, _, _, _, total_ref) in enumerate(sides):
        raw = jnp.dot(hs[k], w_ref[:, stream:], preferred_element_type=F32) * scales[k] + lanes_ref[0:1, :]
        dt = jnp.maximum(raw, 0.0) + jnp.log1p(jnp.exp(-jnp.abs(raw)))
        dt = jnp.where(lane < heads, dt, 0.0)
        steps = -lanes_ref[1:2, :] * dt
        high = steps.astype(BF16).astype(F32)
        mid = (steps - high).astype(BF16).astype(F32)
        low = steps - high - mid
        packed = (high + pltpu.roll(mid, heads, 1) + pltpu.roll(low, 2 * heads, 1)).astype(BF16)
        mask = jnp.where(jnp.logical_and(same, (r <= c) if reverse else (r >= c)), 1.0, 0.0).astype(BF16)
        sums = jnp.dot(mask, packed, preferred_element_type=F32)
        sums = sums + pltpu.roll(sums, 128 - heads, 1) + pltpu.roll(sums, 128 - 2 * heads, 1)
        cum = jnp.where(lane < heads, sums, 0.0)
        small_ref[...] = dt + pltpu.roll(cum, heads, 1)
        running = total_ref[...]
        tails = [None] * count
        aux = [None] * count
        for i in range(count):
            n = count - 1 - i if reverse else i
            at = slice(n * CHUNK, (n + 1) * CHUNK)
            cumt_ref[:, at] = jnp.transpose(cum[at])[:heads]
            end = cum[n * CHUNK : n * CHUNK + 1] if reverse else cum[(n + 1) * CHUNK - 1 : (n + 1) * CHUNK]
            tails[n] = dt[at] * jnp.exp(end - cum[at])
            aux[n] = jnp.where(row8 == 0, jnp.exp(end), jnp.exp(running))
            running = running + end
        total_ref[...] = running
        tail_rows += tails
        aux_rows += aux
    weights = spread(jnp.concatenate(tail_rows + aux_rows, axis=0), copy_ref[...])

    for g in range(0, stream, 256):
        for k, (reverse, _, _, w_ref, act_ref, _, _, _, _, buf, _, _) in enumerate(sides):
            edge = rows if reverse else 0
            body = 0 if reverse else 8
            out = jnp.dot(hs[k], w_ref[:, g : g + 256], preferred_element_type=F32) * scales[k]
            for j in range(g // 128, g // 128 + 2):
                x = out[:, j * 128 - g : (j + 1) * 128 - g]
                buf[j, body : body + rows, :] = x
                own = j * 128 - (0 if j * 128 < inner else inner)
                taps = (convx_ref if j * 128 < inner else convbc_ref)[:, own : own + 128]
                total = taps[3:4] * x
                for d in (1, 2, 3):
                    at = body + d if reverse else body - d
                    total = total + taps[3 - d : 4 - d] * buf[j, at : at + rows, :]
                act_ref[:, j * 128 : (j + 1) * 128] = silu(total).astype(BF16)
                buf[j, edge : edge + 8, :] = x[:8] if reverse else x[rows - 8 :]

    for i in range(count):
        for k, (reverse, _, _, _, act_ref, _, _, enter_ref, prior_ref, _, state, _) in enumerate(sides):
            n = count - 1 - i if reverse else i
            at = slice(n * CHUNK, (n + 1) * CHUNK)
            own = weights[(k * count + n) * CHUNK : (k * count + n + 1) * CHUNK]
            aux = weights[2 * rows + (k * count + n) * 8 : 2 * rows + (k * count + n + 1) * 8]
            tails = (act_ref[at, :inner].astype(F32) * own).astype(BF16)
            ends = lax.dot_general(act_ref[at, inner : inner + STATE], tails, (((0,), (0,)), ((), ())),
                                   preferred_element_type=F32)
            before = state[...]
            enter_ref[n] = before.astype(BF16)
            prior_ref[n] = aux
            state[...] = before * aux[:1] + ends

    @pl.when(step == last)
    def _():
        for k, side in enumerate(sides):
            state, total = side[-2:]
            at = k * (STATE + TAIL)
            msg_ref[at : at + STATE, :] = state[...].astype(BF16)
            t = total[...]
            high = t.astype(BF16).astype(F32)
            mid = (t - high).astype(BF16).astype(F32)
            low = t - high - mid
            packed = jnp.where(row8 == 0, high, jnp.where(row8 == 1, mid, jnp.where(row8 == 2, low, 0.0)))
            rows3 = spread(packed, copy_ref[...])
            msg_ref[at + STATE : at + STATE + TAIL, :] = jnp.concatenate(
                [rows3, jnp.zeros_like(rows3)], axis=0).astype(BF16)


def project(hidden, rim_f, rim_r, w_f, w_r, conv_x, conv_bc, lanes, copy, heads, inner):
    rows, depth = hidden.shape
    stream = inner + 2 * STATE
    n = rows // TILE
    per = TILE // CHUNK
    up, down = (lambda i: i), (lambda i: n - 1 - i)
    by_rows = lambda width, at: pl.BlockSpec((TILE, width), lambda i: (at(i), 0))
    out_specs, out_shape = [], []
    for at in (up, down):
        out_specs += [by_rows(stream, at), by_rows(128, at),
                      pl.BlockSpec((heads, TILE), lambda i, at=at: (0, at(i))),
                      pl.BlockSpec((per, STATE, inner), lambda i, at=at: (at(i), 0, 0)),
                      pl.BlockSpec((per, 8, inner), lambda i, at=at: (at(i), 0, 0))]
        out_shape += [jax.ShapeDtypeStruct((rows, stream), BF16),
                      jax.ShapeDtypeStruct((rows, 128), F32), jax.ShapeDtypeStruct((heads, rows), F32),
                      jax.ShapeDtypeStruct((n * per, STATE, inner), BF16),
                      jax.ShapeDtypeStruct((n * per, 8, inner), F32)]
    message = (2 * (STATE + TAIL), inner)
    buf = pltpu.VMEM((stream // 128, TILE + 8, 128), F32)
    state, total = pltpu.VMEM((STATE, inner), F32), pltpu.VMEM((8, 128), F32)
    return pl.pallas_call(
        functools.partial(project_kernel, heads, inner),
        grid=(n,),
        in_specs=[by_rows(depth, up), by_rows(depth, down), whole(rim_f.shape), whole(rim_r.shape),
                  whole(w_f.shape), whole(w_r.shape), whole(conv_x.shape), whole(conv_bc.shape), whole(lanes.shape),
                  whole(copy.shape)],
        out_specs=out_specs + [whole(message)],
        out_shape=out_shape + [jax.ShapeDtypeStruct(message, BF16)],
        scratch_shapes=[buf, buf, state, state, total, total],
        compiler_params=params(58),
        cost_estimate=cost(22e9, 40e6),
        name="project",
    )(hidden, hidden, rim_f, rim_r, w_f, w_r, conv_x, conv_bc, lanes, copy)


def gates_kernel(h_ref, wf_ref, wr_ref, zf_ref, zr_ref):
    h = h_ref[...]
    scale = row_scale(h)
    for w_ref, z_ref in ((wf_ref, zf_ref), (wr_ref, zr_ref)):
        z_ref[...] = (jnp.dot(h, w_ref[...], preferred_element_type=F32) * scale).astype(BF16)


def gates(hidden, w_f, w_r):
    rows, depth = hidden.shape
    inner = w_f.shape[1]
    by_rows = lambda width: pl.BlockSpec((TILE, width), lambda i: (i, 0))
    return pl.pallas_call(
        gates_kernel,
        grid=(rows // TILE,),
        in_specs=[by_rows(depth), whole(w_f.shape), whole(w_r.shape)],
        out_specs=[by_rows(inner)] * 2,
        out_shape=[jax.ShapeDtypeStruct((rows, inner), BF16)] * 2,
        compiler_params=params(58),
        cost_estimate=cost(10e9, 10e6),
        name="gates",
    )(hidden, w_f, w_r)


def inside_kernel(heads, inner, actf_ref, smallf_ref, cumtf_ref, actr_ref, smallr_ref, cumtr_ref, lanes_ref, copy_ref,
                  basef_ref, baser_ref):
    width = inner // heads
    per = 128 // width
    size = actf_ref.shape[0]
    lane = lax.broadcasted_iota(jnp.int32, (size, 128), 1)
    group = lax.broadcasted_iota(jnp.int32, (CHUNK, 128), 1) // width
    dts = [jnp.where(lane < heads, ref[...], 0.0) for ref in (smallf_ref, smallr_ref)]
    wide = spread(jnp.concatenate(dts + [jnp.broadcast_to(lanes_ref[2:3, :], (8, 128))], axis=0), copy_ref[...])
    skip = wide[2 * size : 2 * size + 1]
    sides = ((False, actf_ref, smallf_ref, cumtf_ref, basef_ref), (True, actr_ref, smallr_ref, cumtr_ref, baser_ref))
    for c in range(0, size, CHUNK):
        rows = slice(c, c + CHUNK)
        for k, (reverse, act_ref, small_ref, cumt_ref, base_ref) in enumerate(sides):
            small = small_ref[rows, :]
            values = act_ref[rows, :inner].astype(F32)
            weighted = (values * wide[k * size + c : k * size + c + CHUNK]).astype(BF16)
            scores = lax.dot_general(act_ref[rows, inner + STATE :], act_ref[rows, inner : inner + STATE],
                                     (((1,), (1,)), ((), ())), preferred_element_type=F32)
            scores = jnp.where(tri(CHUNK, reverse), scores, 0.0)
            for p in range(inner // 128):
                cols = slice(p * 128, (p + 1) * 128)
                pair = weighted[:, cols]
                mixing, stacked = [], []
                for q in range(per):
                    h = p * per + q
                    gap = jnp.minimum(small[:, heads + h : heads + h + 1] - cumt_ref[h : h + 1, rows], 0.0)
                    mixing.append((scores * jnp.exp(gap)).astype(BF16))
                    stacked.append(jnp.where(group == q, pair, jnp.zeros_like(pair)))
                out = jnp.dot(jnp.concatenate(mixing, axis=1), jnp.concatenate(stacked, axis=0),
                              preferred_element_type=F32)
                base_ref[rows, cols] = (out + skip[:, cols] * values[:, cols]).astype(BF16)


def inside(tile, blocks, strands, lanes, copy, heads, inner, work):
    count, at = blocks
    columns = strands[0][0].shape[1]
    by_rows = lambda width: pl.BlockSpec((tile, width), lambda i: (at(i), 0))
    one = [by_rows(columns), by_rows(128), pl.BlockSpec((heads, tile), lambda i: (0, at(i)))]
    return pl.pallas_call(
        functools.partial(inside_kernel, heads, inner),
        grid=(count,),
        in_specs=one + one + [whole(lanes.shape), whole(copy.shape)],
        out_specs=[pl.BlockSpec((tile, inner), lambda i: (i, 0))] * 2,
        out_shape=[jax.ShapeDtypeStruct((count * tile, inner), BF16)] * 2,
        compiler_params=params(58),
        cost_estimate=cost(work, 1e6),
        name="inside",
    )(*strands[0], *strands[1], lanes, copy)


def finish_kernel(heads, inner, *refs):
    (cf_ref, zf_ref, ef_ref, pf_ref, sf_ref, cr_ref, zr_ref, er_ref, pr_ref, sr_ref, bf_ref, br_ref,
     in_ref, copy_ref, out_ref) = refs
    width = inner // heads
    size = cf_ref.shape[0]
    row = lax.broadcasted_iota(jnp.int32, (256, 256), 0) // width
    column = lax.broadcasted_iota(jnp.int32, (256, 256), 1) // width
    mean = jnp.where(row == column, 1.0 / width, 0.0).astype(BF16)
    grown = spread(jnp.exp(jnp.minimum(jnp.concatenate([sf_ref[...], sr_ref[...]], axis=0), 0.0)), copy_ref[...])
    both = None
    for k, (c_ref, b_ref, z_ref, e_ref, p_ref) in enumerate(
            ((cf_ref, bf_ref, zf_ref, ef_ref, pf_ref), (cr_ref, br_ref, zr_ref, er_ref, pr_ref))):
        parts = []
        for c in range(e_ref.shape[0]):
            entering = (e_ref[c].astype(F32) + p_ref[c, 1:2, :] * in_ref[k]).astype(BF16)
            parts.append(jnp.dot(c_ref[c * CHUNK : (c + 1) * CHUNK, :], entering, preferred_element_type=F32))
        reads = jnp.concatenate(parts, axis=0)
        out = b_ref[...].astype(F32) + reads * grown[k * size : (k + 1) * size]
        gated = out * silu(z_ref[...].astype(F32))
        squares = (gated * gated).astype(BF16)
        means = jnp.concatenate(
            [jnp.dot(squares[:, g : g + 256], mean, preferred_element_type=F32) for g in range(0, inner, 256)], axis=1)
        result = gated * lax.rsqrt(means + EPS)
        both = result if both is None else both + result
    out_ref[...] = both.astype(BF16)


def finish(tile, blocks, strands, bases, entering, copy, heads, inner):
    count, at = blocks
    per = tile // CHUNK
    last = strands[0][0].shape[1] // STATE - 1
    by_rows = lambda width: pl.BlockSpec((tile, width), lambda i: (at(i), 0))
    in_order = pl.BlockSpec((tile, inner), lambda i: (i, 0))
    one = [pl.BlockSpec((tile, STATE), lambda i: (at(i), last)), by_rows(inner),
           pl.BlockSpec((per, STATE, inner), lambda i: (at(i), 0, 0)),
           pl.BlockSpec((per, 8, inner), lambda i: (at(i), 0, 0)), by_rows(128)]
    return pl.pallas_call(
        functools.partial(finish_kernel, heads, inner),
        grid=(count,),
        in_specs=one + one + [in_order, in_order, whole((2, STATE, inner)), whole(copy.shape)],
        out_specs=in_order,
        out_shape=jax.ShapeDtypeStruct((count * tile, inner), BF16),
        compiler_params=params(58),
        cost_estimate=cost(1e8, 1e6),
        name="finish",
    )(*strands[0], *strands[1], *bases, entering, copy)


def read_message(ref, at):
    tail = ref[at + STATE : at + STATE + TAIL, :].astype(F32)
    return ref[at : at + STATE, :].astype(F32), tail[0:1] + tail[1:2] + tail[2:3]


def hop_kernel(first, *refs):
    upper_ref, mine_ref, other_ref = refs[:3]
    into_ref = None if first else refs[3]
    new_ref, msg_ref = refs[-2:]
    upper = upper_ref[0].astype(F32)
    for k in (0, 1):
        later = upper if k == 0 else 1.0 - upper
        at = k * (STATE + TAIL)
        o_state, o_log = read_message(other_ref, at)
        if first:
            new_state, new_log = later * o_state, later * o_log
        else:
            into_log = into_ref[k, STATE : STATE + 1, :]
            new_state = into_ref[k, :STATE, :] + later * jnp.exp(into_log) * o_state
            new_log = into_log + later * o_log
        new_ref[k, :STATE, :] = new_state
        new_ref[k, STATE:, :] = jnp.broadcast_to(new_log, (8, new_log.shape[1]))
        state, log = read_message(mine_ref, at)
        of_other = later * jnp.exp(log) + (1.0 - later)
        of_mine = later + (1.0 - later) * jnp.exp(o_log)
        msg_ref[at : at + STATE, :] = (of_other * o_state + of_mine * state).astype(BF16)
        t = log + o_log
        high = t.astype(BF16).astype(F32)
        mid = (t - high).astype(BF16).astype(F32)
        low = t - high - mid
        row = lax.broadcasted_iota(jnp.int32, (TAIL, t.shape[1]), 0)
        packed = jnp.where(row == 0, high, jnp.where(row == 1, mid, jnp.where(row == 2, low, 0.0)))
        msg_ref[at + STATE : at + STATE + TAIL, :] = packed.astype(BF16)


def local_call(kernel, name, smem, operands, out_shape):
    return pl.pallas_call(
        kernel,
        grid=(1,),
        in_specs=[pl.BlockSpec(memory_space=pltpu.SMEM)] + [whole(x.shape) for x in operands],
        out_specs=[whole(x.shape) for x in out_shape],
        out_shape=out_shape,
        compiler_params=params(10),
        cost_estimate=cost(1e6, 1.5e6),
        name=name,
    )(smem, *operands)


def join_kernel(count, *refs):
    place_ref, into_ref = refs[:2]
    slots, out_ref = refs[2:-1], refs[-1]
    place = place_ref[0]
    groups = [place ^ d for d in range(1, count)]
    read = [read_message(ref, 0) for ref in slots]
    ones = lambda condition: jnp.where(condition, 1.0, 0.0)
    sums = [None, None]
    for j, (state, _) in zip(groups, read):
        lower = ones(j < place)
        log = None
        for i, (_, other) in zip(groups, read):
            between = jnp.logical_or(jnp.logical_and(j < i, i < place), jnp.logical_and(place < i, i < j))
            term = ones(between) * other
            log = term if log is None else log + term
        part = jnp.exp(log) * state
        for k, share in enumerate((lower, 1.0 - lower)):
            sums[k] = share * part if sums[k] is None else sums[k] + share * part
    for k in (0, 1):
        out_ref[k] = into_ref[k, :STATE, :] + jnp.exp(into_ref[k, STATE : STATE + 1, :]) * sums[k]


def incoming(message, axis):
    count, index = lax.axis_size(axis), lax.axis_index(axis)
    inner = message.shape[1]
    into = None
    distance = 1
    while count // distance > 4:
        other = lax.ppermute(message, axis, [(i, i ^ distance) for i in range(count)])
        upper = ((index // distance) % 2).astype(jnp.int32).reshape(1)
        operands = [message, other] + ([] if into is None else [into])
        out_shape = [jax.ShapeDtypeStruct((2, STATE + 8, inner), F32), jax.ShapeDtypeStruct(message.shape, BF16)]
        into, message = local_call(functools.partial(hop_kernel, into is None), "hop", upper, operands, out_shape)
        distance *= 2
    if into is None:
        into = jnp.zeros((2, STATE + 8, inner), F32)
    groups = count // distance
    place = index // distance
    half = STATE + TAIL
    slots = []
    for d in range(1, groups):
        highest = 1 << (d.bit_length() - 1)
        above = (place // highest) % 2
        block = lax.dynamic_slice_in_dim(message, above * half, half, 0)
        slots.append(lax.ppermute(block, axis, [(i, i ^ (d * distance)) for i in range(count)]))
    return local_call(functools.partial(join_kernel, groups), "join", place.astype(jnp.int32).reshape(1), [into] + slots,
                      [jax.ShapeDtypeStruct((2, STATE, inner), F32)])[0]


def shifted(block, axis, distance):
    devices = range(lax.axis_size(axis))
    return lax.ppermute(block, axis, [(i - distance, i) for i in devices if i - distance in devices])


def on_device(
    hidden, norm_gain, w_zx, w_bc, w_dt, dt_bias, decay_rate, skip_gain, conv_x, conv_bc, w_out
):
    rows, depth = hidden.shape
    inner = conv_x.shape[1]
    heads = dt_bias.shape[0]
    width = inner // heads
    n_ctx, n_head = lax.axis_size("ctx"), lax.axis_size("head")
    ctx, head = lax.axis_index("ctx"), lax.axis_index("head")

    rim_f = shifted(hidden[rows - RIM :], "ctx", 1)
    rim_r = shifted(hidden[:RIM], "ctx", -1)

    part = w_out.shape[0] // n_ctx
    own = lax.dynamic_slice_in_dim(w_out, ctx * part, part, 0)
    gathered = lax.all_gather(own, ("ctx", "head"), axis=0)
    gathered = gathered.reshape(n_ctx, n_head, part, depth)

    w_f, w_r, g_f, g_r = prepare(w_zx, w_bc, w_dt, norm_gain)
    lanes = jnp.pad(jnp.stack([dt_bias, decay_rate, skip_gain]), [(0, 0), (0, 128 - heads)])
    copy_first = spread_matrix(0, heads, width)
    copy_second = spread_matrix(heads, heads, width)
    (act_f, small_f, cumt_f, enter_f, prior_f, act_r, small_r, cumt_r, enter_r, prior_r,
     message) = project(hidden, rim_f, rim_r, w_f, w_r, conv_x, conv_bc, lanes, copy_first, heads, inner)
    entering = incoming(message, "ctx")
    z_f, z_r = gates(hidden, g_f, g_r)

    share = rows // n_head
    pieces = 2 if share % (2 * CHUNK) == 0 else 1
    size = share // pieces
    tile = min(TILE, size)
    inner_blocks, share_blocks = size // tile, share // tile
    w_groups = gathered.transpose(1, 0, 2, 3).reshape(n_head, n_ctx * part, depth)
    own_rows = lax.dynamic_slice_in_dim(hidden, head * share, share, 0)
    arrived = [[None] * n_head for _ in range(pieces)]

    def rotated(blocks, d):
        return lax.ppermute(blocks, "head", [(i, (i + d) % n_head) for i in range(n_head)])

    combined = None
    for k in range(pieces):
        blocks = (n_head * inner_blocks,
                  lambda i, k=k: (i // inner_blocks) * share_blocks + k * inner_blocks + i % inner_blocks)
        if combined is not None:
            act_f, act_r, combined = lax.optimization_barrier((act_f, act_r, combined))
        bases = inside(tile, blocks, ((act_f, small_f, cumt_f), (act_r, small_r, cumt_r)), lanes, copy_first, heads, inner,
                       1e8 if k else 8e9)
        combined = finish(tile, blocks, ((act_f, z_f, enter_f, prior_f, small_f), (act_r, z_r, enter_r, prior_r, small_r)),
                          bases, entering, copy_second, heads, inner)
        if k:
            combined, *arrived[k - 1] = lax.optimization_barrier((combined, *arrived[k - 1]))
        for d in range(n_head):
            block = lax.dynamic_slice_in_dim(combined, ((head + d) % n_head) * size, size, 0)
            arrived[k][d] = rotated(block, d) if d else block
    outs = []
    for k in range(pieces):
        total = own_rows[k * size : (k + 1) * size].astype(F32)
        for d in range(n_head):
            weights = lax.dynamic_index_in_dim(w_groups, (head - d) % n_head, 0, keepdims=False)
            total = total + jnp.dot(arrived[k][d], weights, preferred_element_type=F32)
        outs.append(total.astype(BF16))
    return jnp.concatenate(outs, axis=0)


def solution(mesh):
    placed = (
        P("ctx", None),
        P(),
        P(None, None, "head"),
        P(),
        P(None, "head"),
        P("head"),
        P("head"),
        P("head"),
        P(None, "head"),
        P(),
        P("head", None),
    )
    return jax.shard_map(
        on_device, mesh=mesh, in_specs=placed, out_specs=P(("ctx", "head"), None), check_vma=False
    )
```

```python
import functools

import jax
import jax.numpy as jnp
import numpy as np
from jax import lax
from jax.experimental import pallas as pl
from jax.experimental.pallas import tpu as pltpu
from jax.sharding import PartitionSpec as P

STATE = 128
CHUNK = 128
TILE = 256
EPS = 1e-05
RIM = 16
TAIL = 16
F32 = jnp.float32
BF16 = jnp.bfloat16
MIB = 2**20


def params(limit):
    return pltpu.CompilerParams(
        dimension_semantics=("arbitrary",), vmem_limit_bytes=limit * MIB
    )


def cost(flops, bytes_accessed):
    return pl.CostEstimate(flops=int(flops), bytes_accessed=int(bytes_accessed), transcendentals=0)


def whole(shape):
    return pl.BlockSpec(shape, lambda *_: (0,) * len(shape), pipeline_mode=pl.Buffered(1))


def silu(x):
    half = 0.5 * x
    return half + half * jnp.tanh(half)


def tri(rows, reverse):
    r = lax.broadcasted_iota(jnp.int32, (rows, rows), 0)
    c = lax.broadcasted_iota(jnp.int32, (rows, rows), 1)
    return (r <= c) if reverse else (r >= c)


def spread_matrix(first, heads, width):
    r = np.arange(2 * 128)[:, None] % 128
    c = np.arange(heads * width)[None, :] // width
    return jnp.asarray((r == c + first).astype(BF16))


def spread(q, matrix):
    high = q.astype(BF16)
    low = (q - high.astype(F32)).astype(BF16)
    return jnp.dot(jnp.concatenate([high, low], axis=1), matrix, preferred_element_type=F32)


def prepare_kernel(inner, zx_ref, bc_ref, dt_ref, gain_ref, wf_ref, wr_ref, gf_ref, gr_ref):
    rows = zx_ref.shape[0]
    gain = jnp.transpose(jnp.broadcast_to(gain_ref[...], (128, rows)))
    zx = zx_ref[...].astype(F32).reshape(rows, 2 * inner)
    steps = dt_ref[...].astype(F32)
    steps = jnp.transpose(jnp.concatenate([steps, jnp.zeros((128 - steps.shape[0], rows), F32)], axis=0))
    r = lax.broadcasted_iota(jnp.int32, (rows, rows), 0)
    c = lax.broadcasted_iota(jnp.int32, (rows, rows), 1)
    turn = (r + c == rows - 1).astype(BF16)

    def put(part, at, forward_ref, turned_ref):
        size = part.shape[1]
        scaled = jnp.concatenate([part[:, g : g + 128] * gain for g in range(0, size, 128)], axis=1).astype(BF16)
        forward_ref[:, at : at + size] = scaled
        turned_ref[:, at : at + size] = jnp.dot(turn, scaled, preferred_element_type=F32).astype(BF16)

    put(zx[:, inner:], 0, wf_ref, wr_ref)
    put(bc_ref[...].astype(F32), inner, wf_ref, wr_ref)
    put(steps, inner + bc_ref.shape[1], wf_ref, wr_ref)
    put(zx[:, :inner], 0, gf_ref, gr_ref)


def prepare(w_zx, w_bc, w_dt, gain):
    depth, _, inner = w_zx.shape
    tile = min(256, depth)
    n = depth // tile
    wide = inner + w_bc.shape[1] + 128
    forward, turned = (lambda i: (i, 0)), (lambda i: (n - 1 - i, 0))
    return pl.pallas_call(
        functools.partial(prepare_kernel, inner),
        grid=(n,),
        in_specs=[pl.BlockSpec((tile, 2, inner), lambda i: (i, 0, 0)),
                  pl.BlockSpec((tile, w_bc.shape[1]), forward),
                  pl.BlockSpec((w_dt.shape[1], tile), lambda i: (0, i)),
                  pl.BlockSpec((1, tile), lambda i: (0, i))],
        out_specs=[pl.BlockSpec((tile, wide), forward), pl.BlockSpec((tile, wide), turned),
                   pl.BlockSpec((tile, inner), forward), pl.BlockSpec((tile, inner), turned)],
        out_shape=[jax.ShapeDtypeStruct((depth, wide), BF16)] * 2 + [jax.ShapeDtypeStruct((depth, inner), BF16)] * 2,
        compiler_params=params(58),
        cost_estimate=cost(4e9, 8e6),
        name="prepare",
    )(w_zx, w_bc, w_dt.T, gain[None, :])


def row_scale(h):
    hf = h.astype(F32)
    return lax.rsqrt(jnp.mean(hf * hf, axis=-1, keepdims=True) + EPS)


def project_kernel(heads, inner, *refs):
    (hf_ref, hr_ref, rimf_ref, rimr_ref, wf_ref, wr_ref, convx_ref, convbc_ref, lanes_ref, copy_ref,
     actf_ref, smallf_ref, cumtf_ref, enterf_ref, priorf_ref,
     actr_ref, smallr_ref, cumtr_ref, enterr_ref, priorr_ref,
     msg_ref, buff, bufr, statef, stater, totalf, totalr) = refs
    step = pl.program_id(0)
    last = pl.num_programs(0) - 1
    stream = inner + 2 * STATE
    blocks = stream // 128
    rows = hf_ref.shape[0]
    count = rows // CHUNK
    sides = (
        (False, hf_ref, rimf_ref, wf_ref, actf_ref, smallf_ref, cumtf_ref, enterf_ref, priorf_ref, buff, statef, totalf),
        (True, hr_ref, rimr_ref, wr_ref, actr_ref, smallr_ref, cumtr_ref, enterr_ref, priorr_ref, bufr, stater, totalr),
    )

    @pl.when(step == 0)
    def _():
        for reverse, _, rim_ref, w_ref, _, _, _, _, _, buf, state, total in sides:
            edge = rows if reverse else 0
            state[...] = jnp.zeros_like(state)
            total[...] = jnp.zeros_like(total)
            rim = rim_ref[...]
            out = jnp.dot(rim, w_ref[:, :stream], preferred_element_type=F32) * row_scale(rim)
            for j in range(blocks):
                part = out[:, j * 128 : (j + 1) * 128]
                buf[j, edge : edge + 8, :] = part[:8] if reverse else part[RIM - 8 :]

    lane = lax.broadcasted_iota(jnp.int32, (rows, 128), 1)
    row8 = lax.broadcasted_iota(jnp.int32, (8, 128), 0)
    r = lax.broadcasted_iota(jnp.int32, (rows, rows), 0)
    c = lax.broadcasted_iota(jnp.int32, (rows, rows), 1)
    same = r // CHUNK == c // CHUNK
    hs = [side[1][...] for side in sides]
    scales = [row_scale(h) for h in hs]
    tail_rows, aux_rows = [], []
    for k, (reverse, _, _, w_ref, _, small_ref, cumt_ref, _, _, _, _, total_ref) in enumerate(sides):
        raw = jnp.dot(hs[k], w_ref[:, stream:], preferred_element_type=F32) * scales[k] + lanes_ref[0:1, :]
        dt = jnp.maximum(raw, 0.0) + jnp.log1p(jnp.exp(-jnp.abs(raw)))
        dt = jnp.where(lane < heads, dt, 0.0)
        steps = -lanes_ref[1:2, :] * dt
        high = steps.astype(BF16).astype(F32)
        mid = (steps - high).astype(BF16).astype(F32)
        low = steps - high - mid
        packed = (high + pltpu.roll(mid, heads, 1) + pltpu.roll(low, 2 * heads, 1)).astype(BF16)
        mask = jnp.where(jnp.logical_and(same, (r <= c) if reverse else (r >= c)), 1.0, 0.0).astype(BF16)
        sums = jnp.dot(mask, packed, preferred_element_type=F32)
        sums = sums + pltpu.roll(sums, 128 - heads, 1) + pltpu.roll(sums, 128 - 2 * heads, 1)
        cum = jnp.where(lane < heads, sums, 0.0)
        small_ref[...] = dt + pltpu.roll(cum, heads, 1)
        running = total_ref[...]
        tails = [None] * count
        aux = [None] * count
        for i in range(count):
            n = count - 1 - i if reverse else i
            at = slice(n * CHUNK, (n + 1) * CHUNK)
            cumt_ref[:, at] = jnp.transpose(cum[at])[:heads]
            end = cum[n * CHUNK : n * CHUNK + 1] if reverse else cum[(n + 1) * CHUNK - 1 : (n + 1) * CHUNK]
            tails[n] = dt[at] * jnp.exp(end - cum[at])
            aux[n] = jnp.where(row8 == 0, jnp.exp(end), jnp.exp(running))
            running = running + end
        total_ref[...] = running
        tail_rows += tails
        aux_rows += aux
    weights = spread(jnp.concatenate(tail_rows + aux_rows, axis=0), copy_ref[...])

    for g in range(0, stream, 256):
        for k, (reverse, _, _, w_ref, act_ref, _, _, _, _, buf, _, _) in enumerate(sides):
            edge = rows if reverse else 0
            body = 0 if reverse else 8
            out = jnp.dot(hs[k], w_ref[:, g : g + 256], preferred_element_type=F32) * scales[k]
            for j in range(g // 128, g // 128 + 2):
                x = out[:, j * 128 - g : (j + 1) * 128 - g]
                buf[j, body : body + rows, :] = x
                own = j * 128 - (0 if j * 128 < inner else inner)
                taps = (convx_ref if j * 128 < inner else convbc_ref)[:, own : own + 128]
                total = taps[3:4] * x
                for d in (1, 2, 3):
                    at = body + d if reverse else body - d
                    total = total + taps[3 - d : 4 - d] * buf[j, at : at + rows, :]
                act_ref[:, j * 128 : (j + 1) * 128] = silu(total).astype(BF16)
                buf[j, edge : edge + 8, :] = x[:8] if reverse else x[rows - 8 :]

    for i in range(count):
        for k, (reverse, _, _, _, act_ref, _, _, enter_ref, prior_ref, _, state, _) in enumerate(sides):
            n = count - 1 - i if reverse else i
            at = slice(n * CHUNK, (n + 1) * CHUNK)
            own = weights[(k * count + n) * CHUNK : (k * count + n + 1) * CHUNK]
            aux = weights[2 * rows + (k * count + n) * 8 : 2 * rows + (k * count + n + 1) * 8]
            tails = (act_ref[at, :inner].astype(F32) * own).astype(BF16)
            ends = lax.dot_general(act_ref[at, inner : inner + STATE], tails, (((0,), (0,)), ((), ())),
                                   preferred_element_type=F32)
            before = state[...]
            enter_ref[n] = before.astype(BF16)
            prior_ref[n] = aux
            state[...] = before * aux[:1] + ends

    @pl.when(step == last)
    def _():
        for k, side in enumerate(sides):
            state, total = side[-2:]
            at = k * (STATE + TAIL)
            msg_ref[at : at + STATE, :] = state[...].astype(BF16)
            t = total[...]
            high = t.astype(BF16).astype(F32)
            mid = (t - high).astype(BF16).astype(F32)
            low = t - high - mid
            packed = jnp.where(row8 == 0, high, jnp.where(row8 == 1, mid, jnp.where(row8 == 2, low, 0.0)))
            rows3 = spread(packed, copy_ref[...])
            msg_ref[at + STATE : at + STATE + TAIL, :] = jnp.concatenate(
                [rows3, jnp.zeros_like(rows3)], axis=0).astype(BF16)


def project(hidden, rim_f, rim_r, w_f, w_r, conv_x, conv_bc, lanes, copy, heads, inner):
    rows, depth = hidden.shape
    stream = inner + 2 * STATE
    n = rows // TILE
    per = TILE // CHUNK
    up, down = (lambda i: i), (lambda i: n - 1 - i)
    by_rows = lambda width, at: pl.BlockSpec((TILE, width), lambda i: (at(i), 0))
    out_specs, out_shape = [], []
    for at in (up, down):
        out_specs += [by_rows(stream, at), by_rows(128, at),
                      pl.BlockSpec((heads, TILE), lambda i, at=at: (0, at(i))),
                      pl.BlockSpec((per, STATE, inner), lambda i, at=at: (at(i), 0, 0)),
                      pl.BlockSpec((per, 8, inner), lambda i, at=at: (at(i), 0, 0))]
        out_shape += [jax.ShapeDtypeStruct((rows, stream), BF16),
                      jax.ShapeDtypeStruct((rows, 128), F32), jax.ShapeDtypeStruct((heads, rows), F32),
                      jax.ShapeDtypeStruct((n * per, STATE, inner), BF16),
                      jax.ShapeDtypeStruct((n * per, 8, inner), F32)]
    message = (2 * (STATE + TAIL), inner)
    buf = pltpu.VMEM((stream // 128, TILE + 8, 128), F32)
    state, total = pltpu.VMEM((STATE, inner), F32), pltpu.VMEM((8, 128), F32)
    return pl.pallas_call(
        functools.partial(project_kernel, heads, inner),
        grid=(n,),
        in_specs=[by_rows(depth, up), by_rows(depth, down), whole(rim_f.shape), whole(rim_r.shape),
                  whole(w_f.shape), whole(w_r.shape), whole(conv_x.shape), whole(conv_bc.shape), whole(lanes.shape),
                  whole(copy.shape)],
        out_specs=out_specs + [whole(message)],
        out_shape=out_shape + [jax.ShapeDtypeStruct(message, BF16)],
        scratch_shapes=[buf, buf, state, state, total, total],
        compiler_params=params(58),
        cost_estimate=cost(22e9, 40e6),
        name="project",
    )(hidden, hidden, rim_f, rim_r, w_f, w_r, conv_x, conv_bc, lanes, copy)


def gates_kernel(h_ref, wf_ref, wr_ref, zf_ref, zr_ref):
    h = h_ref[...]
    scale = row_scale(h)
    for w_ref, z_ref in ((wf_ref, zf_ref), (wr_ref, zr_ref)):
        z_ref[...] = (jnp.dot(h, w_ref[...], preferred_element_type=F32) * scale).astype(BF16)


def gates(hidden, w_f, w_r):
    rows, depth = hidden.shape
    inner = w_f.shape[1]
    by_rows = lambda width: pl.BlockSpec((TILE, width), lambda i: (i, 0))
    return pl.pallas_call(
        gates_kernel,
        grid=(rows // TILE,),
        in_specs=[by_rows(depth), whole(w_f.shape), whole(w_r.shape)],
        out_specs=[by_rows(inner)] * 2,
        out_shape=[jax.ShapeDtypeStruct((rows, inner), BF16)] * 2,
        compiler_params=params(58),
        cost_estimate=cost(10e9, 10e6),
        name="gates",
    )(hidden, w_f, w_r)


def inside_kernel(heads, inner, actf_ref, smallf_ref, cumtf_ref, actr_ref, smallr_ref, cumtr_ref, lanes_ref, copy_ref,
                  basef_ref, baser_ref):
    width = inner // heads
    per = 128 // width
    size = actf_ref.shape[0]
    lane = lax.broadcasted_iota(jnp.int32, (size, 128), 1)
    group = lax.broadcasted_iota(jnp.int32, (CHUNK, 128), 1) // width
    dts = [jnp.where(lane < heads, ref[...], 0.0) for ref in (smallf_ref, smallr_ref)]
    wide = spread(jnp.concatenate(dts + [jnp.broadcast_to(lanes_ref[2:3, :], (8, 128))], axis=0), copy_ref[...])
    skip = wide[2 * size : 2 * size + 1]
    sides = ((False, actf_ref, smallf_ref, cumtf_ref, basef_ref), (True, actr_ref, smallr_ref, cumtr_ref, baser_ref))
    for c in range(0, size, CHUNK):
        rows = slice(c, c + CHUNK)
        for k, (reverse, act_ref, small_ref, cumt_ref, base_ref) in enumerate(sides):
            small = small_ref[rows, :]
            values = act_ref[rows, :inner].astype(F32)
            weighted = (values * wide[k * size + c : k * size + c + CHUNK]).astype(BF16)
            scores = lax.dot_general(act_ref[rows, inner + STATE :], act_ref[rows, inner : inner + STATE],
                                     (((1,), (1,)), ((), ())), preferred_element_type=F32)
            scores = jnp.where(tri(CHUNK, reverse), scores, 0.0)
            for p in range(inner // 128):
                cols = slice(p * 128, (p + 1) * 128)
                pair = weighted[:, cols]
                mixing, stacked = [], []
                for q in range(per):
                    h = p * per + q
                    gap = jnp.minimum(small[:, heads + h : heads + h + 1] - cumt_ref[h : h + 1, rows], 0.0)
                    mixing.append((scores * jnp.exp(gap)).astype(BF16))
                    stacked.append(jnp.where(group == q, pair, jnp.zeros_like(pair)))
                out = jnp.dot(jnp.concatenate(mixing, axis=1), jnp.concatenate(stacked, axis=0),
                              preferred_element_type=F32)
                base_ref[rows, cols] = (out + skip[:, cols] * values[:, cols]).astype(BF16)


def inside(tile, blocks, strands, lanes, copy, heads, inner, work):
    count, at = blocks
    columns = strands[0][0].shape[1]
    by_rows = lambda width: pl.BlockSpec((tile, width), lambda i: (at(i), 0))
    one = [by_rows(columns), by_rows(128), pl.BlockSpec((heads, tile), lambda i: (0, at(i)))]
    return pl.pallas_call(
        functools.partial(inside_kernel, heads, inner),
        grid=(count,),
        in_specs=one + one + [whole(lanes.shape), whole(copy.shape)],
        out_specs=[pl.BlockSpec((tile, inner), lambda i: (i, 0))] * 2,
        out_shape=[jax.ShapeDtypeStruct((count * tile, inner), BF16)] * 2,
        compiler_params=params(58),
        cost_estimate=cost(work, 1e6),
        name="inside",
    )(*strands[0], *strands[1], lanes, copy)


def finish_kernel(heads, inner, *refs):
    (cf_ref, zf_ref, ef_ref, pf_ref, sf_ref, cr_ref, zr_ref, er_ref, pr_ref, sr_ref, bf_ref, br_ref,
     in_ref, copy_ref, out_ref) = refs
    width = inner // heads
    size = cf_ref.shape[0]
    row = lax.broadcasted_iota(jnp.int32, (256, 256), 0) // width
    column = lax.broadcasted_iota(jnp.int32, (256, 256), 1) // width
    mean = jnp.where(row == column, 1.0 / width, 0.0).astype(BF16)
    grown = spread(jnp.exp(jnp.minimum(jnp.concatenate([sf_ref[...], sr_ref[...]], axis=0), 0.0)), copy_ref[...])
    both = None
    for k, (c_ref, b_ref, z_ref, e_ref, p_ref) in enumerate(
            ((cf_ref, bf_ref, zf_ref, ef_ref, pf_ref), (cr_ref, br_ref, zr_ref, er_ref, pr_ref))):
        parts = []
        for c in range(e_ref.shape[0]):
            entering = (e_ref[c].astype(F32) + p_ref[c, 1:2, :] * in_ref[k]).astype(BF16)
            parts.append(jnp.dot(c_ref[c * CHUNK : (c + 1) * CHUNK, :], entering, preferred_element_type=F32))
        reads = jnp.concatenate(parts, axis=0)
        out = b_ref[...].astype(F32) + reads * grown[k * size : (k + 1) * size]
        gated = out * silu(z_ref[...].astype(F32))
        squares = (gated * gated).astype(BF16)
        means = jnp.concatenate(
            [jnp.dot(squares[:, g : g + 256], mean, preferred_element_type=F32) for g in range(0, inner, 256)], axis=1)
        result = gated * lax.rsqrt(means + EPS)
        both = result if both is None else both + result
    out_ref[...] = both.astype(BF16)


def finish(tile, blocks, strands, bases, entering, copy, heads, inner):
    count, at = blocks
    per = tile // CHUNK
    last = strands[0][0].shape[1] // STATE - 1
    by_rows = lambda width: pl.BlockSpec((tile, width), lambda i: (at(i), 0))
    in_order = pl.BlockSpec((tile, inner), lambda i: (i, 0))
    one = [pl.BlockSpec((tile, STATE), lambda i: (at(i), last)), by_rows(inner),
           pl.BlockSpec((per, STATE, inner), lambda i: (at(i), 0, 0)),
           pl.BlockSpec((per, 8, inner), lambda i: (at(i), 0, 0)), by_rows(128)]
    return pl.pallas_call(
        functools.partial(finish_kernel, heads, inner),
        grid=(count,),
        in_specs=one + one + [in_order, in_order, whole((2, STATE, inner)), whole(copy.shape)],
        out_specs=in_order,
        out_shape=jax.ShapeDtypeStruct((count * tile, inner), BF16),
        compiler_params=params(58),
        cost_estimate=cost(1e8, 1e6),
        name="finish",
    )(*strands[0], *strands[1], *bases, entering, copy)


def read_message(ref, at):
    tail = ref[at + STATE : at + STATE + TAIL, :].astype(F32)
    return ref[at : at + STATE, :].astype(F32), tail[0:1] + tail[1:2] + tail[2:3]


def hop_kernel(first, *refs):
    upper_ref, mine_ref, other_ref = refs[:3]
    into_ref = None if first else refs[3]
    new_ref, msg_ref = refs[-2:]
    upper = upper_ref[0].astype(F32)
    for k in (0, 1):
        later = upper if k == 0 else 1.0 - upper
        at = k * (STATE + TAIL)
        o_state, o_log = read_message(other_ref, at)
        if first:
            new_state, new_log = later * o_state, later * o_log
        else:
            into_log = into_ref[k, STATE : STATE + 1, :]
            new_state = into_ref[k, :STATE, :] + later * jnp.exp(into_log) * o_state
            new_log = into_log + later * o_log
        new_ref[k, :STATE, :] = new_state
        new_ref[k, STATE:, :] = jnp.broadcast_to(new_log, (8, new_log.shape[1]))
        state, log = read_message(mine_ref, at)
        of_other = later * jnp.exp(log) + (1.0 - later)
        of_mine = later + (1.0 - later) * jnp.exp(o_log)
        msg_ref[at : at + STATE, :] = (of_other * o_state + of_mine * state).astype(BF16)
        t = log + o_log
        high = t.astype(BF16).astype(F32)
        mid = (t - high).astype(BF16).astype(F32)
        low = t - high - mid
        row = lax.broadcasted_iota(jnp.int32, (TAIL, t.shape[1]), 0)
        packed = jnp.where(row == 0, high, jnp.where(row == 1, mid, jnp.where(row == 2, low, 0.0)))
        msg_ref[at + STATE : at + STATE + TAIL, :] = packed.astype(BF16)


def local_call(kernel, name, smem, operands, out_shape):
    return pl.pallas_call(
        kernel,
        grid=(1,),
        in_specs=[pl.BlockSpec(memory_space=pltpu.SMEM)] + [whole(x.shape) for x in operands],
        out_specs=[whole(x.shape) for x in out_shape],
        out_shape=out_shape,
        compiler_params=params(10),
        cost_estimate=cost(1e6, 1.5e6),
        name=name,
    )(smem, *operands)


def join_kernel(count, *refs):
    place_ref, into_ref = refs[:2]
    slots, out_ref = refs[2:-1], refs[-1]
    place = place_ref[0]
    groups = [place ^ d for d in range(1, count)]
    read = [read_message(ref, 0) for ref in slots]
    ones = lambda condition: jnp.where(condition, 1.0, 0.0)
    sums = [None, None]
    for j, (state, _) in zip(groups, read):
        lower = ones(j < place)
        log = None
        for i, (_, other) in zip(groups, read):
            between = jnp.logical_or(jnp.logical_and(j < i, i < place), jnp.logical_and(place < i, i < j))
            term = ones(between) * other
            log = term if log is None else log + term
        part = jnp.exp(log) * state
        for k, share in enumerate((lower, 1.0 - lower)):
            sums[k] = share * part if sums[k] is None else sums[k] + share * part
    for k in (0, 1):
        out_ref[k] = into_ref[k, :STATE, :] + jnp.exp(into_ref[k, STATE : STATE + 1, :]) * sums[k]


def incoming(message, axis, beside, before):
    count, index = lax.axis_size(axis), lax.axis_index(axis)
    inner = message.shape[1]
    into = None
    distance = 1
    while count // distance > 4:
        other = lax.ppermute(message, axis, [(i, i ^ distance) for i in range(count)])
        if into is None:
            other, *beside = lax.optimization_barrier((other, *beside))
        upper = ((index // distance) % 2).astype(jnp.int32).reshape(1)
        operands = [message, other] + ([] if into is None else [into])
        out_shape = [jax.ShapeDtypeStruct((2, STATE + 8, inner), F32), jax.ShapeDtypeStruct(message.shape, BF16)]
        into, message = local_call(functools.partial(hop_kernel, into is None), "hop", upper, operands, out_shape)
        distance *= 2
    if into is None:
        into = jnp.zeros((2, STATE + 8, inner), F32)
    message, *before = lax.optimization_barrier((message, *before))
    groups = count // distance
    place = index // distance
    half = STATE + TAIL
    slots = []
    for d in range(1, groups):
        highest = 1 << (d.bit_length() - 1)
        above = (place // highest) % 2
        block = lax.dynamic_slice_in_dim(message, above * half, half, 0)
        slots.append(lax.ppermute(block, axis, [(i, i ^ (d * distance)) for i in range(count)]))
    joined = local_call(functools.partial(join_kernel, groups), "join", place.astype(jnp.int32).reshape(1), [into] + slots,
                        [jax.ShapeDtypeStruct((2, STATE, inner), F32)])[0]
    return joined, beside, before


def shifted(block, axis, distance):
    devices = range(lax.axis_size(axis))
    return lax.ppermute(block, axis, [(i - distance, i) for i in devices if i - distance in devices])


def rotated(block, d, count):
    return lax.ppermute(block, "head", [(i, (i + d) % count) for i in range(count)])


def on_device(
    hidden, norm_gain, w_zx, w_bc, w_dt, dt_bias, decay_rate, skip_gain, conv_x, conv_bc, w_out
):
    rows, depth = hidden.shape
    inner = conv_x.shape[1]
    heads = dt_bias.shape[0]
    width = inner // heads
    n_ctx, n_head = lax.axis_size("ctx"), lax.axis_size("head")
    ctx, head = lax.axis_index("ctx"), lax.axis_index("head")

    rim_f = shifted(hidden[rows - RIM :], "ctx", 1)
    rim_r = shifted(hidden[:RIM], "ctx", -1)

    half = w_out.shape[0] // 2
    parity = ctx % 2
    own_half = lax.dynamic_slice_in_dim(w_out, parity * half, half, 0)
    same = [rotated(own_half, d, n_head) for d in range(1, n_head)]

    w_f, w_r, g_f, g_r = prepare(w_zx, w_bc, w_dt, norm_gain)
    lanes = jnp.pad(jnp.stack([dt_bias, decay_rate, skip_gain]), [(0, 0), (0, 128 - heads)])
    copy_first = spread_matrix(0, heads, width)
    copy_second = spread_matrix(heads, heads, width)
    (act_f, small_f, cumt_f, enter_f, prior_f, act_r, small_r, cumt_r, enter_r, prior_r,
     message) = project(hidden, rim_f, rim_r, w_f, w_r, conv_x, conv_bc, lanes, copy_first, heads, inner)
    entering, (z_f, z_r), same = incoming(message, "ctx", gates(hidden, g_f, g_r), same)

    share = rows // n_head
    pieces = 2 if share % (2 * CHUNK) == 0 else 1
    size = share // pieces
    tile = min(TILE, size)
    inner_blocks, share_blocks = size // tile, share // tile
    other = lax.ppermute(jnp.concatenate(same, axis=0), "ctx", [(i, i ^ 1) for i in range(n_ctx)])
    entering, other = lax.optimization_barrier((entering, other))
    other = [other[i * half : (i + 1) * half] for i in range(n_head - 1)]
    groups = [w_out]
    own_rows = lax.dynamic_slice_in_dim(hidden, head * share, share, 0)
    arrived = [[None] * n_head for _ in range(pieces)]

    combined = None
    for k in range(pieces):
        blocks = (n_head * inner_blocks,
                  lambda i, k=k: (i // inner_blocks) * share_blocks + k * inner_blocks + i % inner_blocks)
        if combined is not None:
            act_f, act_r, combined = lax.optimization_barrier((act_f, act_r, combined))
        bases = inside(tile, blocks, ((act_f, small_f, cumt_f), (act_r, small_r, cumt_r)), lanes, copy_first, heads, inner,
                       1e8 if k else 8e9)
        combined = finish(tile, blocks, ((act_f, z_f, enter_f, prior_f, small_f), (act_r, z_r, enter_r, prior_r, small_r)),
                          bases, entering, copy_second, heads, inner)
        if k:
            combined, *arrived[k - 1] = lax.optimization_barrier((combined, *arrived[k - 1]))
        parts = [lax.dynamic_slice_in_dim(combined, ((head + d) % n_head) * size, size, 0) for d in range(n_head)]
        arrived[k] = [rotated(block, d, n_head) if d else block for d, block in enumerate(parts)]
    for one, two in zip(same, other):
        groups.append(jnp.concatenate([jnp.where(parity == 0, one, two), jnp.where(parity == 0, two, one)], axis=0))
    result = None
    for k in range(pieces):
        total = own_rows[k * size : (k + 1) * size].astype(F32)
        for block, weights in zip(arrived[k], groups):
            total = total + jnp.dot(block, weights, preferred_element_type=F32)
        total = total.astype(BF16)
        if result is None:
            result = jnp.pad(total, ((0, share - size), (0, 0)))
        else:
            result = lax.dynamic_update_slice(result, total, (k * size, 0))
    return result


def solution(mesh):
    placed = (
        P("ctx", None),
        P(),
        P(None, None, "head"),
        P(),
        P(None, "head"),
        P("head"),
        P("head"),
        P("head"),
        P(None, "head"),
        P(),
        P("head", None),
    )
    return jax.shard_map(
        on_device, mesh=mesh, in_specs=placed, out_specs=P(("ctx", "head"), None), check_vma=False
    )
```

```python
import functools

import jax
import jax.numpy as jnp
import numpy as np
from jax import lax
from jax.experimental import pallas as pl
from jax.experimental.pallas import tpu as pltpu
from jax.sharding import PartitionSpec as P

STATE = 128
CHUNK = 128
TILE = 256
EPS = 1e-05
RIM = 16
TAIL = 16
F32 = jnp.float32
BF16 = jnp.bfloat16
MIB = 2**20


def params(limit):
    return pltpu.CompilerParams(
        dimension_semantics=("arbitrary",), vmem_limit_bytes=limit * MIB
    )


def cost(flops, bytes_accessed):
    return pl.CostEstimate(flops=int(flops), bytes_accessed=int(bytes_accessed), transcendentals=0)


def whole(shape):
    return pl.BlockSpec(shape, lambda *_: (0,) * len(shape), pipeline_mode=pl.Buffered(1))


def silu(x):
    half = 0.5 * x
    return half + half * jnp.tanh(half)


def tri(rows, reverse):
    r = lax.broadcasted_iota(jnp.int32, (rows, rows), 0)
    c = lax.broadcasted_iota(jnp.int32, (rows, rows), 1)
    return (r <= c) if reverse else (r >= c)


def spread_matrix(first, heads, width):
    r = np.arange(2 * 128)[:, None] % 128
    c = np.arange(heads * width)[None, :] // width
    return jnp.asarray((r == c + first).astype(BF16))


def spread(q, matrix):
    high = q.astype(BF16)
    low = (q - high.astype(F32)).astype(BF16)
    return jnp.dot(jnp.concatenate([high, low], axis=1), matrix, preferred_element_type=F32)


def prepare_kernel(inner, zx_ref, bc_ref, dt_ref, gain_ref, wf_ref, wr_ref, gf_ref, gr_ref):
    rows = zx_ref.shape[0]
    gain = jnp.transpose(jnp.broadcast_to(gain_ref[...], (128, rows)))
    zx = zx_ref[...].astype(F32).reshape(rows, 2 * inner)
    steps = dt_ref[...].astype(F32)
    steps = jnp.transpose(jnp.concatenate([steps, jnp.zeros((128 - steps.shape[0], rows), F32)], axis=0))
    r = lax.broadcasted_iota(jnp.int32, (rows, rows), 0)
    c = lax.broadcasted_iota(jnp.int32, (rows, rows), 1)
    turn = (r + c == rows - 1).astype(BF16)

    def put(part, at, forward_ref, turned_ref):
        size = part.shape[1]
        scaled = jnp.concatenate([part[:, g : g + 128] * gain for g in range(0, size, 128)], axis=1).astype(BF16)
        forward_ref[:, at : at + size] = scaled
        turned_ref[:, at : at + size] = jnp.dot(turn, scaled, preferred_element_type=F32).astype(BF16)

    put(zx[:, inner:], 0, wf_ref, wr_ref)
    put(bc_ref[...].astype(F32), inner, wf_ref, wr_ref)
    put(steps, inner + bc_ref.shape[1], wf_ref, wr_ref)
    put(zx[:, :inner], 0, gf_ref, gr_ref)


def prepare(w_zx, w_bc, w_dt, gain):
    depth, _, inner = w_zx.shape
    tile = min(256, depth)
    n = depth // tile
    wide = inner + w_bc.shape[1] + 128
    forward, turned = (lambda i: (i, 0)), (lambda i: (n - 1 - i, 0))
    return pl.pallas_call(
        functools.partial(prepare_kernel, inner),
        grid=(n,),
        in_specs=[pl.BlockSpec((tile, 2, inner), lambda i: (i, 0, 0)),
                  pl.BlockSpec((tile, w_bc.shape[1]), forward),
                  pl.BlockSpec((w_dt.shape[1], tile), lambda i: (0, i)),
                  pl.BlockSpec((1, tile), lambda i: (0, i))],
        out_specs=[pl.BlockSpec((tile, wide), forward), pl.BlockSpec((tile, wide), turned),
                   pl.BlockSpec((tile, inner), forward), pl.BlockSpec((tile, inner), turned)],
        out_shape=[jax.ShapeDtypeStruct((depth, wide), BF16)] * 2 + [jax.ShapeDtypeStruct((depth, inner), BF16)] * 2,
        compiler_params=params(58),
        cost_estimate=cost(4e9, 8e6),
        name="prepare",
    )(w_zx, w_bc, w_dt.T, gain[None, :])


def row_scale(h):
    hf = h.astype(F32)
    return lax.rsqrt(jnp.mean(hf * hf, axis=-1, keepdims=True) + EPS)


def project_kernel(heads, inner, *refs):
    (hf_ref, hr_ref, rimf_ref, rimr_ref, wf_ref, wr_ref, convx_ref, convbc_ref, lanes_ref, copy_ref,
     actf_ref, smallf_ref, cumtf_ref, enterf_ref, priorf_ref,
     actr_ref, smallr_ref, cumtr_ref, enterr_ref, priorr_ref,
     msg_ref, buff, bufr, statef, stater, totalf, totalr) = refs
    step = pl.program_id(0)
    last = pl.num_programs(0) - 1
    stream = inner + 2 * STATE
    blocks = stream // 128
    rows = hf_ref.shape[0]
    count = rows // CHUNK
    sides = (
        (False, hf_ref, rimf_ref, wf_ref, actf_ref, smallf_ref, cumtf_ref, enterf_ref, priorf_ref, buff, statef, totalf),
        (True, hr_ref, rimr_ref, wr_ref, actr_ref, smallr_ref, cumtr_ref, enterr_ref, priorr_ref, bufr, stater, totalr),
    )

    @pl.when(step == 0)
    def _():
        for reverse, _, rim_ref, w_ref, _, _, _, _, _, buf, state, total in sides:
            edge = rows if reverse else 0
            state[...] = jnp.zeros_like(state)
            total[...] = jnp.zeros_like(total)
            rim = rim_ref[...]
            out = jnp.dot(rim, w_ref[:, :stream], preferred_element_type=F32) * row_scale(rim)
            for j in range(blocks):
                part = out[:, j * 128 : (j + 1) * 128]
                buf[j, edge : edge + 8, :] = part[:8] if reverse else part[RIM - 8 :]

    lane = lax.broadcasted_iota(jnp.int32, (rows, 128), 1)
    row8 = lax.broadcasted_iota(jnp.int32, (8, 128), 0)
    r = lax.broadcasted_iota(jnp.int32, (rows, rows), 0)
    c = lax.broadcasted_iota(jnp.int32, (rows, rows), 1)
    same = r // CHUNK == c // CHUNK
    hs = [side[1][...] for side in sides]
    scales = [row_scale(h) for h in hs]
    tail_rows, aux_rows = [], []
    for k, (reverse, _, _, w_ref, _, small_ref, cumt_ref, _, _, _, _, total_ref) in enumerate(sides):
        raw = jnp.dot(hs[k], w_ref[:, stream:], preferred_element_type=F32) * scales[k] + lanes_ref[0:1, :]
        dt = jnp.maximum(raw, 0.0) + jnp.log1p(jnp.exp(-jnp.abs(raw)))
        dt = jnp.where(lane < heads, dt, 0.0)
        steps = -lanes_ref[1:2, :] * dt
        high = steps.astype(BF16).astype(F32)
        mid = (steps - high).astype(BF16).astype(F32)
        low = steps - high - mid
        packed = (high + pltpu.roll(mid, heads, 1) + pltpu.roll(low, 2 * heads, 1)).astype(BF16)
        mask = jnp.where(jnp.logical_and(same, (r <= c) if reverse else (r >= c)), 1.0, 0.0).astype(BF16)
        sums = jnp.dot(mask, packed, preferred_element_type=F32)
        sums = sums + pltpu.roll(sums, 128 - heads, 1) + pltpu.roll(sums, 128 - 2 * heads, 1)
        cum = jnp.where(lane < heads, sums, 0.0)
        small_ref[...] = dt + pltpu.roll(cum, heads, 1)
        running = total_ref[...]
        tails = [None] * count
        aux = [None] * count
        for i in range(count):
            n = count - 1 - i if reverse else i
            at = slice(n * CHUNK, (n + 1) * CHUNK)
            cumt_ref[:, at] = jnp.transpose(cum[at])[:heads]
            end = cum[n * CHUNK : n * CHUNK + 1] if reverse else cum[(n + 1) * CHUNK - 1 : (n + 1) * CHUNK]
            tails[n] = dt[at] * jnp.exp(end - cum[at])
            aux[n] = jnp.where(row8 == 0, jnp.exp(end), jnp.exp(running))
            running = running + end
        total_ref[...] = running
        tail_rows += tails
        aux_rows += aux
    weights = spread(jnp.concatenate(tail_rows + aux_rows, axis=0), copy_ref[...])

    for g in range(0, stream, 256):
        for k, (reverse, _, _, w_ref, act_ref, _, _, _, _, buf, _, _) in enumerate(sides):
            edge = rows if reverse else 0
            body = 0 if reverse else 8
            out = jnp.dot(hs[k], w_ref[:, g : g + 256], preferred_element_type=F32) * scales[k]
            for j in range(g // 128, g // 128 + 2):
                x = out[:, j * 128 - g : (j + 1) * 128 - g]
                buf[j, body : body + rows, :] = x
                own = j * 128 - (0 if j * 128 < inner else inner)
                taps = (convx_ref if j * 128 < inner else convbc_ref)[:, own : own + 128]
                total = taps[3:4] * x
                for d in (1, 2, 3):
                    at = body + d if reverse else body - d
                    total = total + taps[3 - d : 4 - d] * buf[j, at : at + rows, :]
                act_ref[:, j * 128 : (j + 1) * 128] = silu(total).astype(BF16)
                buf[j, edge : edge + 8, :] = x[:8] if reverse else x[rows - 8 :]

    for i in range(count):
        for k, (reverse, _, _, _, act_ref, _, _, enter_ref, prior_ref, _, state, _) in enumerate(sides):
            n = count - 1 - i if reverse else i
            at = slice(n * CHUNK, (n + 1) * CHUNK)
            own = weights[(k * count + n) * CHUNK : (k * count + n + 1) * CHUNK]
            aux = weights[2 * rows + (k * count + n) * 8 : 2 * rows + (k * count + n + 1) * 8]
            tails = (act_ref[at, :inner].astype(F32) * own).astype(BF16)
            ends = lax.dot_general(act_ref[at, inner : inner + STATE], tails, (((0,), (0,)), ((), ())),
                                   preferred_element_type=F32)
            before = state[...]
            enter_ref[n] = before.astype(BF16)
            prior_ref[n] = aux
            state[...] = before * aux[:1] + ends

    @pl.when(step == last)
    def _():
        for k, side in enumerate(sides):
            state, total = side[-2:]
            at = k * (STATE + TAIL)
            msg_ref[at : at + STATE, :] = state[...].astype(BF16)
            t = total[...]
            high = t.astype(BF16).astype(F32)
            mid = (t - high).astype(BF16).astype(F32)
            low = t - high - mid
            packed = jnp.where(row8 == 0, high, jnp.where(row8 == 1, mid, jnp.where(row8 == 2, low, 0.0)))
            rows3 = spread(packed, copy_ref[...])
            msg_ref[at + STATE : at + STATE + TAIL, :] = jnp.concatenate(
                [rows3, jnp.zeros_like(rows3)], axis=0).astype(BF16)


def project(hidden, rim_f, rim_r, w_f, w_r, conv_x, conv_bc, lanes, copy, heads, inner):
    rows, depth = hidden.shape
    stream = inner + 2 * STATE
    n = rows // TILE
    per = TILE // CHUNK
    up, down = (lambda i: i), (lambda i: n - 1 - i)
    by_rows = lambda width, at: pl.BlockSpec((TILE, width), lambda i: (at(i), 0))
    out_specs, out_shape = [], []
    for at in (up, down):
        out_specs += [by_rows(stream, at), by_rows(128, at),
                      pl.BlockSpec((heads, TILE), lambda i, at=at: (0, at(i))),
                      pl.BlockSpec((per, STATE, inner), lambda i, at=at: (at(i), 0, 0)),
                      pl.BlockSpec((per, 8, inner), lambda i, at=at: (at(i), 0, 0))]
        out_shape += [jax.ShapeDtypeStruct((rows, stream), BF16),
                      jax.ShapeDtypeStruct((rows, 128), F32), jax.ShapeDtypeStruct((heads, rows), F32),
                      jax.ShapeDtypeStruct((n * per, STATE, inner), BF16),
                      jax.ShapeDtypeStruct((n * per, 8, inner), F32)]
    message = (2 * (STATE + TAIL), inner)
    buf = pltpu.VMEM((stream // 128, TILE + 8, 128), F32)
    state, total = pltpu.VMEM((STATE, inner), F32), pltpu.VMEM((8, 128), F32)
    return pl.pallas_call(
        functools.partial(project_kernel, heads, inner),
        grid=(n,),
        in_specs=[by_rows(depth, up), by_rows(depth, down), whole(rim_f.shape), whole(rim_r.shape),
                  whole(w_f.shape), whole(w_r.shape), whole(conv_x.shape), whole(conv_bc.shape), whole(lanes.shape),
                  whole(copy.shape)],
        out_specs=out_specs + [whole(message)],
        out_shape=out_shape + [jax.ShapeDtypeStruct(message, BF16)],
        scratch_shapes=[buf, buf, state, state, total, total],
        compiler_params=params(58),
        cost_estimate=cost(22e9, 40e6),
        name="project",
    )(hidden, hidden, rim_f, rim_r, w_f, w_r, conv_x, conv_bc, lanes, copy)


def gates_kernel(h_ref, wf_ref, wr_ref, zf_ref, zr_ref):
    h = h_ref[...]
    scale = row_scale(h)
    for w_ref, z_ref in ((wf_ref, zf_ref), (wr_ref, zr_ref)):
        z_ref[...] = (jnp.dot(h, w_ref[...], preferred_element_type=F32) * scale).astype(BF16)


def gates(tile, blocks, hidden, w_f, w_r, work):
    count, at = blocks
    inner = w_f.shape[1]
    return pl.pallas_call(
        gates_kernel,
        grid=(count,),
        in_specs=[pl.BlockSpec((tile, hidden.shape[1]), lambda i: (at(i), 0)), whole(w_f.shape), whole(w_r.shape)],
        out_specs=[pl.BlockSpec((tile, inner), lambda i: (i, 0))] * 2,
        out_shape=[jax.ShapeDtypeStruct((count * tile, inner), BF16)] * 2,
        compiler_params=params(58),
        cost_estimate=cost(work, 1e6),
        name="gates",
    )(hidden, w_f, w_r)


def inside_kernel(heads, inner, actf_ref, smallf_ref, cumtf_ref, actr_ref, smallr_ref, cumtr_ref, lanes_ref, copy_ref,
                  basef_ref, baser_ref):
    width = inner // heads
    per = 128 // width
    size = actf_ref.shape[0]
    lane = lax.broadcasted_iota(jnp.int32, (size, 128), 1)
    group = lax.broadcasted_iota(jnp.int32, (CHUNK, 128), 1) // width
    dts = [jnp.where(lane < heads, ref[...], 0.0) for ref in (smallf_ref, smallr_ref)]
    wide = spread(jnp.concatenate(dts + [jnp.broadcast_to(lanes_ref[2:3, :], (8, 128))], axis=0), copy_ref[...])
    skip = wide[2 * size : 2 * size + 1]
    sides = ((False, actf_ref, smallf_ref, cumtf_ref, basef_ref), (True, actr_ref, smallr_ref, cumtr_ref, baser_ref))
    for c in range(0, size, CHUNK):
        rows = slice(c, c + CHUNK)
        for k, (reverse, act_ref, small_ref, cumt_ref, base_ref) in enumerate(sides):
            small = small_ref[rows, :]
            values = act_ref[rows, :inner].astype(F32)
            weighted = (values * wide[k * size + c : k * size + c + CHUNK]).astype(BF16)
            scores = lax.dot_general(act_ref[rows, inner + STATE :], act_ref[rows, inner : inner + STATE],
                                     (((1,), (1,)), ((), ())), preferred_element_type=F32)
            scores = jnp.where(tri(CHUNK, reverse), scores, 0.0)
            for p in range(inner // 128):
                cols = slice(p * 128, (p + 1) * 128)
                pair = weighted[:, cols]
                mixing, stacked = [], []
                for q in range(per):
                    h = p * per + q
                    gap = jnp.minimum(small[:, heads + h : heads + h + 1] - cumt_ref[h : h + 1, rows], 0.0)
                    mixing.append((scores * jnp.exp(gap)).astype(BF16))
                    stacked.append(jnp.where(group == q, pair, jnp.zeros_like(pair)))
                out = jnp.dot(jnp.concatenate(mixing, axis=1), jnp.concatenate(stacked, axis=0),
                              preferred_element_type=F32)
                base_ref[rows, cols] = (out + skip[:, cols] * values[:, cols]).astype(BF16)


def inside(tile, blocks, strands, lanes, copy, heads, inner, work):
    count, at = blocks
    columns = strands[0][0].shape[1]
    by_rows = lambda width: pl.BlockSpec((tile, width), lambda i: (at(i), 0))
    one = [by_rows(columns), by_rows(128), pl.BlockSpec((heads, tile), lambda i: (0, at(i)))]
    return pl.pallas_call(
        functools.partial(inside_kernel, heads, inner),
        grid=(count,),
        in_specs=one + one + [whole(lanes.shape), whole(copy.shape)],
        out_specs=[pl.BlockSpec((tile, inner), lambda i: (i, 0))] * 2,
        out_shape=[jax.ShapeDtypeStruct((count * tile, inner), BF16)] * 2,
        compiler_params=params(58),
        cost_estimate=cost(work, 1e6),
        name="inside",
    )(*strands[0], *strands[1], lanes, copy)


def finish_kernel(heads, inner, *refs):
    (cf_ref, zf_ref, ef_ref, pf_ref, sf_ref, cr_ref, zr_ref, er_ref, pr_ref, sr_ref, bf_ref, br_ref,
     in_ref, copy_ref, out_ref) = refs
    width = inner // heads
    size = cf_ref.shape[0]
    row = lax.broadcasted_iota(jnp.int32, (256, 256), 0) // width
    column = lax.broadcasted_iota(jnp.int32, (256, 256), 1) // width
    mean = jnp.where(row == column, 1.0 / width, 0.0).astype(BF16)
    grown = spread(jnp.exp(jnp.minimum(jnp.concatenate([sf_ref[...], sr_ref[...]], axis=0), 0.0)), copy_ref[...])
    both = None
    for k, (c_ref, b_ref, z_ref, e_ref, p_ref) in enumerate(
            ((cf_ref, bf_ref, zf_ref, ef_ref, pf_ref), (cr_ref, br_ref, zr_ref, er_ref, pr_ref))):
        parts = []
        for c in range(e_ref.shape[0]):
            entering = (e_ref[c].astype(F32) + p_ref[c, 1:2, :] * in_ref[k]).astype(BF16)
            parts.append(jnp.dot(c_ref[c * CHUNK : (c + 1) * CHUNK, :], entering, preferred_element_type=F32))
        reads = jnp.concatenate(parts, axis=0)
        out = b_ref[...].astype(F32) + reads * grown[k * size : (k + 1) * size]
        gated = out * silu(z_ref[...].astype(F32))
        squares = (gated * gated).astype(BF16)
        means = jnp.concatenate(
            [jnp.dot(squares[:, g : g + 256], mean, preferred_element_type=F32) for g in range(0, inner, 256)], axis=1)
        result = gated * lax.rsqrt(means + EPS)
        both = result if both is None else both + result
    out_ref[...] = both.astype(BF16)


def finish(tile, blocks, strands, bases, entering, copy, heads, inner):
    count, at = blocks
    per = tile // CHUNK
    last = strands[0][0].shape[1] // STATE - 1
    by_rows = lambda width: pl.BlockSpec((tile, width), lambda i: (at(i), 0))
    in_order = pl.BlockSpec((tile, inner), lambda i: (i, 0))
    one = [pl.BlockSpec((tile, STATE), lambda i: (at(i), last)), in_order,
           pl.BlockSpec((per, STATE, inner), lambda i: (at(i), 0, 0)),
           pl.BlockSpec((per, 8, inner), lambda i: (at(i), 0, 0)), by_rows(128)]
    return pl.pallas_call(
        functools.partial(finish_kernel, heads, inner),
        grid=(count,),
        in_specs=one + one + [in_order, in_order, whole((2, STATE, inner)), whole(copy.shape)],
        out_specs=in_order,
        out_shape=jax.ShapeDtypeStruct((count * tile, inner), BF16),
        compiler_params=params(58),
        cost_estimate=cost(1e8, 1e6),
        name="finish",
    )(*strands[0], *strands[1], *bases, entering, copy)


def settle_kernel(heads, inner, *refs):
    (actf_ref, smallf_ref, cumtf_ref, actr_ref, smallr_ref, cumtr_ref, lanes_ref, first_ref,
     zf_ref, ef_ref, pf_ref, zr_ref, er_ref, pr_ref, in_ref, second_ref, out_ref, basef, baser) = refs
    inside_kernel(heads, inner, actf_ref, smallf_ref, cumtf_ref, actr_ref, smallr_ref, cumtr_ref, lanes_ref, first_ref,
                  basef, baser)
    maps = [ref.at[:, pl.ds(inner + STATE, STATE)] for ref in (actf_ref, actr_ref)]
    finish_kernel(heads, inner, maps[0], zf_ref, ef_ref, pf_ref, smallf_ref, maps[1], zr_ref, er_ref, pr_ref, smallr_ref,
                  basef, baser, in_ref, second_ref, out_ref)


def settle(tile, blocks, strands, ends, lanes, first, entering, second, heads, inner):
    count, at = blocks
    per = tile // CHUNK
    columns = strands[0][0].shape[1]
    by_rows = lambda width: pl.BlockSpec((tile, width), lambda i: (at(i), 0))
    in_order = pl.BlockSpec((tile, inner), lambda i: (i, 0))
    one = [by_rows(columns), by_rows(128), pl.BlockSpec((heads, tile), lambda i: (0, at(i)))]
    two = [in_order, pl.BlockSpec((per, STATE, inner), lambda i: (at(i), 0, 0)),
           pl.BlockSpec((per, 8, inner), lambda i: (at(i), 0, 0))]
    return pl.pallas_call(
        functools.partial(settle_kernel, heads, inner),
        grid=(count,),
        in_specs=one + one + [whole(lanes.shape), whole(first.shape)] + two + two
        + [whole((2, STATE, inner)), whole(second.shape)],
        out_specs=in_order,
        out_shape=jax.ShapeDtypeStruct((count * tile, inner), BF16),
        scratch_shapes=[pltpu.VMEM((tile, inner), BF16)] * 2,
        compiler_params=params(58),
        cost_estimate=cost(1e8, 1e6),
        name="settle",
    )(*strands[0], *strands[1], lanes, first, *ends[0], *ends[1], entering, second)


def read_message(ref, at):
    tail = ref[at + STATE : at + STATE + TAIL, :].astype(F32)
    return ref[at : at + STATE, :].astype(F32), tail[0:1] + tail[1:2] + tail[2:3]


def hop_kernel(first, *refs):
    upper_ref, mine_ref, other_ref = refs[:3]
    into_ref = None if first else refs[3]
    new_ref, msg_ref = refs[-2:]
    upper = upper_ref[0].astype(F32)
    for k in (0, 1):
        later = upper if k == 0 else 1.0 - upper
        at = k * (STATE + TAIL)
        o_state, o_log = read_message(other_ref, at)
        if first:
            new_state, new_log = later * o_state, later * o_log
        else:
            into_log = into_ref[k, STATE : STATE + 1, :]
            new_state = into_ref[k, :STATE, :] + later * jnp.exp(into_log) * o_state
            new_log = into_log + later * o_log
        new_ref[k, :STATE, :] = new_state
        new_ref[k, STATE:, :] = jnp.broadcast_to(new_log, (8, new_log.shape[1]))
        state, log = read_message(mine_ref, at)
        of_other = later * jnp.exp(log) + (1.0 - later)
        of_mine = later + (1.0 - later) * jnp.exp(o_log)
        msg_ref[at : at + STATE, :] = (of_other * o_state + of_mine * state).astype(BF16)
        t = log + o_log
        high = t.astype(BF16).astype(F32)
        mid = (t - high).astype(BF16).astype(F32)
        low = t - high - mid
        row = lax.broadcasted_iota(jnp.int32, (TAIL, t.shape[1]), 0)
        packed = jnp.where(row == 0, high, jnp.where(row == 1, mid, jnp.where(row == 2, low, 0.0)))
        msg_ref[at + STATE : at + STATE + TAIL, :] = packed.astype(BF16)


def local_call(kernel, name, smem, operands, out_shape):
    return pl.pallas_call(
        kernel,
        grid=(1,),
        in_specs=[pl.BlockSpec(memory_space=pltpu.SMEM)] + [whole(x.shape) for x in operands],
        out_specs=[whole(x.shape) for x in out_shape],
        out_shape=out_shape,
        compiler_params=params(10),
        cost_estimate=cost(1e6, 1.5e6),
        name=name,
    )(smem, *operands)


def join_kernel(count, *refs):
    place_ref, into_ref = refs[:2]
    slots, out_ref = refs[2:-1], refs[-1]
    place = place_ref[0]
    groups = [place ^ d for d in range(1, count)]
    read = [read_message(ref, 0) for ref in slots]
    ones = lambda condition: jnp.where(condition, 1.0, 0.0)
    sums = [None, None]
    for j, (state, _) in zip(groups, read):
        lower = ones(j < place)
        log = None
        for i, (_, other) in zip(groups, read):
            between = jnp.logical_or(jnp.logical_and(j < i, i < place), jnp.logical_and(place < i, i < j))
            term = ones(between) * other
            log = term if log is None else log + term
        part = jnp.exp(log) * state
        for k, share in enumerate((lower, 1.0 - lower)):
            sums[k] = share * part if sums[k] is None else sums[k] + share * part
    for k in (0, 1):
        out_ref[k] = into_ref[k, :STATE, :] + jnp.exp(into_ref[k, STATE : STATE + 1, :]) * sums[k]


def incoming(message, axis, beside, before):
    count, index = lax.axis_size(axis), lax.axis_index(axis)
    inner = message.shape[1]
    into = None
    distance = 1
    while count // distance > 4:
        other = lax.ppermute(message, axis, [(i, i ^ distance) for i in range(count)])
        if into is None:
            other, *beside = lax.optimization_barrier((other, *beside))
        upper = ((index // distance) % 2).astype(jnp.int32).reshape(1)
        operands = [message, other] + ([] if into is None else [into])
        out_shape = [jax.ShapeDtypeStruct((2, STATE + 8, inner), F32), jax.ShapeDtypeStruct(message.shape, BF16)]
        into, message = local_call(functools.partial(hop_kernel, into is None), "hop", upper, operands, out_shape)
        distance *= 2
    if into is None:
        into = jnp.zeros((2, STATE + 8, inner), F32)
    message, *before = lax.optimization_barrier((message, *before))
    groups = count // distance
    place = index // distance
    half = STATE + TAIL
    slots = []
    for d in range(1, groups):
        highest = 1 << (d.bit_length() - 1)
        above = (place // highest) % 2
        block = lax.dynamic_slice_in_dim(message, above * half, half, 0)
        slots.append(lax.ppermute(block, axis, [(i, i ^ (d * distance)) for i in range(count)]))
    joined = local_call(functools.partial(join_kernel, groups), "join", place.astype(jnp.int32).reshape(1), [into] + slots,
                        [jax.ShapeDtypeStruct((2, STATE, inner), F32)])[0]
    return joined, beside, before


def shifted(block, axis, distance):
    devices = range(lax.axis_size(axis))
    return lax.ppermute(block, axis, [(i - distance, i) for i in devices if i - distance in devices])


def rotated(block, d, count):
    return lax.ppermute(block, "head", [(i, (i + d) % count) for i in range(count)])


def on_device(
    hidden, norm_gain, w_zx, w_bc, w_dt, dt_bias, decay_rate, skip_gain, conv_x, conv_bc, w_out
):
    rows, depth = hidden.shape
    inner = conv_x.shape[1]
    heads = dt_bias.shape[0]
    width = inner // heads
    n_ctx, n_head = lax.axis_size("ctx"), lax.axis_size("head")
    ctx, head = lax.axis_index("ctx"), lax.axis_index("head")

    rim_f = shifted(hidden[rows - RIM :], "ctx", 1)
    rim_r = shifted(hidden[:RIM], "ctx", -1)

    half = w_out.shape[0] // 2
    parity = ctx % 2
    own_half = lax.dynamic_slice_in_dim(w_out, parity * half, half, 0)
    same = [rotated(own_half, d, n_head) for d in range(1, n_head)]

    w_f, w_r, g_f, g_r = prepare(w_zx, w_bc, w_dt, norm_gain)
    lanes = jnp.pad(jnp.stack([dt_bias, decay_rate, skip_gain]), [(0, 0), (0, 128 - heads)])
    copy_first = spread_matrix(0, heads, width)
    copy_second = spread_matrix(heads, heads, width)
    (act_f, small_f, cumt_f, enter_f, prior_f, act_r, small_r, cumt_r, enter_r, prior_r,
     message) = project(hidden, rim_f, rim_r, w_f, w_r, conv_x, conv_bc, lanes, copy_first, heads, inner)
    share = rows // n_head
    pieces = 2 if share % (2 * CHUNK) == 0 else 1
    size = share // pieces
    tile = min(TILE, size)
    inner_blocks, share_blocks = size // tile, share // tile

    def piece(k):
        return (n_head * inner_blocks,
                lambda i: (i // inner_blocks) * share_blocks + k * inner_blocks + i % inner_blocks)

    entering, (z_f, z_r), same = incoming(message, "ctx", gates(tile, piece(0), hidden, g_f, g_r, 5e9), same)
    other = lax.ppermute(jnp.concatenate(same, axis=0), "ctx", [(i, i ^ 1) for i in range(n_ctx)])
    entering, other = lax.optimization_barrier((entering, other))
    other = [other[i * half : (i + 1) * half] for i in range(n_head - 1)]
    groups = [w_out]
    own_rows = lax.dynamic_slice_in_dim(hidden, head * share, share, 0)
    arrived = [[None] * n_head for _ in range(pieces)]

    combined = None
    for k in range(pieces):
        if k == 0:
            bases = inside(tile, piece(k), ((act_f, small_f, cumt_f), (act_r, small_r, cumt_r)), lanes, copy_first,
                           heads, inner, 8e9)
            combined = finish(tile, piece(k), ((act_f, z_f, enter_f, prior_f, small_f),
                                               (act_r, z_r, enter_r, prior_r, small_r)),
                              bases, entering, copy_second, heads, inner)
        else:
            g_f, g_r, combined = lax.optimization_barrier((g_f, g_r, combined))
            z_f, z_r = gates(tile, piece(k), hidden, g_f, g_r, 1e8)
            combined = settle(tile, piece(k), ((act_f, small_f, cumt_f), (act_r, small_r, cumt_r)),
                              ((z_f, enter_f, prior_f), (z_r, enter_r, prior_r)), lanes, copy_first, entering, copy_second,
                              heads, inner)
        if k:
            combined, *arrived[k - 1] = lax.optimization_barrier((combined, *arrived[k - 1]))
        parts = [lax.dynamic_slice_in_dim(combined, ((head + d) % n_head) * size, size, 0) for d in range(n_head)]
        arrived[k] = [rotated(block, d, n_head) if d else block for d, block in enumerate(parts)]
    for one, two in zip(same, other):
        groups.append(jnp.concatenate([jnp.where(parity == 0, one, two), jnp.where(parity == 0, two, one)], axis=0))
    result = None
    for k in range(pieces):
        total = own_rows[k * size : (k + 1) * size].astype(F32)
        for block, weights in zip(arrived[k], groups):
            total = total + jnp.dot(block, weights, preferred_element_type=F32)
        total = total.astype(BF16)
        if result is None:
            result = jnp.pad(total, ((0, share - size), (0, 0)))
        else:
            result = lax.dynamic_update_slice(result, total, (k * size, 0))
    return result


def solution(mesh):
    placed = (
        P("ctx", None),
        P(),
        P(None, None, "head"),
        P(),
        P(None, "head"),
        P("head"),
        P("head"),
        P("head"),
        P(None, "head"),
        P(),
        P("head", None),
    )
    return jax.shard_map(
        on_device, mesh=mesh, in_specs=placed, out_specs=P(("ctx", "head"), None), check_vma=False
    )
```

```python
import functools

import jax
import jax.numpy as jnp
import numpy as np
from jax import lax
from jax.experimental import pallas as pl
from jax.experimental.pallas import tpu as pltpu
from jax.sharding import PartitionSpec as P

STATE = 128
CHUNK = 128
TILE = 256
EPS = 1e-05
RIM = 16
TAIL = 16
F32 = jnp.float32
BF16 = jnp.bfloat16
MIB = 2**20


def params(limit):
    return pltpu.CompilerParams(
        dimension_semantics=("arbitrary",), vmem_limit_bytes=limit * MIB
    )


def cost(flops, bytes_accessed):
    return pl.CostEstimate(flops=int(flops), bytes_accessed=int(bytes_accessed), transcendentals=0)


def whole(shape):
    return pl.BlockSpec(shape, lambda *_: (0,) * len(shape), pipeline_mode=pl.Buffered(1))


def silu(x):
    half = 0.5 * x
    return half + half * jnp.tanh(half)


def tri(rows, reverse):
    r = lax.broadcasted_iota(jnp.int32, (rows, rows), 0)
    c = lax.broadcasted_iota(jnp.int32, (rows, rows), 1)
    return (r <= c) if reverse else (r >= c)


def spread_matrix(first, heads, width):
    r = np.arange(2 * 128)[:, None] % 128
    c = np.arange(heads * width)[None, :] // width
    return jnp.asarray((r == c + first).astype(BF16))


def spread(q, matrix):
    high = q.astype(BF16)
    low = (q - high.astype(F32)).astype(BF16)
    return jnp.dot(jnp.concatenate([high, low], axis=1), matrix, preferred_element_type=F32)


def prepare(inner, zx_ref, bc_ref, dt_ref, gain_ref, wf_ref, wr_ref, gf_ref, gr_ref):
    depth = zx_ref.shape[0]
    rows = min(256, depth)
    r = lax.broadcasted_iota(jnp.int32, (rows, rows), 0)
    c = lax.broadcasted_iota(jnp.int32, (rows, rows), 1)
    turn = (r + c == rows - 1).astype(BF16)
    for b in range(0, depth, rows):
        here, there = slice(b, b + rows), slice(depth - rows - b, depth - b)
        gain = jnp.transpose(jnp.broadcast_to(gain_ref[:, here], (128, rows)))
        zx = zx_ref[here].astype(F32).reshape(rows, 2 * inner)
        steps = dt_ref[:, here].astype(F32)
        steps = jnp.transpose(jnp.concatenate([steps, jnp.zeros((128 - steps.shape[0], rows), F32)], axis=0))

        def put(part, at, forward_ref, turned_ref):
            size = part.shape[1]
            scaled = jnp.concatenate([part[:, g : g + 128] * gain for g in range(0, size, 128)], axis=1).astype(BF16)
            forward_ref[here, at : at + size] = scaled
            turned_ref[there, at : at + size] = jnp.dot(turn, scaled, preferred_element_type=F32).astype(BF16)

        put(zx[:, inner:], 0, wf_ref, wr_ref)
        put(bc_ref[here].astype(F32), inner, wf_ref, wr_ref)
        put(steps, inner + bc_ref.shape[1], wf_ref, wr_ref)
        put(zx[:, :inner], 0, gf_ref, gr_ref)


def row_scale(h):
    hf = h.astype(F32)
    return lax.rsqrt(jnp.mean(hf * hf, axis=-1, keepdims=True) + EPS)


def project_kernel(heads, inner, *refs):
    (hf_ref, hr_ref, rimf_ref, rimr_ref, zx_ref, bc_ref, wdt_ref, gain_ref, convx_ref, convbc_ref, lanes_ref, copy_ref,
     actf_ref, smallf_ref, cumtf_ref, enterf_ref, priorf_ref,
     actr_ref, smallr_ref, cumtr_ref, enterr_ref, priorr_ref,
     msg_ref, gf_ref, gr_ref, wf_ref, wr_ref, buff, bufr, statef, stater, totalf, totalr) = refs
    step = pl.program_id(0)
    last = pl.num_programs(0) - 1
    stream = inner + 2 * STATE
    blocks = stream // 128
    rows = hf_ref.shape[0]
    count = rows // CHUNK
    sides = (
        (False, hf_ref, rimf_ref, wf_ref, actf_ref, smallf_ref, cumtf_ref, enterf_ref, priorf_ref, buff, statef, totalf),
        (True, hr_ref, rimr_ref, wr_ref, actr_ref, smallr_ref, cumtr_ref, enterr_ref, priorr_ref, bufr, stater, totalr),
    )

    @pl.when(step == 0)
    def _():
        prepare(inner, zx_ref, bc_ref, wdt_ref, gain_ref, wf_ref, wr_ref, gf_ref, gr_ref)
        for reverse, _, rim_ref, w_ref, _, _, _, _, _, buf, state, total in sides:
            edge = rows if reverse else 0
            state[...] = jnp.zeros_like(state)
            total[...] = jnp.zeros_like(total)
            rim = rim_ref[...]
            out = jnp.dot(rim, w_ref[:, :stream], preferred_element_type=F32) * row_scale(rim)
            for j in range(blocks):
                part = out[:, j * 128 : (j + 1) * 128]
                buf[j, edge : edge + 8, :] = part[:8] if reverse else part[RIM - 8 :]

    lane = lax.broadcasted_iota(jnp.int32, (rows, 128), 1)
    row8 = lax.broadcasted_iota(jnp.int32, (8, 128), 0)
    r = lax.broadcasted_iota(jnp.int32, (rows, rows), 0)
    c = lax.broadcasted_iota(jnp.int32, (rows, rows), 1)
    same = r // CHUNK == c // CHUNK
    hs = [side[1][...] for side in sides]
    scales = [row_scale(h) for h in hs]
    tail_rows, aux_rows = [], []
    for k, (reverse, _, _, w_ref, _, small_ref, cumt_ref, _, _, _, _, total_ref) in enumerate(sides):
        raw = jnp.dot(hs[k], w_ref[:, stream:], preferred_element_type=F32) * scales[k] + lanes_ref[0:1, :]
        dt = jnp.maximum(raw, 0.0) + jnp.log1p(jnp.exp(-jnp.abs(raw)))
        dt = jnp.where(lane < heads, dt, 0.0)
        steps = -lanes_ref[1:2, :] * dt
        high = steps.astype(BF16).astype(F32)
        mid = (steps - high).astype(BF16).astype(F32)
        low = steps - high - mid
        packed = (high + pltpu.roll(mid, heads, 1) + pltpu.roll(low, 2 * heads, 1)).astype(BF16)
        mask = jnp.where(jnp.logical_and(same, (r <= c) if reverse else (r >= c)), 1.0, 0.0).astype(BF16)
        sums = jnp.dot(mask, packed, preferred_element_type=F32)
        sums = sums + pltpu.roll(sums, 128 - heads, 1) + pltpu.roll(sums, 128 - 2 * heads, 1)
        cum = jnp.where(lane < heads, sums, 0.0)
        small_ref[...] = dt + pltpu.roll(cum, heads, 1)
        running = total_ref[...]
        tails = [None] * count
        aux = [None] * count
        for i in range(count):
            n = count - 1 - i if reverse else i
            at = slice(n * CHUNK, (n + 1) * CHUNK)
            cumt_ref[:, at] = jnp.transpose(cum[at])[:heads]
            end = cum[n * CHUNK : n * CHUNK + 1] if reverse else cum[(n + 1) * CHUNK - 1 : (n + 1) * CHUNK]
            tails[n] = dt[at] * jnp.exp(end - cum[at])
            aux[n] = jnp.where(row8 == 0, jnp.exp(end), jnp.exp(running))
            running = running + end
        total_ref[...] = running
        tail_rows += tails
        aux_rows += aux
    weights = spread(jnp.concatenate(tail_rows + aux_rows, axis=0), copy_ref[...])

    for g in range(0, stream, 256):
        for k, (reverse, _, _, w_ref, act_ref, _, _, _, _, buf, _, _) in enumerate(sides):
            edge = rows if reverse else 0
            body = 0 if reverse else 8
            out = jnp.dot(hs[k], w_ref[:, g : g + 256], preferred_element_type=F32) * scales[k]
            for j in range(g // 128, g // 128 + 2):
                x = out[:, j * 128 - g : (j + 1) * 128 - g]
                buf[j, body : body + rows, :] = x
                own = j * 128 - (0 if j * 128 < inner else inner)
                taps = (convx_ref if j * 128 < inner else convbc_ref)[:, own : own + 128]
                total = taps[3:4] * x
                for d in (1, 2, 3):
                    at = body + d if reverse else body - d
                    total = total + taps[3 - d : 4 - d] * buf[j, at : at + rows, :]
                act_ref[:, j * 128 : (j + 1) * 128] = silu(total).astype(BF16)
                buf[j, edge : edge + 8, :] = x[:8] if reverse else x[rows - 8 :]

    for i in range(count):
        for k, (reverse, _, _, _, act_ref, _, _, enter_ref, prior_ref, _, state, _) in enumerate(sides):
            n = count - 1 - i if reverse else i
            at = slice(n * CHUNK, (n + 1) * CHUNK)
            own = weights[(k * count + n) * CHUNK : (k * count + n + 1) * CHUNK]
            aux = weights[2 * rows + (k * count + n) * 8 : 2 * rows + (k * count + n + 1) * 8]
            tails = (act_ref[at, :inner].astype(F32) * own).astype(BF16)
            ends = lax.dot_general(act_ref[at, inner : inner + STATE], tails, (((0,), (0,)), ((), ())),
                                   preferred_element_type=F32)
            before = state[...]
            enter_ref[n] = before.astype(BF16)
            prior_ref[n] = aux
            state[...] = before * aux[:1] + ends

    @pl.when(step == last)
    def _():
        for k, side in enumerate(sides):
            state, total = side[-2:]
            at = k * (STATE + TAIL)
            msg_ref[at : at + STATE, :] = state[...].astype(BF16)
            t = total[...]
            high = t.astype(BF16).astype(F32)
            mid = (t - high).astype(BF16).astype(F32)
            low = t - high - mid
            packed = jnp.where(row8 == 0, high, jnp.where(row8 == 1, mid, jnp.where(row8 == 2, low, 0.0)))
            rows3 = spread(packed, copy_ref[...])
            msg_ref[at + STATE : at + STATE + TAIL, :] = jnp.concatenate(
                [rows3, jnp.zeros_like(rows3)], axis=0).astype(BF16)


def project(hidden, rim_f, rim_r, weights, conv_x, conv_bc, lanes, copy, heads, inner):
    rows, depth = hidden.shape
    stream = inner + 2 * STATE
    n = rows // TILE
    per = TILE // CHUNK
    up, down = (lambda i: i), (lambda i: n - 1 - i)
    by_rows = lambda width, at: pl.BlockSpec((TILE, width), lambda i: (at(i), 0))
    out_specs, out_shape = [], []
    for at in (up, down):
        out_specs += [by_rows(stream, at), by_rows(128, at),
                      pl.BlockSpec((heads, TILE), lambda i, at=at: (0, at(i))),
                      pl.BlockSpec((per, STATE, inner), lambda i, at=at: (at(i), 0, 0)),
                      pl.BlockSpec((per, 8, inner), lambda i, at=at: (at(i), 0, 0))]
        out_shape += [jax.ShapeDtypeStruct((rows, stream), BF16),
                      jax.ShapeDtypeStruct((rows, 128), F32), jax.ShapeDtypeStruct((heads, rows), F32),
                      jax.ShapeDtypeStruct((n * per, STATE, inner), BF16),
                      jax.ShapeDtypeStruct((n * per, 8, inner), F32)]
    message = (2 * (STATE + TAIL), inner)
    buf = pltpu.VMEM((stream // 128, TILE + 8, 128), F32)
    state, total = pltpu.VMEM((STATE, inner), F32), pltpu.VMEM((8, 128), F32)
    return pl.pallas_call(
        functools.partial(project_kernel, heads, inner),
        grid=(n,),
        in_specs=[by_rows(depth, up), by_rows(depth, down), whole(rim_f.shape), whole(rim_r.shape),
                  *[whole(x.shape) for x in weights], whole(conv_x.shape), whole(conv_bc.shape), whole(lanes.shape),
                  whole(copy.shape)],
        out_specs=out_specs + [whole(message), whole((depth, inner)), whole((depth, inner))],
        out_shape=out_shape + [jax.ShapeDtypeStruct(message, BF16)] + [jax.ShapeDtypeStruct((depth, inner), BF16)] * 2,
        scratch_shapes=[pltpu.VMEM((depth, stream + 128), BF16)] * 2 + [buf, buf, state, state, total, total],
        compiler_params=params(58),
        cost_estimate=cost(22e9, 40e6),
        name="project",
    )(hidden, hidden, rim_f, rim_r, *weights, conv_x, conv_bc, lanes, copy)


def gates_kernel(h_ref, wf_ref, wr_ref, zf_ref, zr_ref):
    h = h_ref[...]
    scale = row_scale(h)
    for w_ref, z_ref in ((wf_ref, zf_ref), (wr_ref, zr_ref)):
        z_ref[...] = (jnp.dot(h, w_ref[...], preferred_element_type=F32) * scale).astype(BF16)


def by_destination(kernel, name, place, rows_in, fixed, by_order, out_shape, out_specs, work, scratch=()):
    k, pieces, tile, rows, head, n_head = place
    share = rows // n_head
    per_piece, per_share = share // pieces // tile, share // tile

    def at(i, head_ref):
        return lax.rem(head_ref[0] + i // per_piece, n_head) * per_share + k * per_piece + lax.rem(i, per_piece)

    def spec(shape, dim, last):
        def index(i, head_ref):
            where = [0] * len(shape)
            where[-1] = last
            where[dim] = at(i, head_ref)
            return tuple(where)

        return pl.BlockSpec(shape, index)

    in_specs = [spec(*one[1:]) for one in rows_in] + [whole(x.shape) for x in fixed]
    in_specs += [pl.BlockSpec((tile, x.shape[1]), lambda i, _: (i, 0)) for x in by_order]
    return pl.pallas_call(
        lambda _, *refs: kernel(*refs),
        grid_spec=pltpu.PrefetchScalarGridSpec(
            num_scalar_prefetch=1,
            grid=(n_head * per_piece,),
            in_specs=in_specs,
            out_specs=out_specs,
            scratch_shapes=scratch,
        ),
        out_shape=out_shape,
        compiler_params=params(58),
        cost_estimate=cost(work, 1e6),
        name=name,
    )(head, *[one[0] for one in rows_in], *fixed, *by_order)


def ordered(place, inner):
    _, pieces, tile, rows, _, _ = place
    return jax.ShapeDtypeStruct((rows // pieces, inner), BF16), pl.BlockSpec((tile, inner), lambda i, _: (i, 0))


def sent(place, inner):
    _, pieces, _, rows, _, n_head = place
    size = rows // n_head // pieces
    return [jax.ShapeDtypeStruct((size, inner), BF16)] * n_head, [whole((size, inner))] * n_head


def gates(place, hidden, w_f, w_r, work):
    shape, spec = ordered(place, w_f.shape[1])
    return by_destination(gates_kernel, "gates", place, [(hidden, (place[2], hidden.shape[1]), 0, 0)], [w_f, w_r], [],
                          [shape] * 2, [spec] * 2, work)


def inside_kernel(heads, inner, actf_ref, smallf_ref, cumtf_ref, actr_ref, smallr_ref, cumtr_ref, lanes_ref, copy_ref,
                  basef_ref, baser_ref):
    width = inner // heads
    per = 128 // width
    size = actf_ref.shape[0]
    lane = lax.broadcasted_iota(jnp.int32, (size, 128), 1)
    group = lax.broadcasted_iota(jnp.int32, (CHUNK, 128), 1) // width
    dts = [jnp.where(lane < heads, ref[...], 0.0) for ref in (smallf_ref, smallr_ref)]
    wide = spread(jnp.concatenate(dts + [jnp.broadcast_to(lanes_ref[2:3, :], (8, 128))], axis=0), copy_ref[...])
    skip = wide[2 * size : 2 * size + 1]
    sides = ((False, actf_ref, smallf_ref, cumtf_ref, basef_ref), (True, actr_ref, smallr_ref, cumtr_ref, baser_ref))
    for c in range(0, size, CHUNK):
        rows = slice(c, c + CHUNK)
        for k, (reverse, act_ref, small_ref, cumt_ref, base_ref) in enumerate(sides):
            small = small_ref[rows, :]
            values = act_ref[rows, :inner].astype(F32)
            weighted = (values * wide[k * size + c : k * size + c + CHUNK]).astype(BF16)
            scores = lax.dot_general(act_ref[rows, inner + STATE :], act_ref[rows, inner : inner + STATE],
                                     (((1,), (1,)), ((), ())), preferred_element_type=F32)
            scores = jnp.where(tri(CHUNK, reverse), scores, 0.0)
            for p in range(inner // 128):
                cols = slice(p * 128, (p + 1) * 128)
                pair = weighted[:, cols]
                mixing, stacked = [], []
                for q in range(per):
                    h = p * per + q
                    gap = jnp.minimum(small[:, heads + h : heads + h + 1] - cumt_ref[h : h + 1, rows], 0.0)
                    mixing.append((scores * jnp.exp(gap)).astype(BF16))
                    stacked.append(jnp.where(group == q, pair, jnp.zeros_like(pair)))
                out = jnp.dot(jnp.concatenate(mixing, axis=1), jnp.concatenate(stacked, axis=0),
                              preferred_element_type=F32)
                base_ref[rows, cols] = (out + skip[:, cols] * values[:, cols]).astype(BF16)


def inside_rows(strands, tile, heads):
    rows_in = []
    for act, small, cumt in strands:
        rows_in += [(act, (tile, act.shape[1]), 0, 0), (small, (tile, 128), 0, 0), (cumt, (heads, tile), 1, 0)]
    return rows_in


def inside(place, strands, lanes, copy, heads, inner, work):
    shape, spec = ordered(place, inner)
    return by_destination(functools.partial(inside_kernel, heads, inner), "inside", place,
                          inside_rows(strands, place[2], heads), [lanes, copy], [], [shape] * 2, [spec] * 2, work)


def finish_kernel(heads, inner, *refs):
    (cf_ref, ef_ref, pf_ref, sf_ref, cr_ref, er_ref, pr_ref, sr_ref, in_ref, copy_ref,
     zf_ref, zr_ref, bf_ref, br_ref, *out_refs) = refs
    width = inner // heads
    size = cf_ref.shape[0]
    row = lax.broadcasted_iota(jnp.int32, (256, 256), 0) // width
    column = lax.broadcasted_iota(jnp.int32, (256, 256), 1) // width
    mean = jnp.where(row == column, 1.0 / width, 0.0).astype(BF16)
    grown = spread(jnp.exp(jnp.minimum(jnp.concatenate([sf_ref[...], sr_ref[...]], axis=0), 0.0)), copy_ref[...])
    both = None
    for k, (c_ref, b_ref, z_ref, e_ref, p_ref) in enumerate(
            ((cf_ref, bf_ref, zf_ref, ef_ref, pf_ref), (cr_ref, br_ref, zr_ref, er_ref, pr_ref))):
        parts = []
        for c in range(e_ref.shape[0]):
            entering = (e_ref[c].astype(F32) + p_ref[c, 1:2, :] * in_ref[k]).astype(BF16)
            parts.append(jnp.dot(c_ref[c * CHUNK : (c + 1) * CHUNK, :], entering, preferred_element_type=F32))
        reads = jnp.concatenate(parts, axis=0)
        out = b_ref[...].astype(F32) + reads * grown[k * size : (k + 1) * size]
        gated = out * silu(z_ref[...].astype(F32))
        squares = (gated * gated).astype(BF16)
        means = jnp.concatenate(
            [jnp.dot(squares[:, g : g + 256], mean, preferred_element_type=F32) for g in range(0, inner, 256)], axis=1)
        result = gated * lax.rsqrt(means + EPS)
        both = result if both is None else both + result
    both = both.astype(BF16)
    step = pl.program_id(0)
    per_piece = out_refs[0].shape[0] // size
    for d, ref in enumerate(out_refs):
        @pl.when(step // per_piece == d)
        def _():
            ref[pl.ds(pl.multiple_of(lax.rem(step, per_piece) * size, size), size), :] = both


def finish_rows(strand, tile, inner):
    enter, prior = strand
    per = tile // CHUNK
    return [(enter, (per, STATE, inner), 0, 0), (prior, (per, 8, inner), 0, 0)]


def finish(place, strands, ends, bases, gated, entering, copy, heads, inner):
    tile = place[2]
    shapes, specs = sent(place, inner)
    rows_in = []
    for (act, small, _), end in zip(strands, ends):
        rows_in += [(act, (tile, STATE), 0, act.shape[1] // STATE - 1)] + finish_rows(end, tile, inner)
        rows_in += [(small, (tile, 128), 0, 0)]
    return by_destination(functools.partial(finish_kernel, heads, inner), "finish", place, rows_in, [entering, copy],
                          [*gated, *bases], shapes, specs, 1e8)


def settle_kernel(heads, inner, *refs):
    (actf_ref, smallf_ref, cumtf_ref, actr_ref, smallr_ref, cumtr_ref, ef_ref, pf_ref, er_ref, pr_ref,
     lanes_ref, first_ref, in_ref, second_ref, zf_ref, zr_ref, *out_refs, basef, baser) = refs
    inside_kernel(heads, inner, actf_ref, smallf_ref, cumtf_ref, actr_ref, smallr_ref, cumtr_ref, lanes_ref, first_ref,
                  basef, baser)
    maps = [ref.at[:, pl.ds(inner + STATE, STATE)] for ref in (actf_ref, actr_ref)]
    finish_kernel(heads, inner, maps[0], ef_ref, pf_ref, smallf_ref, maps[1], er_ref, pr_ref, smallr_ref,
                  in_ref, second_ref, zf_ref, zr_ref, basef, baser, *out_refs)


def settle(place, strands, ends, gated, lanes, first, entering, second, heads, inner):
    tile = place[2]
    shapes, specs = sent(place, inner)
    rows_in = inside_rows(strands, tile, heads) + finish_rows(ends[0], tile, inner) + finish_rows(ends[1], tile, inner)
    return by_destination(functools.partial(settle_kernel, heads, inner), "settle", place, rows_in,
                          [lanes, first, entering, second], list(gated), shapes, specs, 1e8,
                          [pltpu.VMEM((tile, inner), BF16)] * 2)


def read_message(ref, at):
    tail = ref[at + STATE : at + STATE + TAIL, :].astype(F32)
    return ref[at : at + STATE, :].astype(F32), tail[0:1] + tail[1:2] + tail[2:3]


def hop_kernel(first, *refs):
    upper_ref, mine_ref, other_ref = refs[:3]
    into_ref = None if first else refs[3]
    new_ref, msg_ref = refs[-2:]
    upper = upper_ref[0].astype(F32)
    for k in (0, 1):
        later = upper if k == 0 else 1.0 - upper
        at = k * (STATE + TAIL)
        o_state, o_log = read_message(other_ref, at)
        if first:
            new_state, new_log = later * o_state, later * o_log
        else:
            into_log = into_ref[k, STATE : STATE + 1, :]
            new_state = into_ref[k, :STATE, :] + later * jnp.exp(into_log) * o_state
            new_log = into_log + later * o_log
        new_ref[k, :STATE, :] = new_state
        new_ref[k, STATE:, :] = jnp.broadcast_to(new_log, (8, new_log.shape[1]))
        state, log = read_message(mine_ref, at)
        of_other = later * jnp.exp(log) + (1.0 - later)
        of_mine = later + (1.0 - later) * jnp.exp(o_log)
        msg_ref[at : at + STATE, :] = (of_other * o_state + of_mine * state).astype(BF16)
        t = log + o_log
        high = t.astype(BF16).astype(F32)
        mid = (t - high).astype(BF16).astype(F32)
        low = t - high - mid
        row = lax.broadcasted_iota(jnp.int32, (TAIL, t.shape[1]), 0)
        packed = jnp.where(row == 0, high, jnp.where(row == 1, mid, jnp.where(row == 2, low, 0.0)))
        msg_ref[at + STATE : at + STATE + TAIL, :] = packed.astype(BF16)


def local_call(kernel, name, smem, operands, out_shape):
    return pl.pallas_call(
        kernel,
        grid=(1,),
        in_specs=[pl.BlockSpec(memory_space=pltpu.SMEM)] + [whole(x.shape) for x in operands],
        out_specs=[whole(x.shape) for x in out_shape],
        out_shape=out_shape,
        compiler_params=params(10),
        cost_estimate=cost(1e6, 1.5e6),
        name=name,
    )(smem, *operands)


def join_kernel(count, *refs):
    place_ref, into_ref = refs[:2]
    slots, out_ref = refs[2:-1], refs[-1]
    place = place_ref[0]
    groups = [place ^ d for d in range(1, count)]
    read = [read_message(ref, 0) for ref in slots]
    ones = lambda condition: jnp.where(condition, 1.0, 0.0)
    sums = [None, None]
    for j, (state, _) in zip(groups, read):
        lower = ones(j < place)
        log = None
        for i, (_, other) in zip(groups, read):
            between = jnp.logical_or(jnp.logical_and(j < i, i < place), jnp.logical_and(place < i, i < j))
            term = ones(between) * other
            log = term if log is None else log + term
        part = jnp.exp(log) * state
        for k, share in enumerate((lower, 1.0 - lower)):
            sums[k] = share * part if sums[k] is None else sums[k] + share * part
    for k in (0, 1):
        out_ref[k] = into_ref[k, :STATE, :] + jnp.exp(into_ref[k, STATE : STATE + 1, :]) * sums[k]


def incoming(message, axis, beside, before):
    count, index = lax.axis_size(axis), lax.axis_index(axis)
    inner = message.shape[1]
    into = None
    distance = 1
    while count // distance > 4:
        other = lax.ppermute(message, axis, [(i, i ^ distance) for i in range(count)])
        if into is None:
            other, *beside = lax.optimization_barrier((other, *beside))
        upper = ((index // distance) % 2).astype(jnp.int32).reshape(1)
        operands = [message, other] + ([] if into is None else [into])
        out_shape = [jax.ShapeDtypeStruct((2, STATE + 8, inner), F32), jax.ShapeDtypeStruct(message.shape, BF16)]
        into, message = local_call(functools.partial(hop_kernel, into is None), "hop", upper, operands, out_shape)
        distance *= 2
    if into is None:
        into = jnp.zeros((2, STATE + 8, inner), F32)
    message, *before = lax.optimization_barrier((message, *before))
    groups = count // distance
    place = index // distance
    half = STATE + TAIL
    slots = []
    for d in range(1, groups):
        highest = 1 << (d.bit_length() - 1)
        above = (place // highest) % 2
        block = lax.dynamic_slice_in_dim(message, above * half, half, 0)
        slots.append(lax.ppermute(block, axis, [(i, i ^ (d * distance)) for i in range(count)]))
    joined = local_call(functools.partial(join_kernel, groups), "join", place.astype(jnp.int32).reshape(1), [into] + slots,
                        [pltpu.HBM((2, STATE, inner), F32)])[0]
    return joined, beside, before


def shifted(block, axis, distance):
    devices = range(lax.axis_size(axis))
    return lax.ppermute(block, axis, [(i - distance, i) for i in devices if i - distance in devices])


def rotated(block, d, count):
    return lax.ppermute(block, "head", [(i, (i + d) % count) for i in range(count)])


def on_device(
    hidden, norm_gain, w_zx, w_bc, w_dt, dt_bias, decay_rate, skip_gain, conv_x, conv_bc, w_out
):
    rows, depth = hidden.shape
    inner = conv_x.shape[1]
    heads = dt_bias.shape[0]
    width = inner // heads
    n_ctx, n_head = lax.axis_size("ctx"), lax.axis_size("head")
    ctx, head = lax.axis_index("ctx"), lax.axis_index("head")

    rim_f = shifted(hidden[rows - RIM :], "ctx", 1)
    rim_r = shifted(hidden[:RIM], "ctx", -1)

    half = w_out.shape[0] // 2
    parity = ctx % 2
    own_half = lax.dynamic_slice_in_dim(w_out, parity * half, half, 0)
    same = [rotated(own_half, d, n_head) for d in range(1, n_head)]

    lanes = jnp.pad(jnp.stack([dt_bias, decay_rate, skip_gain]), [(0, 0), (0, 128 - heads)])
    copy_first = spread_matrix(0, heads, width)
    copy_second = spread_matrix(heads, heads, width)
    (act_f, small_f, cumt_f, enter_f, prior_f, act_r, small_r, cumt_r, enter_r, prior_r,
     message, g_f, g_r) = project(hidden, rim_f, rim_r, (w_zx, w_bc, w_dt.T, norm_gain[None, :]), conv_x, conv_bc, lanes, copy_first, heads, inner)
    share = rows // n_head
    pieces = 2 if share % (2 * CHUNK) == 0 else 1
    size = share // pieces
    tile = min(TILE, size)
    place = lambda k: (k, pieces, tile, rows, head.astype(jnp.int32).reshape(1), n_head)
    strands = ((act_f, small_f, cumt_f), (act_r, small_r, cumt_r))
    ends = ((enter_f, prior_f), (enter_r, prior_r))
    entering, gated, same = incoming(message, "ctx", gates(place(0), hidden, g_f, g_r, 5e9), same)
    bases = inside(place(0), strands, lanes, copy_first, heads, inner, 8e9)
    parts = finish(place(0), strands, ends, bases, gated, entering, copy_second, heads, inner)
    (g_f, g_r), same, parts = lax.optimization_barrier(((g_f, g_r), same, parts))
    swapped = lambda blocks: lax.ppermute(jnp.concatenate(blocks, axis=0), "ctx", [(i, i ^ 1) for i in range(n_ctx)])
    other = None if pieces > 1 else swapped(same)
    arrived = [[rotated(block, d, n_head) if d else block for d, block in enumerate(parts)]]
    for k in range(1, pieces):
        gated = gates(place(k), hidden, g_f, g_r, 1e8)
        if other is None:
            gated, same = lax.optimization_barrier((gated, same))
            other = swapped(same)
        parts = settle(place(k), strands, ends, gated, lanes, copy_first, entering, copy_second, heads, inner)
        parts, arrived[k - 1], other, same = lax.optimization_barrier((parts, arrived[k - 1], other, same))
        arrived.append([rotated(block, d, n_head) if d else block for d, block in enumerate(parts)])
    own_rows = lax.dynamic_slice_in_dim(hidden, head * share, share, 0)
    groups = [w_out]
    for d, one in enumerate(same):
        two = other[d * half : (d + 1) * half]
        groups.append(jnp.concatenate([jnp.where(parity == 0, one, two), jnp.where(parity == 0, two, one)], axis=0))
    result = None
    for k in range(pieces):
        total = own_rows[k * size : (k + 1) * size].astype(F32)
        for block, weights in zip(arrived[k], groups):
            total = total + jnp.dot(block, weights, preferred_element_type=F32)
        total = total.astype(BF16)
        if result is None:
            result = jnp.pad(total, ((0, share - size), (0, 0)))
        else:
            result = lax.dynamic_update_slice(result, total, (k * size, 0))
    return result


def solution(mesh):
    placed = (
        P("ctx", None),
        P(),
        P(None, None, "head"),
        P(),
        P(None, "head"),
        P("head"),
        P("head"),
        P("head"),
        P(None, "head"),
        P(),
        P("head", None),
    )
    return jax.shard_map(
        on_device, mesh=mesh, in_specs=placed, out_specs=P(("ctx", "head"), None), check_vma=False
    )
```

```python
import functools

import jax
import jax.numpy as jnp
import numpy as np
from jax import lax
from jax.experimental import pallas as pl
from jax.experimental.pallas import tpu as pltpu
from jax.sharding import PartitionSpec as P

STATE = 128
CHUNK = 128
TILE = 256
EPS = 1e-05
RIM = 16
TAIL = 16
F32 = jnp.float32
BF16 = jnp.bfloat16
MIB = 2**20


def params(limit):
    return pltpu.CompilerParams(
        dimension_semantics=("arbitrary",), vmem_limit_bytes=limit * MIB
    )


def cost(flops, bytes_accessed):
    return pl.CostEstimate(flops=int(flops), bytes_accessed=int(bytes_accessed), transcendentals=0)


def whole(shape):
    return pl.BlockSpec(shape, lambda *_: (0,) * len(shape), pipeline_mode=pl.Buffered(1))


def silu(x):
    half = 0.5 * x
    return half + half * jnp.tanh(half)


def tri(rows, reverse):
    r = lax.broadcasted_iota(jnp.int32, (rows, rows), 0)
    c = lax.broadcasted_iota(jnp.int32, (rows, rows), 1)
    return (r <= c) if reverse else (r >= c)


def spread_matrix(first, heads, width):
    r = np.arange(2 * 128)[:, None] % 128
    c = np.arange(heads * width)[None, :] // width
    return jnp.asarray((r == c + first).astype(BF16))


def spread(q, matrix):
    high = q.astype(BF16)
    low = (q - high.astype(F32)).astype(BF16)
    return jnp.dot(jnp.concatenate([high, low], axis=1), matrix, preferred_element_type=F32)


def prepare(inner, zx_ref, bc_ref, dt_ref, gain_ref, wf_ref, wr_ref, gf_ref, gr_ref):
    depth = zx_ref.shape[0]
    rows = min(256, depth)
    r = lax.broadcasted_iota(jnp.int32, (rows, rows), 0)
    c = lax.broadcasted_iota(jnp.int32, (rows, rows), 1)
    turn = (r + c == rows - 1).astype(BF16)
    for b in range(0, depth, rows):
        here, there = slice(b, b + rows), slice(depth - rows - b, depth - b)
        gain = jnp.transpose(jnp.broadcast_to(gain_ref[:, here], (128, rows)))
        zx = zx_ref[here].astype(F32).reshape(rows, 2 * inner)
        steps = dt_ref[:, here].astype(F32)
        steps = jnp.transpose(jnp.concatenate([steps, jnp.zeros((128 - steps.shape[0], rows), F32)], axis=0))

        def put(part, at, forward_ref, turned_ref):
            size = part.shape[1]
            scaled = jnp.concatenate([part[:, g : g + 128] * gain for g in range(0, size, 128)], axis=1).astype(BF16)
            forward_ref[here, at : at + size] = scaled
            turned_ref[there, at : at + size] = jnp.dot(turn, scaled, preferred_element_type=F32).astype(BF16)

        put(zx[:, inner:], 0, wf_ref, wr_ref)
        put(bc_ref[here].astype(F32), inner, wf_ref, wr_ref)
        put(steps, inner + bc_ref.shape[1], wf_ref, wr_ref)
        put(zx[:, :inner], 0, gf_ref, gr_ref)


def row_scale(h):
    hf = h.astype(F32)
    return lax.rsqrt(jnp.mean(hf * hf, axis=-1, keepdims=True) + EPS)


def project_kernel(heads, inner, *refs):
    (hf_ref, hr_ref, rimf_ref, rimr_ref, zx_ref, bc_ref, wdt_ref, gain_ref, convx_ref, convbc_ref, lanes_ref, copy_ref,
     actf_ref, smallf_ref, cumtf_ref, enterf_ref, priorf_ref,
     actr_ref, smallr_ref, cumtr_ref, enterr_ref, priorr_ref,
     msg_ref, gf_ref, gr_ref, wf_ref, wr_ref, buff, bufr, statef, stater, totalf, totalr) = refs
    step = pl.program_id(0)
    last = pl.num_programs(0) - 1
    stream = inner + 2 * STATE
    blocks = stream // 128
    rows = hf_ref.shape[0]
    count = rows // CHUNK
    sides = (
        (False, hf_ref, rimf_ref, wf_ref, actf_ref, smallf_ref, cumtf_ref, enterf_ref, priorf_ref, buff, statef, totalf),
        (True, hr_ref, rimr_ref, wr_ref, actr_ref, smallr_ref, cumtr_ref, enterr_ref, priorr_ref, bufr, stater, totalr),
    )

    @pl.when(step == 0)
    def _():
        prepare(inner, zx_ref, bc_ref, wdt_ref, gain_ref, wf_ref, wr_ref, gf_ref, gr_ref)
        for reverse, _, rim_ref, w_ref, _, _, _, _, _, buf, state, total in sides:
            edge = rows if reverse else 0
            state[...] = jnp.zeros_like(state)
            total[...] = jnp.zeros_like(total)
            rim = rim_ref[...]
            out = jnp.dot(rim, w_ref[:, :stream], preferred_element_type=F32) * row_scale(rim)
            for j in range(blocks):
                part = out[:, j * 128 : (j + 1) * 128]
                buf[j, edge : edge + 8, :] = part[:8] if reverse else part[RIM - 8 :]

    lane = lax.broadcasted_iota(jnp.int32, (rows, 128), 1)
    row8 = lax.broadcasted_iota(jnp.int32, (8, 128), 0)
    r = lax.broadcasted_iota(jnp.int32, (rows, rows), 0)
    c = lax.broadcasted_iota(jnp.int32, (rows, rows), 1)
    same = r // CHUNK == c // CHUNK
    hs = [side[1][...] for side in sides]
    scales = [row_scale(h) for h in hs]
    tail_rows, aux_rows = [], []
    for k, (reverse, _, _, w_ref, _, small_ref, cumt_ref, _, _, _, _, total_ref) in enumerate(sides):
        raw = jnp.dot(hs[k], w_ref[:, stream:], preferred_element_type=F32) * scales[k] + lanes_ref[0:1, :]
        dt = jnp.maximum(raw, 0.0) + jnp.log1p(jnp.exp(-jnp.abs(raw)))
        dt = jnp.where(lane < heads, dt, 0.0)
        steps = -lanes_ref[1:2, :] * dt
        high = steps.astype(BF16).astype(F32)
        mid = (steps - high).astype(BF16).astype(F32)
        low = steps - high - mid
        packed = (high + pltpu.roll(mid, heads, 1) + pltpu.roll(low, 2 * heads, 1)).astype(BF16)
        mask = jnp.where(jnp.logical_and(same, (r <= c) if reverse else (r >= c)), 1.0, 0.0).astype(BF16)
        sums = jnp.dot(mask, packed, preferred_element_type=F32)
        sums = sums + pltpu.roll(sums, 128 - heads, 1) + pltpu.roll(sums, 128 - 2 * heads, 1)
        cum = jnp.where(lane < heads, sums, 0.0)
        small_ref[...] = dt + pltpu.roll(cum, heads, 1)
        running = total_ref[...]
        tails = [None] * count
        aux = [None] * count
        for i in range(count):
            n = count - 1 - i if reverse else i
            at = slice(n * CHUNK, (n + 1) * CHUNK)
            cumt_ref[:, at] = jnp.transpose(cum[at])[:heads]
            end = cum[n * CHUNK : n * CHUNK + 1] if reverse else cum[(n + 1) * CHUNK - 1 : (n + 1) * CHUNK]
            tails[n] = dt[at] * jnp.exp(end - cum[at])
            aux[n] = jnp.where(row8 == 0, jnp.exp(end), jnp.exp(running))
            running = running + end
        total_ref[...] = running
        tail_rows += tails
        aux_rows += aux
    weights = spread(jnp.concatenate(tail_rows + aux_rows, axis=0), copy_ref[...])

    for g in range(0, stream, 256):
        for k, (reverse, _, _, w_ref, act_ref, _, _, _, _, buf, _, _) in enumerate(sides):
            edge = rows if reverse else 0
            body = 0 if reverse else 8
            out = jnp.dot(hs[k], w_ref[:, g : g + 256], preferred_element_type=F32) * scales[k]
            for j in range(g // 128, g // 128 + 2):
                x = out[:, j * 128 - g : (j + 1) * 128 - g]
                buf[j, body : body + rows, :] = x
                own = j * 128 - (0 if j * 128 < inner else inner)
                taps = (convx_ref if j * 128 < inner else convbc_ref)[:, own : own + 128]
                total = taps[3:4] * x
                for d in (1, 2, 3):
                    at = body + d if reverse else body - d
                    total = total + taps[3 - d : 4 - d] * buf[j, at : at + rows, :]
                act_ref[:, j * 128 : (j + 1) * 128] = silu(total).astype(BF16)
                buf[j, edge : edge + 8, :] = x[:8] if reverse else x[rows - 8 :]

    for i in range(count):
        for k, (reverse, _, _, _, act_ref, _, _, enter_ref, prior_ref, _, state, _) in enumerate(sides):
            n = count - 1 - i if reverse else i
            at = slice(n * CHUNK, (n + 1) * CHUNK)
            own = weights[(k * count + n) * CHUNK : (k * count + n + 1) * CHUNK]
            aux = weights[2 * rows + (k * count + n) * 8 : 2 * rows + (k * count + n + 1) * 8]
            tails = (act_ref[at, :inner].astype(F32) * own).astype(BF16)
            ends = lax.dot_general(act_ref[at, inner : inner + STATE], tails, (((0,), (0,)), ((), ())),
                                   preferred_element_type=F32)
            before = state[...]
            enter_ref[n] = before.astype(BF16)
            prior_ref[n] = aux
            state[...] = before * aux[:1] + ends

    @pl.when(step == last)
    def _():
        for k, side in enumerate(sides):
            state, total = side[-2:]
            at = k * (STATE + TAIL)
            msg_ref[at : at + STATE, :] = state[...].astype(BF16)
            t = total[...]
            high = t.astype(BF16).astype(F32)
            mid = (t - high).astype(BF16).astype(F32)
            low = t - high - mid
            packed = jnp.where(row8 == 0, high, jnp.where(row8 == 1, mid, jnp.where(row8 == 2, low, 0.0)))
            rows3 = spread(packed, copy_ref[...])
            msg_ref[at + STATE : at + STATE + TAIL, :] = jnp.concatenate(
                [rows3, jnp.zeros_like(rows3)], axis=0).astype(BF16)


def project(hidden, rim_f, rim_r, weights, conv_x, conv_bc, lanes, copy, heads, inner):
    rows, depth = hidden.shape
    stream = inner + 2 * STATE
    n = rows // TILE
    per = TILE // CHUNK
    up, down = (lambda i: i), (lambda i: n - 1 - i)
    by_rows = lambda width, at: pl.BlockSpec((TILE, width), lambda i: (at(i), 0))
    out_specs, out_shape = [], []
    for at in (up, down):
        out_specs += [by_rows(stream, at), by_rows(128, at),
                      pl.BlockSpec((heads, TILE), lambda i, at=at: (0, at(i))),
                      pl.BlockSpec((per, STATE, inner), lambda i, at=at: (at(i), 0, 0)),
                      pl.BlockSpec((per, 8, inner), lambda i, at=at: (at(i), 0, 0))]
        out_shape += [jax.ShapeDtypeStruct((rows, stream), BF16),
                      jax.ShapeDtypeStruct((rows, 128), F32), jax.ShapeDtypeStruct((heads, rows), F32),
                      jax.ShapeDtypeStruct((n * per, STATE, inner), BF16),
                      jax.ShapeDtypeStruct((n * per, 8, inner), F32)]
    message = (2 * (STATE + TAIL), inner)
    buf = pltpu.VMEM((stream // 128, TILE + 8, 128), F32)
    state, total = pltpu.VMEM((STATE, inner), F32), pltpu.VMEM((8, 128), F32)
    return pl.pallas_call(
        functools.partial(project_kernel, heads, inner),
        grid=(n,),
        in_specs=[by_rows(depth, up), by_rows(depth, down), whole(rim_f.shape), whole(rim_r.shape),
                  *[whole(x.shape) for x in weights], whole(conv_x.shape), whole(conv_bc.shape), whole(lanes.shape),
                  whole(copy.shape)],
        out_specs=out_specs + [whole(message), whole((depth, inner)), whole((depth, inner))],
        out_shape=out_shape + [jax.ShapeDtypeStruct(message, BF16)] + [jax.ShapeDtypeStruct((depth, inner), BF16)] * 2,
        scratch_shapes=[pltpu.VMEM((depth, stream + 128), BF16)] * 2 + [buf, buf, state, state, total, total],
        compiler_params=params(58),
        cost_estimate=cost(22e9, 40e6),
        name="project",
    )(hidden, hidden, rim_f, rim_r, *weights, conv_x, conv_bc, lanes, copy)


def gates_kernel(h_ref, wf_ref, wr_ref, zf_ref, zr_ref):
    h = h_ref[...]
    scale = row_scale(h)
    for w_ref, z_ref in ((wf_ref, zf_ref), (wr_ref, zr_ref)):
        z_ref[...] = (jnp.dot(h, w_ref[...], preferred_element_type=F32) * scale).astype(BF16)


def by_destination(kernel, name, place, rows_in, fixed, by_order, out_shape, out_specs, work, scratch=()):
    k, pieces, tile, rows, head, n_head = place
    share = rows // n_head
    per_piece, per_share = share // pieces // tile, share // tile

    def at(i, head_ref):
        return lax.rem(head_ref[0] + i // per_piece, n_head) * per_share + k * per_piece + lax.rem(i, per_piece)

    def spec(shape, dim, last):
        def index(i, head_ref):
            where = [0] * len(shape)
            where[-1] = last
            where[dim] = at(i, head_ref)
            return tuple(where)

        return pl.BlockSpec(shape, index)

    in_specs = [spec(*one[1:]) for one in rows_in] + [whole(x.shape) for x in fixed]
    in_specs += [pl.BlockSpec((tile, x.shape[1]), lambda i, _: (i, 0)) for x in by_order]
    return pl.pallas_call(
        lambda _, *refs: kernel(*refs),
        grid_spec=pltpu.PrefetchScalarGridSpec(
            num_scalar_prefetch=1,
            grid=(n_head * per_piece,),
            in_specs=in_specs,
            out_specs=out_specs,
            scratch_shapes=scratch,
        ),
        out_shape=out_shape,
        compiler_params=params(58),
        cost_estimate=cost(work, 1e6),
        name=name,
    )(head, *[one[0] for one in rows_in], *fixed, *by_order)


def ordered(place, inner):
    _, pieces, tile, rows, _, _ = place
    return jax.ShapeDtypeStruct((rows // pieces, inner), BF16), pl.BlockSpec((tile, inner), lambda i, _: (i, 0))


def sent(place, inner):
    _, pieces, _, rows, _, n_head = place
    size = rows // n_head // pieces
    return [jax.ShapeDtypeStruct((size, inner), BF16)] * n_head, [whole((size, inner))] * n_head


def gates(place, hidden, w_f, w_r, work):
    shape, spec = ordered(place, w_f.shape[1])
    return by_destination(gates_kernel, "gates", place, [(hidden, (place[2], hidden.shape[1]), 0, 0)], [w_f, w_r], [],
                          [shape] * 2, [spec] * 2, work)


def inside_kernel(heads, inner, actf_ref, smallf_ref, cumtf_ref, actr_ref, smallr_ref, cumtr_ref, lanes_ref, copy_ref,
                  basef_ref, baser_ref):
    width = inner // heads
    per = 128 // width
    size = actf_ref.shape[0]
    lane = lax.broadcasted_iota(jnp.int32, (size, 128), 1)
    group = lax.broadcasted_iota(jnp.int32, (CHUNK, 128), 1) // width
    dts = [jnp.where(lane < heads, ref[...], 0.0) for ref in (smallf_ref, smallr_ref)]
    wide = spread(jnp.concatenate(dts + [jnp.broadcast_to(lanes_ref[2:3, :], (8, 128))], axis=0), copy_ref[...])
    skip = wide[2 * size : 2 * size + 1]
    sides = ((False, actf_ref, smallf_ref, cumtf_ref, basef_ref), (True, actr_ref, smallr_ref, cumtr_ref, baser_ref))
    for c in range(0, size, CHUNK):
        rows = slice(c, c + CHUNK)
        for k, (reverse, act_ref, small_ref, cumt_ref, base_ref) in enumerate(sides):
            small = small_ref[rows, :]
            values = act_ref[rows, :inner].astype(F32)
            weighted = (values * wide[k * size + c : k * size + c + CHUNK]).astype(BF16)
            scores = lax.dot_general(act_ref[rows, inner + STATE :], act_ref[rows, inner : inner + STATE],
                                     (((1,), (1,)), ((), ())), preferred_element_type=F32)
            scores = jnp.where(tri(CHUNK, reverse), scores, 0.0)
            for p in range(inner // 128):
                cols = slice(p * 128, (p + 1) * 128)
                pair = weighted[:, cols]
                mixing, stacked = [], []
                for q in range(per):
                    h = p * per + q
                    gap = jnp.minimum(small[:, heads + h : heads + h + 1] - cumt_ref[h : h + 1, rows], 0.0)
                    mixing.append((scores * jnp.exp(gap)).astype(BF16))
                    stacked.append(jnp.where(group == q, pair, jnp.zeros_like(pair)))
                out = jnp.dot(jnp.concatenate(mixing, axis=1), jnp.concatenate(stacked, axis=0),
                              preferred_element_type=F32)
                base_ref[rows, cols] = (out + skip[:, cols] * values[:, cols]).astype(BF16)


def inside_rows(strands, tile, heads):
    rows_in = []
    for act, small, cumt in strands:
        rows_in += [(act, (tile, act.shape[1]), 0, 0), (small, (tile, 128), 0, 0), (cumt, (heads, tile), 1, 0)]
    return rows_in


def inside(place, strands, lanes, copy, heads, inner, work):
    shape, spec = ordered(place, inner)
    return by_destination(functools.partial(inside_kernel, heads, inner), "inside", place,
                          inside_rows(strands, place[2], heads), [lanes, copy], [], [shape] * 2, [spec] * 2, work)


def finish_kernel(heads, inner, *refs):
    (cf_ref, ef_ref, pf_ref, sf_ref, cr_ref, er_ref, pr_ref, sr_ref, in_ref, copy_ref,
     zf_ref, zr_ref, bf_ref, br_ref, *out_refs) = refs
    width = inner // heads
    size = cf_ref.shape[0]
    row = lax.broadcasted_iota(jnp.int32, (256, 256), 0) // width
    column = lax.broadcasted_iota(jnp.int32, (256, 256), 1) // width
    mean = jnp.where(row == column, 1.0 / width, 0.0).astype(BF16)
    grown = spread(jnp.exp(jnp.minimum(jnp.concatenate([sf_ref[...], sr_ref[...]], axis=0), 0.0)), copy_ref[...])
    both = None
    for k, (c_ref, b_ref, z_ref, e_ref, p_ref) in enumerate(
            ((cf_ref, bf_ref, zf_ref, ef_ref, pf_ref), (cr_ref, br_ref, zr_ref, er_ref, pr_ref))):
        parts = []
        for c in range(e_ref.shape[0]):
            entering = (e_ref[c].astype(F32) + p_ref[c, 1:2, :] * in_ref[k]).astype(BF16)
            parts.append(jnp.dot(c_ref[c * CHUNK : (c + 1) * CHUNK, :], entering, preferred_element_type=F32))
        reads = jnp.concatenate(parts, axis=0)
        out = b_ref[...].astype(F32) + reads * grown[k * size : (k + 1) * size]
        gated = out * silu(z_ref[...].astype(F32))
        squares = (gated * gated).astype(BF16)
        means = jnp.concatenate(
            [jnp.dot(squares[:, g : g + 256], mean, preferred_element_type=F32) for g in range(0, inner, 256)], axis=1)
        result = gated * lax.rsqrt(means + EPS)
        both = result if both is None else both + result
    both = both.astype(BF16)
    step = pl.program_id(0)
    per_piece = out_refs[0].shape[0] // size
    for d, ref in enumerate(out_refs):
        @pl.when(step // per_piece == d)
        def _():
            ref[pl.ds(pl.multiple_of(lax.rem(step, per_piece) * size, size), size), :] = both


def finish_rows(strand, tile, inner):
    enter, prior = strand
    per = tile // CHUNK
    return [(enter, (per, STATE, inner), 0, 0), (prior, (per, 8, inner), 0, 0)]


def finish(place, strands, ends, bases, gated, entering, copy, heads, inner):
    tile = place[2]
    shapes, specs = sent(place, inner)
    rows_in = []
    for (act, small, _), end in zip(strands, ends):
        rows_in += [(act, (tile, STATE), 0, act.shape[1] // STATE - 1)] + finish_rows(end, tile, inner)
        rows_in += [(small, (tile, 128), 0, 0)]
    return by_destination(functools.partial(finish_kernel, heads, inner), "finish", place, rows_in, [entering, copy],
                          [*gated, *bases], shapes, specs, 1e8)


def settle_kernel(heads, inner, *refs):
    (actf_ref, smallf_ref, cumtf_ref, actr_ref, smallr_ref, cumtr_ref, ef_ref, pf_ref, er_ref, pr_ref,
     lanes_ref, first_ref, in_ref, second_ref, zf_ref, zr_ref, *out_refs, basef, baser) = refs
    inside_kernel(heads, inner, actf_ref, smallf_ref, cumtf_ref, actr_ref, smallr_ref, cumtr_ref, lanes_ref, first_ref,
                  basef, baser)
    maps = [ref.at[:, pl.ds(inner + STATE, STATE)] for ref in (actf_ref, actr_ref)]
    finish_kernel(heads, inner, maps[0], ef_ref, pf_ref, smallf_ref, maps[1], er_ref, pr_ref, smallr_ref,
                  in_ref, second_ref, zf_ref, zr_ref, basef, baser, *out_refs)


def settle(place, strands, ends, gated, lanes, first, entering, second, heads, inner):
    tile = place[2]
    shapes, specs = sent(place, inner)
    rows_in = inside_rows(strands, tile, heads) + finish_rows(ends[0], tile, inner) + finish_rows(ends[1], tile, inner)
    return by_destination(functools.partial(settle_kernel, heads, inner), "settle", place, rows_in,
                          [lanes, first, entering, second], list(gated), shapes, specs, 1e8,
                          [pltpu.VMEM((tile, inner), BF16)] * 2)


def read_message(ref, at):
    tail = ref[at + STATE : at + STATE + TAIL, :].astype(F32)
    return ref[at : at + STATE, :].astype(F32), tail[0:1] + tail[1:2] + tail[2:3]


def hop_kernel(first, *refs):
    upper_ref, mine_ref, other_ref = refs[:3]
    into_ref = None if first else refs[3]
    new_ref, msg_ref = refs[-2:]
    upper = upper_ref[0].astype(F32)
    for k in (0, 1):
        later = upper if k == 0 else 1.0 - upper
        at = k * (STATE + TAIL)
        o_state, o_log = read_message(other_ref, at)
        if first:
            new_state, new_log = later * o_state, later * o_log
        else:
            into_log = into_ref[k, STATE : STATE + 1, :]
            new_state = into_ref[k, :STATE, :] + later * jnp.exp(into_log) * o_state
            new_log = into_log + later * o_log
        new_ref[k, :STATE, :] = new_state
        new_ref[k, STATE:, :] = jnp.broadcast_to(new_log, (8, new_log.shape[1]))
        state, log = read_message(mine_ref, at)
        of_other = later * jnp.exp(log) + (1.0 - later)
        of_mine = later + (1.0 - later) * jnp.exp(o_log)
        msg_ref[at : at + STATE, :] = (of_other * o_state + of_mine * state).astype(BF16)
        t = log + o_log
        high = t.astype(BF16).astype(F32)
        mid = (t - high).astype(BF16).astype(F32)
        low = t - high - mid
        row = lax.broadcasted_iota(jnp.int32, (TAIL, t.shape[1]), 0)
        packed = jnp.where(row == 0, high, jnp.where(row == 1, mid, jnp.where(row == 2, low, 0.0)))
        msg_ref[at + STATE : at + STATE + TAIL, :] = packed.astype(BF16)


def local_call(kernel, name, smem, operands, out_shape):
    return pl.pallas_call(
        kernel,
        grid=(1,),
        in_specs=[pl.BlockSpec(memory_space=pltpu.SMEM)] + [whole(x.shape) for x in operands],
        out_specs=[whole(x.shape) for x in out_shape],
        out_shape=out_shape,
        compiler_params=params(10),
        cost_estimate=cost(1e6, 1.5e6),
        name=name,
    )(smem, *operands)


def join_kernel(count, *refs):
    place_ref, into_ref = refs[:2]
    slots, out_ref = refs[2:-1], refs[-1]
    place = place_ref[0]
    groups = [place ^ d for d in range(1, count)]
    read = [read_message(ref, 0) for ref in slots]
    ones = lambda condition: jnp.where(condition, 1.0, 0.0)
    sums = [None, None]
    for j, (state, _) in zip(groups, read):
        lower = ones(j < place)
        log = None
        for i, (_, other) in zip(groups, read):
            between = jnp.logical_or(jnp.logical_and(j < i, i < place), jnp.logical_and(place < i, i < j))
            term = ones(between) * other
            log = term if log is None else log + term
        part = jnp.exp(log) * state
        for k, share in enumerate((lower, 1.0 - lower)):
            sums[k] = share * part if sums[k] is None else sums[k] + share * part
    for k in (0, 1):
        out_ref[k] = into_ref[k, :STATE, :] + jnp.exp(into_ref[k, STATE : STATE + 1, :]) * sums[k]


def incoming(message, axis, beside, before):
    count, index = lax.axis_size(axis), lax.axis_index(axis)
    inner = message.shape[1]
    into = None
    distance = 1
    while count // distance > 4:
        other = lax.ppermute(message, axis, [(i, i ^ distance) for i in range(count)])
        if into is None:
            other, *beside = lax.optimization_barrier((other, *beside))
        upper = ((index // distance) % 2).astype(jnp.int32).reshape(1)
        operands = [message, other] + ([] if into is None else [into])
        out_shape = [jax.ShapeDtypeStruct((2, STATE + 8, inner), F32), jax.ShapeDtypeStruct(message.shape, BF16)]
        into, message = local_call(functools.partial(hop_kernel, into is None), "hop", upper, operands, out_shape)
        distance *= 2
    if into is None:
        into = jnp.zeros((2, STATE + 8, inner), F32)
    message, *before = lax.optimization_barrier((message, *before))
    groups = count // distance
    place = index // distance
    half = STATE + TAIL
    slots = []
    for d in range(1, groups):
        highest = 1 << (d.bit_length() - 1)
        above = (place // highest) % 2
        block = lax.dynamic_slice_in_dim(message, above * half, half, 0)
        slots.append(lax.ppermute(block, axis, [(i, i ^ (d * distance)) for i in range(count)]))
    joined = local_call(functools.partial(join_kernel, groups), "join", place.astype(jnp.int32).reshape(1), [into] + slots,
                        [pltpu.HBM((2, STATE, inner), F32)])[0]
    return joined, beside, before


def shifted(block, axis, distance):
    devices = range(lax.axis_size(axis))
    return lax.ppermute(block, axis, [(i - distance, i) for i in devices if i - distance in devices])


def rotated(block, d, count):
    return lax.ppermute(block, "head", [(i, (i + d) % count) for i in range(count)])


def on_device(
    hidden, norm_gain, w_zx, w_bc, w_dt, dt_bias, decay_rate, skip_gain, conv_x, conv_bc, w_out
):
    rows, depth = hidden.shape
    inner = conv_x.shape[1]
    heads = dt_bias.shape[0]
    width = inner // heads
    n_ctx, n_head = lax.axis_size("ctx"), lax.axis_size("head")
    ctx, head = lax.axis_index("ctx"), lax.axis_index("head")

    rim_f = shifted(hidden[rows - RIM :], "ctx", 1)
    rim_r = shifted(hidden[:RIM], "ctx", -1)

    half = w_out.shape[0] // 2
    parity = ctx % 2
    own_half = lax.dynamic_slice_in_dim(w_out, parity * half, half, 0)
    same = [rotated(own_half, d, n_head) for d in range(1, n_head)]

    lanes = jnp.pad(jnp.stack([dt_bias, decay_rate, skip_gain]), [(0, 0), (0, 128 - heads)])
    copy_first = spread_matrix(0, heads, width)
    copy_second = spread_matrix(heads, heads, width)
    (act_f, small_f, cumt_f, enter_f, prior_f, act_r, small_r, cumt_r, enter_r, prior_r,
     message, g_f, g_r) = project(hidden, rim_f, rim_r, (w_zx, w_bc, w_dt.T, norm_gain[None, :]), conv_x, conv_bc, lanes, copy_first, heads, inner)
    share = rows // n_head
    pieces = 2 if share % (2 * CHUNK) == 0 else 1
    size = share // pieces
    tile = min(TILE, size)
    place = lambda k: (k, pieces, tile, rows, head.astype(jnp.int32).reshape(1), n_head)
    strands = ((act_f, small_f, cumt_f), (act_r, small_r, cumt_r))
    ends = ((enter_f, prior_f), (enter_r, prior_r))
    entering, gated, same = incoming(message, "ctx", gates(place(0), hidden, g_f, g_r, 5e9), same)
    other = lax.ppermute(jnp.concatenate(same, axis=0), "ctx", [(i, i ^ 1) for i in range(n_ctx)])
    entering, other = lax.optimization_barrier((entering, other))
    bases = inside(place(0), strands, lanes, copy_first, heads, inner, 8e9)
    parts = finish(place(0), strands, ends, bases, gated, entering, copy_second, heads, inner)
    (g_f, g_r), parts = lax.optimization_barrier(((g_f, g_r), parts))
    arrived = [[rotated(block, d, n_head) if d else block for d, block in enumerate(parts)]]
    for k in range(1, pieces):
        gated = gates(place(k), hidden, g_f, g_r, 1e8)
        parts = settle(place(k), strands, ends, gated, lanes, copy_first, entering, copy_second, heads, inner)
        parts, arrived[k - 1] = lax.optimization_barrier((parts, arrived[k - 1]))
        arrived.append([rotated(block, d, n_head) if d else block for d, block in enumerate(parts)])
    own_rows = lax.dynamic_slice_in_dim(hidden, head * share, share, 0)
    groups = [w_out]
    for d, one in enumerate(same):
        two = other[d * half : (d + 1) * half]
        groups.append(jnp.concatenate([jnp.where(parity == 0, one, two), jnp.where(parity == 0, two, one)], axis=0))
    result = None
    for k in range(pieces):
        total = own_rows[k * size : (k + 1) * size].astype(F32)
        for block, weights in zip(arrived[k], groups):
            total = total + jnp.dot(block, weights, preferred_element_type=F32)
        total = total.astype(BF16)
        if result is None:
            result = jnp.pad(total, ((0, share - size), (0, 0)))
        else:
            result = lax.dynamic_update_slice(result, total, (k * size, 0))
    return result


def solution(mesh):
    placed = (
        P("ctx", None),
        P(),
        P(None, None, "head"),
        P(),
        P(None, "head"),
        P("head"),
        P("head"),
        P("head"),
        P(None, "head"),
        P(),
        P("head", None),
    )
    return jax.shard_map(
        on_device, mesh=mesh, in_specs=placed, out_specs=P(("ctx", "head"), None), check_vma=False
    )
```

```python
import functools

import jax
import jax.numpy as jnp
import numpy as np
from jax import lax
from jax.experimental import pallas as pl
from jax.experimental.pallas import tpu as pltpu
from jax.sharding import PartitionSpec as P

STATE = 128
CHUNK = 128
TILE = 256
EPS = 1e-05
RIM = 16
TAIL = 16
F32 = jnp.float32
BF16 = jnp.bfloat16
MIB = 2**20


def params(limit):
    return pltpu.CompilerParams(
        dimension_semantics=("arbitrary",), vmem_limit_bytes=limit * MIB
    )


def cost(flops, bytes_accessed):
    return pl.CostEstimate(flops=int(flops), bytes_accessed=int(bytes_accessed), transcendentals=0)


def whole(shape):
    return pl.BlockSpec(shape, lambda *_: (0,) * len(shape), pipeline_mode=pl.Buffered(1))


def silu(x):
    half = 0.5 * x
    return half + half * jnp.tanh(half)


def tri(rows, reverse):
    r = lax.broadcasted_iota(jnp.int32, (rows, rows), 0)
    c = lax.broadcasted_iota(jnp.int32, (rows, rows), 1)
    return (r <= c) if reverse else (r >= c)


def spread_matrix(first, heads, width):
    r = np.arange(2 * 128)[:, None] % 128
    c = np.arange(heads * width)[None, :] // width
    return jnp.asarray((r == c + first).astype(BF16))


def spread(q, matrix):
    high = q.astype(BF16)
    low = (q - high.astype(F32)).astype(BF16)
    return jnp.dot(jnp.concatenate([high, low], axis=1), matrix, preferred_element_type=F32)


def prepare(inner, zx_ref, bc_ref, dt_ref, gain_ref, wf_ref, wr_ref, gf_ref, gr_ref):
    depth = zx_ref.shape[0]
    rows = min(256, depth)
    r = lax.broadcasted_iota(jnp.int32, (rows, rows), 0)
    c = lax.broadcasted_iota(jnp.int32, (rows, rows), 1)
    turn = (r + c == rows - 1).astype(BF16)
    for b in range(0, depth, rows):
        here, there = slice(b, b + rows), slice(depth - rows - b, depth - b)
        gain = jnp.transpose(jnp.broadcast_to(gain_ref[:, here], (128, rows)))
        zx = zx_ref[here].astype(F32).reshape(rows, 2 * inner)
        steps = dt_ref[:, here].astype(F32)
        steps = jnp.transpose(jnp.concatenate([steps, jnp.zeros((128 - steps.shape[0], rows), F32)], axis=0))

        def put(part, at, forward_ref, turned_ref):
            size = part.shape[1]
            scaled = jnp.concatenate([part[:, g : g + 128] * gain for g in range(0, size, 128)], axis=1).astype(BF16)
            forward_ref[here, at : at + size] = scaled
            turned_ref[there, at : at + size] = jnp.dot(turn, scaled, preferred_element_type=F32).astype(BF16)

        put(zx[:, inner:], 0, wf_ref, wr_ref)
        put(bc_ref[here].astype(F32), inner, wf_ref, wr_ref)
        put(steps, inner + bc_ref.shape[1], wf_ref, wr_ref)
        put(zx[:, :inner], 0, gf_ref, gr_ref)


def row_scale(h):
    hf = h.astype(F32)
    return lax.rsqrt(jnp.mean(hf * hf, axis=-1, keepdims=True) + EPS)


def project_kernel(heads, inner, *refs):
    (hf_ref, hr_ref, rimf_ref, rimr_ref, zx_ref, bc_ref, wdt_ref, gain_ref, convx_ref, convbc_ref, lanes_ref, copy_ref,
     actf_ref, smallf_ref, cumtf_ref, enterf_ref, priorf_ref,
     actr_ref, smallr_ref, cumtr_ref, enterr_ref, priorr_ref,
     msg_ref, gf_ref, gr_ref, wf_ref, wr_ref, buff, bufr, statef, stater, totalf, totalr) = refs
    step = pl.program_id(0)
    last = pl.num_programs(0) - 1
    stream = inner + 2 * STATE
    blocks = stream // 128
    rows = hf_ref.shape[0]
    count = rows // CHUNK
    sides = (
        (False, hf_ref, rimf_ref, wf_ref, actf_ref, smallf_ref, cumtf_ref, enterf_ref, priorf_ref, buff, statef, totalf),
        (True, hr_ref, rimr_ref, wr_ref, actr_ref, smallr_ref, cumtr_ref, enterr_ref, priorr_ref, bufr, stater, totalr),
    )

    @pl.when(step == 0)
    def _():
        prepare(inner, zx_ref, bc_ref, wdt_ref, gain_ref, wf_ref, wr_ref, gf_ref, gr_ref)
        for reverse, _, rim_ref, w_ref, _, _, _, _, _, buf, state, total in sides:
            edge = rows if reverse else 0
            state[...] = jnp.zeros_like(state)
            total[...] = jnp.zeros_like(total)
            rim = rim_ref[...]
            out = jnp.dot(rim, w_ref[:, :stream], preferred_element_type=F32) * row_scale(rim)
            for j in range(blocks):
                part = out[:, j * 128 : (j + 1) * 128]
                buf[j, edge : edge + 8, :] = part[:8] if reverse else part[RIM - 8 :]

    lane = lax.broadcasted_iota(jnp.int32, (rows, 128), 1)
    row8 = lax.broadcasted_iota(jnp.int32, (8, 128), 0)
    r = lax.broadcasted_iota(jnp.int32, (rows, rows), 0)
    c = lax.broadcasted_iota(jnp.int32, (rows, rows), 1)
    same = r // CHUNK == c // CHUNK
    hs = [side[1][...] for side in sides]
    scales = [row_scale(h) for h in hs]
    tail_rows, aux_rows = [], []
    for k, (reverse, _, _, w_ref, _, small_ref, cumt_ref, _, _, _, _, total_ref) in enumerate(sides):
        raw = jnp.dot(hs[k], w_ref[:, stream:], preferred_element_type=F32) * scales[k] + lanes_ref[0:1, :]
        dt = jnp.maximum(raw, 0.0) + jnp.log1p(jnp.exp(-jnp.abs(raw)))
        dt = jnp.where(lane < heads, dt, 0.0)
        steps = -lanes_ref[1:2, :] * dt
        high = steps.astype(BF16).astype(F32)
        mid = (steps - high).astype(BF16).astype(F32)
        low = steps - high - mid
        packed = (high + pltpu.roll(mid, heads, 1) + pltpu.roll(low, 2 * heads, 1)).astype(BF16)
        mask = jnp.where(jnp.logical_and(same, (r <= c) if reverse else (r >= c)), 1.0, 0.0).astype(BF16)
        sums = jnp.dot(mask, packed, preferred_element_type=F32)
        sums = sums + pltpu.roll(sums, 128 - heads, 1) + pltpu.roll(sums, 128 - 2 * heads, 1)
        cum = jnp.where(lane < heads, sums, 0.0)
        small_ref[...] = dt + pltpu.roll(cum, heads, 1)
        running = total_ref[...]
        tails = [None] * count
        aux = [None] * count
        for i in range(count):
            n = count - 1 - i if reverse else i
            at = slice(n * CHUNK, (n + 1) * CHUNK)
            cumt_ref[:, at] = jnp.transpose(cum[at])[:heads]
            end = cum[n * CHUNK : n * CHUNK + 1] if reverse else cum[(n + 1) * CHUNK - 1 : (n + 1) * CHUNK]
            tails[n] = dt[at] * jnp.exp(end - cum[at])
            aux[n] = jnp.where(row8 == 0, jnp.exp(end), jnp.exp(running))
            running = running + end
        total_ref[...] = running
        tail_rows += tails
        aux_rows += aux
    weights = spread(jnp.concatenate(tail_rows + aux_rows, axis=0), copy_ref[...])

    for g in range(0, stream, 256):
        for k, (reverse, _, _, w_ref, act_ref, _, _, _, _, buf, _, _) in enumerate(sides):
            edge = rows if reverse else 0
            body = 0 if reverse else 8
            out = jnp.dot(hs[k], w_ref[:, g : g + 256], preferred_element_type=F32) * scales[k]
            for j in range(g // 128, g // 128 + 2):
                x = out[:, j * 128 - g : (j + 1) * 128 - g]
                buf[j, body : body + rows, :] = x
                own = j * 128 - (0 if j * 128 < inner else inner)
                taps = (convx_ref if j * 128 < inner else convbc_ref)[:, own : own + 128]
                total = taps[3:4] * x
                for d in (1, 2, 3):
                    at = body + d if reverse else body - d
                    total = total + taps[3 - d : 4 - d] * buf[j, at : at + rows, :]
                act_ref[:, j * 128 : (j + 1) * 128] = silu(total).astype(BF16)
                buf[j, edge : edge + 8, :] = x[:8] if reverse else x[rows - 8 :]

    for i in range(count):
        for k, (reverse, _, _, _, act_ref, _, _, enter_ref, prior_ref, _, state, _) in enumerate(sides):
            n = count - 1 - i if reverse else i
            at = slice(n * CHUNK, (n + 1) * CHUNK)
            own = weights[(k * count + n) * CHUNK : (k * count + n + 1) * CHUNK]
            aux = weights[2 * rows + (k * count + n) * 8 : 2 * rows + (k * count + n + 1) * 8]
            tails = (act_ref[at, :inner].astype(F32) * own).astype(BF16)
            ends = lax.dot_general(act_ref[at, inner : inner + STATE], tails, (((0,), (0,)), ((), ())),
                                   preferred_element_type=F32)
            before = state[...]
            enter_ref[n] = before.astype(BF16)
            prior_ref[n] = aux
            state[...] = before * aux[:1] + ends

    @pl.when(step == last)
    def _():
        for k, side in enumerate(sides):
            state, total = side[-2:]
            at = k * (STATE + TAIL)
            msg_ref[at : at + STATE, :] = state[...].astype(BF16)
            t = total[...]
            high = t.astype(BF16).astype(F32)
            mid = (t - high).astype(BF16).astype(F32)
            low = t - high - mid
            packed = jnp.where(row8 == 0, high, jnp.where(row8 == 1, mid, jnp.where(row8 == 2, low, 0.0)))
            rows3 = spread(packed, copy_ref[...])
            msg_ref[at + STATE : at + STATE + TAIL, :] = jnp.concatenate(
                [rows3, jnp.zeros_like(rows3)], axis=0).astype(BF16)


def project(hidden, rim_f, rim_r, weights, conv_x, conv_bc, lanes, copy, heads, inner):
    rows, depth = hidden.shape
    stream = inner + 2 * STATE
    n = rows // TILE
    per = TILE // CHUNK
    up, down = (lambda i: i), (lambda i: n - 1 - i)
    by_rows = lambda width, at: pl.BlockSpec((TILE, width), lambda i: (at(i), 0))
    out_specs, out_shape = [], []
    for at in (up, down):
        out_specs += [by_rows(stream, at), by_rows(128, at),
                      pl.BlockSpec((heads, TILE), lambda i, at=at: (0, at(i))),
                      pl.BlockSpec((per, STATE, inner), lambda i, at=at: (at(i), 0, 0)),
                      pl.BlockSpec((per, 8, inner), lambda i, at=at: (at(i), 0, 0))]
        out_shape += [jax.ShapeDtypeStruct((rows, stream), BF16),
                      jax.ShapeDtypeStruct((rows, 128), F32), jax.ShapeDtypeStruct((heads, rows), F32),
                      jax.ShapeDtypeStruct((n * per, STATE, inner), BF16),
                      jax.ShapeDtypeStruct((n * per, 8, inner), F32)]
    message = (2 * (STATE + TAIL), inner)
    buf = pltpu.VMEM((stream // 128, TILE + 8, 128), F32)
    state, total = pltpu.VMEM((STATE, inner), F32), pltpu.VMEM((8, 128), F32)
    return pl.pallas_call(
        functools.partial(project_kernel, heads, inner),
        grid=(n,),
        in_specs=[by_rows(depth, up), by_rows(depth, down), whole(rim_f.shape), whole(rim_r.shape),
                  *[whole(x.shape) for x in weights], whole(conv_x.shape), whole(conv_bc.shape), whole(lanes.shape),
                  whole(copy.shape)],
        out_specs=out_specs + [whole(message), whole((depth, inner)), whole((depth, inner))],
        out_shape=out_shape + [jax.ShapeDtypeStruct(message, BF16)] + [jax.ShapeDtypeStruct((depth, inner), BF16)] * 2,
        scratch_shapes=[pltpu.VMEM((depth, stream + 128), BF16)] * 2 + [buf, buf, state, state, total, total],
        compiler_params=params(58),
        cost_estimate=cost(22e9, 40e6),
        name="project",
    )(hidden, hidden, rim_f, rim_r, *weights, conv_x, conv_bc, lanes, copy)


def gates_kernel(h_ref, wf_ref, wr_ref, zf_ref, zr_ref):
    h = h_ref[...]
    scale = row_scale(h)
    for w_ref, z_ref in ((wf_ref, zf_ref), (wr_ref, zr_ref)):
        z_ref[...] = (jnp.dot(h, w_ref[...], preferred_element_type=F32) * scale).astype(BF16)


def by_destination(kernel, name, place, rows_in, fixed, by_order, out_shape, out_specs, work, scratch=()):
    k, pieces, tile, rows, head, n_head = place
    share = rows // n_head
    per_piece, per_share = share // pieces // tile, share // tile

    def at(i, head_ref):
        return lax.rem(head_ref[0] + i // per_piece, n_head) * per_share + k * per_piece + lax.rem(i, per_piece)

    def spec(shape, dim, last):
        def index(i, head_ref):
            where = [0] * len(shape)
            where[-1] = last
            where[dim] = at(i, head_ref)
            return tuple(where)

        return pl.BlockSpec(shape, index)

    in_specs = [spec(*one[1:]) for one in rows_in] + [whole(x.shape) for x in fixed]
    in_specs += [pl.BlockSpec((tile, x.shape[1]), lambda i, _: (i, 0)) for x in by_order]
    return pl.pallas_call(
        lambda _, *refs: kernel(*refs),
        grid_spec=pltpu.PrefetchScalarGridSpec(
            num_scalar_prefetch=1,
            grid=(n_head * per_piece,),
            in_specs=in_specs,
            out_specs=out_specs,
            scratch_shapes=scratch,
        ),
        out_shape=out_shape,
        compiler_params=params(58),
        cost_estimate=cost(work, 1e6),
        name=name,
    )(head, *[one[0] for one in rows_in], *fixed, *by_order)


def ordered(place, inner):
    _, pieces, tile, rows, _, _ = place
    return jax.ShapeDtypeStruct((rows // pieces, inner), BF16), pl.BlockSpec((tile, inner), lambda i, _: (i, 0))


def sent(place, inner):
    _, pieces, _, rows, _, n_head = place
    size = rows // n_head // pieces
    return [jax.ShapeDtypeStruct((size, inner), BF16)] * n_head, [whole((size, inner))] * n_head


def gates(place, hidden, w_f, w_r, work):
    shape, spec = ordered(place, w_f.shape[1])
    return by_destination(gates_kernel, "gates", place, [(hidden, (place[2], hidden.shape[1]), 0, 0)], [w_f, w_r], [],
                          [shape] * 2, [spec] * 2, work)


def inside_kernel(heads, inner, actf_ref, smallf_ref, cumtf_ref, actr_ref, smallr_ref, cumtr_ref, lanes_ref, copy_ref,
                  basef_ref, baser_ref):
    width = inner // heads
    per = 128 // width
    size = actf_ref.shape[0]
    lane = lax.broadcasted_iota(jnp.int32, (size, 128), 1)
    group = lax.broadcasted_iota(jnp.int32, (CHUNK, 128), 1) // width
    dts = [jnp.where(lane < heads, ref[...], 0.0) for ref in (smallf_ref, smallr_ref)]
    wide = spread(jnp.concatenate(dts + [jnp.broadcast_to(lanes_ref[2:3, :], (8, 128))], axis=0), copy_ref[...])
    skip = wide[2 * size : 2 * size + 1]
    sides = ((False, actf_ref, smallf_ref, cumtf_ref, basef_ref), (True, actr_ref, smallr_ref, cumtr_ref, baser_ref))
    for c in range(0, size, CHUNK):
        rows = slice(c, c + CHUNK)
        for k, (reverse, act_ref, small_ref, cumt_ref, base_ref) in enumerate(sides):
            small = small_ref[rows, :]
            values = act_ref[rows, :inner].astype(F32)
            weighted = (values * wide[k * size + c : k * size + c + CHUNK]).astype(BF16)
            scores = lax.dot_general(act_ref[rows, inner + STATE :], act_ref[rows, inner : inner + STATE],
                                     (((1,), (1,)), ((), ())), preferred_element_type=F32)
            scores = jnp.where(tri(CHUNK, reverse), scores, 0.0)
            for p in range(inner // 128):
                cols = slice(p * 128, (p + 1) * 128)
                pair = weighted[:, cols]
                mixing, stacked = [], []
                for q in range(per):
                    h = p * per + q
                    gap = jnp.minimum(small[:, heads + h : heads + h + 1] - cumt_ref[h : h + 1, rows], 0.0)
                    mixing.append((scores * jnp.exp(gap)).astype(BF16))
                    stacked.append(jnp.where(group == q, pair, jnp.zeros_like(pair)))
                out = jnp.dot(jnp.concatenate(mixing, axis=1), jnp.concatenate(stacked, axis=0),
                              preferred_element_type=F32)
                base_ref[rows, cols] = (out + skip[:, cols] * values[:, cols]).astype(BF16)


def inside_rows(strands, tile, heads):
    rows_in = []
    for act, small, cumt in strands:
        rows_in += [(act, (tile, act.shape[1]), 0, 0), (small, (tile, 128), 0, 0), (cumt, (heads, tile), 1, 0)]
    return rows_in


def inside(place, strands, lanes, copy, heads, inner, work):
    shape, spec = ordered(place, inner)
    return by_destination(functools.partial(inside_kernel, heads, inner), "inside", place,
                          inside_rows(strands, place[2], heads), [lanes, copy], [], [shape] * 2, [spec] * 2, work)


def finish_kernel(heads, inner, *refs):
    (cf_ref, ef_ref, pf_ref, sf_ref, cr_ref, er_ref, pr_ref, sr_ref, in_ref, copy_ref,
     zf_ref, zr_ref, bf_ref, br_ref, *out_refs) = refs
    width = inner // heads
    size = cf_ref.shape[0]
    row = lax.broadcasted_iota(jnp.int32, (256, 256), 0) // width
    column = lax.broadcasted_iota(jnp.int32, (256, 256), 1) // width
    mean = jnp.where(row == column, 1.0 / width, 0.0).astype(BF16)
    grown = spread(jnp.exp(jnp.minimum(jnp.concatenate([sf_ref[...], sr_ref[...]], axis=0), 0.0)), copy_ref[...])
    both = None
    for k, (c_ref, b_ref, z_ref, e_ref, p_ref) in enumerate(
            ((cf_ref, bf_ref, zf_ref, ef_ref, pf_ref), (cr_ref, br_ref, zr_ref, er_ref, pr_ref))):
        parts = []
        for c in range(e_ref.shape[0]):
            entering = (e_ref[c].astype(F32) + p_ref[c, 1:2, :] * in_ref[k]).astype(BF16)
            parts.append(jnp.dot(c_ref[c * CHUNK : (c + 1) * CHUNK, :], entering, preferred_element_type=F32))
        reads = jnp.concatenate(parts, axis=0)
        out = b_ref[...].astype(F32) + reads * grown[k * size : (k + 1) * size]
        gated = out * silu(z_ref[...].astype(F32))
        squares = (gated * gated).astype(BF16)
        means = jnp.concatenate(
            [jnp.dot(squares[:, g : g + 256], mean, preferred_element_type=F32) for g in range(0, inner, 256)], axis=1)
        result = gated * lax.rsqrt(means + EPS)
        both = result if both is None else both + result
    both = both.astype(BF16)
    step = pl.program_id(0)
    per_piece = out_refs[0].shape[0] // size
    for d, ref in enumerate(out_refs):
        @pl.when(step // per_piece == d)
        def _():
            ref[pl.ds(pl.multiple_of(lax.rem(step, per_piece) * size, size), size), :] = both


def finish_rows(strand, tile, inner):
    enter, prior = strand
    per = tile // CHUNK
    return [(enter, (per, STATE, inner), 0, 0), (prior, (per, 8, inner), 0, 0)]


def finish(place, strands, ends, bases, gated, entering, copy, heads, inner):
    tile = place[2]
    shapes, specs = sent(place, inner)
    rows_in = []
    for (act, small, _), end in zip(strands, ends):
        rows_in += [(act, (tile, STATE), 0, act.shape[1] // STATE - 1)] + finish_rows(end, tile, inner)
        rows_in += [(small, (tile, 128), 0, 0)]
    return by_destination(functools.partial(finish_kernel, heads, inner), "finish", place, rows_in, [entering, copy],
                          [*gated, *bases], shapes, specs, 1e8)


def settle_kernel(heads, inner, *refs):
    (actf_ref, smallf_ref, cumtf_ref, actr_ref, smallr_ref, cumtr_ref, ef_ref, pf_ref, er_ref, pr_ref,
     lanes_ref, first_ref, in_ref, second_ref, zf_ref, zr_ref, *out_refs, basef, baser) = refs
    inside_kernel(heads, inner, actf_ref, smallf_ref, cumtf_ref, actr_ref, smallr_ref, cumtr_ref, lanes_ref, first_ref,
                  basef, baser)
    maps = [ref.at[:, pl.ds(inner + STATE, STATE)] for ref in (actf_ref, actr_ref)]
    finish_kernel(heads, inner, maps[0], ef_ref, pf_ref, smallf_ref, maps[1], er_ref, pr_ref, smallr_ref,
                  in_ref, second_ref, zf_ref, zr_ref, basef, baser, *out_refs)


def settle(place, strands, ends, gated, lanes, first, entering, second, heads, inner):
    tile = place[2]
    shapes, specs = sent(place, inner)
    rows_in = inside_rows(strands, tile, heads) + finish_rows(ends[0], tile, inner) + finish_rows(ends[1], tile, inner)
    return by_destination(functools.partial(settle_kernel, heads, inner), "settle", place, rows_in,
                          [lanes, first, entering, second], list(gated), shapes, specs, 1e8,
                          [pltpu.VMEM((tile, inner), BF16)] * 2)


def read_message(ref, at):
    tail = ref[at + STATE : at + STATE + TAIL, :].astype(F32)
    return ref[at : at + STATE, :].astype(F32), tail[0:1] + tail[1:2] + tail[2:3]


def hop_kernel(first, *refs):
    upper_ref, mine_ref, other_ref = refs[:3]
    into_ref = None if first else refs[3]
    new_ref, msg_ref = refs[-2:]
    upper = upper_ref[0].astype(F32)
    for k in (0, 1):
        later = upper if k == 0 else 1.0 - upper
        at = k * (STATE + TAIL)
        o_state, o_log = read_message(other_ref, at)
        if first:
            new_state, new_log = later * o_state, later * o_log
        else:
            into_log = into_ref[k, STATE : STATE + 1, :]
            new_state = into_ref[k, :STATE, :] + later * jnp.exp(into_log) * o_state
            new_log = into_log + later * o_log
        new_ref[k, :STATE, :] = new_state
        new_ref[k, STATE:, :] = jnp.broadcast_to(new_log, (8, new_log.shape[1]))
        state, log = read_message(mine_ref, at)
        of_other = later * jnp.exp(log) + (1.0 - later)
        of_mine = later + (1.0 - later) * jnp.exp(o_log)
        msg_ref[at : at + STATE, :] = (of_other * o_state + of_mine * state).astype(BF16)
        t = log + o_log
        high = t.astype(BF16).astype(F32)
        mid = (t - high).astype(BF16).astype(F32)
        low = t - high - mid
        row = lax.broadcasted_iota(jnp.int32, (TAIL, t.shape[1]), 0)
        packed = jnp.where(row == 0, high, jnp.where(row == 1, mid, jnp.where(row == 2, low, 0.0)))
        msg_ref[at + STATE : at + STATE + TAIL, :] = packed.astype(BF16)


def local_call(kernel, name, smem, operands, out_shape):
    return pl.pallas_call(
        kernel,
        grid=(1,),
        in_specs=[pl.BlockSpec(memory_space=pltpu.SMEM)] + [whole(x.shape) for x in operands],
        out_specs=[whole(x.shape) for x in out_shape],
        out_shape=out_shape,
        compiler_params=params(10),
        cost_estimate=cost(1e6, 1.5e6),
        name=name,
    )(smem, *operands)


def join_kernel(count, *refs):
    place_ref, into_ref = refs[:2]
    slots, out_ref = refs[2:-1], refs[-1]
    place = place_ref[0]
    groups = [place ^ d for d in range(1, count)]
    read = [read_message(ref, 0) for ref in slots]
    ones = lambda condition: jnp.where(condition, 1.0, 0.0)
    sums = [None, None]
    for j, (state, _) in zip(groups, read):
        lower = ones(j < place)
        log = None
        for i, (_, other) in zip(groups, read):
            between = jnp.logical_or(jnp.logical_and(j < i, i < place), jnp.logical_and(place < i, i < j))
            term = ones(between) * other
            log = term if log is None else log + term
        part = jnp.exp(log) * state
        for k, share in enumerate((lower, 1.0 - lower)):
            sums[k] = share * part if sums[k] is None else sums[k] + share * part
    for k in (0, 1):
        out_ref[k] = into_ref[k, :STATE, :] + jnp.exp(into_ref[k, STATE : STATE + 1, :]) * sums[k]


def incoming(message, axis, beside, before):
    count, index = lax.axis_size(axis), lax.axis_index(axis)
    inner = message.shape[1]
    into = None
    distance = 1
    while count // distance > 4:
        other = lax.ppermute(message, axis, [(i, i ^ distance) for i in range(count)])
        if into is None:
            other, *beside = lax.optimization_barrier((other, *beside))
        upper = ((index // distance) % 2).astype(jnp.int32).reshape(1)
        operands = [message, other] + ([] if into is None else [into])
        out_shape = [jax.ShapeDtypeStruct((2, STATE + 8, inner), F32), jax.ShapeDtypeStruct(message.shape, BF16)]
        into, message = local_call(functools.partial(hop_kernel, into is None), "hop", upper, operands, out_shape)
        distance *= 2
    if into is None:
        into = jnp.zeros((2, STATE + 8, inner), F32)
    message, *before = lax.optimization_barrier((message, *before))
    groups = count // distance
    place = index // distance
    half = STATE + TAIL
    slots = []
    for d in range(1, groups):
        highest = 1 << (d.bit_length() - 1)
        above = (place // highest) % 2
        block = lax.dynamic_slice_in_dim(message, above * half, half, 0)
        slots.append(lax.ppermute(block, axis, [(i, i ^ (d * distance)) for i in range(count)]))
    joined = local_call(functools.partial(join_kernel, groups), "join", place.astype(jnp.int32).reshape(1), [into] + slots,
                        [pltpu.HBM((2, STATE, inner), F32)])[0]
    return joined, beside, before


def shifted(block, axis, distance):
    devices = range(lax.axis_size(axis))
    return lax.ppermute(block, axis, [(i - distance, i) for i in devices if i - distance in devices])


def rotated(block, d, count):
    return lax.ppermute(block, "head", [(i, (i + d) % count) for i in range(count)])


def on_device(
    hidden, norm_gain, w_zx, w_bc, w_dt, dt_bias, decay_rate, skip_gain, conv_x, conv_bc, w_out
):
    rows, depth = hidden.shape
    inner = conv_x.shape[1]
    heads = dt_bias.shape[0]
    width = inner // heads
    n_ctx, n_head = lax.axis_size("ctx"), lax.axis_size("head")
    ctx, head = lax.axis_index("ctx"), lax.axis_index("head")

    rim_f = shifted(hidden[rows - RIM :], "ctx", 1)
    rim_r = shifted(hidden[:RIM], "ctx", -1)

    half = w_out.shape[0] // 2
    parity = ctx % 2
    own_half = lax.dynamic_slice_in_dim(w_out, parity * half, half, 0)
    rim_f, rim_r, own_half = lax.optimization_barrier((rim_f, rim_r, own_half))
    same = [rotated(own_half, d, n_head) for d in range(1, n_head)]

    lanes = jnp.pad(jnp.stack([dt_bias, decay_rate, skip_gain]), [(0, 0), (0, 128 - heads)])
    copy_first = spread_matrix(0, heads, width)
    copy_second = spread_matrix(heads, heads, width)
    (act_f, small_f, cumt_f, enter_f, prior_f, act_r, small_r, cumt_r, enter_r, prior_r,
     message, g_f, g_r) = project(hidden, rim_f, rim_r, (w_zx, w_bc, w_dt.T, norm_gain[None, :]), conv_x, conv_bc, lanes, copy_first, heads, inner)
    share = rows // n_head
    pieces = 2 if share % (2 * CHUNK) == 0 else 1
    size = share // pieces
    tile = min(TILE, size)
    place = lambda k: (k, pieces, tile, rows, head.astype(jnp.int32).reshape(1), n_head)
    strands = ((act_f, small_f, cumt_f), (act_r, small_r, cumt_r))
    ends = ((enter_f, prior_f), (enter_r, prior_r))
    entering, gated, same = incoming(message, "ctx", gates(place(0), hidden, g_f, g_r, 5e9), same)
    other = lax.ppermute(jnp.concatenate(same, axis=0), "ctx", [(i, i ^ 1) for i in range(n_ctx)])
    entering, other = lax.optimization_barrier((entering, other))
    bases = inside(place(0), strands, lanes, copy_first, heads, inner, 8e9)
    parts = finish(place(0), strands, ends, bases, gated, entering, copy_second, heads, inner)
    (g_f, g_r), parts = lax.optimization_barrier(((g_f, g_r), parts))
    arrived = [[rotated(block, d, n_head) if d else block for d, block in enumerate(parts)]]
    for k in range(1, pieces):
        gated = gates(place(k), hidden, g_f, g_r, 1e8)
        parts = settle(place(k), strands, ends, gated, lanes, copy_first, entering, copy_second, heads, inner)
        parts, arrived[k - 1] = lax.optimization_barrier((parts, arrived[k - 1]))
        arrived.append([rotated(block, d, n_head) if d else block for d, block in enumerate(parts)])
    own_rows = lax.dynamic_slice_in_dim(hidden, head * share, share, 0)
    groups = [w_out]
    for d, one in enumerate(same):
        two = other[d * half : (d + 1) * half]
        groups.append(jnp.concatenate([jnp.where(parity == 0, one, two), jnp.where(parity == 0, two, one)], axis=0))
    result = None
    for k in range(pieces):
        total = own_rows[k * size : (k + 1) * size].astype(F32)
        for d in sorted(range(n_head), key=lambda d: -abs(2 * d - n_head)):
            total = total + jnp.dot(arrived[k][d], groups[d], preferred_element_type=F32)
        total = total.astype(BF16)
        if result is None:
            result = jnp.pad(total, ((0, share - size), (0, 0)))
        else:
            result = lax.dynamic_update_slice(result, total, (k * size, 0))
    return result


def solution(mesh):
    placed = (
        P("ctx", None),
        P(),
        P(None, None, "head"),
        P(),
        P(None, "head"),
        P("head"),
        P("head"),
        P("head"),
        P(None, "head"),
        P(),
        P("head", None),
    )
    return jax.shard_map(
        on_device, mesh=mesh, in_specs=placed, out_specs=P(("ctx", "head"), None), check_vma=False
    )
```

```python
import functools

import jax
import jax.numpy as jnp
import numpy as np
from jax import lax
from jax.experimental import pallas as pl
from jax.experimental.pallas import tpu as pltpu
from jax.sharding import PartitionSpec as P

STATE = 128
CHUNK = 128
TILE = 256
EPS = 1e-05
RIM = 16
TAIL = 16
F32 = jnp.float32
BF16 = jnp.bfloat16
MIB = 2**20


def params(limit):
    return pltpu.CompilerParams(
        dimension_semantics=("arbitrary",), vmem_limit_bytes=limit * MIB
    )


def cost(flops, bytes_accessed):
    return pl.CostEstimate(flops=int(flops), bytes_accessed=int(bytes_accessed), transcendentals=0)


def whole(shape):
    return pl.BlockSpec(shape, lambda *_: (0,) * len(shape), pipeline_mode=pl.Buffered(1))


def silu(x):
    half = 0.5 * x
    return half + half * jnp.tanh(half)


def tri(rows, reverse):
    r = lax.broadcasted_iota(jnp.int32, (rows, rows), 0)
    c = lax.broadcasted_iota(jnp.int32, (rows, rows), 1)
    return (r <= c) if reverse else (r >= c)


def spread_matrix(first, heads, width):
    r = np.arange(2 * 128)[:, None] % 128
    c = np.arange(heads * width)[None, :] // width
    return jnp.asarray((r == c + first).astype(BF16))


def spread(q, matrix):
    high = q.astype(BF16)
    low = (q - high.astype(F32)).astype(BF16)
    return jnp.dot(jnp.concatenate([high, low], axis=1), matrix, preferred_element_type=F32)


def prepare(inner, zx_ref, bc_ref, dt_ref, gain_ref, wf_ref, wr_ref, gf_ref, gr_ref):
    depth = zx_ref.shape[0]
    rows = min(256, depth)
    r = lax.broadcasted_iota(jnp.int32, (rows, rows), 0)
    c = lax.broadcasted_iota(jnp.int32, (rows, rows), 1)
    turn = (r + c == rows - 1).astype(BF16)
    for b in range(0, depth, rows):
        here, there = slice(b, b + rows), slice(depth - rows - b, depth - b)
        gain = jnp.transpose(jnp.broadcast_to(gain_ref[:, here], (128, rows)))
        zx = zx_ref[here].astype(F32).reshape(rows, 2 * inner)
        steps = dt_ref[:, here].astype(F32)
        steps = jnp.transpose(jnp.concatenate([steps, jnp.zeros((128 - steps.shape[0], rows), F32)], axis=0))

        def put(part, at, forward_ref, turned_ref):
            size = part.shape[1]
            scaled = jnp.concatenate([part[:, g : g + 128] * gain for g in range(0, size, 128)], axis=1).astype(BF16)
            forward_ref[here, at : at + size] = scaled
            turned_ref[there, at : at + size] = jnp.dot(turn, scaled, preferred_element_type=F32).astype(BF16)

        put(zx[:, inner:], 0, wf_ref, wr_ref)
        put(bc_ref[here].astype(F32), inner, wf_ref, wr_ref)
        put(steps, inner + bc_ref.shape[1], wf_ref, wr_ref)
        put(zx[:, :inner], 0, gf_ref, gr_ref)


def row_scale(h):
    hf = h.astype(F32)
    return lax.rsqrt(jnp.mean(hf * hf, axis=-1, keepdims=True) + EPS)


def project_kernel(heads, inner, *refs):
    (hf_ref, hr_ref, rimf_ref, rimr_ref, zx_ref, bc_ref, wdt_ref, gain_ref, convx_ref, convbc_ref, lanes_ref, copy_ref,
     actf_ref, smallf_ref, cumtf_ref, enterf_ref, priorf_ref,
     actr_ref, smallr_ref, cumtr_ref, enterr_ref, priorr_ref,
     msg_ref, gf_ref, gr_ref, wf_ref, wr_ref, buff, bufr, statef, stater, totalf, totalr) = refs
    step = pl.program_id(0)
    last = pl.num_programs(0) - 1
    stream = inner + 2 * STATE
    blocks = stream // 128
    rows = hf_ref.shape[0]
    count = rows // CHUNK
    sides = (
        (False, hf_ref, rimf_ref, wf_ref, actf_ref, smallf_ref, cumtf_ref, enterf_ref, priorf_ref, buff, statef, totalf),
        (True, hr_ref, rimr_ref, wr_ref, actr_ref, smallr_ref, cumtr_ref, enterr_ref, priorr_ref, bufr, stater, totalr),
    )

    @pl.when(step == 0)
    def _():
        prepare(inner, zx_ref, bc_ref, wdt_ref, gain_ref, wf_ref, wr_ref, gf_ref, gr_ref)
        for reverse, _, rim_ref, w_ref, _, _, _, _, _, buf, state, total in sides:
            edge = rows if reverse else 0
            state[...] = jnp.zeros_like(state)
            total[...] = jnp.zeros_like(total)
            rim = rim_ref[...]
            out = jnp.dot(rim, w_ref[:, :stream], preferred_element_type=F32) * row_scale(rim)
            for j in range(blocks):
                part = out[:, j * 128 : (j + 1) * 128]
                buf[j, edge : edge + 8, :] = part[:8] if reverse else part[RIM - 8 :]

    lane = lax.broadcasted_iota(jnp.int32, (rows, 128), 1)
    row8 = lax.broadcasted_iota(jnp.int32, (8, 128), 0)
    r = lax.broadcasted_iota(jnp.int32, (rows, rows), 0)
    c = lax.broadcasted_iota(jnp.int32, (rows, rows), 1)
    same = r // CHUNK == c // CHUNK
    hs = [side[1][...] for side in sides]
    scales = [row_scale(h) for h in hs]
    tail_rows, aux_rows = [], []
    for k, (reverse, _, _, w_ref, _, small_ref, cumt_ref, _, _, _, _, total_ref) in enumerate(sides):
        raw = jnp.dot(hs[k], w_ref[:, stream:], preferred_element_type=F32) * scales[k] + lanes_ref[0:1, :]
        dt = jnp.maximum(raw, 0.0) + jnp.log1p(jnp.exp(-jnp.abs(raw)))
        dt = jnp.where(lane < heads, dt, 0.0)
        steps = -lanes_ref[1:2, :] * dt
        high = steps.astype(BF16).astype(F32)
        mid = (steps - high).astype(BF16).astype(F32)
        low = steps - high - mid
        packed = (high + pltpu.roll(mid, heads, 1) + pltpu.roll(low, 2 * heads, 1)).astype(BF16)
        mask = jnp.where(jnp.logical_and(same, (r <= c) if reverse else (r >= c)), 1.0, 0.0).astype(BF16)
        sums = jnp.dot(mask, packed, preferred_element_type=F32)
        sums = sums + pltpu.roll(sums, 128 - heads, 1) + pltpu.roll(sums, 128 - 2 * heads, 1)
        cum = jnp.where(lane < heads, sums, 0.0)
        small_ref[...] = dt + pltpu.roll(cum, heads, 1)
        running = total_ref[...]
        tails = [None] * count
        aux = [None] * count
        for i in range(count):
            n = count - 1 - i if reverse else i
            at = slice(n * CHUNK, (n + 1) * CHUNK)
            cumt_ref[:, at] = jnp.transpose(cum[at])[:heads]
            end = cum[n * CHUNK : n * CHUNK + 1] if reverse else cum[(n + 1) * CHUNK - 1 : (n + 1) * CHUNK]
            tails[n] = dt[at] * jnp.exp(end - cum[at])
            aux[n] = jnp.where(row8 == 0, jnp.exp(end), jnp.exp(running))
            running = running + end
        total_ref[...] = running
        tail_rows += tails
        aux_rows += aux
    weights = spread(jnp.concatenate(tail_rows + aux_rows, axis=0), copy_ref[...])

    for g in range(0, stream, 256):
        for k, (reverse, _, _, w_ref, act_ref, _, _, _, _, buf, _, _) in enumerate(sides):
            edge = rows if reverse else 0
            body = 0 if reverse else 8
            out = jnp.dot(hs[k], w_ref[:, g : g + 256], preferred_element_type=F32) * scales[k]
            for j in range(g // 128, g // 128 + 2):
                x = out[:, j * 128 - g : (j + 1) * 128 - g]
                buf[j, body : body + rows, :] = x
                own = j * 128 - (0 if j * 128 < inner else inner)
                taps = (convx_ref if j * 128 < inner else convbc_ref)[:, own : own + 128]
                total = taps[3:4] * x
                for d in (1, 2, 3):
                    at = body + d if reverse else body - d
                    total = total + taps[3 - d : 4 - d] * buf[j, at : at + rows, :]
                act_ref[:, j * 128 : (j + 1) * 128] = silu(total).astype(BF16)
                buf[j, edge : edge + 8, :] = x[:8] if reverse else x[rows - 8 :]

    for i in range(count):
        for k, (reverse, _, _, _, act_ref, _, _, enter_ref, prior_ref, _, state, _) in enumerate(sides):
            n = count - 1 - i if reverse else i
            at = slice(n * CHUNK, (n + 1) * CHUNK)
            own = weights[(k * count + n) * CHUNK : (k * count + n + 1) * CHUNK]
            aux = weights[2 * rows + (k * count + n) * 8 : 2 * rows + (k * count + n + 1) * 8]
            tails = (act_ref[at, :inner].astype(F32) * own).astype(BF16)
            ends = lax.dot_general(act_ref[at, inner : inner + STATE], tails, (((0,), (0,)), ((), ())),
                                   preferred_element_type=F32)
            before = state[...]
            enter_ref[n] = before.astype(BF16)
            prior_ref[n] = aux
            state[...] = before * aux[:1] + ends

    @pl.when(step == last)
    def _():
        for k, side in enumerate(sides):
            state, total = side[-2:]
            at = k * (STATE + TAIL)
            msg_ref[at : at + STATE, :] = state[...].astype(BF16)
            t = total[...]
            high = t.astype(BF16).astype(F32)
            mid = (t - high).astype(BF16).astype(F32)
            low = t - high - mid
            packed = jnp.where(row8 == 0, high, jnp.where(row8 == 1, mid, jnp.where(row8 == 2, low, 0.0)))
            rows3 = spread(packed, copy_ref[...])
            msg_ref[at + STATE : at + STATE + TAIL, :] = jnp.concatenate(
                [rows3, jnp.zeros_like(rows3)], axis=0).astype(BF16)


def project(hidden, rim_f, rim_r, weights, conv_x, conv_bc, lanes, copy, heads, inner):
    rows, depth = hidden.shape
    stream = inner + 2 * STATE
    n = rows // TILE
    per = TILE // CHUNK
    up, down = (lambda i: i), (lambda i: n - 1 - i)
    by_rows = lambda width, at: pl.BlockSpec((TILE, width), lambda i: (at(i), 0))
    out_specs, out_shape = [], []
    for at in (up, down):
        out_specs += [by_rows(stream, at), by_rows(128, at),
                      pl.BlockSpec((heads, TILE), lambda i, at=at: (0, at(i))),
                      pl.BlockSpec((per, STATE, inner), lambda i, at=at: (at(i), 0, 0)),
                      pl.BlockSpec((per, 8, inner), lambda i, at=at: (at(i), 0, 0))]
        out_shape += [jax.ShapeDtypeStruct((rows, stream), BF16),
                      jax.ShapeDtypeStruct((rows, 128), F32), jax.ShapeDtypeStruct((heads, rows), F32),
                      jax.ShapeDtypeStruct((n * per, STATE, inner), BF16),
                      jax.ShapeDtypeStruct((n * per, 8, inner), F32)]
    message = (2 * (STATE + TAIL), inner)
    buf = pltpu.VMEM((stream // 128, TILE + 8, 128), F32)
    state, total = pltpu.VMEM((STATE, inner), F32), pltpu.VMEM((8, 128), F32)
    return pl.pallas_call(
        functools.partial(project_kernel, heads, inner),
        grid=(n,),
        in_specs=[by_rows(depth, up), by_rows(depth, down), whole(rim_f.shape), whole(rim_r.shape),
                  *[whole(x.shape) for x in weights], whole(conv_x.shape), whole(conv_bc.shape), whole(lanes.shape),
                  whole(copy.shape)],
        out_specs=out_specs + [whole(message), whole((depth, inner)), whole((depth, inner))],
        out_shape=out_shape + [jax.ShapeDtypeStruct(message, BF16)] + [jax.ShapeDtypeStruct((depth, inner), BF16)] * 2,
        scratch_shapes=[pltpu.VMEM((depth, stream + 128), BF16)] * 2 + [buf, buf, state, state, total, total],
        compiler_params=params(58),
        cost_estimate=cost(22e9, 40e6),
        name="project",
    )(hidden, hidden, rim_f, rim_r, *weights, conv_x, conv_bc, lanes, copy)


def gates_kernel(h_ref, wf_ref, wr_ref, zf_ref, zr_ref):
    h = h_ref[...]
    scale = row_scale(h)
    for w_ref, z_ref in ((wf_ref, zf_ref), (wr_ref, zr_ref)):
        z_ref[...] = (jnp.dot(h, w_ref[...], preferred_element_type=F32) * scale).astype(BF16)


def by_destination(kernel, name, place, rows_in, fixed, by_order, out_shape, out_specs, work, scratch=()):
    k, pieces, tile, rows, head, n_head = place
    share = rows // n_head
    per_piece, per_share = share // pieces // tile, share // tile

    def at(i, head_ref):
        return lax.rem(head_ref[0] + i // per_piece, n_head) * per_share + k * per_piece + lax.rem(i, per_piece)

    def spec(shape, dim, last):
        def index(i, head_ref):
            where = [0] * len(shape)
            where[-1] = last
            where[dim] = at(i, head_ref)
            return tuple(where)

        return pl.BlockSpec(shape, index)

    in_specs = [spec(*one[1:]) for one in rows_in] + [whole(x.shape) for x in fixed]
    in_specs += [pl.BlockSpec((tile, x.shape[1]), lambda i, _: (i, 0)) for x in by_order]
    return pl.pallas_call(
        lambda _, *refs: kernel(*refs),
        grid_spec=pltpu.PrefetchScalarGridSpec(
            num_scalar_prefetch=1,
            grid=(n_head * per_piece,),
            in_specs=in_specs,
            out_specs=out_specs,
            scratch_shapes=scratch,
        ),
        out_shape=out_shape,
        compiler_params=params(58),
        cost_estimate=cost(work, 1e6),
        name=name,
    )(head, *[one[0] for one in rows_in], *fixed, *by_order)


def ordered(place, inner):
    _, pieces, tile, rows, _, _ = place
    return jax.ShapeDtypeStruct((rows // pieces, inner), BF16), pl.BlockSpec((tile, inner), lambda i, _: (i, 0))


def sent(place, inner):
    _, pieces, _, rows, _, n_head = place
    size = rows // n_head // pieces
    return [jax.ShapeDtypeStruct((size, inner), BF16)] * n_head, [whole((size, inner))] * n_head


def gates(place, hidden, w_f, w_r, work):
    shape, spec = ordered(place, w_f.shape[1])
    return by_destination(gates_kernel, "gates", place, [(hidden, (place[2], hidden.shape[1]), 0, 0)], [w_f, w_r], [],
                          [shape] * 2, [spec] * 2, work)


def inside_kernel(heads, inner, actf_ref, smallf_ref, cumtf_ref, actr_ref, smallr_ref, cumtr_ref, lanes_ref, copy_ref,
                  basef_ref, baser_ref):
    width = inner // heads
    per = 128 // width
    size = actf_ref.shape[0]
    lane = lax.broadcasted_iota(jnp.int32, (size, 128), 1)
    group = lax.broadcasted_iota(jnp.int32, (CHUNK, 128), 1) // width
    dts = [jnp.where(lane < heads, ref[...], 0.0) for ref in (smallf_ref, smallr_ref)]
    wide = spread(jnp.concatenate(dts + [jnp.broadcast_to(lanes_ref[2:3, :], (8, 128))], axis=0), copy_ref[...])
    skip = wide[2 * size : 2 * size + 1]
    sides = ((False, actf_ref, smallf_ref, cumtf_ref, basef_ref), (True, actr_ref, smallr_ref, cumtr_ref, baser_ref))
    for c in range(0, size, CHUNK):
        rows = slice(c, c + CHUNK)
        for k, (reverse, act_ref, small_ref, cumt_ref, base_ref) in enumerate(sides):
            small = small_ref[rows, :]
            values = act_ref[rows, :inner].astype(F32)
            weighted = (values * wide[k * size + c : k * size + c + CHUNK]).astype(BF16)
            scores = lax.dot_general(act_ref[rows, inner + STATE :], act_ref[rows, inner : inner + STATE],
                                     (((1,), (1,)), ((), ())), preferred_element_type=F32)
            scores = jnp.where(tri(CHUNK, reverse), scores, 0.0)
            for p in range(inner // 128):
                cols = slice(p * 128, (p + 1) * 128)
                pair = weighted[:, cols]
                mixing, stacked = [], []
                for q in range(per):
                    h = p * per + q
                    gap = jnp.minimum(small[:, heads + h : heads + h + 1] - cumt_ref[h : h + 1, rows], 0.0)
                    mixing.append((scores * jnp.exp(gap)).astype(BF16))
                    stacked.append(jnp.where(group == q, pair, jnp.zeros_like(pair)))
                out = jnp.dot(jnp.concatenate(mixing, axis=1), jnp.concatenate(stacked, axis=0),
                              preferred_element_type=F32)
                base_ref[rows, cols] = (out + skip[:, cols] * values[:, cols]).astype(BF16)


def inside_rows(strands, tile, heads):
    rows_in = []
    for act, small, cumt in strands:
        rows_in += [(act, (tile, act.shape[1]), 0, 0), (small, (tile, 128), 0, 0), (cumt, (heads, tile), 1, 0)]
    return rows_in


def inside(place, strands, lanes, copy, heads, inner, work):
    shape, spec = ordered(place, inner)
    return by_destination(functools.partial(inside_kernel, heads, inner), "inside", place,
                          inside_rows(strands, place[2], heads), [lanes, copy], [], [shape] * 2, [spec] * 2, work)


def finish_kernel(heads, inner, *refs):
    (cf_ref, ef_ref, pf_ref, sf_ref, cr_ref, er_ref, pr_ref, sr_ref, in_ref, copy_ref,
     zf_ref, zr_ref, bf_ref, br_ref, *out_refs) = refs
    width = inner // heads
    size = cf_ref.shape[0]
    row = lax.broadcasted_iota(jnp.int32, (256, 256), 0) // width
    column = lax.broadcasted_iota(jnp.int32, (256, 256), 1) // width
    mean = jnp.where(row == column, 1.0 / width, 0.0).astype(BF16)
    grown = spread(jnp.exp(jnp.minimum(jnp.concatenate([sf_ref[...], sr_ref[...]], axis=0), 0.0)), copy_ref[...])
    both = None
    for k, (c_ref, b_ref, z_ref, e_ref, p_ref) in enumerate(
            ((cf_ref, bf_ref, zf_ref, ef_ref, pf_ref), (cr_ref, br_ref, zr_ref, er_ref, pr_ref))):
        parts = []
        for c in range(e_ref.shape[0]):
            entering = (e_ref[c].astype(F32) + p_ref[c, 1:2, :] * in_ref[k]).astype(BF16)
            parts.append(jnp.dot(c_ref[c * CHUNK : (c + 1) * CHUNK, :], entering, preferred_element_type=F32))
        reads = jnp.concatenate(parts, axis=0)
        out = b_ref[...].astype(F32) + reads * grown[k * size : (k + 1) * size]
        gated = out * silu(z_ref[...].astype(F32))
        squares = (gated * gated).astype(BF16)
        means = jnp.concatenate(
            [jnp.dot(squares[:, g : g + 256], mean, preferred_element_type=F32) for g in range(0, inner, 256)], axis=1)
        result = gated * lax.rsqrt(means + EPS)
        both = result if both is None else both + result
    both = both.astype(BF16)
    step = pl.program_id(0)
    per_piece = out_refs[0].shape[0] // size
    for d, ref in enumerate(out_refs):
        @pl.when(step // per_piece == d)
        def _():
            ref[pl.ds(pl.multiple_of(lax.rem(step, per_piece) * size, size), size), :] = both


def finish_rows(strand, tile, inner):
    enter, prior = strand
    per = tile // CHUNK
    return [(enter, (per, STATE, inner), 0, 0), (prior, (per, 8, inner), 0, 0)]


def finish(place, strands, ends, bases, gated, entering, copy, heads, inner):
    tile = place[2]
    shapes, specs = sent(place, inner)
    rows_in = []
    for (act, small, _), end in zip(strands, ends):
        rows_in += [(act, (tile, STATE), 0, act.shape[1] // STATE - 1)] + finish_rows(end, tile, inner)
        rows_in += [(small, (tile, 128), 0, 0)]
    return by_destination(functools.partial(finish_kernel, heads, inner), "finish", place, rows_in, [entering, copy],
                          [*gated, *bases], shapes, specs, 1e8)


def settle_kernel(heads, inner, *refs):
    (actf_ref, smallf_ref, cumtf_ref, actr_ref, smallr_ref, cumtr_ref, ef_ref, pf_ref, er_ref, pr_ref,
     lanes_ref, first_ref, in_ref, second_ref, zf_ref, zr_ref, *out_refs, basef, baser) = refs
    inside_kernel(heads, inner, actf_ref, smallf_ref, cumtf_ref, actr_ref, smallr_ref, cumtr_ref, lanes_ref, first_ref,
                  basef, baser)
    maps = [ref.at[:, pl.ds(inner + STATE, STATE)] for ref in (actf_ref, actr_ref)]
    finish_kernel(heads, inner, maps[0], ef_ref, pf_ref, smallf_ref, maps[1], er_ref, pr_ref, smallr_ref,
                  in_ref, second_ref, zf_ref, zr_ref, basef, baser, *out_refs)


def settle(place, strands, ends, gated, lanes, first, entering, second, heads, inner):
    tile = place[2]
    shapes, specs = sent(place, inner)
    rows_in = inside_rows(strands, tile, heads) + finish_rows(ends[0], tile, inner) + finish_rows(ends[1], tile, inner)
    return by_destination(functools.partial(settle_kernel, heads, inner), "settle", place, rows_in,
                          [lanes, first, entering, second], list(gated), shapes, specs, 1e8,
                          [pltpu.VMEM((tile, inner), BF16)] * 2)


def read_message(ref, at):
    tail = ref[at + STATE : at + STATE + TAIL, :].astype(F32)
    return ref[at : at + STATE, :].astype(F32), tail[0:1] + tail[1:2] + tail[2:3]


def hop_kernel(first, *refs):
    upper_ref, mine_ref, other_ref = refs[:3]
    into_ref = None if first else refs[3]
    new_ref, msg_ref = refs[-2:]
    upper = upper_ref[0].astype(F32)
    for k in (0, 1):
        later = upper if k == 0 else 1.0 - upper
        at = k * (STATE + TAIL)
        o_state, o_log = read_message(other_ref, at)
        if first:
            new_state, new_log = later * o_state, later * o_log
        else:
            into_log = into_ref[k, STATE : STATE + 1, :]
            new_state = into_ref[k, :STATE, :] + later * jnp.exp(into_log) * o_state
            new_log = into_log + later * o_log
        new_ref[k, :STATE, :] = new_state
        new_ref[k, STATE:, :] = jnp.broadcast_to(new_log, (8, new_log.shape[1]))
        state, log = read_message(mine_ref, at)
        of_other = later * jnp.exp(log) + (1.0 - later)
        of_mine = later + (1.0 - later) * jnp.exp(o_log)
        msg_ref[at : at + STATE, :] = (of_other * o_state + of_mine * state).astype(BF16)
        t = log + o_log
        high = t.astype(BF16).astype(F32)
        mid = (t - high).astype(BF16).astype(F32)
        low = t - high - mid
        row = lax.broadcasted_iota(jnp.int32, (TAIL, t.shape[1]), 0)
        packed = jnp.where(row == 0, high, jnp.where(row == 1, mid, jnp.where(row == 2, low, 0.0)))
        msg_ref[at + STATE : at + STATE + TAIL, :] = packed.astype(BF16)


def local_call(kernel, name, smem, operands, out_shape):
    return pl.pallas_call(
        kernel,
        grid=(1,),
        in_specs=[pl.BlockSpec(memory_space=pltpu.SMEM)] + [whole(x.shape) for x in operands],
        out_specs=[whole(x.shape) for x in out_shape],
        out_shape=out_shape,
        compiler_params=params(10),
        cost_estimate=cost(1e6, 1.5e6),
        name=name,
    )(smem, *operands)


def join_kernel(count, *refs):
    place_ref, into_ref = refs[:2]
    slots, out_ref = refs[2:-1], refs[-1]
    place = place_ref[0]
    groups = [place ^ d for d in range(1, count)]
    read = [read_message(ref, 0) for ref in slots]
    ones = lambda condition: jnp.where(condition, 1.0, 0.0)
    sums = [None, None]
    for j, (state, _) in zip(groups, read):
        lower = ones(j < place)
        log = None
        for i, (_, other) in zip(groups, read):
            between = jnp.logical_or(jnp.logical_and(j < i, i < place), jnp.logical_and(place < i, i < j))
            term = ones(between) * other
            log = term if log is None else log + term
        part = jnp.exp(log) * state
        for k, share in enumerate((lower, 1.0 - lower)):
            sums[k] = share * part if sums[k] is None else sums[k] + share * part
    for k in (0, 1):
        out_ref[k] = into_ref[k, :STATE, :] + jnp.exp(into_ref[k, STATE : STATE + 1, :]) * sums[k]


def incoming(message, axis, beside, before):
    count, index = lax.axis_size(axis), lax.axis_index(axis)
    inner = message.shape[1]
    into = None
    distance = 1
    while count // distance > 4:
        other = lax.ppermute(message, axis, [(i, i ^ distance) for i in range(count)])
        if into is None:
            other, *beside = lax.optimization_barrier((other, *beside))
        upper = ((index // distance) % 2).astype(jnp.int32).reshape(1)
        operands = [message, other] + ([] if into is None else [into])
        out_shape = [jax.ShapeDtypeStruct((2, STATE + 8, inner), F32), jax.ShapeDtypeStruct(message.shape, BF16)]
        into, message = local_call(functools.partial(hop_kernel, into is None), "hop", upper, operands, out_shape)
        distance *= 2
    if into is None:
        into = jnp.zeros((2, STATE + 8, inner), F32)
    message, *before = lax.optimization_barrier((message, *before))
    groups = count // distance
    place = index // distance
    half = STATE + TAIL
    slots = []
    for d in range(1, groups):
        highest = 1 << (d.bit_length() - 1)
        above = (place // highest) % 2
        block = lax.dynamic_slice_in_dim(message, above * half, half, 0)
        slots.append(lax.ppermute(block, axis, [(i, i ^ (d * distance)) for i in range(count)]))
    joined = local_call(functools.partial(join_kernel, groups), "join", place.astype(jnp.int32).reshape(1), [into] + slots,
                        [pltpu.HBM((2, STATE, inner), F32)])[0]
    return joined, beside, before


def shifted(block, axis, distance):
    devices = range(lax.axis_size(axis))
    return lax.ppermute(block, axis, [(i - distance, i) for i in devices if i - distance in devices])


def rotated(block, d, count):
    return lax.ppermute(block, "head", [(i, (i + d) % count) for i in range(count)])


def on_device(
    hidden, norm_gain, w_zx, w_bc, w_dt, dt_bias, decay_rate, skip_gain, conv_x, conv_bc, w_out
):
    rows, depth = hidden.shape
    inner = conv_x.shape[1]
    heads = dt_bias.shape[0]
    width = inner // heads
    n_ctx, n_head = lax.axis_size("ctx"), lax.axis_size("head")
    ctx, head = lax.axis_index("ctx"), lax.axis_index("head")

    rim_f = shifted(hidden[rows - RIM :], "ctx", 1)
    rim_r = shifted(hidden[:RIM], "ctx", -1)

    half = w_out.shape[0] // 2
    parity = ctx % 2
    own_half = lax.dynamic_slice_in_dim(w_out, parity * half, half, 0)
    rim_f, rim_r, own_half = lax.optimization_barrier((rim_f, rim_r, own_half))
    middle = n_head // 2
    early = [d for d in range(1, n_head) if d != middle]
    same = [rotated(own_half, d, n_head) for d in early]

    lanes = jnp.pad(jnp.stack([dt_bias, decay_rate, skip_gain]), [(0, 0), (0, 128 - heads)])
    copy_first = spread_matrix(0, heads, width)
    copy_second = spread_matrix(heads, heads, width)
    (act_f, small_f, cumt_f, enter_f, prior_f, act_r, small_r, cumt_r, enter_r, prior_r,
     message, g_f, g_r) = project(hidden, rim_f, rim_r, (w_zx, w_bc, w_dt.T, norm_gain[None, :]), conv_x, conv_bc, lanes, copy_first, heads, inner)
    share = rows // n_head
    pieces = 2 if share % (2 * CHUNK) == 0 else 1
    size = share // pieces
    tile = min(TILE, size)
    place = lambda k: (k, pieces, tile, rows, head.astype(jnp.int32).reshape(1), n_head)
    strands = ((act_f, small_f, cumt_f), (act_r, small_r, cumt_r))
    ends = ((enter_f, prior_f), (enter_r, prior_r))
    message, own_half, *same = lax.optimization_barrier((message, own_half, *same))
    across = rotated(same[early.index(middle - 1)], 1, n_head) if middle > 1 else rotated(own_half, 1, n_head)
    entering, gated, same = incoming(message, "ctx", gates(place(0), hidden, g_f, g_r, 5e9), same)
    other = lax.ppermute(jnp.concatenate(same, axis=0), "ctx", [(i, i ^ 1) for i in range(n_ctx)])
    entering, other = lax.optimization_barrier((entering, other))
    bases = inside(place(0), strands, lanes, copy_first, heads, inner, 8e9)
    parts = finish(place(0), strands, ends, bases, gated, entering, copy_second, heads, inner)
    (g_f, g_r), parts, across = lax.optimization_barrier(((g_f, g_r), parts, across))
    across_other = lax.ppermute(across, "ctx", [(i, i ^ 1) for i in range(n_ctx)])
    arrived = [[rotated(block, d, n_head) if d else block for d, block in enumerate(parts)]]
    for k in range(1, pieces):
        gated = gates(place(k), hidden, g_f, g_r, 1e8)
        parts = settle(place(k), strands, ends, gated, lanes, copy_first, entering, copy_second, heads, inner)
        parts, arrived[k - 1], across_other = lax.optimization_barrier((parts, arrived[k - 1], across_other))
        arrived.append([rotated(block, d, n_head) if d else block for d, block in enumerate(parts)])
    own_rows = lax.dynamic_slice_in_dim(hidden, head * share, share, 0)
    pairs = {d: (one, other[i * half : (i + 1) * half]) for i, (d, one) in enumerate(zip(early, same))}
    pairs[middle] = (across, across_other)
    groups = [w_out]
    for d in range(1, n_head):
        one, two = pairs[d]
        groups.append(jnp.concatenate([jnp.where(parity == 0, one, two), jnp.where(parity == 0, two, one)], axis=0))
    result = None
    for k in range(pieces):
        total = own_rows[k * size : (k + 1) * size].astype(F32)
        for d in sorted(range(n_head), key=lambda d: -abs(2 * d - n_head)):
            total = total + jnp.dot(arrived[k][d], groups[d], preferred_element_type=F32)
        total = total.astype(BF16)
        if result is None:
            result = jnp.pad(total, ((0, share - size), (0, 0)))
        else:
            result = lax.dynamic_update_slice(result, total, (k * size, 0))
    return result


def solution(mesh):
    placed = (
        P("ctx", None),
        P(),
        P(None, None, "head"),
        P(),
        P(None, "head"),
        P("head"),
        P("head"),
        P("head"),
        P(None, "head"),
        P(),
        P("head", None),
    )
    return jax.shard_map(
        on_device, mesh=mesh, in_specs=placed, out_specs=P(("ctx", "head"), None), check_vma=False
    )
```

```python
import functools

import jax
import jax.numpy as jnp
import numpy as np
from jax import lax
from jax.experimental import pallas as pl
from jax.experimental.pallas import tpu as pltpu
from jax.sharding import PartitionSpec as P

STATE = 128
CHUNK = 128
TILE = 256
EPS = 1e-05
RIM = 16
TAIL = 16
F32 = jnp.float32
BF16 = jnp.bfloat16
MIB = 2**20


def params(limit):
    return pltpu.CompilerParams(
        dimension_semantics=("arbitrary",), vmem_limit_bytes=limit * MIB
    )


def cost(flops, bytes_accessed):
    return pl.CostEstimate(flops=int(flops), bytes_accessed=int(bytes_accessed), transcendentals=0)


def whole(shape):
    return pl.BlockSpec(shape, lambda *_: (0,) * len(shape), pipeline_mode=pl.Buffered(1))


def silu(x):
    half = 0.5 * x
    return half + half * jnp.tanh(half)


def tri(rows, reverse):
    r = lax.broadcasted_iota(jnp.int32, (rows, rows), 0)
    c = lax.broadcasted_iota(jnp.int32, (rows, rows), 1)
    return (r <= c) if reverse else (r >= c)


def spread_matrix(first, heads, width):
    r = np.arange(2 * 128)[:, None] % 128
    c = np.arange(heads * width)[None, :] // width
    return jnp.asarray((r == c + first).astype(BF16))


def spread(q, matrix):
    high = q.astype(BF16)
    low = (q - high.astype(F32)).astype(BF16)
    return jnp.dot(jnp.concatenate([high, low], axis=1), matrix, preferred_element_type=F32)


def prepare(inner, zx_ref, bc_ref, dt_ref, gain_ref, wf_ref, wr_ref, gf_ref, gr_ref):
    depth = zx_ref.shape[0]
    rows = min(256, depth)
    r = lax.broadcasted_iota(jnp.int32, (rows, rows), 0)
    c = lax.broadcasted_iota(jnp.int32, (rows, rows), 1)
    turn = (r + c == rows - 1).astype(BF16)
    for b in range(0, depth, rows):
        here, there = slice(b, b + rows), slice(depth - rows - b, depth - b)
        gain = jnp.transpose(jnp.broadcast_to(gain_ref[:, here], (128, rows)))
        zx = zx_ref[here].astype(F32).reshape(rows, 2 * inner)
        steps = dt_ref[:, here].astype(F32)
        steps = jnp.transpose(jnp.concatenate([steps, jnp.zeros((128 - steps.shape[0], rows), F32)], axis=0))

        def put(part, at, forward_ref, turned_ref):
            size = part.shape[1]
            scaled = jnp.concatenate([part[:, g : g + 128] * gain for g in range(0, size, 128)], axis=1).astype(BF16)
            forward_ref[here, at : at + size] = scaled
            turned_ref[there, at : at + size] = jnp.dot(turn, scaled, preferred_element_type=F32).astype(BF16)

        put(zx[:, inner:], 0, wf_ref, wr_ref)
        put(bc_ref[here].astype(F32), inner, wf_ref, wr_ref)
        put(steps, inner + bc_ref.shape[1], wf_ref, wr_ref)
        put(zx[:, :inner], 0, gf_ref, gr_ref)


def row_scale(h):
    hf = h.astype(F32)
    return lax.rsqrt(jnp.mean(hf * hf, axis=-1, keepdims=True) + EPS)


def project_kernel(heads, inner, *refs):
    (hf_ref, hr_ref, rimf_ref, rimr_ref, zx_ref, bc_ref, wdt_ref, gain_ref, convx_ref, convbc_ref, lanes_ref, copy_ref,
     actf_ref, smallf_ref, cumtf_ref, enterf_ref, priorf_ref,
     actr_ref, smallr_ref, cumtr_ref, enterr_ref, priorr_ref,
     msg_ref, gf_ref, gr_ref, wf_ref, wr_ref, buff, bufr, statef, stater, totalf, totalr) = refs
    step = pl.program_id(0)
    last = pl.num_programs(0) - 1
    stream = inner + 2 * STATE
    blocks = stream // 128
    rows = hf_ref.shape[0]
    count = rows // CHUNK
    sides = (
        (False, hf_ref, rimf_ref, wf_ref, actf_ref, smallf_ref, cumtf_ref, enterf_ref, priorf_ref, buff, statef, totalf),
        (True, hr_ref, rimr_ref, wr_ref, actr_ref, smallr_ref, cumtr_ref, enterr_ref, priorr_ref, bufr, stater, totalr),
    )

    @pl.when(step == 0)
    def _():
        prepare(inner, zx_ref, bc_ref, wdt_ref, gain_ref, wf_ref, wr_ref, gf_ref, gr_ref)
        for reverse, _, rim_ref, w_ref, _, _, _, _, _, buf, state, total in sides:
            edge = rows if reverse else 0
            state[...] = jnp.zeros_like(state)
            total[...] = jnp.zeros_like(total)
            rim = rim_ref[...]
            out = jnp.dot(rim, w_ref[:, :stream], preferred_element_type=F32) * row_scale(rim)
            for j in range(blocks):
                part = out[:, j * 128 : (j + 1) * 128]
                buf[j, edge : edge + 8, :] = part[:8] if reverse else part[RIM - 8 :]

    lane = lax.broadcasted_iota(jnp.int32, (rows, 128), 1)
    row8 = lax.broadcasted_iota(jnp.int32, (8, 128), 0)
    r = lax.broadcasted_iota(jnp.int32, (rows, rows), 0)
    c = lax.broadcasted_iota(jnp.int32, (rows, rows), 1)
    same = r // CHUNK == c // CHUNK
    hs = [side[1][...] for side in sides]
    scales = [row_scale(h) for h in hs]
    tail_rows, aux_rows = [], []
    for k, (reverse, _, _, w_ref, _, small_ref, cumt_ref, _, _, _, _, total_ref) in enumerate(sides):
        raw = jnp.dot(hs[k], w_ref[:, stream:], preferred_element_type=F32) * scales[k] + lanes_ref[0:1, :]
        dt = jnp.maximum(raw, 0.0) + jnp.log1p(jnp.exp(-jnp.abs(raw)))
        dt = jnp.where(lane < heads, dt, 0.0)
        steps = -lanes_ref[1:2, :] * dt
        high = steps.astype(BF16).astype(F32)
        mid = (steps - high).astype(BF16).astype(F32)
        low = steps - high - mid
        packed = (high + pltpu.roll(mid, heads, 1) + pltpu.roll(low, 2 * heads, 1)).astype(BF16)
        mask = jnp.where(jnp.logical_and(same, (r <= c) if reverse else (r >= c)), 1.0, 0.0).astype(BF16)
        sums = jnp.dot(mask, packed, preferred_element_type=F32)
        sums = sums + pltpu.roll(sums, 128 - heads, 1) + pltpu.roll(sums, 128 - 2 * heads, 1)
        cum = jnp.where(lane < heads, sums, 0.0)
        small_ref[...] = dt + pltpu.roll(cum, heads, 1)
        running = total_ref[...]
        tails = [None] * count
        aux = [None] * count
        for i in range(count):
            n = count - 1 - i if reverse else i
            at = slice(n * CHUNK, (n + 1) * CHUNK)
            cumt_ref[:, at] = jnp.transpose(cum[at])[:heads]
            end = cum[n * CHUNK : n * CHUNK + 1] if reverse else cum[(n + 1) * CHUNK - 1 : (n + 1) * CHUNK]
            tails[n] = dt[at] * jnp.exp(end - cum[at])
            aux[n] = jnp.where(row8 == 0, jnp.exp(end), jnp.exp(running))
            running = running + end
        total_ref[...] = running
        tail_rows += tails
        aux_rows += aux
    weights = spread(jnp.concatenate(tail_rows + aux_rows, axis=0), copy_ref[...])

    for g in range(0, stream, 256):
        for k, (reverse, _, _, w_ref, act_ref, _, _, _, _, buf, _, _) in enumerate(sides):
            edge = rows if reverse else 0
            body = 0 if reverse else 8
            out = jnp.dot(hs[k], w_ref[:, g : g + 256], preferred_element_type=F32) * scales[k]
            for j in range(g // 128, g // 128 + 2):
                x = out[:, j * 128 - g : (j + 1) * 128 - g]
                buf[j, body : body + rows, :] = x
                own = j * 128 - (0 if j * 128 < inner else inner)
                taps = (convx_ref if j * 128 < inner else convbc_ref)[:, own : own + 128]
                total = taps[3:4] * x
                for d in (1, 2, 3):
                    at = body + d if reverse else body - d
                    total = total + taps[3 - d : 4 - d] * buf[j, at : at + rows, :]
                act_ref[:, j * 128 : (j + 1) * 128] = silu(total).astype(BF16)
                buf[j, edge : edge + 8, :] = x[:8] if reverse else x[rows - 8 :]

    for i in range(count):
        for k, (reverse, _, _, _, act_ref, _, _, enter_ref, prior_ref, _, state, _) in enumerate(sides):
            n = count - 1 - i if reverse else i
            at = slice(n * CHUNK, (n + 1) * CHUNK)
            own = weights[(k * count + n) * CHUNK : (k * count + n + 1) * CHUNK]
            aux = weights[2 * rows + (k * count + n) * 8 : 2 * rows + (k * count + n + 1) * 8]
            tails = (act_ref[at, :inner].astype(F32) * own).astype(BF16)
            ends = lax.dot_general(act_ref[at, inner : inner + STATE], tails, (((0,), (0,)), ((), ())),
                                   preferred_element_type=F32)
            before = state[...]
            enter_ref[n] = before.astype(BF16)
            prior_ref[n] = aux
            state[...] = before * aux[:1] + ends

    @pl.when(step == last)
    def _():
        for k, side in enumerate(sides):
            state, total = side[-2:]
            at = k * (STATE + TAIL)
            msg_ref[at : at + STATE, :] = state[...].astype(BF16)
            t = total[...]
            high = t.astype(BF16).astype(F32)
            mid = (t - high).astype(BF16).astype(F32)
            low = t - high - mid
            packed = jnp.where(row8 == 0, high, jnp.where(row8 == 1, mid, jnp.where(row8 == 2, low, 0.0)))
            rows3 = spread(packed, copy_ref[...])
            msg_ref[at + STATE : at + STATE + TAIL, :] = jnp.concatenate(
                [rows3, jnp.zeros_like(rows3)], axis=0).astype(BF16)


def project(hidden, rim_f, rim_r, weights, conv_x, conv_bc, lanes, copy, heads, inner):
    rows, depth = hidden.shape
    stream = inner + 2 * STATE
    n = rows // TILE
    per = TILE // CHUNK
    up, down = (lambda i: i), (lambda i: n - 1 - i)
    by_rows = lambda width, at: pl.BlockSpec((TILE, width), lambda i: (at(i), 0))
    out_specs, out_shape = [], []
    for at in (up, down):
        out_specs += [by_rows(stream, at), by_rows(128, at),
                      pl.BlockSpec((heads, TILE), lambda i, at=at: (0, at(i))),
                      pl.BlockSpec((per, STATE, inner), lambda i, at=at: (at(i), 0, 0)),
                      pl.BlockSpec((per, 8, inner), lambda i, at=at: (at(i), 0, 0))]
        out_shape += [jax.ShapeDtypeStruct((rows, stream), BF16),
                      jax.ShapeDtypeStruct((rows, 128), F32), jax.ShapeDtypeStruct((heads, rows), F32),
                      jax.ShapeDtypeStruct((n * per, STATE, inner), BF16),
                      jax.ShapeDtypeStruct((n * per, 8, inner), F32)]
    message = (2 * (STATE + TAIL), inner)
    buf = pltpu.VMEM((stream // 128, TILE + 8, 128), F32)
    state, total = pltpu.VMEM((STATE, inner), F32), pltpu.VMEM((8, 128), F32)
    return pl.pallas_call(
        functools.partial(project_kernel, heads, inner),
        grid=(n,),
        in_specs=[by_rows(depth, up), by_rows(depth, down), whole(rim_f.shape), whole(rim_r.shape),
                  *[whole(x.shape) for x in weights], whole(conv_x.shape), whole(conv_bc.shape), whole(lanes.shape),
                  whole(copy.shape)],
        out_specs=out_specs + [whole(message), whole((depth, inner)), whole((depth, inner))],
        out_shape=out_shape + [jax.ShapeDtypeStruct(message, BF16)] + [jax.ShapeDtypeStruct((depth, inner), BF16)] * 2,
        scratch_shapes=[pltpu.VMEM((depth, stream + 128), BF16)] * 2 + [buf, buf, state, state, total, total],
        compiler_params=params(58),
        cost_estimate=cost(22e9, 40e6),
        name="project",
    )(hidden, hidden, rim_f, rim_r, *weights, conv_x, conv_bc, lanes, copy)


def gates_kernel(h_ref, wf_ref, wr_ref, zf_ref, zr_ref):
    h = h_ref[...]
    scale = row_scale(h)
    for w_ref, z_ref in ((wf_ref, zf_ref), (wr_ref, zr_ref)):
        z_ref[...] = (jnp.dot(h, w_ref[...], preferred_element_type=F32) * scale).astype(BF16)


def by_destination(kernel, name, place, rows_in, fixed, by_order, out_shape, out_specs, work, scratch=()):
    k, pieces, tile, rows, head, n_head = place
    share = rows // n_head
    per_piece, per_share = share // pieces // tile, share // tile

    def at(i, head_ref):
        return lax.rem(head_ref[0] + i // per_piece, n_head) * per_share + k * per_piece + lax.rem(i, per_piece)

    def spec(shape, dim, last):
        def index(i, head_ref):
            where = [0] * len(shape)
            where[-1] = last
            where[dim] = at(i, head_ref)
            return tuple(where)

        return pl.BlockSpec(shape, index)

    in_specs = [spec(*one[1:]) for one in rows_in] + [whole(x.shape) for x in fixed]
    in_specs += [pl.BlockSpec((tile, x.shape[1]), lambda i, _: (i, 0)) for x in by_order]
    return pl.pallas_call(
        lambda _, *refs: kernel(*refs),
        grid_spec=pltpu.PrefetchScalarGridSpec(
            num_scalar_prefetch=1,
            grid=(n_head * per_piece,),
            in_specs=in_specs,
            out_specs=out_specs,
            scratch_shapes=scratch,
        ),
        out_shape=out_shape,
        compiler_params=params(58),
        cost_estimate=cost(work, 1e6),
        name=name,
    )(head, *[one[0] for one in rows_in], *fixed, *by_order)


def ordered(place, inner):
    _, pieces, tile, rows, _, _ = place
    return jax.ShapeDtypeStruct((rows // pieces, inner), BF16), pl.BlockSpec((tile, inner), lambda i, _: (i, 0))


def sent(place, inner):
    _, pieces, _, rows, _, n_head = place
    size = rows // n_head // pieces
    return [jax.ShapeDtypeStruct((size, inner), BF16)] * n_head, [whole((size, inner))] * n_head


def gates(place, hidden, w_f, w_r, work):
    shape, spec = ordered(place, w_f.shape[1])
    return by_destination(gates_kernel, "gates", place, [(hidden, (place[2], hidden.shape[1]), 0, 0)], [w_f, w_r], [],
                          [shape] * 2, [spec] * 2, work)


def inside_kernel(heads, inner, actf_ref, smallf_ref, cumtf_ref, actr_ref, smallr_ref, cumtr_ref, lanes_ref, copy_ref,
                  basef_ref, baser_ref):
    width = inner // heads
    per = 128 // width
    size = actf_ref.shape[0]
    lane = lax.broadcasted_iota(jnp.int32, (size, 128), 1)
    group = lax.broadcasted_iota(jnp.int32, (CHUNK, 128), 1) // width
    dts = [jnp.where(lane < heads, ref[...], 0.0) for ref in (smallf_ref, smallr_ref)]
    wide = spread(jnp.concatenate(dts + [jnp.broadcast_to(lanes_ref[2:3, :], (8, 128))], axis=0), copy_ref[...])
    skip = wide[2 * size : 2 * size + 1]
    sides = ((False, actf_ref, smallf_ref, cumtf_ref, basef_ref), (True, actr_ref, smallr_ref, cumtr_ref, baser_ref))
    for c in range(0, size, CHUNK):
        rows = slice(c, c + CHUNK)
        for k, (reverse, act_ref, small_ref, cumt_ref, base_ref) in enumerate(sides):
            small = small_ref[rows, :]
            values = act_ref[rows, :inner].astype(F32)
            weighted = (values * wide[k * size + c : k * size + c + CHUNK]).astype(BF16)
            scores = lax.dot_general(act_ref[rows, inner + STATE :], act_ref[rows, inner : inner + STATE],
                                     (((1,), (1,)), ((), ())), preferred_element_type=F32)
            scores = jnp.where(tri(CHUNK, reverse), scores, 0.0)
            for p in range(inner // 128):
                cols = slice(p * 128, (p + 1) * 128)
                pair = weighted[:, cols]
                mixing, stacked = [], []
                for q in range(per):
                    h = p * per + q
                    gap = jnp.minimum(small[:, heads + h : heads + h + 1] - cumt_ref[h : h + 1, rows], 0.0)
                    mixing.append((scores * jnp.exp(gap)).astype(BF16))
                    stacked.append(jnp.where(group == q, pair, jnp.zeros_like(pair)))
                out = jnp.dot(jnp.concatenate(mixing, axis=1), jnp.concatenate(stacked, axis=0),
                              preferred_element_type=F32)
                base_ref[rows, cols] = (out + skip[:, cols] * values[:, cols]).astype(BF16)


def inside_rows(strands, tile, heads):
    rows_in = []
    for act, small, cumt in strands:
        rows_in += [(act, (tile, act.shape[1]), 0, 0), (small, (tile, 128), 0, 0), (cumt, (heads, tile), 1, 0)]
    return rows_in


def inside(place, strands, lanes, copy, heads, inner, work):
    shape, spec = ordered(place, inner)
    return by_destination(functools.partial(inside_kernel, heads, inner), "inside", place,
                          inside_rows(strands, place[2], heads), [lanes, copy], [], [shape] * 2, [spec] * 2, work)


def finish_kernel(heads, inner, *refs):
    (cf_ref, ef_ref, pf_ref, sf_ref, cr_ref, er_ref, pr_ref, sr_ref, in_ref, copy_ref,
     zf_ref, zr_ref, bf_ref, br_ref, *out_refs) = refs
    width = inner // heads
    size = cf_ref.shape[0]
    row = lax.broadcasted_iota(jnp.int32, (256, 256), 0) // width
    column = lax.broadcasted_iota(jnp.int32, (256, 256), 1) // width
    mean = jnp.where(row == column, 1.0 / width, 0.0).astype(BF16)
    grown = spread(jnp.exp(jnp.minimum(jnp.concatenate([sf_ref[...], sr_ref[...]], axis=0), 0.0)), copy_ref[...])
    both = None
    for k, (c_ref, b_ref, z_ref, e_ref, p_ref) in enumerate(
            ((cf_ref, bf_ref, zf_ref, ef_ref, pf_ref), (cr_ref, br_ref, zr_ref, er_ref, pr_ref))):
        parts = []
        for c in range(e_ref.shape[0]):
            entering = (e_ref[c].astype(F32) + p_ref[c, 1:2, :] * in_ref[k]).astype(BF16)
            parts.append(jnp.dot(c_ref[c * CHUNK : (c + 1) * CHUNK, :], entering, preferred_element_type=F32))
        reads = jnp.concatenate(parts, axis=0)
        out = b_ref[...].astype(F32) + reads * grown[k * size : (k + 1) * size]
        gated = out * silu(z_ref[...].astype(F32))
        squares = (gated * gated).astype(BF16)
        means = jnp.concatenate(
            [jnp.dot(squares[:, g : g + 256], mean, preferred_element_type=F32) for g in range(0, inner, 256)], axis=1)
        result = gated * lax.rsqrt(means + EPS)
        both = result if both is None else both + result
    both = both.astype(BF16)
    step = pl.program_id(0)
    per_piece = out_refs[0].shape[0] // size
    for d, ref in enumerate(out_refs):
        @pl.when(step // per_piece == d)
        def _():
            ref[pl.ds(pl.multiple_of(lax.rem(step, per_piece) * size, size), size), :] = both


def finish_rows(strand, tile, inner):
    enter, prior = strand
    per = tile // CHUNK
    return [(enter, (per, STATE, inner), 0, 0), (prior, (per, 8, inner), 0, 0)]


def finish(place, strands, ends, bases, gated, entering, copy, heads, inner):
    tile = place[2]
    shapes, specs = sent(place, inner)
    rows_in = []
    for (act, small, _), end in zip(strands, ends):
        rows_in += [(act, (tile, STATE), 0, act.shape[1] // STATE - 1)] + finish_rows(end, tile, inner)
        rows_in += [(small, (tile, 128), 0, 0)]
    return by_destination(functools.partial(finish_kernel, heads, inner), "finish", place, rows_in, [entering, copy],
                          [*gated, *bases], shapes, specs, 1e8)


def settle_kernel(heads, inner, *refs):
    (actf_ref, smallf_ref, cumtf_ref, actr_ref, smallr_ref, cumtr_ref, ef_ref, pf_ref, er_ref, pr_ref,
     lanes_ref, first_ref, in_ref, second_ref, zf_ref, zr_ref, *out_refs, basef, baser) = refs
    inside_kernel(heads, inner, actf_ref, smallf_ref, cumtf_ref, actr_ref, smallr_ref, cumtr_ref, lanes_ref, first_ref,
                  basef, baser)
    maps = [ref.at[:, pl.ds(inner + STATE, STATE)] for ref in (actf_ref, actr_ref)]
    finish_kernel(heads, inner, maps[0], ef_ref, pf_ref, smallf_ref, maps[1], er_ref, pr_ref, smallr_ref,
                  in_ref, second_ref, zf_ref, zr_ref, basef, baser, *out_refs)


def settle(place, strands, ends, gated, lanes, first, entering, second, heads, inner):
    tile = place[2]
    shapes, specs = sent(place, inner)
    rows_in = inside_rows(strands, tile, heads) + finish_rows(ends[0], tile, inner) + finish_rows(ends[1], tile, inner)
    return by_destination(functools.partial(settle_kernel, heads, inner), "settle", place, rows_in,
                          [lanes, first, entering, second], list(gated), shapes, specs, 1e8,
                          [pltpu.VMEM((tile, inner), BF16)] * 2)


def read_message(ref, at):
    tail = ref[at + STATE : at + STATE + TAIL, :].astype(F32)
    return ref[at : at + STATE, :].astype(F32), tail[0:1] + tail[1:2] + tail[2:3]


def hop_kernel(first, *refs):
    upper_ref, mine_ref, other_ref = refs[:3]
    into_ref = None if first else refs[3]
    new_ref, msg_ref = refs[-2:]
    upper = upper_ref[0].astype(F32)
    for k in (0, 1):
        later = upper if k == 0 else 1.0 - upper
        at = k * (STATE + TAIL)
        o_state, o_log = read_message(other_ref, at)
        if first:
            new_state, new_log = later * o_state, later * o_log
        else:
            into_log = into_ref[k, STATE : STATE + 1, :]
            new_state = into_ref[k, :STATE, :] + later * jnp.exp(into_log) * o_state
            new_log = into_log + later * o_log
        new_ref[k, :STATE, :] = new_state
        new_ref[k, STATE:, :] = jnp.broadcast_to(new_log, (8, new_log.shape[1]))
        state, log = read_message(mine_ref, at)
        of_other = later * jnp.exp(log) + (1.0 - later)
        of_mine = later + (1.0 - later) * jnp.exp(o_log)
        msg_ref[at : at + STATE, :] = (of_other * o_state + of_mine * state).astype(BF16)
        t = log + o_log
        high = t.astype(BF16).astype(F32)
        mid = (t - high).astype(BF16).astype(F32)
        low = t - high - mid
        row = lax.broadcasted_iota(jnp.int32, (TAIL, t.shape[1]), 0)
        packed = jnp.where(row == 0, high, jnp.where(row == 1, mid, jnp.where(row == 2, low, 0.0)))
        msg_ref[at + STATE : at + STATE + TAIL, :] = packed.astype(BF16)


def local_call(kernel, name, smem, operands, out_shape):
    return pl.pallas_call(
        kernel,
        grid=(1,),
        in_specs=[pl.BlockSpec(memory_space=pltpu.SMEM)] + [whole(x.shape) for x in operands],
        out_specs=[whole(x.shape) for x in out_shape],
        out_shape=out_shape,
        compiler_params=params(10),
        cost_estimate=cost(1e6, 1.5e6),
        name=name,
    )(smem, *operands)


def join_kernel(count, *refs):
    place_ref, into_ref = refs[:2]
    slots, out_ref = refs[2:-1], refs[-1]
    place = place_ref[0]
    groups = [place ^ d for d in range(1, count)]
    read = [read_message(ref, 0) for ref in slots]
    ones = lambda condition: jnp.where(condition, 1.0, 0.0)
    sums = [None, None]
    for j, (state, _) in zip(groups, read):
        lower = ones(j < place)
        log = None
        for i, (_, other) in zip(groups, read):
            between = jnp.logical_or(jnp.logical_and(j < i, i < place), jnp.logical_and(place < i, i < j))
            term = ones(between) * other
            log = term if log is None else log + term
        part = jnp.exp(log) * state
        for k, share in enumerate((lower, 1.0 - lower)):
            sums[k] = share * part if sums[k] is None else sums[k] + share * part
    for k in (0, 1):
        out_ref[k] = into_ref[k, :STATE, :] + jnp.exp(into_ref[k, STATE : STATE + 1, :]) * sums[k]


def incoming(message, axis, beside, before):
    count, index = lax.axis_size(axis), lax.axis_index(axis)
    inner = message.shape[1]
    into = None
    distance = 1
    while count // distance > 4:
        other = lax.ppermute(message, axis, [(i, i ^ distance) for i in range(count)])
        if into is None:
            other, *beside = lax.optimization_barrier((other, *beside))
        upper = ((index // distance) % 2).astype(jnp.int32).reshape(1)
        operands = [message, other] + ([] if into is None else [into])
        out_shape = [jax.ShapeDtypeStruct((2, STATE + 8, inner), F32), jax.ShapeDtypeStruct(message.shape, BF16)]
        into, message = local_call(functools.partial(hop_kernel, into is None), "hop", upper, operands, out_shape)
        distance *= 2
    if into is None:
        into = jnp.zeros((2, STATE + 8, inner), F32)
    message, *before = lax.optimization_barrier((message, *before))
    groups = count // distance
    place = index // distance
    half = STATE + TAIL
    slots = []
    for d in range(1, groups):
        highest = 1 << (d.bit_length() - 1)
        above = (place // highest) % 2
        block = lax.dynamic_slice_in_dim(message, above * half, half, 0)
        slots.append(lax.ppermute(block, axis, [(i, i ^ (d * distance)) for i in range(count)]))
    joined = local_call(functools.partial(join_kernel, groups), "join", place.astype(jnp.int32).reshape(1), [into] + slots,
                        [pltpu.HBM((2, STATE, inner), F32)])[0]
    return joined, beside, before


def shifted(block, axis, distance):
    devices = range(lax.axis_size(axis))
    return lax.ppermute(block, axis, [(i - distance, i) for i in devices if i - distance in devices])


def rotated(block, d, count):
    return lax.ppermute(block, "head", [(i, (i + d) % count) for i in range(count)])


def on_device(
    hidden, norm_gain, w_zx, w_bc, w_dt, dt_bias, decay_rate, skip_gain, conv_x, conv_bc, w_out
):
    rows, depth = hidden.shape
    inner = conv_x.shape[1]
    heads = dt_bias.shape[0]
    width = inner // heads
    n_ctx, n_head = lax.axis_size("ctx"), lax.axis_size("head")
    ctx, head = lax.axis_index("ctx"), lax.axis_index("head")

    rim_f = shifted(hidden[rows - RIM :], "ctx", 1)
    rim_r = shifted(hidden[:RIM], "ctx", -1)

    half = w_out.shape[0] // 2
    parity = ctx % 2
    own_half = lax.dynamic_slice_in_dim(w_out, parity * half, half, 0)
    rim_f, rim_r, own_half = lax.optimization_barrier((rim_f, rim_r, own_half))
    middle = n_head // 2
    early = [d for d in range(1, n_head) if d != middle]
    same = [rotated(own_half, d, n_head) for d in early]

    lanes = jnp.pad(jnp.stack([dt_bias, decay_rate, skip_gain]), [(0, 0), (0, 128 - heads)])
    copy_first = spread_matrix(0, heads, width)
    copy_second = spread_matrix(heads, heads, width)
    (act_f, small_f, cumt_f, enter_f, prior_f, act_r, small_r, cumt_r, enter_r, prior_r,
     message, g_f, g_r) = project(hidden, rim_f, rim_r, (w_zx, w_bc, w_dt.T, norm_gain[None, :]), conv_x, conv_bc, lanes, copy_first, heads, inner)
    share = rows // n_head
    pieces = 2 if share % (2 * CHUNK) == 0 else 1
    size = share // pieces
    tile = min(TILE, size)
    place = lambda k: (k, pieces, tile, rows, head.astype(jnp.int32).reshape(1), n_head)
    strands = ((act_f, small_f, cumt_f), (act_r, small_r, cumt_r))
    ends = ((enter_f, prior_f), (enter_r, prior_r))
    message, own_half, *same = lax.optimization_barrier((message, own_half, *same))
    across = rotated(same[early.index(middle - 1)], 1, n_head) if middle > 1 else rotated(own_half, 1, n_head)
    entering, gated, same = incoming(message, "ctx", gates(place(0), hidden, g_f, g_r, 5e9), same)
    other = lax.ppermute(jnp.concatenate(same, axis=0), "ctx", [(i, i ^ 1) for i in range(n_ctx)])
    entering, other = lax.optimization_barrier((entering, other))
    bases = inside(place(0), strands, lanes, copy_first, heads, inner, 8e9)
    parts = finish(place(0), strands, ends, bases, gated, entering, copy_second, heads, inner)
    (g_f, g_r), parts, across = lax.optimization_barrier(((g_f, g_r), parts, across))
    across_other = lax.ppermute(across, "ctx", [(i, i ^ 1) for i in range(n_ctx)])
    middle_first = sorted(range(1, n_head), key=lambda d: abs(2 * d - n_head))
    arrived = [{0: parts[0], **{d: rotated(parts[d], d, n_head) for d in middle_first}}]
    for k in range(1, pieces):
        gated = gates(place(k), hidden, g_f, g_r, 1e8)
        parts = settle(place(k), strands, ends, gated, lanes, copy_first, entering, copy_second, heads, inner)
        parts, arrived[k - 1], across_other = lax.optimization_barrier((parts, arrived[k - 1], across_other))
        arrived.append({0: parts[0], **{d: rotated(parts[d], d, n_head) for d in middle_first}})
    own_rows = lax.dynamic_slice_in_dim(hidden, head * share, share, 0)
    pairs = {d: (one, other[i * half : (i + 1) * half]) for i, (d, one) in enumerate(zip(early, same))}
    pairs[middle] = (across, across_other)
    groups = [w_out]
    for d in range(1, n_head):
        one, two = pairs[d]
        groups.append(jnp.concatenate([jnp.where(parity == 0, one, two), jnp.where(parity == 0, two, one)], axis=0))
    result = None
    order = sorted(range(n_head), key=lambda d: (-abs(2 * d - n_head), -d))
    order = order[:-2] + order[:-3:-1]
    for k in range(pieces):
        total = own_rows[k * size : (k + 1) * size].astype(F32)
        for d in order[:-1]:
            total = total + jnp.dot(arrived[k][d], groups[d], preferred_element_type=F32)
        if k == pieces - 1:
            total = lax.optimization_barrier(total)
        total = (total + jnp.dot(arrived[k][order[-1]], groups[order[-1]], preferred_element_type=F32)).astype(BF16)
        if result is None:
            result = jnp.pad(total, ((0, share - size), (0, 0)))
        else:
            result = lax.dynamic_update_slice(result, total, (k * size, 0))
    return result


def solution(mesh):
    placed = (
        P("ctx", None),
        P(),
        P(None, None, "head"),
        P(),
        P(None, "head"),
        P("head"),
        P("head"),
        P("head"),
        P(None, "head"),
        P(),
        P("head", None),
    )
    return jax.shard_map(
        on_device, mesh=mesh, in_specs=placed, out_specs=P(("ctx", "head"), None), check_vma=False
    )
```

```python
import functools

import jax
import jax.numpy as jnp
import numpy as np
from jax import lax
from jax.experimental import pallas as pl
from jax.experimental.pallas import tpu as pltpu
from jax.sharding import PartitionSpec as P

STATE = 128
CHUNK = 128
TILE = 256
PROJECT_TILE = 512
EPS = 1e-05
RIM = 16
TAIL = 16
F32 = jnp.float32
BF16 = jnp.bfloat16
MIB = 2**20


def params(limit):
    return pltpu.CompilerParams(
        dimension_semantics=("arbitrary",), vmem_limit_bytes=limit * MIB
    )


def cost(flops, bytes_accessed):
    return pl.CostEstimate(flops=int(flops), bytes_accessed=int(bytes_accessed), transcendentals=0)


def whole(shape):
    return pl.BlockSpec(shape, lambda *_: (0,) * len(shape), pipeline_mode=pl.Buffered(1))


def silu(x):
    half = 0.5 * x
    return half + half * jnp.tanh(half)


def tri(rows, reverse):
    r = lax.broadcasted_iota(jnp.int32, (rows, rows), 0)
    c = lax.broadcasted_iota(jnp.int32, (rows, rows), 1)
    return (r <= c) if reverse else (r >= c)


def spread_matrix(first, heads, width):
    r = np.arange(2 * 128)[:, None] % 128
    c = np.arange(heads * width)[None, :] // width
    return jnp.asarray((r == c + first).astype(BF16))


def spread(q, matrix):
    high = q.astype(BF16)
    low = (q - high.astype(F32)).astype(BF16)
    return jnp.dot(jnp.concatenate([high, low], axis=1), matrix, preferred_element_type=F32)


def prepare(inner, zx_ref, bc_ref, dt_ref, gain_ref, wf_ref, wr_ref, gf_ref, gr_ref):
    depth = zx_ref.shape[0]
    rows = min(256, depth)
    r = lax.broadcasted_iota(jnp.int32, (rows, rows), 0)
    c = lax.broadcasted_iota(jnp.int32, (rows, rows), 1)
    turn = (r + c == rows - 1).astype(BF16)
    for b in range(0, depth, rows):
        here, there = slice(b, b + rows), slice(depth - rows - b, depth - b)
        gain = jnp.transpose(jnp.broadcast_to(gain_ref[:, here], (128, rows)))
        zx = zx_ref[here].astype(F32).reshape(rows, 2 * inner)
        steps = dt_ref[:, here].astype(F32)
        steps = jnp.transpose(jnp.concatenate([steps, jnp.zeros((128 - steps.shape[0], rows), F32)], axis=0))

        def put(part, at, forward_ref, turned_ref):
            size = part.shape[1]
            scaled = jnp.concatenate([part[:, g : g + 128] * gain for g in range(0, size, 128)], axis=1).astype(BF16)
            forward_ref[here, at : at + size] = scaled
            turned_ref[there, at : at + size] = jnp.dot(turn, scaled, preferred_element_type=F32).astype(BF16)

        put(zx[:, inner:], 0, wf_ref, wr_ref)
        put(bc_ref[here].astype(F32), inner, wf_ref, wr_ref)
        put(steps, inner + bc_ref.shape[1], wf_ref, wr_ref)
        put(zx[:, :inner], 0, gf_ref, gr_ref)


def row_scale(h):
    hf = h.astype(F32)
    return lax.rsqrt(jnp.mean(hf * hf, axis=-1, keepdims=True) + EPS)


def project_kernel(heads, inner, *refs):
    (hf_ref, hr_ref, rimf_ref, rimr_ref, zx_ref, bc_ref, wdt_ref, gain_ref, convx_ref, convbc_ref, lanes_ref, copy_ref,
     actf_ref, smallf_ref, cumtf_ref, enterf_ref, priorf_ref,
     actr_ref, smallr_ref, cumtr_ref, enterr_ref, priorr_ref,
     msg_ref, gf_ref, gr_ref, wf_ref, wr_ref, buff, bufr, statef, stater, totalf, totalr) = refs
    step = pl.program_id(0)
    last = pl.num_programs(0) - 1
    stream = inner + 2 * STATE
    blocks = stream // 128
    rows = hf_ref.shape[0]
    count = rows // CHUNK
    sides = (
        (False, hf_ref, rimf_ref, wf_ref, actf_ref, smallf_ref, cumtf_ref, enterf_ref, priorf_ref, buff, statef, totalf),
        (True, hr_ref, rimr_ref, wr_ref, actr_ref, smallr_ref, cumtr_ref, enterr_ref, priorr_ref, bufr, stater, totalr),
    )

    @pl.when(step == 0)
    def _():
        prepare(inner, zx_ref, bc_ref, wdt_ref, gain_ref, wf_ref, wr_ref, gf_ref, gr_ref)
        for reverse, _, rim_ref, w_ref, _, _, _, _, _, buf, state, total in sides:
            edge = rows if reverse else 0
            state[...] = jnp.zeros_like(state)
            total[...] = jnp.zeros_like(total)
            rim = rim_ref[...]
            out = jnp.dot(rim, w_ref[:, :stream], preferred_element_type=F32) * row_scale(rim)
            for j in range(blocks):
                part = out[:, j * 128 : (j + 1) * 128]
                buf[j, edge : edge + 8, :] = part[:8] if reverse else part[RIM - 8 :]

    lane = lax.broadcasted_iota(jnp.int32, (rows, 128), 1)
    row8 = lax.broadcasted_iota(jnp.int32, (8, 128), 0)
    r = lax.broadcasted_iota(jnp.int32, (rows, rows), 0)
    c = lax.broadcasted_iota(jnp.int32, (rows, rows), 1)
    same = r // CHUNK == c // CHUNK
    hs = [side[1][...] for side in sides]
    scales = [row_scale(h) for h in hs]
    tail_rows, aux_rows = [], []
    for k, (reverse, _, _, w_ref, _, small_ref, cumt_ref, _, _, _, _, total_ref) in enumerate(sides):
        raw = jnp.dot(hs[k], w_ref[:, stream:], preferred_element_type=F32) * scales[k] + lanes_ref[0:1, :]
        dt = jnp.maximum(raw, 0.0) + jnp.log1p(jnp.exp(-jnp.abs(raw)))
        dt = jnp.where(lane < heads, dt, 0.0)
        steps = -lanes_ref[1:2, :] * dt
        high = steps.astype(BF16).astype(F32)
        mid = (steps - high).astype(BF16).astype(F32)
        low = steps - high - mid
        packed = (high + pltpu.roll(mid, heads, 1) + pltpu.roll(low, 2 * heads, 1)).astype(BF16)
        mask = jnp.where(jnp.logical_and(same, (r <= c) if reverse else (r >= c)), 1.0, 0.0).astype(BF16)
        sums = jnp.dot(mask, packed, preferred_element_type=F32)
        sums = sums + pltpu.roll(sums, 128 - heads, 1) + pltpu.roll(sums, 128 - 2 * heads, 1)
        cum = jnp.where(lane < heads, sums, 0.0)
        small_ref[...] = dt + pltpu.roll(cum, heads, 1)
        running = total_ref[...]
        tails = [None] * count
        aux = [None] * count
        for i in range(count):
            n = count - 1 - i if reverse else i
            at = slice(n * CHUNK, (n + 1) * CHUNK)
            cumt_ref[:, at] = jnp.transpose(cum[at])[:heads]
            end = cum[n * CHUNK : n * CHUNK + 1] if reverse else cum[(n + 1) * CHUNK - 1 : (n + 1) * CHUNK]
            tails[n] = dt[at] * jnp.exp(end - cum[at])
            aux[n] = jnp.where(row8 == 0, jnp.exp(end), jnp.exp(running))
            running = running + end
        total_ref[...] = running
        tail_rows += tails
        aux_rows += aux
    weights = spread(jnp.concatenate(tail_rows + aux_rows, axis=0), copy_ref[...])

    for g in range(0, stream, 256):
        for k, (reverse, _, _, w_ref, act_ref, _, _, _, _, buf, _, _) in enumerate(sides):
            edge = rows if reverse else 0
            body = 0 if reverse else 8
            out = jnp.dot(hs[k], w_ref[:, g : g + 256], preferred_element_type=F32) * scales[k]
            for j in range(g // 128, g // 128 + 2):
                x = out[:, j * 128 - g : (j + 1) * 128 - g]
                buf[j, body : body + rows, :] = x
                own = j * 128 - (0 if j * 128 < inner else inner)
                taps = (convx_ref if j * 128 < inner else convbc_ref)[:, own : own + 128]
                total = taps[3:4] * x
                for d in (1, 2, 3):
                    at = body + d if reverse else body - d
                    total = total + taps[3 - d : 4 - d] * buf[j, at : at + rows, :]
                act_ref[:, j * 128 : (j + 1) * 128] = silu(total).astype(BF16)
                buf[j, edge : edge + 8, :] = x[:8] if reverse else x[rows - 8 :]

    for i in range(count):
        for k, (reverse, _, _, _, act_ref, _, _, enter_ref, prior_ref, _, state, _) in enumerate(sides):
            n = count - 1 - i if reverse else i
            at = slice(n * CHUNK, (n + 1) * CHUNK)
            own = weights[(k * count + n) * CHUNK : (k * count + n + 1) * CHUNK]
            aux = weights[2 * rows + (k * count + n) * 8 : 2 * rows + (k * count + n + 1) * 8]
            tails = (act_ref[at, :inner].astype(F32) * own).astype(BF16)
            ends = lax.dot_general(act_ref[at, inner : inner + STATE], tails, (((0,), (0,)), ((), ())),
                                   preferred_element_type=F32)
            before = state[...]
            enter_ref[n] = before.astype(BF16)
            prior_ref[n] = aux
            state[...] = before * aux[:1] + ends

    @pl.when(step == last)
    def _():
        for k, side in enumerate(sides):
            state, total = side[-2:]
            at = k * (STATE + TAIL)
            msg_ref[at : at + STATE, :] = state[...].astype(BF16)
            t = total[...]
            high = t.astype(BF16).astype(F32)
            mid = (t - high).astype(BF16).astype(F32)
            low = t - high - mid
            packed = jnp.where(row8 == 0, high, jnp.where(row8 == 1, mid, jnp.where(row8 == 2, low, 0.0)))
            rows3 = spread(packed, copy_ref[...])
            msg_ref[at + STATE : at + STATE + TAIL, :] = jnp.concatenate(
                [rows3, jnp.zeros_like(rows3)], axis=0).astype(BF16)


def project(hidden, rim_f, rim_r, weights, conv_x, conv_bc, lanes, copy, heads, inner):
    rows, depth = hidden.shape
    stream = inner + 2 * STATE
    n = rows // PROJECT_TILE
    per = PROJECT_TILE // CHUNK
    up, down = (lambda i: i), (lambda i: n - 1 - i)
    by_rows = lambda width, at: pl.BlockSpec((PROJECT_TILE, width), lambda i: (at(i), 0))
    out_specs, out_shape = [], []
    for at in (up, down):
        out_specs += [by_rows(stream, at), by_rows(128, at),
                      pl.BlockSpec((heads, PROJECT_TILE), lambda i, at=at: (0, at(i))),
                      pl.BlockSpec((per, STATE, inner), lambda i, at=at: (at(i), 0, 0)),
                      pl.BlockSpec((per, 8, inner), lambda i, at=at: (at(i), 0, 0))]
        out_shape += [jax.ShapeDtypeStruct((rows, stream), BF16),
                      jax.ShapeDtypeStruct((rows, 128), F32), jax.ShapeDtypeStruct((heads, rows), F32),
                      jax.ShapeDtypeStruct((n * per, STATE, inner), BF16),
                      jax.ShapeDtypeStruct((n * per, 8, inner), F32)]
    message = (2 * (STATE + TAIL), inner)
    buf = pltpu.VMEM((stream // 128, PROJECT_TILE + 8, 128), F32)
    state, total = pltpu.VMEM((STATE, inner), F32), pltpu.VMEM((8, 128), F32)
    return pl.pallas_call(
        functools.partial(project_kernel, heads, inner),
        grid=(n,),
        in_specs=[by_rows(depth, up), by_rows(depth, down), whole(rim_f.shape), whole(rim_r.shape),
                  *[whole(x.shape) for x in weights], whole(conv_x.shape), whole(conv_bc.shape), whole(lanes.shape),
                  whole(copy.shape)],
        out_specs=out_specs + [whole(message), whole((depth, inner)), whole((depth, inner))],
        out_shape=out_shape + [jax.ShapeDtypeStruct(message, BF16)] + [jax.ShapeDtypeStruct((depth, inner), BF16)] * 2,
        scratch_shapes=[pltpu.VMEM((depth, stream + 128), BF16)] * 2 + [buf, buf, state, state, total, total],
        compiler_params=params(58),
        cost_estimate=cost(22e9, 40e6),
        name="project",
    )(hidden, hidden, rim_f, rim_r, *weights, conv_x, conv_bc, lanes, copy)


def gates_kernel(h_ref, wf_ref, wr_ref, zf_ref, zr_ref):
    h = h_ref[...]
    scale = row_scale(h)
    for w_ref, z_ref in ((wf_ref, zf_ref), (wr_ref, zr_ref)):
        z_ref[...] = (jnp.dot(h, w_ref[...], preferred_element_type=F32) * scale).astype(BF16)


def by_destination(kernel, name, place, rows_in, fixed, by_order, out_shape, out_specs, work, scratch=()):
    k, pieces, tile, rows, head, n_head = place
    share = rows // n_head
    per_piece, per_share = share // pieces // tile, share // tile

    def at(i, head_ref):
        return lax.rem(head_ref[0] + i // per_piece, n_head) * per_share + k * per_piece + lax.rem(i, per_piece)

    def spec(shape, dim, last):
        def index(i, head_ref):
            where = [0] * len(shape)
            where[-1] = last
            where[dim] = at(i, head_ref)
            return tuple(where)

        return pl.BlockSpec(shape, index)

    in_specs = [spec(*one[1:]) for one in rows_in] + [whole(x.shape) for x in fixed]
    in_specs += [pl.BlockSpec((tile, x.shape[1]), lambda i, _: (i, 0)) for x in by_order]
    return pl.pallas_call(
        lambda _, *refs: kernel(*refs),
        grid_spec=pltpu.PrefetchScalarGridSpec(
            num_scalar_prefetch=1,
            grid=(n_head * per_piece,),
            in_specs=in_specs,
            out_specs=out_specs,
            scratch_shapes=scratch,
        ),
        out_shape=out_shape,
        compiler_params=params(58),
        cost_estimate=cost(work, 1e6),
        name=name,
    )(head, *[one[0] for one in rows_in], *fixed, *by_order)


def ordered(place, inner):
    _, pieces, tile, rows, _, _ = place
    return jax.ShapeDtypeStruct((rows // pieces, inner), BF16), pl.BlockSpec((tile, inner), lambda i, _: (i, 0))


def sent(place, inner):
    _, pieces, _, rows, _, n_head = place
    size = rows // n_head // pieces
    return [jax.ShapeDtypeStruct((size, inner), BF16)] * n_head, [whole((size, inner))] * n_head


def gates(place, hidden, w_f, w_r, work):
    shape, spec = ordered(place, w_f.shape[1])
    return by_destination(gates_kernel, "gates", place, [(hidden, (place[2], hidden.shape[1]), 0, 0)], [w_f, w_r], [],
                          [shape] * 2, [spec] * 2, work)


def inside_kernel(heads, inner, actf_ref, smallf_ref, cumtf_ref, actr_ref, smallr_ref, cumtr_ref, lanes_ref, copy_ref,
                  basef_ref, baser_ref):
    width = inner // heads
    per = 128 // width
    size = actf_ref.shape[0]
    lane = lax.broadcasted_iota(jnp.int32, (size, 128), 1)
    group = lax.broadcasted_iota(jnp.int32, (CHUNK, 128), 1) // width
    dts = [jnp.where(lane < heads, ref[...], 0.0) for ref in (smallf_ref, smallr_ref)]
    wide = spread(jnp.concatenate(dts + [jnp.broadcast_to(lanes_ref[2:3, :], (8, 128))], axis=0), copy_ref[...])
    skip = wide[2 * size : 2 * size + 1]
    sides = ((False, actf_ref, smallf_ref, cumtf_ref, basef_ref), (True, actr_ref, smallr_ref, cumtr_ref, baser_ref))
    for c in range(0, size, CHUNK):
        rows = slice(c, c + CHUNK)
        for k, (reverse, act_ref, small_ref, cumt_ref, base_ref) in enumerate(sides):
            small = small_ref[rows, :]
            values = act_ref[rows, :inner].astype(F32)
            weighted = (values * wide[k * size + c : k * size + c + CHUNK]).astype(BF16)
            scores = lax.dot_general(act_ref[rows, inner + STATE :], act_ref[rows, inner : inner + STATE],
                                     (((1,), (1,)), ((), ())), preferred_element_type=F32)
            scores = jnp.where(tri(CHUNK, reverse), scores, 0.0)
            for p in range(inner // 128):
                cols = slice(p * 128, (p + 1) * 128)
                pair = weighted[:, cols]
                mixing, stacked = [], []
                for q in range(per):
                    h = p * per + q
                    gap = jnp.minimum(small[:, heads + h : heads + h + 1] - cumt_ref[h : h + 1, rows], 0.0)
                    mixing.append((scores * jnp.exp(gap)).astype(BF16))
                    stacked.append(jnp.where(group == q, pair, jnp.zeros_like(pair)))
                out = jnp.dot(jnp.concatenate(mixing, axis=1), jnp.concatenate(stacked, axis=0),
                              preferred_element_type=F32)
                base_ref[rows, cols] = (out + skip[:, cols] * values[:, cols]).astype(BF16)


def inside_rows(strands, tile, heads):
    rows_in = []
    for act, small, cumt in strands:
        rows_in += [(act, (tile, act.shape[1]), 0, 0), (small, (tile, 128), 0, 0), (cumt, (heads, tile), 1, 0)]
    return rows_in


def inside(place, strands, lanes, copy, heads, inner, work):
    shape, spec = ordered(place, inner)
    return by_destination(functools.partial(inside_kernel, heads, inner), "inside", place,
                          inside_rows(strands, place[2], heads), [lanes, copy], [], [shape] * 2, [spec] * 2, work)


def finish_kernel(heads, inner, *refs):
    (cf_ref, ef_ref, pf_ref, sf_ref, cr_ref, er_ref, pr_ref, sr_ref, in_ref, copy_ref,
     zf_ref, zr_ref, bf_ref, br_ref, *out_refs) = refs
    width = inner // heads
    size = cf_ref.shape[0]
    row = lax.broadcasted_iota(jnp.int32, (256, 256), 0) // width
    column = lax.broadcasted_iota(jnp.int32, (256, 256), 1) // width
    mean = jnp.where(row == column, 1.0 / width, 0.0).astype(BF16)
    grown = spread(jnp.exp(jnp.minimum(jnp.concatenate([sf_ref[...], sr_ref[...]], axis=0), 0.0)), copy_ref[...])
    both = None
    for k, (c_ref, b_ref, z_ref, e_ref, p_ref) in enumerate(
            ((cf_ref, bf_ref, zf_ref, ef_ref, pf_ref), (cr_ref, br_ref, zr_ref, er_ref, pr_ref))):
        parts = []
        for c in range(e_ref.shape[0]):
            entering = (e_ref[c].astype(F32) + p_ref[c, 1:2, :] * in_ref[k]).astype(BF16)
            parts.append(jnp.dot(c_ref[c * CHUNK : (c + 1) * CHUNK, :], entering, preferred_element_type=F32))
        reads = jnp.concatenate(parts, axis=0)
        out = b_ref[...].astype(F32) + reads * grown[k * size : (k + 1) * size]
        gated = out * silu(z_ref[...].astype(F32))
        squares = (gated * gated).astype(BF16)
        means = jnp.concatenate(
            [jnp.dot(squares[:, g : g + 256], mean, preferred_element_type=F32) for g in range(0, inner, 256)], axis=1)
        result = gated * lax.rsqrt(means + EPS)
        both = result if both is None else both + result
    both = both.astype(BF16)
    step = pl.program_id(0)
    per_piece = out_refs[0].shape[0] // size
    for d, ref in enumerate(out_refs):
        @pl.when(step // per_piece == d)
        def _():
            ref[pl.ds(pl.multiple_of(lax.rem(step, per_piece) * size, size), size), :] = both


def finish_rows(strand, tile, inner):
    enter, prior = strand
    per = tile // CHUNK
    return [(enter, (per, STATE, inner), 0, 0), (prior, (per, 8, inner), 0, 0)]


def finish(place, strands, ends, bases, gated, entering, copy, heads, inner):
    tile = place[2]
    shapes, specs = sent(place, inner)
    rows_in = []
    for (act, small, _), end in zip(strands, ends):
        rows_in += [(act, (tile, STATE), 0, act.shape[1] // STATE - 1)] + finish_rows(end, tile, inner)
        rows_in += [(small, (tile, 128), 0, 0)]
    return by_destination(functools.partial(finish_kernel, heads, inner), "finish", place, rows_in, [entering, copy],
                          [*gated, *bases], shapes, specs, 1e8)


def settle_kernel(heads, inner, *refs):
    (actf_ref, smallf_ref, cumtf_ref, actr_ref, smallr_ref, cumtr_ref, ef_ref, pf_ref, er_ref, pr_ref,
     lanes_ref, first_ref, in_ref, second_ref, zf_ref, zr_ref, *out_refs, basef, baser) = refs
    inside_kernel(heads, inner, actf_ref, smallf_ref, cumtf_ref, actr_ref, smallr_ref, cumtr_ref, lanes_ref, first_ref,
                  basef, baser)
    maps = [ref.at[:, pl.ds(inner + STATE, STATE)] for ref in (actf_ref, actr_ref)]
    finish_kernel(heads, inner, maps[0], ef_ref, pf_ref, smallf_ref, maps[1], er_ref, pr_ref, smallr_ref,
                  in_ref, second_ref, zf_ref, zr_ref, basef, baser, *out_refs)


def settle(place, strands, ends, gated, lanes, first, entering, second, heads, inner):
    tile = place[2]
    shapes, specs = sent(place, inner)
    rows_in = inside_rows(strands, tile, heads) + finish_rows(ends[0], tile, inner) + finish_rows(ends[1], tile, inner)
    return by_destination(functools.partial(settle_kernel, heads, inner), "settle", place, rows_in,
                          [lanes, first, entering, second], list(gated), shapes, specs, 1e8,
                          [pltpu.VMEM((tile, inner), BF16)] * 2)


def read_message(ref, at):
    tail = ref[at + STATE : at + STATE + TAIL, :].astype(F32)
    return ref[at : at + STATE, :].astype(F32), tail[0:1] + tail[1:2] + tail[2:3]


def hop_kernel(first, *refs):
    upper_ref, mine_ref, other_ref = refs[:3]
    into_ref = None if first else refs[3]
    new_ref, msg_ref = refs[-2:]
    upper = upper_ref[0].astype(F32)
    for k in (0, 1):
        later = upper if k == 0 else 1.0 - upper
        at = k * (STATE + TAIL)
        o_state, o_log = read_message(other_ref, at)
        if first:
            new_state, new_log = later * o_state, later * o_log
        else:
            into_log = into_ref[k, STATE : STATE + 1, :]
            new_state = into_ref[k, :STATE, :] + later * jnp.exp(into_log) * o_state
            new_log = into_log + later * o_log
        new_ref[k, :STATE, :] = new_state
        new_ref[k, STATE:, :] = jnp.broadcast_to(new_log, (8, new_log.shape[1]))
        state, log = read_message(mine_ref, at)
        of_other = later * jnp.exp(log) + (1.0 - later)
        of_mine = later + (1.0 - later) * jnp.exp(o_log)
        msg_ref[at : at + STATE, :] = (of_other * o_state + of_mine * state).astype(BF16)
        t = log + o_log
        high = t.astype(BF16).astype(F32)
        mid = (t - high).astype(BF16).astype(F32)
        low = t - high - mid
        row = lax.broadcasted_iota(jnp.int32, (TAIL, t.shape[1]), 0)
        packed = jnp.where(row == 0, high, jnp.where(row == 1, mid, jnp.where(row == 2, low, 0.0)))
        msg_ref[at + STATE : at + STATE + TAIL, :] = packed.astype(BF16)


def local_call(kernel, name, smem, operands, out_shape):
    return pl.pallas_call(
        kernel,
        grid=(1,),
        in_specs=[pl.BlockSpec(memory_space=pltpu.SMEM)] + [whole(x.shape) for x in operands],
        out_specs=[whole(x.shape) for x in out_shape],
        out_shape=out_shape,
        compiler_params=params(10),
        cost_estimate=cost(1e6, 1.5e6),
        name=name,
    )(smem, *operands)


def join_kernel(count, *refs):
    place_ref, into_ref = refs[:2]
    slots, out_ref = refs[2:-1], refs[-1]
    place = place_ref[0]
    groups = [place ^ d for d in range(1, count)]
    read = [read_message(ref, 0) for ref in slots]
    ones = lambda condition: jnp.where(condition, 1.0, 0.0)
    sums = [None, None]
    for j, (state, _) in zip(groups, read):
        lower = ones(j < place)
        log = None
        for i, (_, other) in zip(groups, read):
            between = jnp.logical_or(jnp.logical_and(j < i, i < place), jnp.logical_and(place < i, i < j))
            term = ones(between) * other
            log = term if log is None else log + term
        part = jnp.exp(log) * state
        for k, share in enumerate((lower, 1.0 - lower)):
            sums[k] = share * part if sums[k] is None else sums[k] + share * part
    for k in (0, 1):
        out_ref[k] = into_ref[k, :STATE, :] + jnp.exp(into_ref[k, STATE : STATE + 1, :]) * sums[k]


def incoming(message, axis, beside, before):
    count, index = lax.axis_size(axis), lax.axis_index(axis)
    inner = message.shape[1]
    into = None
    distance = 1
    while count // distance > 4:
        other = lax.ppermute(message, axis, [(i, i ^ distance) for i in range(count)])
        if into is None:
            other, *beside = lax.optimization_barrier((other, *beside))
        upper = ((index // distance) % 2).astype(jnp.int32).reshape(1)
        operands = [message, other] + ([] if into is None else [into])
        out_shape = [jax.ShapeDtypeStruct((2, STATE + 8, inner), F32), jax.ShapeDtypeStruct(message.shape, BF16)]
        into, message = local_call(functools.partial(hop_kernel, into is None), "hop", upper, operands, out_shape)
        distance *= 2
    if into is None:
        into = jnp.zeros((2, STATE + 8, inner), F32)
    message, *before = lax.optimization_barrier((message, *before))
    groups = count // distance
    place = index // distance
    half = STATE + TAIL
    slots = []
    for d in range(1, groups):
        highest = 1 << (d.bit_length() - 1)
        above = (place // highest) % 2
        block = lax.dynamic_slice_in_dim(message, above * half, half, 0)
        slots.append(lax.ppermute(block, axis, [(i, i ^ (d * distance)) for i in range(count)]))
    joined = local_call(functools.partial(join_kernel, groups), "join", place.astype(jnp.int32).reshape(1), [into] + slots,
                        [pltpu.HBM((2, STATE, inner), F32)])[0]
    return joined, beside, before


def shifted(block, axis, distance):
    devices = range(lax.axis_size(axis))
    return lax.ppermute(block, axis, [(i - distance, i) for i in devices if i - distance in devices])


def rotated(block, d, count):
    return lax.ppermute(block, "head", [(i, (i + d) % count) for i in range(count)])


def on_device(
    hidden, norm_gain, w_zx, w_bc, w_dt, dt_bias, decay_rate, skip_gain, conv_x, conv_bc, w_out
):
    rows, depth = hidden.shape
    inner = conv_x.shape[1]
    heads = dt_bias.shape[0]
    width = inner // heads
    n_ctx, n_head = lax.axis_size("ctx"), lax.axis_size("head")
    ctx, head = lax.axis_index("ctx"), lax.axis_index("head")

    rim_f = shifted(hidden[rows - RIM :], "ctx", 1)
    rim_r = shifted(hidden[:RIM], "ctx", -1)

    half = w_out.shape[0] // 2
    parity = ctx % 2
    own_half = lax.dynamic_slice_in_dim(w_out, parity * half, half, 0)
    rim_f, rim_r, own_half = lax.optimization_barrier((rim_f, rim_r, own_half))
    middle = n_head // 2
    early = [d for d in range(1, n_head) if d != middle]
    same = [rotated(own_half, d, n_head) for d in early]

    lanes = jnp.pad(jnp.stack([dt_bias, decay_rate, skip_gain]), [(0, 0), (0, 128 - heads)])
    copy_first = spread_matrix(0, heads, width)
    copy_second = spread_matrix(heads, heads, width)
    (act_f, small_f, cumt_f, enter_f, prior_f, act_r, small_r, cumt_r, enter_r, prior_r,
     message, g_f, g_r) = project(hidden, rim_f, rim_r, (w_zx, w_bc, w_dt.T, norm_gain[None, :]), conv_x, conv_bc, lanes, copy_first, heads, inner)
    share = rows // n_head
    pieces = 2 if share % (2 * CHUNK) == 0 else 1
    size = share // pieces
    tile = min(TILE, size)
    place = lambda k: (k, pieces, tile, rows, head.astype(jnp.int32).reshape(1), n_head)
    strands = ((act_f, small_f, cumt_f), (act_r, small_r, cumt_r))
    ends = ((enter_f, prior_f), (enter_r, prior_r))
    message, own_half, *same = lax.optimization_barrier((message, own_half, *same))
    across = rotated(same[early.index(middle - 1)], 1, n_head) if middle > 1 else rotated(own_half, 1, n_head)
    entering, gated, same = incoming(message, "ctx", gates(place(0), hidden, g_f, g_r, 5e9), same)
    other = lax.ppermute(jnp.concatenate(same, axis=0), "ctx", [(i, i ^ 1) for i in range(n_ctx)])
    entering, other = lax.optimization_barrier((entering, other))
    bases = inside(place(0), strands, lanes, copy_first, heads, inner, 8e9)
    parts = finish(place(0), strands, ends, bases, gated, entering, copy_second, heads, inner)
    (g_f, g_r), parts, across = lax.optimization_barrier(((g_f, g_r), parts, across))
    across_other = lax.ppermute(across, "ctx", [(i, i ^ 1) for i in range(n_ctx)])
    middle_first = sorted(range(1, n_head), key=lambda d: abs(2 * d - n_head))
    arrived = [{0: parts[0], **{d: rotated(parts[d], d, n_head) for d in middle_first}}]
    for k in range(1, pieces):
        gated = gates(place(k), hidden, g_f, g_r, 1e8)
        parts = settle(place(k), strands, ends, gated, lanes, copy_first, entering, copy_second, heads, inner)
        keys = [*middle_first, 0]
        parts, blocks, across_other = lax.optimization_barrier((parts, [arrived[k - 1][d] for d in keys], across_other))
        arrived[k - 1] = dict(zip(keys, blocks))
        arrived.append({0: parts[0], **{d: rotated(parts[d], d, n_head) for d in middle_first}})
    own_rows = lax.dynamic_slice_in_dim(hidden, head * share, share, 0)
    pairs = {d: (one, other[i * half : (i + 1) * half]) for i, (d, one) in enumerate(zip(early, same))}
    pairs[middle] = (across, across_other)
    groups = [w_out]
    for d in range(1, n_head):
        one, two = pairs[d]
        groups.append(jnp.concatenate([jnp.where(parity == 0, one, two), jnp.where(parity == 0, two, one)], axis=0))
    result = None
    order = sorted(range(n_head), key=lambda d: (-abs(2 * d - n_head), -d))
    order = order[:-2] + order[:-3:-1]
    for k in range(pieces):
        total = own_rows[k * size : (k + 1) * size].astype(F32)
        for d in order[:-1]:
            total = total + jnp.dot(arrived[k][d], groups[d], preferred_element_type=F32)
        if k == pieces - 1:
            total = lax.optimization_barrier(total)
        total = (total + jnp.dot(arrived[k][order[-1]], groups[order[-1]], preferred_element_type=F32)).astype(BF16)
        if result is None:
            result = jnp.pad(total, ((0, share - size), (0, 0)))
        else:
            result = lax.dynamic_update_slice(result, total, (k * size, 0))
    return result


def solution(mesh):
    placed = (
        P("ctx", None),
        P(),
        P(None, None, "head"),
        P(),
        P(None, "head"),
        P("head"),
        P("head"),
        P("head"),
        P(None, "head"),
        P(),
        P("head", None),
    )
    return jax.shard_map(
        on_device, mesh=mesh, in_specs=placed, out_specs=P(("ctx", "head"), None), check_vma=False
    )
```

```python
import functools

import jax
import jax.numpy as jnp
import numpy as np
from jax import lax
from jax.experimental import pallas as pl
from jax.experimental.pallas import tpu as pltpu
from jax.sharding import PartitionSpec as P

STATE = 128
CHUNK = 128
TILE = 256
PROJECT_TILE = 512
EPS = 1e-05
RIM = 16
TAIL = 16
F32 = jnp.float32
BF16 = jnp.bfloat16
MIB = 2**20


def params(limit):
    return pltpu.CompilerParams(
        dimension_semantics=("arbitrary",), vmem_limit_bytes=limit * MIB
    )


def cost(flops, bytes_accessed):
    return pl.CostEstimate(flops=int(flops), bytes_accessed=int(bytes_accessed), transcendentals=0)


def whole(shape):
    return pl.BlockSpec(shape, lambda *_: (0,) * len(shape), pipeline_mode=pl.Buffered(1))


def silu(x):
    half = 0.5 * x
    return half + half * jnp.tanh(half)


def tri(rows, reverse):
    r = lax.broadcasted_iota(jnp.int32, (rows, rows), 0)
    c = lax.broadcasted_iota(jnp.int32, (rows, rows), 1)
    return (r <= c) if reverse else (r >= c)


def spread_matrix(first, heads, width):
    r = np.arange(2 * 128)[:, None] % 128
    c = np.arange(heads * width)[None, :] // width
    return jnp.asarray((r == c + first).astype(BF16))


def spread(q, matrix):
    high = q.astype(BF16)
    low = (q - high.astype(F32)).astype(BF16)
    return jnp.dot(jnp.concatenate([high, low], axis=1), matrix, preferred_element_type=F32)


def prepare(inner, zx_ref, bc_ref, dt_ref, gain_ref, wf_ref, wr_ref, gf_ref, gr_ref):
    depth = zx_ref.shape[0]
    rows = min(256, depth)
    r = lax.broadcasted_iota(jnp.int32, (rows, rows), 0)
    c = lax.broadcasted_iota(jnp.int32, (rows, rows), 1)
    turn = (r + c == rows - 1).astype(BF16)
    for b in range(0, depth, rows):
        here, there = slice(b, b + rows), slice(depth - rows - b, depth - b)
        gain = jnp.transpose(jnp.broadcast_to(gain_ref[:, here], (128, rows)))
        zx = zx_ref[here].astype(F32).reshape(rows, 2 * inner)
        steps = dt_ref[:, here].astype(F32)
        steps = jnp.transpose(jnp.concatenate([steps, jnp.zeros((128 - steps.shape[0], rows), F32)], axis=0))

        def put(part, at, forward_ref, turned_ref):
            size = part.shape[1]
            scaled = jnp.concatenate([part[:, g : g + 128] * gain for g in range(0, size, 128)], axis=1).astype(BF16)
            forward_ref[here, at : at + size] = scaled
            turned_ref[there, at : at + size] = jnp.dot(turn, scaled, preferred_element_type=F32).astype(BF16)

        put(zx[:, inner:], 0, wf_ref, wr_ref)
        put(bc_ref[here].astype(F32), inner, wf_ref, wr_ref)
        put(steps, inner + bc_ref.shape[1], wf_ref, wr_ref)
        put(zx[:, :inner], 0, gf_ref, gr_ref)


def row_scale(h):
    hf = h.astype(F32)
    return lax.rsqrt(jnp.mean(hf * hf, axis=-1, keepdims=True) + EPS)


def project_kernel(heads, inner, *refs):
    (hf_ref, hr_ref, rimf_ref, rimr_ref, zx_ref, bc_ref, wdt_ref, gain_ref, convx_ref, convbc_ref, lanes_ref, copy_ref,
     actf_ref, smallf_ref, cumtf_ref, enterf_ref, priorf_ref,
     actr_ref, smallr_ref, cumtr_ref, enterr_ref, priorr_ref,
     msg_ref, gf_ref, gr_ref, wf_ref, wr_ref, buff, bufr, statef, stater, totalf, totalr) = refs
    step = pl.program_id(0)
    last = pl.num_programs(0) - 1
    stream = inner + 2 * STATE
    blocks = stream // 128
    rows = hf_ref.shape[0]
    count = rows // CHUNK
    sides = (
        (False, hf_ref, rimf_ref, wf_ref, actf_ref, smallf_ref, cumtf_ref, enterf_ref, priorf_ref, buff, statef, totalf),
        (True, hr_ref, rimr_ref, wr_ref, actr_ref, smallr_ref, cumtr_ref, enterr_ref, priorr_ref, bufr, stater, totalr),
    )

    @pl.when(step == 0)
    def _():
        prepare(inner, zx_ref, bc_ref, wdt_ref, gain_ref, wf_ref, wr_ref, gf_ref, gr_ref)
        for reverse, _, rim_ref, w_ref, _, _, _, _, _, buf, state, total in sides:
            edge = rows if reverse else 0
            state[...] = jnp.zeros_like(state)
            total[...] = jnp.zeros_like(total)
            rim = rim_ref[...]
            out = jnp.dot(rim, w_ref[:, :stream], preferred_element_type=F32) * row_scale(rim)
            for j in range(blocks):
                part = out[:, j * 128 : (j + 1) * 128]
                buf[j, edge : edge + 8, :] = part[:8] if reverse else part[RIM - 8 :]

    lane = lax.broadcasted_iota(jnp.int32, (rows, 128), 1)
    row8 = lax.broadcasted_iota(jnp.int32, (8, 128), 0)
    r = lax.broadcasted_iota(jnp.int32, (rows, rows), 0)
    c = lax.broadcasted_iota(jnp.int32, (rows, rows), 1)
    same = r // CHUNK == c // CHUNK
    hs = [side[1][...] for side in sides]
    scales = [row_scale(h) for h in hs]
    tail_rows, aux_rows = [], []
    for k, (reverse, _, _, w_ref, _, small_ref, cumt_ref, _, _, _, _, total_ref) in enumerate(sides):
        raw = jnp.dot(hs[k], w_ref[:, stream:], preferred_element_type=F32) * scales[k] + lanes_ref[0:1, :]
        dt = jnp.maximum(raw, 0.0) + jnp.log1p(jnp.exp(-jnp.abs(raw)))
        dt = jnp.where(lane < heads, dt, 0.0)
        steps = -lanes_ref[1:2, :] * dt
        high = steps.astype(BF16).astype(F32)
        mid = (steps - high).astype(BF16).astype(F32)
        low = steps - high - mid
        packed = (high + pltpu.roll(mid, heads, 1) + pltpu.roll(low, 2 * heads, 1)).astype(BF16)
        mask = jnp.where(jnp.logical_and(same, (r <= c) if reverse else (r >= c)), 1.0, 0.0).astype(BF16)
        sums = jnp.dot(mask, packed, preferred_element_type=F32)
        sums = sums + pltpu.roll(sums, 128 - heads, 1) + pltpu.roll(sums, 128 - 2 * heads, 1)
        cum = jnp.where(lane < heads, sums, 0.0)
        small_ref[...] = dt + pltpu.roll(cum, heads, 1)
        running = total_ref[...]
        tails = [None] * count
        aux = [None] * count
        for i in range(count):
            n = count - 1 - i if reverse else i
            at = slice(n * CHUNK, (n + 1) * CHUNK)
            cumt_ref[:, at] = jnp.transpose(cum[at])[:heads]
            end = cum[n * CHUNK : n * CHUNK + 1] if reverse else cum[(n + 1) * CHUNK - 1 : (n + 1) * CHUNK]
            tails[n] = dt[at] * jnp.exp(end - cum[at])
            aux[n] = jnp.where(row8 == 0, jnp.exp(end), jnp.exp(running))
            running = running + end
        total_ref[...] = running
        tail_rows += tails
        aux_rows += aux
    weights = spread(jnp.concatenate(tail_rows + aux_rows, axis=0), copy_ref[...])

    for g in range(0, stream, 256):
        for k, (reverse, _, _, w_ref, act_ref, _, _, _, _, buf, _, _) in enumerate(sides):
            edge = rows if reverse else 0
            body = 0 if reverse else 8
            out = jnp.dot(hs[k], w_ref[:, g : g + 256], preferred_element_type=F32) * scales[k]
            for j in range(g // 128, g // 128 + 2):
                x = out[:, j * 128 - g : (j + 1) * 128 - g]
                buf[j, body : body + rows, :] = x
                own = j * 128 - (0 if j * 128 < inner else inner)
                taps = (convx_ref if j * 128 < inner else convbc_ref)[:, own : own + 128]
                total = taps[3:4] * x
                for d in (1, 2, 3):
                    at = body + d if reverse else body - d
                    total = total + taps[3 - d : 4 - d] * buf[j, at : at + rows, :]
                act_ref[:, j * 128 : (j + 1) * 128] = silu(total).astype(BF16)
                buf[j, edge : edge + 8, :] = x[:8] if reverse else x[rows - 8 :]

    for i in range(count):
        for k, (reverse, _, _, _, act_ref, _, _, enter_ref, prior_ref, _, state, _) in enumerate(sides):
            n = count - 1 - i if reverse else i
            at = slice(n * CHUNK, (n + 1) * CHUNK)
            own = weights[(k * count + n) * CHUNK : (k * count + n + 1) * CHUNK]
            aux = weights[2 * rows + (k * count + n) * 8 : 2 * rows + (k * count + n + 1) * 8]
            tails = (act_ref[at, :inner].astype(F32) * own).astype(BF16)
            ends = lax.dot_general(act_ref[at, inner : inner + STATE], tails, (((0,), (0,)), ((), ())),
                                   preferred_element_type=F32)
            before = state[...]
            enter_ref[n] = before.astype(BF16)
            prior_ref[n] = aux
            state[...] = before * aux[:1] + ends

    @pl.when(step == last)
    def _():
        for k, side in enumerate(sides):
            state, total = side[-2:]
            at = k * (STATE + TAIL)
            msg_ref[at : at + STATE, :] = state[...].astype(BF16)
            t = total[...]
            high = t.astype(BF16).astype(F32)
            mid = (t - high).astype(BF16).astype(F32)
            low = t - high - mid
            packed = jnp.where(row8 == 0, high, jnp.where(row8 == 1, mid, jnp.where(row8 == 2, low, 0.0)))
            rows3 = spread(packed, copy_ref[...])
            msg_ref[at + STATE : at + STATE + TAIL, :] = jnp.concatenate(
                [rows3, jnp.zeros_like(rows3)], axis=0).astype(BF16)


def project(hidden, rim_f, rim_r, weights, conv_x, conv_bc, lanes, copy, heads, inner):
    rows, depth = hidden.shape
    stream = inner + 2 * STATE
    n = rows // PROJECT_TILE
    per = PROJECT_TILE // CHUNK
    up, down = (lambda i: i), (lambda i: n - 1 - i)
    by_rows = lambda width, at: pl.BlockSpec((PROJECT_TILE, width), lambda i: (at(i), 0))
    out_specs, out_shape = [], []
    for at in (up, down):
        out_specs += [by_rows(stream, at), by_rows(128, at),
                      pl.BlockSpec((heads, PROJECT_TILE), lambda i, at=at: (0, at(i))),
                      pl.BlockSpec((per, STATE, inner), lambda i, at=at: (at(i), 0, 0)),
                      pl.BlockSpec((per, 8, inner), lambda i, at=at: (at(i), 0, 0))]
        out_shape += [jax.ShapeDtypeStruct((rows, stream), BF16),
                      jax.ShapeDtypeStruct((rows, 128), F32), jax.ShapeDtypeStruct((heads, rows), F32),
                      jax.ShapeDtypeStruct((n * per, STATE, inner), BF16),
                      jax.ShapeDtypeStruct((n * per, 8, inner), F32)]
    message = (2 * (STATE + TAIL), inner)
    buf = pltpu.VMEM((stream // 128, PROJECT_TILE + 8, 128), F32)
    state, total = pltpu.VMEM((STATE, inner), F32), pltpu.VMEM((8, 128), F32)
    return pl.pallas_call(
        functools.partial(project_kernel, heads, inner),
        grid=(n,),
        in_specs=[by_rows(depth, up), by_rows(depth, down), whole(rim_f.shape), whole(rim_r.shape),
                  *[whole(x.shape) for x in weights], whole(conv_x.shape), whole(conv_bc.shape), whole(lanes.shape),
                  whole(copy.shape)],
        out_specs=out_specs + [whole(message), whole((depth, inner)), whole((depth, inner))],
        out_shape=out_shape + [jax.ShapeDtypeStruct(message, BF16)] + [jax.ShapeDtypeStruct((depth, inner), BF16)] * 2,
        scratch_shapes=[pltpu.VMEM((depth, stream + 128), BF16)] * 2 + [buf, buf, state, state, total, total],
        compiler_params=params(58),
        cost_estimate=cost(22e9, 40e6),
        name="project",
    )(hidden, hidden, rim_f, rim_r, *weights, conv_x, conv_bc, lanes, copy)


def gates_kernel(h_ref, wf_ref, wr_ref, zf_ref, zr_ref):
    h = h_ref[...]
    scale = row_scale(h)
    for w_ref, z_ref in ((wf_ref, zf_ref), (wr_ref, zr_ref)):
        z_ref[...] = (jnp.dot(h, w_ref[...], preferred_element_type=F32) * scale).astype(BF16)


def by_destination(kernel, name, place, rows_in, fixed, by_order, out_shape, out_specs, work, scratch=()):
    k, pieces, tile, rows, head, n_head = place
    share = rows // n_head
    per_piece, per_share = share // pieces // tile, share // tile

    def at(i, head_ref):
        return lax.rem(head_ref[0] + i // per_piece, n_head) * per_share + k * per_piece + lax.rem(i, per_piece)

    def spec(shape, dim, last):
        def index(i, head_ref):
            where = [0] * len(shape)
            where[-1] = last
            where[dim] = at(i, head_ref)
            return tuple(where)

        return pl.BlockSpec(shape, index)

    in_specs = [spec(*one[1:]) for one in rows_in] + [whole(x.shape) for x in fixed]
    in_specs += [pl.BlockSpec((tile, x.shape[1]), lambda i, _: (i, 0)) for x in by_order]
    return pl.pallas_call(
        lambda _, *refs: kernel(*refs),
        grid_spec=pltpu.PrefetchScalarGridSpec(
            num_scalar_prefetch=1,
            grid=(n_head * per_piece,),
            in_specs=in_specs,
            out_specs=out_specs,
            scratch_shapes=scratch,
        ),
        out_shape=out_shape,
        compiler_params=params(58),
        cost_estimate=cost(work, 1e6),
        name=name,
    )(head, *[one[0] for one in rows_in], *fixed, *by_order)


def ordered(place, inner):
    _, pieces, tile, rows, _, _ = place
    return jax.ShapeDtypeStruct((rows // pieces, inner), BF16), pl.BlockSpec((tile, inner), lambda i, _: (i, 0))


def sent(place, inner):
    _, pieces, _, rows, _, n_head = place
    size = rows // n_head // pieces
    return [jax.ShapeDtypeStruct((size, inner), BF16)] * n_head, [whole((size, inner))] * n_head


def gates(place, hidden, w_f, w_r, work):
    shape, spec = ordered(place, w_f.shape[1])
    return by_destination(gates_kernel, "gates", place, [(hidden, (place[2], hidden.shape[1]), 0, 0)], [w_f, w_r], [],
                          [shape] * 2, [spec] * 2, work)


def inside_kernel(heads, inner, actf_ref, smallf_ref, cumtf_ref, actr_ref, smallr_ref, cumtr_ref, lanes_ref, copy_ref,
                  basef_ref, baser_ref):
    width = inner // heads
    per = 128 // width
    size = actf_ref.shape[0]
    lane = lax.broadcasted_iota(jnp.int32, (size, 128), 1)
    group = lax.broadcasted_iota(jnp.int32, (CHUNK, 128), 1) // width
    dts = [jnp.where(lane < heads, ref[...], 0.0) for ref in (smallf_ref, smallr_ref)]
    wide = spread(jnp.concatenate(dts + [jnp.broadcast_to(lanes_ref[2:3, :], (8, 128))], axis=0), copy_ref[...])
    skip = wide[2 * size : 2 * size + 1]
    sides = ((False, actf_ref, smallf_ref, cumtf_ref, basef_ref), (True, actr_ref, smallr_ref, cumtr_ref, baser_ref))
    for c in range(0, size, CHUNK):
        rows = slice(c, c + CHUNK)
        for k, (reverse, act_ref, small_ref, cumt_ref, base_ref) in enumerate(sides):
            small = small_ref[rows, :]
            values = act_ref[rows, :inner].astype(F32)
            weighted = (values * wide[k * size + c : k * size + c + CHUNK]).astype(BF16)
            scores = lax.dot_general(act_ref[rows, inner + STATE :], act_ref[rows, inner : inner + STATE],
                                     (((1,), (1,)), ((), ())), preferred_element_type=F32)
            scores = jnp.where(tri(CHUNK, reverse), scores, 0.0)
            for p in range(inner // 128):
                cols = slice(p * 128, (p + 1) * 128)
                pair = weighted[:, cols]
                mixing, stacked = [], []
                for q in range(per):
                    h = p * per + q
                    gap = jnp.minimum(small[:, heads + h : heads + h + 1] - cumt_ref[h : h + 1, rows], 0.0)
                    mixing.append((scores * jnp.exp(gap)).astype(BF16))
                    stacked.append(jnp.where(group == q, pair, jnp.zeros_like(pair)))
                out = jnp.dot(jnp.concatenate(mixing, axis=1), jnp.concatenate(stacked, axis=0),
                              preferred_element_type=F32)
                base_ref[rows, cols] = (out + skip[:, cols] * values[:, cols]).astype(BF16)


def inside_rows(strands, tile, heads):
    rows_in = []
    for act, small, cumt in strands:
        rows_in += [(act, (tile, act.shape[1]), 0, 0), (small, (tile, 128), 0, 0), (cumt, (heads, tile), 1, 0)]
    return rows_in


def inside(place, strands, lanes, copy, heads, inner, work):
    shape, spec = ordered(place, inner)
    return by_destination(functools.partial(inside_kernel, heads, inner), "inside", place,
                          inside_rows(strands, place[2], heads), [lanes, copy], [], [shape] * 2, [spec] * 2, work)


def finish_kernel(heads, inner, *refs):
    (cf_ref, ef_ref, pf_ref, sf_ref, cr_ref, er_ref, pr_ref, sr_ref, in_ref, copy_ref,
     zf_ref, zr_ref, bf_ref, br_ref, *out_refs) = refs
    width = inner // heads
    size = cf_ref.shape[0]
    row = lax.broadcasted_iota(jnp.int32, (256, 256), 0) // width
    column = lax.broadcasted_iota(jnp.int32, (256, 256), 1) // width
    mean = jnp.where(row == column, 1.0 / width, 0.0).astype(BF16)
    grown = spread(jnp.exp(jnp.minimum(jnp.concatenate([sf_ref[...], sr_ref[...]], axis=0), 0.0)), copy_ref[...])
    both = None
    for k, (c_ref, b_ref, z_ref, e_ref, p_ref) in enumerate(
            ((cf_ref, bf_ref, zf_ref, ef_ref, pf_ref), (cr_ref, br_ref, zr_ref, er_ref, pr_ref))):
        parts = []
        for c in range(e_ref.shape[0]):
            entering = (e_ref[c].astype(F32) + p_ref[c, 1:2, :] * in_ref[k]).astype(BF16)
            parts.append(jnp.dot(c_ref[c * CHUNK : (c + 1) * CHUNK, :], entering, preferred_element_type=F32))
        reads = jnp.concatenate(parts, axis=0)
        out = b_ref[...].astype(F32) + reads * grown[k * size : (k + 1) * size]
        gated = out * silu(z_ref[...].astype(F32))
        squares = (gated * gated).astype(BF16)
        means = jnp.concatenate(
            [jnp.dot(squares[:, g : g + 256], mean, preferred_element_type=F32) for g in range(0, inner, 256)], axis=1)
        result = gated * lax.rsqrt(means + EPS)
        both = result if both is None else both + result
    both = both.astype(BF16)
    step = pl.program_id(0)
    per_piece = out_refs[0].shape[0] // size
    for d, ref in enumerate(out_refs):
        @pl.when(step // per_piece == d)
        def _():
            ref[pl.ds(pl.multiple_of(lax.rem(step, per_piece) * size, size), size), :] = both


def finish_rows(strand, tile, inner):
    enter, prior = strand
    per = tile // CHUNK
    return [(enter, (per, STATE, inner), 0, 0), (prior, (per, 8, inner), 0, 0)]


def finish(place, strands, ends, bases, gated, entering, copy, heads, inner):
    tile = place[2]
    shapes, specs = sent(place, inner)
    rows_in = []
    for (act, small, _), end in zip(strands, ends):
        rows_in += [(act, (tile, STATE), 0, act.shape[1] // STATE - 1)] + finish_rows(end, tile, inner)
        rows_in += [(small, (tile, 128), 0, 0)]
    return by_destination(functools.partial(finish_kernel, heads, inner), "finish", place, rows_in, [entering, copy],
                          [*gated, *bases], shapes, specs, 1e8)


def settle_kernel(heads, inner, *refs):
    (actf_ref, smallf_ref, cumtf_ref, actr_ref, smallr_ref, cumtr_ref, ef_ref, pf_ref, er_ref, pr_ref,
     lanes_ref, first_ref, in_ref, second_ref, zf_ref, zr_ref, *out_refs, basef, baser) = refs
    inside_kernel(heads, inner, actf_ref, smallf_ref, cumtf_ref, actr_ref, smallr_ref, cumtr_ref, lanes_ref, first_ref,
                  basef, baser)
    maps = [ref.at[:, pl.ds(inner + STATE, STATE)] for ref in (actf_ref, actr_ref)]
    finish_kernel(heads, inner, maps[0], ef_ref, pf_ref, smallf_ref, maps[1], er_ref, pr_ref, smallr_ref,
                  in_ref, second_ref, zf_ref, zr_ref, basef, baser, *out_refs)


def settle(place, strands, ends, gated, lanes, first, entering, second, heads, inner):
    tile = place[2]
    shapes, specs = sent(place, inner)
    rows_in = inside_rows(strands, tile, heads) + finish_rows(ends[0], tile, inner) + finish_rows(ends[1], tile, inner)
    return by_destination(functools.partial(settle_kernel, heads, inner), "settle", place, rows_in,
                          [lanes, first, entering, second], list(gated), shapes, specs, 1e8,
                          [pltpu.VMEM((tile, inner), BF16)] * 2)


def read_message(ref, at):
    tail = ref[at + STATE : at + STATE + TAIL, :].astype(F32)
    return ref[at : at + STATE, :].astype(F32), tail[0:1] + tail[1:2] + tail[2:3]


def hop_kernel(first, *refs):
    upper_ref, mine_ref, other_ref = refs[:3]
    into_ref = None if first else refs[3]
    new_ref, msg_ref = refs[-2:]
    upper = upper_ref[0].astype(F32)
    for k in (0, 1):
        later = upper if k == 0 else 1.0 - upper
        at = k * (STATE + TAIL)
        o_state, o_log = read_message(other_ref, at)
        if first:
            new_state, new_log = later * o_state, later * o_log
        else:
            into_log = into_ref[k, STATE : STATE + 1, :]
            new_state = into_ref[k, :STATE, :] + later * jnp.exp(into_log) * o_state
            new_log = into_log + later * o_log
        new_ref[k, :STATE, :] = new_state
        new_ref[k, STATE:, :] = jnp.broadcast_to(new_log, (8, new_log.shape[1]))
        state, log = read_message(mine_ref, at)
        of_other = later * jnp.exp(log) + (1.0 - later)
        of_mine = later + (1.0 - later) * jnp.exp(o_log)
        msg_ref[at : at + STATE, :] = (of_other * o_state + of_mine * state).astype(BF16)
        t = log + o_log
        high = t.astype(BF16).astype(F32)
        mid = (t - high).astype(BF16).astype(F32)
        low = t - high - mid
        row = lax.broadcasted_iota(jnp.int32, (TAIL, t.shape[1]), 0)
        packed = jnp.where(row == 0, high, jnp.where(row == 1, mid, jnp.where(row == 2, low, 0.0)))
        msg_ref[at + STATE : at + STATE + TAIL, :] = packed.astype(BF16)


def local_call(kernel, name, smem, operands, out_shape):
    return pl.pallas_call(
        kernel,
        grid=(1,),
        in_specs=[pl.BlockSpec(memory_space=pltpu.SMEM)] + [whole(x.shape) for x in operands],
        out_specs=[whole(x.shape) for x in out_shape],
        out_shape=out_shape,
        compiler_params=params(10),
        cost_estimate=cost(1e6, 1.5e6),
        name=name,
    )(smem, *operands)


def join_kernel(count, *refs):
    place_ref, into_ref = refs[:2]
    slots, out_ref = refs[2:-1], refs[-1]
    place = place_ref[0]
    groups = [place ^ d for d in range(1, count)]
    read = [read_message(ref, 0) for ref in slots]
    ones = lambda condition: jnp.where(condition, 1.0, 0.0)
    sums = [None, None]
    for j, (state, _) in zip(groups, read):
        lower = ones(j < place)
        log = None
        for i, (_, other) in zip(groups, read):
            between = jnp.logical_or(jnp.logical_and(j < i, i < place), jnp.logical_and(place < i, i < j))
            term = ones(between) * other
            log = term if log is None else log + term
        part = jnp.exp(log) * state
        for k, share in enumerate((lower, 1.0 - lower)):
            sums[k] = share * part if sums[k] is None else sums[k] + share * part
    for k in (0, 1):
        out_ref[k] = into_ref[k, :STATE, :] + jnp.exp(into_ref[k, STATE : STATE + 1, :]) * sums[k]


def incoming(message, axis, beside, before):
    count, index = lax.axis_size(axis), lax.axis_index(axis)
    inner = message.shape[1]
    into = None
    distance = 1
    while count // distance > 4:
        other = lax.ppermute(message, axis, [(i, i ^ distance) for i in range(count)])
        if into is None:
            other, *beside = lax.optimization_barrier((other, *beside))
        upper = ((index // distance) % 2).astype(jnp.int32).reshape(1)
        operands = [message, other] + ([] if into is None else [into])
        out_shape = [jax.ShapeDtypeStruct((2, STATE + 8, inner), F32), jax.ShapeDtypeStruct(message.shape, BF16)]
        into, message = local_call(functools.partial(hop_kernel, into is None), "hop", upper, operands, out_shape)
        distance *= 2
    if into is None:
        into = jnp.zeros((2, STATE + 8, inner), F32)
    message, *before = lax.optimization_barrier((message, *before))
    groups = count // distance
    place = index // distance
    half = STATE + TAIL
    slots = []
    for d in range(1, groups):
        highest = 1 << (d.bit_length() - 1)
        above = (place // highest) % 2
        block = lax.dynamic_slice_in_dim(message, above * half, half, 0)
        slots.append(lax.ppermute(block, axis, [(i, i ^ (d * distance)) for i in range(count)]))
    joined = local_call(functools.partial(join_kernel, groups), "join", place.astype(jnp.int32).reshape(1), [into] + slots,
                        [pltpu.HBM((2, STATE, inner), F32)])[0]
    return joined, beside, before


def shifted(block, axis, distance):
    devices = range(lax.axis_size(axis))
    return lax.ppermute(block, axis, [(i - distance, i) for i in devices if i - distance in devices])


def rotated(block, d, count):
    return lax.ppermute(block, "head", [(i, (i + d) % count) for i in range(count)])


def on_device(
    hidden, norm_gain, w_zx, w_bc, w_dt, dt_bias, decay_rate, skip_gain, conv_x, conv_bc, w_out
):
    rows, depth = hidden.shape
    inner = conv_x.shape[1]
    heads = dt_bias.shape[0]
    width = inner // heads
    n_ctx, n_head = lax.axis_size("ctx"), lax.axis_size("head")
    ctx, head = lax.axis_index("ctx"), lax.axis_index("head")

    rim_f = shifted(hidden[rows - RIM :], "ctx", 1)
    rim_r = shifted(hidden[:RIM], "ctx", -1)

    half = w_out.shape[0] // 2
    parity = ctx % 2
    own_half = lax.dynamic_slice_in_dim(w_out, parity * half, half, 0)
    rim_f, rim_r, own_half = lax.optimization_barrier((rim_f, rim_r, own_half))
    middle = n_head // 2
    early = [d for d in range(1, n_head) if d != middle]
    same = [rotated(own_half, d, n_head) for d in early]

    lanes = jnp.pad(jnp.stack([dt_bias, decay_rate, skip_gain]), [(0, 0), (0, 128 - heads)])
    copy_first = spread_matrix(0, heads, width)
    copy_second = spread_matrix(heads, heads, width)
    (act_f, small_f, cumt_f, enter_f, prior_f, act_r, small_r, cumt_r, enter_r, prior_r,
     message, g_f, g_r) = project(hidden, rim_f, rim_r, (w_zx, w_bc, w_dt.T, norm_gain[None, :]), conv_x, conv_bc, lanes, copy_first, heads, inner)
    share = rows // n_head
    pieces = 2 if share % (2 * CHUNK) == 0 else 1
    size = share // pieces
    tile = min(TILE, size)
    place = lambda k: (k, pieces, tile, rows, head.astype(jnp.int32).reshape(1), n_head)
    strands = ((act_f, small_f, cumt_f), (act_r, small_r, cumt_r))
    ends = ((enter_f, prior_f), (enter_r, prior_r))
    message, own_half, *same = lax.optimization_barrier((message, own_half, *same))
    across = rotated(same[early.index(middle - 1)], 1, n_head) if middle > 1 else rotated(own_half, 1, n_head)
    entering, gated, same = incoming(message, "ctx", gates(place(0), hidden, g_f, g_r, 5e9), same)
    other = lax.ppermute(jnp.concatenate(same, axis=0), "ctx", [(i, i ^ 1) for i in range(n_ctx)])
    entering, other = lax.optimization_barrier((entering, other))
    bases = inside(place(0), strands, lanes, copy_first, heads, inner, 8e9)
    parts = finish(place(0), strands, ends, bases, gated, entering, copy_second, heads, inner)
    (g_f, g_r), parts, across = lax.optimization_barrier(((g_f, g_r), parts, across))
    across_other = lax.ppermute(across, "ctx", [(i, i ^ 1) for i in range(n_ctx)])
    middle_first = sorted(range(1, n_head), key=lambda d: abs(2 * d - n_head))
    arrived = [{0: parts[0], **{d: rotated(parts[d], d, n_head) for d in middle_first}}]
    for k in range(1, pieces):
        gated = gates(place(k), hidden, g_f, g_r, 1e8)
        parts = settle(place(k), strands, ends, gated, lanes, copy_first, entering, copy_second, heads, inner)
        parts, arrived[k - 1], across_other, other, same = lax.optimization_barrier(
            (parts, arrived[k - 1], across_other, other, same))
        arrived.append({0: parts[0], **{d: rotated(parts[d], d, n_head) for d in middle_first}})
    own_rows = lax.dynamic_slice_in_dim(hidden, head * share, share, 0)
    pairs = {d: (one, other[i * half : (i + 1) * half]) for i, (d, one) in enumerate(zip(early, same))}
    pairs[middle] = (across, across_other)
    groups = [w_out]
    for d in range(1, n_head):
        one, two = pairs[d]
        groups.append(jnp.concatenate([jnp.where(parity == 0, one, two), jnp.where(parity == 0, two, one)], axis=0))
    result = None
    order = sorted(range(n_head), key=lambda d: (-abs(2 * d - n_head), -d))
    order = order[:-2] + order[:-3:-1]
    for k in range(pieces):
        total = own_rows[k * size : (k + 1) * size].astype(F32)
        for d in order[:-1]:
            total = total + jnp.dot(arrived[k][d], groups[d], preferred_element_type=F32)
        if k == pieces - 1:
            total = lax.optimization_barrier(total)
        total = (total + jnp.dot(arrived[k][order[-1]], groups[order[-1]], preferred_element_type=F32)).astype(BF16)
        if result is None:
            result = jnp.pad(total, ((0, share - size), (0, 0)))
        else:
            result = lax.dynamic_update_slice(result, total, (k * size, 0))
    return result


def solution(mesh):
    placed = (
        P("ctx", None),
        P(),
        P(None, None, "head"),
        P(),
        P(None, "head"),
        P("head"),
        P("head"),
        P("head"),
        P(None, "head"),
        P(),
        P("head", None),
    )
    return jax.shard_map(
        on_device, mesh=mesh, in_specs=placed, out_specs=P(("ctx", "head"), None), check_vma=False
    )
```

```python
import functools

import jax
import jax.numpy as jnp
import numpy as np
from jax import lax
from jax.experimental import pallas as pl
from jax.experimental.pallas import tpu as pltpu
from jax.sharding import PartitionSpec as P

STATE = 128
CHUNK = 128
TILE = 256
PROJECT_TILE = 512
EPS = 1e-05
RIM = 16
TAIL = 16
F32 = jnp.float32
BF16 = jnp.bfloat16
MIB = 2**20


def params(limit):
    return pltpu.CompilerParams(
        dimension_semantics=("arbitrary",), vmem_limit_bytes=limit * MIB
    )


def cost(flops, bytes_accessed):
    return pl.CostEstimate(flops=int(flops), bytes_accessed=int(bytes_accessed), transcendentals=0)


def whole(shape):
    return pl.BlockSpec(shape, lambda *_: (0,) * len(shape), pipeline_mode=pl.Buffered(1))


def silu(x):
    half = 0.5 * x
    return half + half * jnp.tanh(half)


def tri(rows, reverse):
    r = lax.broadcasted_iota(jnp.int32, (rows, rows), 0)
    c = lax.broadcasted_iota(jnp.int32, (rows, rows), 1)
    return (r <= c) if reverse else (r >= c)


def spread_matrix(first, heads, width):
    r = np.arange(2 * 128)[:, None] % 128
    c = np.arange(heads * width)[None, :] // width
    return jnp.asarray((r == c + first).astype(BF16))


def spread(q, matrix):
    high = q.astype(BF16)
    low = (q - high.astype(F32)).astype(BF16)
    return jnp.dot(jnp.concatenate([high, low], axis=1), matrix, preferred_element_type=F32)


def prepare(inner, zx_ref, bc_ref, dt_ref, gain_ref, wf_ref, wr_ref, gf_ref, gr_ref):
    depth = zx_ref.shape[0]
    rows = min(256, depth)
    r = lax.broadcasted_iota(jnp.int32, (rows, rows), 0)
    c = lax.broadcasted_iota(jnp.int32, (rows, rows), 1)
    turn = (r + c == rows - 1).astype(BF16)
    for b in range(0, depth, rows):
        here, there = slice(b, b + rows), slice(depth - rows - b, depth - b)
        gain = jnp.transpose(jnp.broadcast_to(gain_ref[:, here], (128, rows)))
        zx = zx_ref[here].astype(F32).reshape(rows, 2 * inner)
        steps = dt_ref[:, here].astype(F32)
        steps = jnp.transpose(jnp.concatenate([steps, jnp.zeros((128 - steps.shape[0], rows), F32)], axis=0))

        def put(part, at, forward_ref, turned_ref):
            size = part.shape[1]
            scaled = jnp.concatenate([part[:, g : g + 128] * gain for g in range(0, size, 128)], axis=1).astype(BF16)
            forward_ref[here, at : at + size] = scaled
            turned_ref[there, at : at + size] = jnp.dot(turn, scaled, preferred_element_type=F32).astype(BF16)

        put(zx[:, inner:], 0, wf_ref, wr_ref)
        put(bc_ref[here].astype(F32), inner, wf_ref, wr_ref)
        put(steps, inner + bc_ref.shape[1], wf_ref, wr_ref)
        put(zx[:, :inner], 0, gf_ref, gr_ref)


def row_scale(h):
    hf = h.astype(F32)
    return lax.rsqrt(jnp.mean(hf * hf, axis=-1, keepdims=True) + EPS)


def project_kernel(heads, inner, *refs):
    (hf_ref, hr_ref, rimf_ref, rimr_ref, zx_ref, bc_ref, wdt_ref, gain_ref, convx_ref, convbc_ref, lanes_ref, copy_ref,
     actf_ref, smallf_ref, cumtf_ref, enterf_ref, priorf_ref,
     actr_ref, smallr_ref, cumtr_ref, enterr_ref, priorr_ref,
     msg_ref, gf_ref, gr_ref, wf_ref, wr_ref, buff, bufr, statef, stater, totalf, totalr) = refs
    step = pl.program_id(0)
    last = pl.num_programs(0) - 1
    stream = inner + 2 * STATE
    blocks = stream // 128
    rows = hf_ref.shape[0]
    count = rows // CHUNK
    sides = (
        (False, hf_ref, rimf_ref, wf_ref, actf_ref, smallf_ref, cumtf_ref, enterf_ref, priorf_ref, buff, statef, totalf),
        (True, hr_ref, rimr_ref, wr_ref, actr_ref, smallr_ref, cumtr_ref, enterr_ref, priorr_ref, bufr, stater, totalr),
    )

    @pl.when(step == 0)
    def _():
        prepare(inner, zx_ref, bc_ref, wdt_ref, gain_ref, wf_ref, wr_ref, gf_ref, gr_ref)
        for reverse, _, rim_ref, w_ref, _, _, _, _, _, buf, state, total in sides:
            edge = rows if reverse else 0
            state[...] = jnp.zeros_like(state)
            total[...] = jnp.zeros_like(total)
            rim = rim_ref[...]
            out = jnp.dot(rim, w_ref[:, :stream], preferred_element_type=F32) * row_scale(rim)
            for j in range(blocks):
                part = out[:, j * 128 : (j + 1) * 128]
                buf[j, edge : edge + 8, :] = part[:8] if reverse else part[RIM - 8 :]

    lane = lax.broadcasted_iota(jnp.int32, (rows, 128), 1)
    row8 = lax.broadcasted_iota(jnp.int32, (8, 128), 0)
    r = lax.broadcasted_iota(jnp.int32, (rows, rows), 0)
    c = lax.broadcasted_iota(jnp.int32, (rows, rows), 1)
    same = r // CHUNK == c // CHUNK
    hs = [side[1][...] for side in sides]
    scales = [row_scale(h) for h in hs]
    tail_rows, aux_rows = [], []
    for k, (reverse, _, _, w_ref, _, small_ref, cumt_ref, _, _, _, _, total_ref) in enumerate(sides):
        raw = jnp.dot(hs[k], w_ref[:, stream:], preferred_element_type=F32) * scales[k] + lanes_ref[0:1, :]
        dt = jnp.maximum(raw, 0.0) + jnp.log1p(jnp.exp(-jnp.abs(raw)))
        dt = jnp.where(lane < heads, dt, 0.0)
        steps = -lanes_ref[1:2, :] * dt
        high = steps.astype(BF16).astype(F32)
        mid = (steps - high).astype(BF16).astype(F32)
        low = steps - high - mid
        packed = (high + pltpu.roll(mid, heads, 1) + pltpu.roll(low, 2 * heads, 1)).astype(BF16)
        mask = jnp.where(jnp.logical_and(same, (r <= c) if reverse else (r >= c)), 1.0, 0.0).astype(BF16)
        sums = jnp.dot(mask, packed, preferred_element_type=F32)
        sums = sums + pltpu.roll(sums, 128 - heads, 1) + pltpu.roll(sums, 128 - 2 * heads, 1)
        cum = jnp.where(lane < heads, sums, 0.0)
        small_ref[...] = dt + pltpu.roll(cum, heads, 1)
        running = total_ref[...]
        tails = [None] * count
        aux = [None] * count
        for i in range(count):
            n = count - 1 - i if reverse else i
            at = slice(n * CHUNK, (n + 1) * CHUNK)
            cumt_ref[:, at] = jnp.transpose(cum[at])[:heads]
            end = cum[n * CHUNK : n * CHUNK + 1] if reverse else cum[(n + 1) * CHUNK - 1 : (n + 1) * CHUNK]
            tails[n] = dt[at] * jnp.exp(end - cum[at])
            aux[n] = jnp.where(row8 == 0, jnp.exp(end), jnp.exp(running))
            running = running + end
        total_ref[...] = running
        tail_rows += tails
        aux_rows += aux
    weights = spread(jnp.concatenate(tail_rows + aux_rows, axis=0), copy_ref[...])

    for g in range(0, stream, 256):
        for k, (reverse, _, _, w_ref, act_ref, _, _, _, _, buf, _, _) in enumerate(sides):
            edge = rows if reverse else 0
            body = 0 if reverse else 8
            out = jnp.dot(hs[k], w_ref[:, g : g + 256], preferred_element_type=F32) * scales[k]
            for j in range(g // 128, g // 128 + 2):
                x = out[:, j * 128 - g : (j + 1) * 128 - g]
                buf[j, body : body + rows, :] = x
                own = j * 128 - (0 if j * 128 < inner else inner)
                taps = (convx_ref if j * 128 < inner else convbc_ref)[:, own : own + 128]
                total = taps[3:4] * x
                for d in (1, 2, 3):
                    at = body + d if reverse else body - d
                    total = total + taps[3 - d : 4 - d] * buf[j, at : at + rows, :]
                act_ref[:, j * 128 : (j + 1) * 128] = silu(total).astype(BF16)
                buf[j, edge : edge + 8, :] = x[:8] if reverse else x[rows - 8 :]

    for i in range(count):
        for k, (reverse, _, _, _, act_ref, _, _, enter_ref, prior_ref, _, state, _) in enumerate(sides):
            n = count - 1 - i if reverse else i
            at = slice(n * CHUNK, (n + 1) * CHUNK)
            own = weights[(k * count + n) * CHUNK : (k * count + n + 1) * CHUNK]
            aux = weights[2 * rows + (k * count + n) * 8 : 2 * rows + (k * count + n + 1) * 8]
            tails = (act_ref[at, :inner].astype(F32) * own).astype(BF16)
            ends = lax.dot_general(act_ref[at, inner : inner + STATE], tails, (((0,), (0,)), ((), ())),
                                   preferred_element_type=F32)
            before = state[...]
            enter_ref[n] = before.astype(BF16)
            prior_ref[n] = aux
            state[...] = before * aux[:1] + ends

    @pl.when(step == last)
    def _():
        for k, side in enumerate(sides):
            state, total = side[-2:]
            at = k * (STATE + TAIL)
            msg_ref[at : at + STATE, :] = state[...].astype(BF16)
            t = total[...]
            high = t.astype(BF16).astype(F32)
            mid = (t - high).astype(BF16).astype(F32)
            low = t - high - mid
            packed = jnp.where(row8 == 0, high, jnp.where(row8 == 1, mid, jnp.where(row8 == 2, low, 0.0)))
            rows3 = spread(packed, copy_ref[...])
            msg_ref[at + STATE : at + STATE + TAIL, :] = jnp.concatenate(
                [rows3, jnp.zeros_like(rows3)], axis=0).astype(BF16)


def project(hidden, rim_f, rim_r, weights, conv_x, conv_bc, lanes, copy, heads, inner):
    rows, depth = hidden.shape
    stream = inner + 2 * STATE
    n = rows // PROJECT_TILE
    per = PROJECT_TILE // CHUNK
    up, down = (lambda i: i), (lambda i: n - 1 - i)
    by_rows = lambda width, at: pl.BlockSpec((PROJECT_TILE, width), lambda i: (at(i), 0))
    out_specs, out_shape = [], []
    for at in (up, down):
        out_specs += [by_rows(stream, at), by_rows(128, at),
                      pl.BlockSpec((heads, PROJECT_TILE), lambda i, at=at: (0, at(i))),
                      pl.BlockSpec((per, STATE, inner), lambda i, at=at: (at(i), 0, 0)),
                      pl.BlockSpec((per, 8, inner), lambda i, at=at: (at(i), 0, 0))]
        out_shape += [jax.ShapeDtypeStruct((rows, stream), BF16),
                      jax.ShapeDtypeStruct((rows, 128), F32), jax.ShapeDtypeStruct((heads, rows), F32),
                      jax.ShapeDtypeStruct((n * per, STATE, inner), BF16),
                      jax.ShapeDtypeStruct((n * per, 8, inner), F32)]
    message = (2 * (STATE + TAIL), inner)
    buf = pltpu.VMEM((stream // 128, PROJECT_TILE + 8, 128), F32)
    state, total = pltpu.VMEM((STATE, inner), F32), pltpu.VMEM((8, 128), F32)
    return pl.pallas_call(
        functools.partial(project_kernel, heads, inner),
        grid=(n,),
        in_specs=[by_rows(depth, up), by_rows(depth, down), whole(rim_f.shape), whole(rim_r.shape),
                  *[whole(x.shape) for x in weights], whole(conv_x.shape), whole(conv_bc.shape), whole(lanes.shape),
                  whole(copy.shape)],
        out_specs=out_specs + [whole(message), whole((depth, inner)), whole((depth, inner))],
        out_shape=out_shape + [jax.ShapeDtypeStruct(message, BF16)] + [jax.ShapeDtypeStruct((depth, inner), BF16)] * 2,
        scratch_shapes=[pltpu.VMEM((depth, stream + 128), BF16)] * 2 + [buf, buf, state, state, total, total],
        compiler_params=params(58),
        cost_estimate=cost(22e9, 40e6),
        name="project",
    )(hidden, hidden, rim_f, rim_r, *weights, conv_x, conv_bc, lanes, copy)


def gates_kernel(h_ref, wf_ref, wr_ref, zf_ref, zr_ref):
    h = h_ref[...]
    scale = row_scale(h)
    for w_ref, z_ref in ((wf_ref, zf_ref), (wr_ref, zr_ref)):
        z_ref[...] = (jnp.dot(h, w_ref[...], preferred_element_type=F32) * scale).astype(BF16)


def by_destination(kernel, name, place, rows_in, fixed, by_order, out_shape, out_specs, work, scratch=()):
    k, pieces, tile, rows, head, n_head = place
    share = rows // n_head
    per_piece, per_share = share // pieces // tile, share // tile

    def at(i, head_ref):
        return lax.rem(head_ref[0] + i // per_piece, n_head) * per_share + k * per_piece + lax.rem(i, per_piece)

    def spec(shape, dim, last):
        def index(i, head_ref):
            where = [0] * len(shape)
            where[-1] = last
            where[dim] = at(i, head_ref)
            return tuple(where)

        return pl.BlockSpec(shape, index)

    in_specs = [spec(*one[1:]) for one in rows_in] + [whole(x.shape) for x in fixed]
    in_specs += [pl.BlockSpec((tile, x.shape[1]), lambda i, _: (i, 0)) for x in by_order]
    return pl.pallas_call(
        lambda _, *refs: kernel(*refs),
        grid_spec=pltpu.PrefetchScalarGridSpec(
            num_scalar_prefetch=1,
            grid=(n_head * per_piece,),
            in_specs=in_specs,
            out_specs=out_specs,
            scratch_shapes=scratch,
        ),
        out_shape=out_shape,
        compiler_params=params(58),
        cost_estimate=cost(work, 1e6),
        name=name,
    )(head, *[one[0] for one in rows_in], *fixed, *by_order)


def ordered(place, inner):
    _, pieces, tile, rows, _, _ = place
    return jax.ShapeDtypeStruct((rows // pieces, inner), BF16), pl.BlockSpec((tile, inner), lambda i, _: (i, 0))


def sent(place, inner):
    _, pieces, _, rows, _, n_head = place
    size = rows // n_head // pieces
    return [jax.ShapeDtypeStruct((size, inner), BF16)] * n_head, [whole((size, inner))] * n_head


def gates(place, hidden, w_f, w_r, work):
    shape, spec = ordered(place, w_f.shape[1])
    return by_destination(gates_kernel, "gates", place, [(hidden, (place[2], hidden.shape[1]), 0, 0)], [w_f, w_r], [],
                          [shape] * 2, [spec] * 2, work)


def inside_kernel(heads, inner, actf_ref, smallf_ref, cumtf_ref, actr_ref, smallr_ref, cumtr_ref, lanes_ref, copy_ref,
                  basef_ref, baser_ref):
    width = inner // heads
    per = 128 // width
    size = actf_ref.shape[0]
    lane = lax.broadcasted_iota(jnp.int32, (size, 128), 1)
    group = lax.broadcasted_iota(jnp.int32, (CHUNK, 128), 1) // width
    dts = [jnp.where(lane < heads, ref[...], 0.0) for ref in (smallf_ref, smallr_ref)]
    wide = spread(jnp.concatenate(dts + [jnp.broadcast_to(lanes_ref[2:3, :], (8, 128))], axis=0), copy_ref[...])
    skip = wide[2 * size : 2 * size + 1]
    sides = ((False, actf_ref, smallf_ref, cumtf_ref, basef_ref), (True, actr_ref, smallr_ref, cumtr_ref, baser_ref))
    for c in range(0, size, CHUNK):
        rows = slice(c, c + CHUNK)
        for k, (reverse, act_ref, small_ref, cumt_ref, base_ref) in enumerate(sides):
            small = small_ref[rows, :]
            values = act_ref[rows, :inner].astype(F32)
            weighted = (values * wide[k * size + c : k * size + c + CHUNK]).astype(BF16)
            scores = lax.dot_general(act_ref[rows, inner + STATE :], act_ref[rows, inner : inner + STATE],
                                     (((1,), (1,)), ((), ())), preferred_element_type=F32)
            scores = jnp.where(tri(CHUNK, reverse), scores, 0.0)
            for p in range(inner // 128):
                cols = slice(p * 128, (p + 1) * 128)
                pair = weighted[:, cols]
                mixing, stacked = [], []
                for q in range(per):
                    h = p * per + q
                    gap = jnp.minimum(small[:, heads + h : heads + h + 1] - cumt_ref[h : h + 1, rows], 0.0)
                    mixing.append((scores * jnp.exp(gap)).astype(BF16))
                    stacked.append(jnp.where(group == q, pair, jnp.zeros_like(pair)))
                out = jnp.dot(jnp.concatenate(mixing, axis=1), jnp.concatenate(stacked, axis=0),
                              preferred_element_type=F32)
                base_ref[rows, cols] = (out + skip[:, cols] * values[:, cols]).astype(BF16)


def inside_rows(strands, tile, heads):
    rows_in = []
    for act, small, cumt in strands:
        rows_in += [(act, (tile, act.shape[1]), 0, 0), (small, (tile, 128), 0, 0), (cumt, (heads, tile), 1, 0)]
    return rows_in


def inside(place, strands, lanes, copy, heads, inner, work):
    shape, spec = ordered(place, inner)
    return by_destination(functools.partial(inside_kernel, heads, inner), "inside", place,
                          inside_rows(strands, place[2], heads), [lanes, copy], [], [shape] * 2, [spec] * 2, work)


def finish_kernel(heads, inner, *refs):
    (cf_ref, ef_ref, pf_ref, sf_ref, cr_ref, er_ref, pr_ref, sr_ref, in_ref, copy_ref,
     zf_ref, zr_ref, bf_ref, br_ref, *out_refs) = refs
    width = inner // heads
    size = cf_ref.shape[0]
    row = lax.broadcasted_iota(jnp.int32, (256, 256), 0) // width
    column = lax.broadcasted_iota(jnp.int32, (256, 256), 1) // width
    mean = jnp.where(row == column, 1.0 / width, 0.0).astype(BF16)
    grown = spread(jnp.exp(jnp.minimum(jnp.concatenate([sf_ref[...], sr_ref[...]], axis=0), 0.0)), copy_ref[...])
    both = None
    for k, (c_ref, b_ref, z_ref, e_ref, p_ref) in enumerate(
            ((cf_ref, bf_ref, zf_ref, ef_ref, pf_ref), (cr_ref, br_ref, zr_ref, er_ref, pr_ref))):
        parts = []
        for c in range(e_ref.shape[0]):
            entering = (e_ref[c].astype(F32) + p_ref[c, 1:2, :] * in_ref[k]).astype(BF16)
            parts.append(jnp.dot(c_ref[c * CHUNK : (c + 1) * CHUNK, :], entering, preferred_element_type=F32))
        reads = jnp.concatenate(parts, axis=0)
        out = b_ref[...].astype(F32) + reads * grown[k * size : (k + 1) * size]
        gated = out * silu(z_ref[...].astype(F32))
        squares = (gated * gated).astype(BF16)
        means = jnp.concatenate(
            [jnp.dot(squares[:, g : g + 256], mean, preferred_element_type=F32) for g in range(0, inner, 256)], axis=1)
        result = gated * lax.rsqrt(means + EPS)
        both = result if both is None else both + result
    both = both.astype(BF16)
    step = pl.program_id(0)
    per_piece = out_refs[0].shape[0] // size
    for d, ref in enumerate(out_refs):
        @pl.when(step // per_piece == d)
        def _():
            ref[pl.ds(pl.multiple_of(lax.rem(step, per_piece) * size, size), size), :] = both


def finish_rows(strand, tile, inner):
    enter, prior = strand
    per = tile // CHUNK
    return [(enter, (per, STATE, inner), 0, 0), (prior, (per, 8, inner), 0, 0)]


def finish(place, strands, ends, bases, gated, entering, copy, heads, inner):
    tile = place[2]
    shapes, specs = sent(place, inner)
    rows_in = []
    for (act, small, _), end in zip(strands, ends):
        rows_in += [(act, (tile, STATE), 0, act.shape[1] // STATE - 1)] + finish_rows(end, tile, inner)
        rows_in += [(small, (tile, 128), 0, 0)]
    return by_destination(functools.partial(finish_kernel, heads, inner), "finish", place, rows_in, [entering, copy],
                          [*gated, *bases], shapes, specs, 1e8)


def settle_kernel(heads, inner, *refs):
    (actf_ref, smallf_ref, cumtf_ref, actr_ref, smallr_ref, cumtr_ref, ef_ref, pf_ref, er_ref, pr_ref,
     lanes_ref, first_ref, in_ref, second_ref, zf_ref, zr_ref, *out_refs, basef, baser) = refs
    inside_kernel(heads, inner, actf_ref, smallf_ref, cumtf_ref, actr_ref, smallr_ref, cumtr_ref, lanes_ref, first_ref,
                  basef, baser)
    maps = [ref.at[:, pl.ds(inner + STATE, STATE)] for ref in (actf_ref, actr_ref)]
    finish_kernel(heads, inner, maps[0], ef_ref, pf_ref, smallf_ref, maps[1], er_ref, pr_ref, smallr_ref,
                  in_ref, second_ref, zf_ref, zr_ref, basef, baser, *out_refs)


def settle(place, strands, ends, gated, lanes, first, entering, second, heads, inner):
    tile = place[2]
    shapes, specs = sent(place, inner)
    rows_in = inside_rows(strands, tile, heads) + finish_rows(ends[0], tile, inner) + finish_rows(ends[1], tile, inner)
    return by_destination(functools.partial(settle_kernel, heads, inner), "settle", place, rows_in,
                          [lanes, first, entering, second], list(gated), shapes, specs, 1e8,
                          [pltpu.VMEM((tile, inner), BF16)] * 2)


def read_message(ref, at):
    tail = ref[at + STATE : at + STATE + TAIL, :].astype(F32)
    return ref[at : at + STATE, :].astype(F32), tail[0:1] + tail[1:2] + tail[2:3]


def hop_kernel(first, *refs):
    upper_ref, mine_ref, other_ref = refs[:3]
    into_ref = None if first else refs[3]
    new_ref, msg_ref = refs[-2:]
    upper = upper_ref[0].astype(F32)
    for k in (0, 1):
        later = upper if k == 0 else 1.0 - upper
        at = k * (STATE + TAIL)
        o_state, o_log = read_message(other_ref, at)
        if first:
            new_state, new_log = later * o_state, later * o_log
        else:
            into_log = into_ref[k, STATE : STATE + 1, :]
            new_state = into_ref[k, :STATE, :] + later * jnp.exp(into_log) * o_state
            new_log = into_log + later * o_log
        new_ref[k, :STATE, :] = new_state
        new_ref[k, STATE:, :] = jnp.broadcast_to(new_log, (8, new_log.shape[1]))
        state, log = read_message(mine_ref, at)
        of_other = later * jnp.exp(log) + (1.0 - later)
        of_mine = later + (1.0 - later) * jnp.exp(o_log)
        msg_ref[at : at + STATE, :] = (of_other * o_state + of_mine * state).astype(BF16)
        t = log + o_log
        high = t.astype(BF16).astype(F32)
        mid = (t - high).astype(BF16).astype(F32)
        low = t - high - mid
        row = lax.broadcasted_iota(jnp.int32, (TAIL, t.shape[1]), 0)
        packed = jnp.where(row == 0, high, jnp.where(row == 1, mid, jnp.where(row == 2, low, 0.0)))
        msg_ref[at + STATE : at + STATE + TAIL, :] = packed.astype(BF16)


def local_call(kernel, name, smem, operands, out_shape):
    return pl.pallas_call(
        kernel,
        grid=(1,),
        in_specs=[pl.BlockSpec(memory_space=pltpu.SMEM)] + [whole(x.shape) for x in operands],
        out_specs=[whole(x.shape) for x in out_shape],
        out_shape=out_shape,
        compiler_params=params(10),
        cost_estimate=cost(1e6, 1.5e6),
        name=name,
    )(smem, *operands)


def join_kernel(count, *refs):
    place_ref, into_ref = refs[:2]
    slots, out_ref = refs[2:-1], refs[-1]
    place = place_ref[0]
    groups = [place ^ d for d in range(1, count)]
    read = [read_message(ref, 0) for ref in slots]
    ones = lambda condition: jnp.where(condition, 1.0, 0.0)
    sums = [None, None]
    for j, (state, _) in zip(groups, read):
        lower = ones(j < place)
        log = None
        for i, (_, other) in zip(groups, read):
            between = jnp.logical_or(jnp.logical_and(j < i, i < place), jnp.logical_and(place < i, i < j))
            term = ones(between) * other
            log = term if log is None else log + term
        part = jnp.exp(log) * state
        for k, share in enumerate((lower, 1.0 - lower)):
            sums[k] = share * part if sums[k] is None else sums[k] + share * part
    for k in (0, 1):
        out_ref[k] = into_ref[k, :STATE, :] + jnp.exp(into_ref[k, STATE : STATE + 1, :]) * sums[k]


def incoming(message, axis, beside, before):
    count, index = lax.axis_size(axis), lax.axis_index(axis)
    inner = message.shape[1]
    into = None
    distance = 1
    while count // distance > 4:
        other = lax.ppermute(message, axis, [(i, i ^ distance) for i in range(count)])
        if into is None:
            other, *beside = lax.optimization_barrier((other, *beside))
        upper = ((index // distance) % 2).astype(jnp.int32).reshape(1)
        operands = [message, other] + ([] if into is None else [into])
        out_shape = [jax.ShapeDtypeStruct((2, STATE + 8, inner), F32), jax.ShapeDtypeStruct(message.shape, BF16)]
        into, message = local_call(functools.partial(hop_kernel, into is None), "hop", upper, operands, out_shape)
        distance *= 2
    if into is None:
        into = jnp.zeros((2, STATE + 8, inner), F32)
    message, *before = lax.optimization_barrier((message, *before))
    groups = count // distance
    place = index // distance
    half = STATE + TAIL
    slots = []
    for d in range(1, groups):
        highest = 1 << (d.bit_length() - 1)
        above = (place // highest) % 2
        block = lax.dynamic_slice_in_dim(message, above * half, half, 0)
        slots.append(lax.ppermute(block, axis, [(i, i ^ (d * distance)) for i in range(count)]))
    joined = local_call(functools.partial(join_kernel, groups), "join", place.astype(jnp.int32).reshape(1), [into] + slots,
                        [pltpu.HBM((2, STATE, inner), F32)])[0]
    return joined, beside, before


def shifted(block, axis, distance):
    devices = range(lax.axis_size(axis))
    return lax.ppermute(block, axis, [(i - distance, i) for i in devices if i - distance in devices])


def rotated(block, d, count):
    return lax.ppermute(block, "head", [(i, (i + d) % count) for i in range(count)])


def on_device(
    hidden, norm_gain, w_zx, w_bc, w_dt, dt_bias, decay_rate, skip_gain, conv_x, conv_bc, w_out
):
    rows, depth = hidden.shape
    inner = conv_x.shape[1]
    heads = dt_bias.shape[0]
    width = inner // heads
    n_ctx, n_head = lax.axis_size("ctx"), lax.axis_size("head")
    ctx, head = lax.axis_index("ctx"), lax.axis_index("head")

    rim_f = shifted(hidden[rows - RIM :], "ctx", 1)
    rim_r = shifted(hidden[:RIM], "ctx", -1)

    half = w_out.shape[0] // 2
    parity = ctx % 2
    own_half = lax.dynamic_slice_in_dim(w_out, parity * half, half, 0)
    rim_f, rim_r, own_half = lax.optimization_barrier((rim_f, rim_r, own_half))
    middle = n_head // 2
    early = [d for d in range(1, n_head) if d != middle]
    same = [rotated(own_half, d, n_head) for d in early]

    lanes = jnp.pad(jnp.stack([dt_bias, decay_rate, skip_gain]), [(0, 0), (0, 128 - heads)])
    copy_first = spread_matrix(0, heads, width)
    copy_second = spread_matrix(heads, heads, width)
    (act_f, small_f, cumt_f, enter_f, prior_f, act_r, small_r, cumt_r, enter_r, prior_r,
     message, g_f, g_r) = project(hidden, rim_f, rim_r, (w_zx, w_bc, w_dt.T, norm_gain[None, :]), conv_x, conv_bc, lanes, copy_first, heads, inner)
    share = rows // n_head
    pieces = 2 if share % (2 * CHUNK) == 0 else 1
    size = share // pieces
    tile = min(TILE, size)
    place = lambda k: (k, pieces, tile, rows, head.astype(jnp.int32).reshape(1), n_head)
    strands = ((act_f, small_f, cumt_f), (act_r, small_r, cumt_r))
    ends = ((enter_f, prior_f), (enter_r, prior_r))
    message, own_half, *same = lax.optimization_barrier((message, own_half, *same))
    across = rotated(same[early.index(middle - 1)], 1, n_head) if middle > 1 else rotated(own_half, 1, n_head)
    entering, gated, same = incoming(message, "ctx", gates(place(0), hidden, g_f, g_r, 5e9), same)
    other = lax.ppermute(jnp.concatenate(same, axis=0), "ctx", [(i, i ^ 1) for i in range(n_ctx)])
    entering, other = lax.optimization_barrier((entering, other))
    bases = inside(place(0), strands, lanes, copy_first, heads, inner, 8e9)
    parts = finish(place(0), strands, ends, bases, gated, entering, copy_second, heads, inner)
    (g_f, g_r), parts, across = lax.optimization_barrier(((g_f, g_r), parts, across))
    across_other = lax.ppermute(across, "ctx", [(i, i ^ 1) for i in range(n_ctx)])
    middle_first = sorted(range(1, n_head), key=lambda d: abs(2 * d - n_head))
    arrived = [{0: parts[0], **{d: rotated(parts[d], d, n_head) for d in middle_first}}]
    for k in range(1, pieces):
        gated = gates(place(k), hidden, g_f, g_r, 1e8)
        parts = settle(place(k), strands, ends, gated, lanes, copy_first, entering, copy_second, heads, inner)
        parts = list(parts)
        before = arrived[k - 1]
        middle = middle_first[0]
        parts[middle], before[1] = lax.optimization_barrier((parts[middle], before[1]))
        rest = [d for d in range(n_head) if d != middle]
        moved, before, across_other, other, same = lax.optimization_barrier(
            ([parts[d] for d in rest], before, across_other, other, same))
        arrived[k - 1] = before
        for d, block in zip(rest, moved):
            parts[d] = block
        arrived.append({0: parts[0], **{d: rotated(parts[d], d, n_head) for d in middle_first}})
    own_rows = lax.dynamic_slice_in_dim(hidden, head * share, share, 0)
    pairs = {d: (one, other[i * half : (i + 1) * half]) for i, (d, one) in enumerate(zip(early, same))}
    pairs[middle] = (across, across_other)
    groups = [w_out]
    for d in range(1, n_head):
        one, two = pairs[d]
        groups.append(jnp.concatenate([jnp.where(parity == 0, one, two), jnp.where(parity == 0, two, one)], axis=0))
    result = None
    order = sorted(range(n_head), key=lambda d: (-abs(2 * d - n_head), -d))
    order = order[:-2] + order[:-3:-1]
    for k in range(pieces):
        total = own_rows[k * size : (k + 1) * size].astype(F32)
        for d in order[:-1]:
            total = total + jnp.dot(arrived[k][d], groups[d], preferred_element_type=F32)
        if k == pieces - 1:
            total = lax.optimization_barrier(total)
        total = (total + jnp.dot(arrived[k][order[-1]], groups[order[-1]], preferred_element_type=F32)).astype(BF16)
        if result is None:
            result = jnp.pad(total, ((0, share - size), (0, 0)))
        else:
            result = lax.dynamic_update_slice(result, total, (k * size, 0))
    return result


def solution(mesh):
    placed = (
        P("ctx", None),
        P(),
        P(None, None, "head"),
        P(),
        P(None, "head"),
        P("head"),
        P("head"),
        P("head"),
        P(None, "head"),
        P(),
        P("head", None),
    )
    return jax.shard_map(
        on_device, mesh=mesh, in_specs=placed, out_specs=P(("ctx", "head"), None), check_vma=False
    )
```

```python
import functools

import jax
import jax.numpy as jnp
import numpy as np
from jax import lax
from jax.experimental import pallas as pl
from jax.experimental.pallas import tpu as pltpu
from jax.sharding import PartitionSpec as P

STATE = 128
CHUNK = 128
TILE = 256
PROJECT_TILE = 512
EPS = 1e-05
RIM = 16
TAIL = 16
F32 = jnp.float32
BF16 = jnp.bfloat16
MIB = 2**20


def params(limit):
    return pltpu.CompilerParams(
        dimension_semantics=("arbitrary",), vmem_limit_bytes=limit * MIB
    )


def cost(flops, bytes_accessed):
    return pl.CostEstimate(flops=int(flops), bytes_accessed=int(bytes_accessed), transcendentals=0)


def whole(shape):
    return pl.BlockSpec(shape, lambda *_: (0,) * len(shape), pipeline_mode=pl.Buffered(1))


def silu(x):
    half = 0.5 * x
    return half + half * jnp.tanh(half)


def tri(rows, reverse):
    r = lax.broadcasted_iota(jnp.int32, (rows, rows), 0)
    c = lax.broadcasted_iota(jnp.int32, (rows, rows), 1)
    return (r <= c) if reverse else (r >= c)


def spread_matrix(first, heads, width):
    r = np.arange(2 * 128)[:, None] % 128
    c = np.arange(heads * width)[None, :] // width
    return jnp.asarray((r == c + first).astype(BF16))


def spread(q, matrix):
    high = q.astype(BF16)
    low = (q - high.astype(F32)).astype(BF16)
    return jnp.dot(jnp.concatenate([high, low], axis=1), matrix, preferred_element_type=F32)


def prepare(inner, zx_ref, bc_ref, dt_ref, gain_ref, wf_ref, wr_ref, gf_ref, gr_ref):
    depth = zx_ref.shape[0]
    rows = min(256, depth)
    r = lax.broadcasted_iota(jnp.int32, (rows, rows), 0)
    c = lax.broadcasted_iota(jnp.int32, (rows, rows), 1)
    turn = (r + c == rows - 1).astype(BF16)
    for b in range(0, depth, rows):
        here, there = slice(b, b + rows), slice(depth - rows - b, depth - b)
        gain = jnp.transpose(jnp.broadcast_to(gain_ref[:, here], (128, rows)))
        zx = zx_ref[here].astype(F32).reshape(rows, 2 * inner)
        steps = dt_ref[:, here].astype(F32)
        steps = jnp.transpose(jnp.concatenate([steps, jnp.zeros((128 - steps.shape[0], rows), F32)], axis=0))

        def put(part, at, forward_ref, turned_ref):
            size = part.shape[1]
            scaled = jnp.concatenate([part[:, g : g + 128] * gain for g in range(0, size, 128)], axis=1).astype(BF16)
            forward_ref[here, at : at + size] = scaled
            turned_ref[there, at : at + size] = jnp.dot(turn, scaled, preferred_element_type=F32).astype(BF16)

        put(zx[:, inner:], 0, wf_ref, wr_ref)
        put(bc_ref[here].astype(F32), inner, wf_ref, wr_ref)
        put(steps, inner + bc_ref.shape[1], wf_ref, wr_ref)
        put(zx[:, :inner], 0, gf_ref, gr_ref)


def row_scale(h):
    hf = h.astype(F32)
    return lax.rsqrt(jnp.mean(hf * hf, axis=-1, keepdims=True) + EPS)


def project_kernel(heads, inner, *refs):
    (hf_ref, hr_ref, rimf_ref, rimr_ref, zx_ref, bc_ref, wdt_ref, gain_ref, convx_ref, convbc_ref, lanes_ref, copy_ref,
     actf_ref, smallf_ref, cumtf_ref, enterf_ref, priorf_ref,
     actr_ref, smallr_ref, cumtr_ref, enterr_ref, priorr_ref,
     msg_ref, gf_ref, gr_ref, wf_ref, wr_ref, buff, bufr, statef, stater, totalf, totalr) = refs
    step = pl.program_id(0)
    last = pl.num_programs(0) - 1
    stream = inner + 2 * STATE
    blocks = stream // 128
    rows = hf_ref.shape[0]
    count = rows // CHUNK
    sides = (
        (False, hf_ref, rimf_ref, wf_ref, actf_ref, smallf_ref, cumtf_ref, enterf_ref, priorf_ref, buff, statef, totalf),
        (True, hr_ref, rimr_ref, wr_ref, actr_ref, smallr_ref, cumtr_ref, enterr_ref, priorr_ref, bufr, stater, totalr),
    )

    @pl.when(step == 0)
    def _():
        prepare(inner, zx_ref, bc_ref, wdt_ref, gain_ref, wf_ref, wr_ref, gf_ref, gr_ref)
        for reverse, _, rim_ref, w_ref, _, _, _, _, _, buf, state, total in sides:
            edge = rows if reverse else 0
            state[...] = jnp.zeros_like(state)
            total[...] = jnp.zeros_like(total)
            rim = rim_ref[...]
            out = jnp.dot(rim, w_ref[:, :stream], preferred_element_type=F32) * row_scale(rim)
            for j in range(blocks):
                part = out[:, j * 128 : (j + 1) * 128]
                buf[j, edge : edge + 8, :] = part[:8] if reverse else part[RIM - 8 :]

    lane = lax.broadcasted_iota(jnp.int32, (rows, 128), 1)
    row8 = lax.broadcasted_iota(jnp.int32, (8, 128), 0)
    r = lax.broadcasted_iota(jnp.int32, (rows, rows), 0)
    c = lax.broadcasted_iota(jnp.int32, (rows, rows), 1)
    same = r // CHUNK == c // CHUNK
    hs = [side[1][...] for side in sides]
    scales = [row_scale(h) for h in hs]
    tail_rows, aux_rows = [], []
    for k, (reverse, _, _, w_ref, _, small_ref, cumt_ref, _, _, _, _, total_ref) in enumerate(sides):
        raw = jnp.dot(hs[k], w_ref[:, stream:], preferred_element_type=F32) * scales[k] + lanes_ref[0:1, :]
        dt = jnp.maximum(raw, 0.0) + jnp.log1p(jnp.exp(-jnp.abs(raw)))
        dt = jnp.where(lane < heads, dt, 0.0)
        steps = -lanes_ref[1:2, :] * dt
        high = steps.astype(BF16).astype(F32)
        mid = (steps - high).astype(BF16).astype(F32)
        low = steps - high - mid
        packed = (high + pltpu.roll(mid, heads, 1) + pltpu.roll(low, 2 * heads, 1)).astype(BF16)
        mask = jnp.where(jnp.logical_and(same, (r <= c) if reverse else (r >= c)), 1.0, 0.0).astype(BF16)
        sums = jnp.dot(mask, packed, preferred_element_type=F32)
        sums = sums + pltpu.roll(sums, 128 - heads, 1) + pltpu.roll(sums, 128 - 2 * heads, 1)
        cum = jnp.where(lane < heads, sums, 0.0)
        small_ref[...] = dt + pltpu.roll(cum, heads, 1)
        running = total_ref[...]
        tails = [None] * count
        aux = [None] * count
        for i in range(count):
            n = count - 1 - i if reverse else i
            at = slice(n * CHUNK, (n + 1) * CHUNK)
            cumt_ref[:, at] = jnp.transpose(cum[at])[:heads]
            end = cum[n * CHUNK : n * CHUNK + 1] if reverse else cum[(n + 1) * CHUNK - 1 : (n + 1) * CHUNK]
            tails[n] = dt[at] * jnp.exp(end - cum[at])
            aux[n] = jnp.where(row8 == 0, jnp.exp(end), jnp.exp(running))
            running = running + end
        total_ref[...] = running
        tail_rows += tails
        aux_rows += aux
    weights = spread(jnp.concatenate(tail_rows + aux_rows, axis=0), copy_ref[...])

    for g in range(0, stream, 256):
        for k, (reverse, _, _, w_ref, act_ref, _, _, _, _, buf, _, _) in enumerate(sides):
            edge = rows if reverse else 0
            body = 0 if reverse else 8
            out = jnp.dot(hs[k], w_ref[:, g : g + 256], preferred_element_type=F32) * scales[k]
            for j in range(g // 128, g // 128 + 2):
                x = out[:, j * 128 - g : (j + 1) * 128 - g]
                buf[j, body : body + rows, :] = x
                own = j * 128 - (0 if j * 128 < inner else inner)
                taps = (convx_ref if j * 128 < inner else convbc_ref)[:, own : own + 128]
                total = taps[3:4] * x
                for d in (1, 2, 3):
                    at = body + d if reverse else body - d
                    total = total + taps[3 - d : 4 - d] * buf[j, at : at + rows, :]
                act_ref[:, j * 128 : (j + 1) * 128] = silu(total).astype(BF16)
                buf[j, edge : edge + 8, :] = x[:8] if reverse else x[rows - 8 :]

    for i in range(count):
        for k, (reverse, _, _, _, act_ref, _, _, enter_ref, prior_ref, _, state, _) in enumerate(sides):
            n = count - 1 - i if reverse else i
            at = slice(n * CHUNK, (n + 1) * CHUNK)
            own = weights[(k * count + n) * CHUNK : (k * count + n + 1) * CHUNK]
            aux = weights[2 * rows + (k * count + n) * 8 : 2 * rows + (k * count + n + 1) * 8]
            tails = (act_ref[at, :inner].astype(F32) * own).astype(BF16)
            ends = lax.dot_general(act_ref[at, inner : inner + STATE], tails, (((0,), (0,)), ((), ())),
                                   preferred_element_type=F32)
            before = state[...]
            enter_ref[n] = before.astype(BF16)
            prior_ref[n] = aux
            state[...] = before * aux[:1] + ends

    @pl.when(step == last)
    def _():
        for k, side in enumerate(sides):
            state, total = side[-2:]
            at = k * (STATE + TAIL)
            msg_ref[at : at + STATE, :] = state[...].astype(BF16)
            t = total[...]
            high = t.astype(BF16).astype(F32)
            mid = (t - high).astype(BF16).astype(F32)
            low = t - high - mid
            packed = jnp.where(row8 == 0, high, jnp.where(row8 == 1, mid, jnp.where(row8 == 2, low, 0.0)))
            rows3 = spread(packed, copy_ref[...])
            msg_ref[at + STATE : at + STATE + TAIL, :] = jnp.concatenate(
                [rows3, jnp.zeros_like(rows3)], axis=0).astype(BF16)


def project(hidden, rim_f, rim_r, weights, conv_x, conv_bc, lanes, copy, heads, inner):
    rows, depth = hidden.shape
    stream = inner + 2 * STATE
    n = rows // PROJECT_TILE
    per = PROJECT_TILE // CHUNK
    up, down = (lambda i: i), (lambda i: n - 1 - i)
    by_rows = lambda width, at: pl.BlockSpec((PROJECT_TILE, width), lambda i: (at(i), 0))
    out_specs, out_shape = [], []
    for at in (up, down):
        out_specs += [by_rows(stream, at), by_rows(128, at),
                      pl.BlockSpec((heads, PROJECT_TILE), lambda i, at=at: (0, at(i))),
                      pl.BlockSpec((per, STATE, inner), lambda i, at=at: (at(i), 0, 0)),
                      pl.BlockSpec((per, 8, inner), lambda i, at=at: (at(i), 0, 0))]
        out_shape += [jax.ShapeDtypeStruct((rows, stream), BF16),
                      jax.ShapeDtypeStruct((rows, 128), F32), jax.ShapeDtypeStruct((heads, rows), F32),
                      jax.ShapeDtypeStruct((n * per, STATE, inner), BF16),
                      jax.ShapeDtypeStruct((n * per, 8, inner), F32)]
    message = (2 * (STATE + TAIL), inner)
    buf = pltpu.VMEM((stream // 128, PROJECT_TILE + 8, 128), F32)
    state, total = pltpu.VMEM((STATE, inner), F32), pltpu.VMEM((8, 128), F32)
    return pl.pallas_call(
        functools.partial(project_kernel, heads, inner),
        grid=(n,),
        in_specs=[by_rows(depth, up), by_rows(depth, down), whole(rim_f.shape), whole(rim_r.shape),
                  *[whole(x.shape) for x in weights], whole(conv_x.shape), whole(conv_bc.shape), whole(lanes.shape),
                  whole(copy.shape)],
        out_specs=out_specs + [whole(message), whole((depth, inner)), whole((depth, inner))],
        out_shape=out_shape + [jax.ShapeDtypeStruct(message, BF16)] + [jax.ShapeDtypeStruct((depth, inner), BF16)] * 2,
        scratch_shapes=[pltpu.VMEM((depth, stream + 128), BF16)] * 2 + [buf, buf, state, state, total, total],
        compiler_params=params(58),
        cost_estimate=cost(22e9, 40e6),
        name="project",
    )(hidden, hidden, rim_f, rim_r, *weights, conv_x, conv_bc, lanes, copy)


def gates_kernel(h_ref, wf_ref, wr_ref, zf_ref, zr_ref):
    h = h_ref[...]
    scale = row_scale(h)
    for w_ref, z_ref in ((wf_ref, zf_ref), (wr_ref, zr_ref)):
        z_ref[...] = (jnp.dot(h, w_ref[...], preferred_element_type=F32) * scale).astype(BF16)


def by_destination(kernel, name, place, rows_in, fixed, by_order, out_shape, out_specs, work, scratch=()):
    k, pieces, tile, rows, head, n_head = place
    share = rows // n_head
    per_piece, per_share = share // pieces // tile, share // tile

    def at(i, head_ref):
        return lax.rem(head_ref[0] + i // per_piece, n_head) * per_share + k * per_piece + lax.rem(i, per_piece)

    def spec(shape, dim, last):
        def index(i, head_ref):
            where = [0] * len(shape)
            where[-1] = last
            where[dim] = at(i, head_ref)
            return tuple(where)

        return pl.BlockSpec(shape, index)

    in_specs = [spec(*one[1:]) for one in rows_in] + [whole(x.shape) for x in fixed]
    in_specs += [pl.BlockSpec((tile, x.shape[1]), lambda i, _: (i, 0)) for x in by_order]
    return pl.pallas_call(
        lambda _, *refs: kernel(*refs),
        grid_spec=pltpu.PrefetchScalarGridSpec(
            num_scalar_prefetch=1,
            grid=(n_head * per_piece,),
            in_specs=in_specs,
            out_specs=out_specs,
            scratch_shapes=scratch,
        ),
        out_shape=out_shape,
        compiler_params=params(58),
        cost_estimate=cost(work, 1e6),
        name=name,
    )(head, *[one[0] for one in rows_in], *fixed, *by_order)


def ordered(place, inner):
    _, pieces, tile, rows, _, _ = place
    return jax.ShapeDtypeStruct((rows // pieces, inner), BF16), pl.BlockSpec((tile, inner), lambda i, _: (i, 0))


def sent(place, inner):
    _, pieces, _, rows, _, n_head = place
    size = rows // n_head // pieces
    return [jax.ShapeDtypeStruct((size, inner), BF16)] * n_head, [whole((size, inner))] * n_head


def gates(place, hidden, w_f, w_r, work):
    shape, spec = ordered(place, w_f.shape[1])
    return by_destination(gates_kernel, "gates", place, [(hidden, (place[2], hidden.shape[1]), 0, 0)], [w_f, w_r], [],
                          [shape] * 2, [spec] * 2, work)


def inside_kernel(heads, inner, actf_ref, smallf_ref, cumtf_ref, actr_ref, smallr_ref, cumtr_ref, lanes_ref, copy_ref,
                  basef_ref, baser_ref):
    width = inner // heads
    per = 128 // width
    size = actf_ref.shape[0]
    lane = lax.broadcasted_iota(jnp.int32, (size, 128), 1)
    group = lax.broadcasted_iota(jnp.int32, (CHUNK, 128), 1) // width
    dts = [jnp.where(lane < heads, ref[...], 0.0) for ref in (smallf_ref, smallr_ref)]
    wide = spread(jnp.concatenate(dts + [jnp.broadcast_to(lanes_ref[2:3, :], (8, 128))], axis=0), copy_ref[...])
    skip = wide[2 * size : 2 * size + 1]
    sides = ((False, actf_ref, smallf_ref, cumtf_ref, basef_ref), (True, actr_ref, smallr_ref, cumtr_ref, baser_ref))
    for c in range(0, size, CHUNK):
        rows = slice(c, c + CHUNK)
        for k, (reverse, act_ref, small_ref, cumt_ref, base_ref) in enumerate(sides):
            small = small_ref[rows, :]
            values = act_ref[rows, :inner].astype(F32)
            weighted = (values * wide[k * size + c : k * size + c + CHUNK]).astype(BF16)
            scores = lax.dot_general(act_ref[rows, inner + STATE :], act_ref[rows, inner : inner + STATE],
                                     (((1,), (1,)), ((), ())), preferred_element_type=F32)
            scores = jnp.where(tri(CHUNK, reverse), scores, 0.0)
            for p in range(inner // 128):
                cols = slice(p * 128, (p + 1) * 128)
                pair = weighted[:, cols]
                mixing, stacked = [], []
                for q in range(per):
                    h = p * per + q
                    gap = jnp.minimum(small[:, heads + h : heads + h + 1] - cumt_ref[h : h + 1, rows], 0.0)
                    mixing.append((scores * jnp.exp(gap)).astype(BF16))
                    stacked.append(jnp.where(group == q, pair, jnp.zeros_like(pair)))
                out = jnp.dot(jnp.concatenate(mixing, axis=1), jnp.concatenate(stacked, axis=0),
                              preferred_element_type=F32)
                base_ref[rows, cols] = (out + skip[:, cols] * values[:, cols]).astype(BF16)


def inside_rows(strands, tile, heads):
    rows_in = []
    for act, small, cumt in strands:
        rows_in += [(act, (tile, act.shape[1]), 0, 0), (small, (tile, 128), 0, 0), (cumt, (heads, tile), 1, 0)]
    return rows_in


def inside(place, strands, lanes, copy, heads, inner, work):
    shape, spec = ordered(place, inner)
    return by_destination(functools.partial(inside_kernel, heads, inner), "inside", place,
                          inside_rows(strands, place[2], heads), [lanes, copy], [], [shape] * 2, [spec] * 2, work)


def finish_kernel(heads, inner, *refs):
    (cf_ref, ef_ref, pf_ref, sf_ref, cr_ref, er_ref, pr_ref, sr_ref, in_ref, copy_ref,
     zf_ref, zr_ref, bf_ref, br_ref, *out_refs) = refs
    width = inner // heads
    size = cf_ref.shape[0]
    row = lax.broadcasted_iota(jnp.int32, (256, 256), 0) // width
    column = lax.broadcasted_iota(jnp.int32, (256, 256), 1) // width
    mean = jnp.where(row == column, 1.0 / width, 0.0).astype(BF16)
    grown = spread(jnp.exp(jnp.minimum(jnp.concatenate([sf_ref[...], sr_ref[...]], axis=0), 0.0)), copy_ref[...])
    both = None
    for k, (c_ref, b_ref, z_ref, e_ref, p_ref) in enumerate(
            ((cf_ref, bf_ref, zf_ref, ef_ref, pf_ref), (cr_ref, br_ref, zr_ref, er_ref, pr_ref))):
        parts = []
        for c in range(e_ref.shape[0]):
            entering = (e_ref[c].astype(F32) + p_ref[c, 1:2, :] * in_ref[k]).astype(BF16)
            parts.append(jnp.dot(c_ref[c * CHUNK : (c + 1) * CHUNK, :], entering, preferred_element_type=F32))
        reads = jnp.concatenate(parts, axis=0)
        out = b_ref[...].astype(F32) + reads * grown[k * size : (k + 1) * size]
        gated = out * silu(z_ref[...].astype(F32))
        squares = (gated * gated).astype(BF16)
        means = jnp.concatenate(
            [jnp.dot(squares[:, g : g + 256], mean, preferred_element_type=F32) for g in range(0, inner, 256)], axis=1)
        result = gated * lax.rsqrt(means + EPS)
        both = result if both is None else both + result
    both = both.astype(BF16)
    step = pl.program_id(0)
    per_piece = out_refs[0].shape[0] // size
    for d, ref in enumerate(out_refs):
        @pl.when(step // per_piece == d)
        def _():
            ref[pl.ds(pl.multiple_of(lax.rem(step, per_piece) * size, size), size), :] = both


def finish_rows(strand, tile, inner):
    enter, prior = strand
    per = tile // CHUNK
    return [(enter, (per, STATE, inner), 0, 0), (prior, (per, 8, inner), 0, 0)]


def finish(place, strands, ends, bases, gated, entering, copy, heads, inner):
    tile = place[2]
    shapes, specs = sent(place, inner)
    rows_in = []
    for (act, small, _), end in zip(strands, ends):
        rows_in += [(act, (tile, STATE), 0, act.shape[1] // STATE - 1)] + finish_rows(end, tile, inner)
        rows_in += [(small, (tile, 128), 0, 0)]
    return by_destination(functools.partial(finish_kernel, heads, inner), "finish", place, rows_in, [entering, copy],
                          [*gated, *bases], shapes, specs, 1e8)


def settle_kernel(heads, inner, *refs):
    (actf_ref, smallf_ref, cumtf_ref, actr_ref, smallr_ref, cumtr_ref, ef_ref, pf_ref, er_ref, pr_ref,
     lanes_ref, first_ref, in_ref, second_ref, zf_ref, zr_ref, *out_refs, basef, baser) = refs
    inside_kernel(heads, inner, actf_ref, smallf_ref, cumtf_ref, actr_ref, smallr_ref, cumtr_ref, lanes_ref, first_ref,
                  basef, baser)
    maps = [ref.at[:, pl.ds(inner + STATE, STATE)] for ref in (actf_ref, actr_ref)]
    finish_kernel(heads, inner, maps[0], ef_ref, pf_ref, smallf_ref, maps[1], er_ref, pr_ref, smallr_ref,
                  in_ref, second_ref, zf_ref, zr_ref, basef, baser, *out_refs)


def settle(place, strands, ends, gated, lanes, first, entering, second, heads, inner):
    tile = place[2]
    shapes, specs = sent(place, inner)
    rows_in = inside_rows(strands, tile, heads) + finish_rows(ends[0], tile, inner) + finish_rows(ends[1], tile, inner)
    return by_destination(functools.partial(settle_kernel, heads, inner), "settle", place, rows_in,
                          [lanes, first, entering, second], list(gated), shapes, specs, 1e8,
                          [pltpu.VMEM((tile, inner), BF16)] * 2)


def read_message(ref, at):
    tail = ref[at + STATE : at + STATE + TAIL, :].astype(F32)
    return ref[at : at + STATE, :].astype(F32), tail[0:1] + tail[1:2] + tail[2:3]


def hop_kernel(first, *refs):
    upper_ref, mine_ref, other_ref = refs[:3]
    into_ref = None if first else refs[3]
    new_ref, msg_ref = refs[-2:]
    upper = upper_ref[0].astype(F32)
    for k in (0, 1):
        later = upper if k == 0 else 1.0 - upper
        at = k * (STATE + TAIL)
        o_state, o_log = read_message(other_ref, at)
        if first:
            new_state, new_log = later * o_state, later * o_log
        else:
            into_log = into_ref[k, STATE : STATE + 1, :]
            new_state = into_ref[k, :STATE, :] + later * jnp.exp(into_log) * o_state
            new_log = into_log + later * o_log
        new_ref[k, :STATE, :] = new_state
        new_ref[k, STATE:, :] = jnp.broadcast_to(new_log, (8, new_log.shape[1]))
        state, log = read_message(mine_ref, at)
        of_other = later * jnp.exp(log) + (1.0 - later)
        of_mine = later + (1.0 - later) * jnp.exp(o_log)
        msg_ref[at : at + STATE, :] = (of_other * o_state + of_mine * state).astype(BF16)
        t = log + o_log
        high = t.astype(BF16).astype(F32)
        mid = (t - high).astype(BF16).astype(F32)
        low = t - high - mid
        row = lax.broadcasted_iota(jnp.int32, (TAIL, t.shape[1]), 0)
        packed = jnp.where(row == 0, high, jnp.where(row == 1, mid, jnp.where(row == 2, low, 0.0)))
        msg_ref[at + STATE : at + STATE + TAIL, :] = packed.astype(BF16)


def local_call(kernel, name, smem, operands, out_shape):
    return pl.pallas_call(
        kernel,
        grid=(1,),
        in_specs=[pl.BlockSpec(memory_space=pltpu.SMEM)] + [whole(x.shape) for x in operands],
        out_specs=[whole(x.shape) for x in out_shape],
        out_shape=out_shape,
        compiler_params=params(10),
        cost_estimate=cost(1e6, 1.5e6),
        name=name,
    )(smem, *operands)


def join_kernel(count, *refs):
    place_ref, into_ref = refs[:2]
    slots, out_ref = refs[2:-1], refs[-1]
    place = place_ref[0]
    groups = [place ^ d for d in range(1, count)]
    read = [read_message(ref, 0) for ref in slots]
    ones = lambda condition: jnp.where(condition, 1.0, 0.0)
    sums = [None, None]
    for j, (state, _) in zip(groups, read):
        lower = ones(j < place)
        log = None
        for i, (_, other) in zip(groups, read):
            between = jnp.logical_or(jnp.logical_and(j < i, i < place), jnp.logical_and(place < i, i < j))
            term = ones(between) * other
            log = term if log is None else log + term
        part = jnp.exp(log) * state
        for k, share in enumerate((lower, 1.0 - lower)):
            sums[k] = share * part if sums[k] is None else sums[k] + share * part
    for k in (0, 1):
        out_ref[k] = into_ref[k, :STATE, :] + jnp.exp(into_ref[k, STATE : STATE + 1, :]) * sums[k]


def incoming(message, axis, beside, before):
    count, index = lax.axis_size(axis), lax.axis_index(axis)
    inner = message.shape[1]
    into = None
    distance = 1
    while count // distance > 4:
        other = lax.ppermute(message, axis, [(i, i ^ distance) for i in range(count)])
        if into is None:
            other, *beside = lax.optimization_barrier((other, *beside))
        upper = ((index // distance) % 2).astype(jnp.int32).reshape(1)
        operands = [message, other] + ([] if into is None else [into])
        out_shape = [jax.ShapeDtypeStruct((2, STATE + 8, inner), F32), jax.ShapeDtypeStruct(message.shape, BF16)]
        into, message = local_call(functools.partial(hop_kernel, into is None), "hop", upper, operands, out_shape)
        distance *= 2
    if into is None:
        into = jnp.zeros((2, STATE + 8, inner), F32)
    message, *before = lax.optimization_barrier((message, *before))
    groups = count // distance
    place = index // distance
    half = STATE + TAIL
    slots = []
    for d in range(1, groups):
        highest = 1 << (d.bit_length() - 1)
        above = (place // highest) % 2
        block = lax.dynamic_slice_in_dim(message, above * half, half, 0)
        slots.append(lax.ppermute(block, axis, [(i, i ^ (d * distance)) for i in range(count)]))
    joined = local_call(functools.partial(join_kernel, groups), "join", place.astype(jnp.int32).reshape(1), [into] + slots,
                        [pltpu.HBM((2, STATE, inner), F32)])[0]
    return joined, beside, before


def shifted(block, axis, distance):
    devices = range(lax.axis_size(axis))
    return lax.ppermute(block, axis, [(i - distance, i) for i in devices if i - distance in devices])


def rotated(block, d, count):
    return lax.ppermute(block, "head", [(i, (i + d) % count) for i in range(count)])


def on_device(
    hidden, norm_gain, w_zx, w_bc, w_dt, dt_bias, decay_rate, skip_gain, conv_x, conv_bc, w_out
):
    rows, depth = hidden.shape
    inner = conv_x.shape[1]
    heads = dt_bias.shape[0]
    width = inner // heads
    n_ctx, n_head = lax.axis_size("ctx"), lax.axis_size("head")
    ctx, head = lax.axis_index("ctx"), lax.axis_index("head")

    rim_f = shifted(hidden[rows - RIM :], "ctx", 1)
    rim_r = shifted(hidden[:RIM], "ctx", -1)

    half = w_out.shape[0] // 2
    parity = ctx % 2
    own_half = lax.dynamic_slice_in_dim(w_out, parity * half, half, 0)
    rim_f, rim_r, own_half = lax.optimization_barrier((rim_f, rim_r, own_half))
    middle = n_head // 2
    early = [d for d in range(1, n_head) if d != middle]
    same = [rotated(own_half, d, n_head) for d in early]

    lanes = jnp.pad(jnp.stack([dt_bias, decay_rate, skip_gain]), [(0, 0), (0, 128 - heads)])
    copy_first = spread_matrix(0, heads, width)
    copy_second = spread_matrix(heads, heads, width)
    (act_f, small_f, cumt_f, enter_f, prior_f, act_r, small_r, cumt_r, enter_r, prior_r,
     message, g_f, g_r) = project(hidden, rim_f, rim_r, (w_zx, w_bc, w_dt.T, norm_gain[None, :]), conv_x, conv_bc, lanes, copy_first, heads, inner)
    share = rows // n_head
    pieces = 2 if share % (2 * CHUNK) == 0 else 1
    size = share // pieces
    tile = min(TILE, size)
    place = lambda k: (k, pieces, tile, rows, head.astype(jnp.int32).reshape(1), n_head)
    strands = ((act_f, small_f, cumt_f), (act_r, small_r, cumt_r))
    ends = ((enter_f, prior_f), (enter_r, prior_r))
    message, own_half, *same = lax.optimization_barrier((message, own_half, *same))
    across = rotated(same[early.index(middle - 1)], 1, n_head) if middle > 1 else rotated(own_half, 1, n_head)
    entering, gated, same = incoming(message, "ctx", gates(place(0), hidden, g_f, g_r, 5e9), same)
    other = lax.ppermute(jnp.concatenate(same, axis=0), "ctx", [(i, i ^ 1) for i in range(n_ctx)])
    entering, other = lax.optimization_barrier((entering, other))
    bases = inside(place(0), strands, lanes, copy_first, heads, inner, 8e9)
    parts = finish(place(0), strands, ends, bases, gated, entering, copy_second, heads, inner)
    (g_f, g_r), parts, across = lax.optimization_barrier(((g_f, g_r), parts, across))
    across_other = lax.ppermute(across, "ctx", [(i, i ^ 1) for i in range(n_ctx)])
    middle_first = sorted(range(1, n_head), key=lambda d: abs(2 * d - n_head))
    arrived = [{0: parts[0], **{d: rotated(parts[d], d, n_head) for d in middle_first}}]
    for k in range(1, pieces):
        gated = gates(place(k), hidden, g_f, g_r, 1e8)
        parts = settle(place(k), strands, ends, gated, lanes, copy_first, entering, copy_second, heads, inner)
        parts, arrived[k - 1], across_other, other, same = lax.optimization_barrier(
            (parts, arrived[k - 1], across_other, other, same))
        arrived.append({0: parts[0], **{d: rotated(parts[d], d, n_head) for d in middle_first}})
    own_rows = lax.dynamic_slice_in_dim(hidden, head * share, share, 0)
    pairs = {d: (one, other[i * half : (i + 1) * half]) for i, (d, one) in enumerate(zip(early, same))}
    pairs[middle] = (across, across_other)
    groups = [w_out]
    for d in range(1, n_head):
        one, two = pairs[d]
        groups.append(jnp.concatenate([jnp.where(parity == 0, one, two), jnp.where(parity == 0, two, one)], axis=0))
    result = None
    order = sorted(range(n_head), key=lambda d: (-abs(2 * d - n_head), -d))
    order = order[:-2] + order[:-3:-1]
    for k in range(pieces):
        total = own_rows[k * size : (k + 1) * size].astype(F32)
        for d in order[:-1]:
            total = total + jnp.dot(arrived[k][d], groups[d], preferred_element_type=F32)
        if k == pieces - 1:
            total = lax.optimization_barrier(total)
        total = (total + jnp.dot(arrived[k][order[-1]], groups[order[-1]], preferred_element_type=F32)).astype(BF16)
        if result is None:
            result = lax.optimization_barrier(jnp.pad(total, ((0, share - size), (0, 0))))
        else:
            result = lax.dynamic_update_slice(result, total, (k * size, 0))
    return result


def solution(mesh):
    placed = (
        P("ctx", None),
        P(),
        P(None, None, "head"),
        P(),
        P(None, "head"),
        P("head"),
        P("head"),
        P("head"),
        P(None, "head"),
        P(),
        P("head", None),
    )
    return jax.shard_map(
        on_device, mesh=mesh, in_specs=placed, out_specs=P(("ctx", "head"), None), check_vma=False
    )
```

```python
import functools

import jax
import jax.numpy as jnp
import numpy as np
from jax import lax
from jax.experimental import pallas as pl
from jax.experimental.pallas import tpu as pltpu
from jax.sharding import PartitionSpec as P

STATE = 128
CHUNK = 128
TILE = 256
PROJECT_TILE = 1024
EPS = 1e-05
RIM = 16
TAIL = 16
F32 = jnp.float32
BF16 = jnp.bfloat16
MIB = 2**20


def params(limit):
    return pltpu.CompilerParams(
        dimension_semantics=("arbitrary",), vmem_limit_bytes=limit * MIB
    )


def cost(flops, bytes_accessed):
    return pl.CostEstimate(flops=int(flops), bytes_accessed=int(bytes_accessed), transcendentals=0)


def whole(shape):
    return pl.BlockSpec(shape, lambda *_: (0,) * len(shape), pipeline_mode=pl.Buffered(1))


def silu(x):
    half = 0.5 * x
    return half + half * jnp.tanh(half)


def tri(rows, reverse):
    r = lax.broadcasted_iota(jnp.int32, (rows, rows), 0)
    c = lax.broadcasted_iota(jnp.int32, (rows, rows), 1)
    return (r <= c) if reverse else (r >= c)


def spread_matrix(first, heads, width):
    r = np.arange(2 * 128)[:, None] % 128
    c = np.arange(heads * width)[None, :] // width
    return jnp.asarray((r == c + first).astype(BF16))


def spread(q, matrix):
    high = q.astype(BF16)
    low = (q - high.astype(F32)).astype(BF16)
    return jnp.dot(jnp.concatenate([high, low], axis=1), matrix, preferred_element_type=F32)


def prepare(inner, zx_ref, bc_ref, dt_ref, gain_ref, wf_ref, wr_ref, gf_ref, gr_ref):
    depth = zx_ref.shape[0]
    rows = min(256, depth)
    r = lax.broadcasted_iota(jnp.int32, (rows, rows), 0)
    c = lax.broadcasted_iota(jnp.int32, (rows, rows), 1)
    turn = (r + c == rows - 1).astype(BF16)
    for b in range(0, depth, rows):
        here, there = slice(b, b + rows), slice(depth - rows - b, depth - b)
        gain = jnp.transpose(jnp.broadcast_to(gain_ref[:, here], (128, rows)))
        zx = zx_ref[here].astype(F32).reshape(rows, 2 * inner)
        steps = dt_ref[:, here].astype(F32)
        steps = jnp.transpose(jnp.concatenate([steps, jnp.zeros((128 - steps.shape[0], rows), F32)], axis=0))

        def put(part, at, forward_ref, turned_ref):
            size = part.shape[1]
            scaled = jnp.concatenate([part[:, g : g + 128] * gain for g in range(0, size, 128)], axis=1).astype(BF16)
            forward_ref[here, at : at + size] = scaled
            turned_ref[there, at : at + size] = jnp.dot(turn, scaled, preferred_element_type=F32).astype(BF16)

        put(zx[:, inner:], 0, wf_ref, wr_ref)
        put(bc_ref[here].astype(F32), inner, wf_ref, wr_ref)
        put(steps, inner + bc_ref.shape[1], wf_ref, wr_ref)
        put(zx[:, :inner], 0, gf_ref, gr_ref)


def row_scale(h):
    hf = h.astype(F32)
    return lax.rsqrt(jnp.mean(hf * hf, axis=-1, keepdims=True) + EPS)


def project_kernel(heads, inner, *refs):
    (hf_ref, hr_ref, rimf_ref, rimr_ref, zx_ref, bc_ref, wdt_ref, gain_ref, convx_ref, convbc_ref, lanes_ref, copy_ref,
     actf_ref, smallf_ref, cumtf_ref, enterf_ref, priorf_ref,
     actr_ref, smallr_ref, cumtr_ref, enterr_ref, priorr_ref,
     msg_ref, gf_ref, gr_ref, wf_ref, wr_ref, buff, bufr, statef, stater, totalf, totalr) = refs
    step = pl.program_id(0)
    last = pl.num_programs(0) - 1
    stream = inner + 2 * STATE
    blocks = stream // 128
    rows = hf_ref.shape[0]
    count = rows // CHUNK
    sides = (
        (False, hf_ref, rimf_ref, wf_ref, actf_ref, smallf_ref, cumtf_ref, enterf_ref, priorf_ref, buff, statef, totalf),
        (True, hr_ref, rimr_ref, wr_ref, actr_ref, smallr_ref, cumtr_ref, enterr_ref, priorr_ref, bufr, stater, totalr),
    )

    @pl.when(step == 0)
    def _():
        prepare(inner, zx_ref, bc_ref, wdt_ref, gain_ref, wf_ref, wr_ref, gf_ref, gr_ref)
        for reverse, _, rim_ref, w_ref, _, _, _, _, _, buf, state, total in sides:
            edge = rows if reverse else 0
            state[...] = jnp.zeros_like(state)
            total[...] = jnp.zeros_like(total)
            rim = rim_ref[...]
            out = jnp.dot(rim, w_ref[:, :stream], preferred_element_type=F32) * row_scale(rim)
            for j in range(blocks):
                part = out[:, j * 128 : (j + 1) * 128]
                buf[j, edge : edge + 8, :] = part[:8] if reverse else part[RIM - 8 :]

    lane = lax.broadcasted_iota(jnp.int32, (rows, 128), 1)
    row8 = lax.broadcasted_iota(jnp.int32, (8, 128), 0)
    r = lax.broadcasted_iota(jnp.int32, (rows, rows), 0)
    c = lax.broadcasted_iota(jnp.int32, (rows, rows), 1)
    same = r // CHUNK == c // CHUNK
    hs = [side[1][...] for side in sides]
    scales = [row_scale(h) for h in hs]
    tail_rows, aux_rows = [], []
    for k, (reverse, _, _, w_ref, _, small_ref, cumt_ref, _, _, _, _, total_ref) in enumerate(sides):
        raw = jnp.dot(hs[k], w_ref[:, stream:], preferred_element_type=F32) * scales[k] + lanes_ref[0:1, :]
        dt = jnp.maximum(raw, 0.0) + jnp.log1p(jnp.exp(-jnp.abs(raw)))
        dt = jnp.where(lane < heads, dt, 0.0)
        steps = -lanes_ref[1:2, :] * dt
        high = steps.astype(BF16).astype(F32)
        mid = (steps - high).astype(BF16).astype(F32)
        low = steps - high - mid
        packed = (high + pltpu.roll(mid, heads, 1) + pltpu.roll(low, 2 * heads, 1)).astype(BF16)
        mask = jnp.where(jnp.logical_and(same, (r <= c) if reverse else (r >= c)), 1.0, 0.0).astype(BF16)
        sums = jnp.dot(mask, packed, preferred_element_type=F32)
        sums = sums + pltpu.roll(sums, 128 - heads, 1) + pltpu.roll(sums, 128 - 2 * heads, 1)
        cum = jnp.where(lane < heads, sums, 0.0)
        small_ref[...] = dt + pltpu.roll(cum, heads, 1)
        running = total_ref[...]
        tails = [None] * count
        aux = [None] * count
        for i in range(count):
            n = count - 1 - i if reverse else i
            at = slice(n * CHUNK, (n + 1) * CHUNK)
            cumt_ref[:, at] = jnp.transpose(cum[at])[:heads]
            end = cum[n * CHUNK : n * CHUNK + 1] if reverse else cum[(n + 1) * CHUNK - 1 : (n + 1) * CHUNK]
            tails[n] = dt[at] * jnp.exp(end - cum[at])
            aux[n] = jnp.where(row8 == 0, jnp.exp(end), jnp.exp(running))
            running = running + end
        total_ref[...] = running
        tail_rows += tails
        aux_rows += aux
    weights = spread(jnp.concatenate(tail_rows + aux_rows, axis=0), copy_ref[...])

    for g in range(0, stream, 256):
        for k, (reverse, _, _, w_ref, act_ref, _, _, _, _, buf, _, _) in enumerate(sides):
            edge = rows if reverse else 0
            body = 0 if reverse else 8
            out = jnp.dot(hs[k], w_ref[:, g : g + 256], preferred_element_type=F32) * scales[k]
            for j in range(g // 128, g // 128 + 2):
                x = out[:, j * 128 - g : (j + 1) * 128 - g]
                buf[j, body : body + rows, :] = x
                own = j * 128 - (0 if j * 128 < inner else inner)
                taps = (convx_ref if j * 128 < inner else convbc_ref)[:, own : own + 128]
                total = taps[3:4] * x
                for d in (1, 2, 3):
                    at = body + d if reverse else body - d
                    total = total + taps[3 - d : 4 - d] * buf[j, at : at + rows, :]
                act_ref[:, j * 128 : (j + 1) * 128] = silu(total).astype(BF16)
                buf[j, edge : edge + 8, :] = x[:8] if reverse else x[rows - 8 :]

    for i in range(count):
        for k, (reverse, _, _, _, act_ref, _, _, enter_ref, prior_ref, _, state, _) in enumerate(sides):
            n = count - 1 - i if reverse else i
            at = slice(n * CHUNK, (n + 1) * CHUNK)
            own = weights[(k * count + n) * CHUNK : (k * count + n + 1) * CHUNK]
            aux = weights[2 * rows + (k * count + n) * 8 : 2 * rows + (k * count + n + 1) * 8]
            tails = (act_ref[at, :inner].astype(F32) * own).astype(BF16)
            ends = lax.dot_general(act_ref[at, inner : inner + STATE], tails, (((0,), (0,)), ((), ())),
                                   preferred_element_type=F32)
            before = state[...]
            enter_ref[n] = before.astype(BF16)
            prior_ref[n] = aux
            state[...] = before * aux[:1] + ends

    @pl.when(step == last)
    def _():
        for k, side in enumerate(sides):
            state, total = side[-2:]
            at = k * (STATE + TAIL)
            msg_ref[at : at + STATE, :] = state[...].astype(BF16)
            t = total[...]
            high = t.astype(BF16).astype(F32)
            mid = (t - high).astype(BF16).astype(F32)
            low = t - high - mid
            packed = jnp.where(row8 == 0, high, jnp.where(row8 == 1, mid, jnp.where(row8 == 2, low, 0.0)))
            rows3 = spread(packed, copy_ref[...])
            msg_ref[at + STATE : at + STATE + TAIL, :] = jnp.concatenate(
                [rows3, jnp.zeros_like(rows3)], axis=0).astype(BF16)


def project(hidden, rim_f, rim_r, weights, conv_x, conv_bc, lanes, copy, heads, inner):
    rows, depth = hidden.shape
    stream = inner + 2 * STATE
    n = rows // PROJECT_TILE
    per = PROJECT_TILE // CHUNK
    up, down = (lambda i: i), (lambda i: n - 1 - i)
    by_rows = lambda width, at: pl.BlockSpec((PROJECT_TILE, width), lambda i: (at(i), 0))
    out_specs, out_shape = [], []
    for at in (up, down):
        out_specs += [by_rows(stream, at), by_rows(128, at),
                      pl.BlockSpec((heads, PROJECT_TILE), lambda i, at=at: (0, at(i))),
                      pl.BlockSpec((per, STATE, inner), lambda i, at=at: (at(i), 0, 0)),
                      pl.BlockSpec((per, 8, inner), lambda i, at=at: (at(i), 0, 0))]
        out_shape += [jax.ShapeDtypeStruct((rows, stream), BF16),
                      jax.ShapeDtypeStruct((rows, 128), F32), jax.ShapeDtypeStruct((heads, rows), F32),
                      jax.ShapeDtypeStruct((n * per, STATE, inner), BF16),
                      jax.ShapeDtypeStruct((n * per, 8, inner), F32)]
    message = (2 * (STATE + TAIL), inner)
    buf = pltpu.VMEM((stream // 128, PROJECT_TILE + 8, 128), F32)
    state, total = pltpu.VMEM((STATE, inner), F32), pltpu.VMEM((8, 128), F32)
    return pl.pallas_call(
        functools.partial(project_kernel, heads, inner),
        grid=(n,),
        in_specs=[by_rows(depth, up), by_rows(depth, down), whole(rim_f.shape), whole(rim_r.shape),
                  *[whole(x.shape) for x in weights], whole(conv_x.shape), whole(conv_bc.shape), whole(lanes.shape),
                  whole(copy.shape)],
        out_specs=out_specs + [whole(message), whole((depth, inner)), whole((depth, inner))],
        out_shape=out_shape + [jax.ShapeDtypeStruct(message, BF16)] + [jax.ShapeDtypeStruct((depth, inner), BF16)] * 2,
        scratch_shapes=[pltpu.VMEM((depth, stream + 128), BF16)] * 2 + [buf, buf, state, state, total, total],
        compiler_params=params(58),
        cost_estimate=cost(22e9, 40e6),
        name="project",
    )(hidden, hidden, rim_f, rim_r, *weights, conv_x, conv_bc, lanes, copy)


def gates_kernel(h_ref, wf_ref, wr_ref, zf_ref, zr_ref):
    h = h_ref[...]
    scale = row_scale(h)
    for w_ref, z_ref in ((wf_ref, zf_ref), (wr_ref, zr_ref)):
        z_ref[...] = (jnp.dot(h, w_ref[...], preferred_element_type=F32) * scale).astype(BF16)


def by_destination(kernel, name, place, rows_in, fixed, by_order, out_shape, out_specs, work, scratch=()):
    k, pieces, tile, rows, head, n_head = place
    share = rows // n_head
    per_piece, per_share = share // pieces // tile, share // tile

    def at(i, head_ref):
        return lax.rem(head_ref[0] + i // per_piece, n_head) * per_share + k * per_piece + lax.rem(i, per_piece)

    def spec(shape, dim, last):
        def index(i, head_ref):
            where = [0] * len(shape)
            where[-1] = last
            where[dim] = at(i, head_ref)
            return tuple(where)

        return pl.BlockSpec(shape, index)

    in_specs = [spec(*one[1:]) for one in rows_in] + [whole(x.shape) for x in fixed]
    in_specs += [pl.BlockSpec((tile, x.shape[1]), lambda i, _: (i, 0)) for x in by_order]
    return pl.pallas_call(
        lambda _, *refs: kernel(*refs),
        grid_spec=pltpu.PrefetchScalarGridSpec(
            num_scalar_prefetch=1,
            grid=(n_head * per_piece,),
            in_specs=in_specs,
            out_specs=out_specs,
            scratch_shapes=scratch,
        ),
        out_shape=out_shape,
        compiler_params=params(58),
        cost_estimate=cost(work, 1e6),
        name=name,
    )(head, *[one[0] for one in rows_in], *fixed, *by_order)


def ordered(place, inner):
    _, pieces, tile, rows, _, _ = place
    return jax.ShapeDtypeStruct((rows // pieces, inner), BF16), pl.BlockSpec((tile, inner), lambda i, _: (i, 0))


def sent(place, inner):
    _, pieces, _, rows, _, n_head = place
    size = rows // n_head // pieces
    return [jax.ShapeDtypeStruct((size, inner), BF16)] * n_head, [whole((size, inner))] * n_head


def gates(place, hidden, w_f, w_r, work):
    shape, spec = ordered(place, w_f.shape[1])
    return by_destination(gates_kernel, "gates", place, [(hidden, (place[2], hidden.shape[1]), 0, 0)], [w_f, w_r], [],
                          [shape] * 2, [spec] * 2, work)


def inside_kernel(heads, inner, actf_ref, smallf_ref, cumtf_ref, actr_ref, smallr_ref, cumtr_ref, lanes_ref, copy_ref,
                  basef_ref, baser_ref):
    width = inner // heads
    per = 128 // width
    size = actf_ref.shape[0]
    lane = lax.broadcasted_iota(jnp.int32, (size, 128), 1)
    group = lax.broadcasted_iota(jnp.int32, (CHUNK, 128), 1) // width
    dts = [jnp.where(lane < heads, ref[...], 0.0) for ref in (smallf_ref, smallr_ref)]
    wide = spread(jnp.concatenate(dts + [jnp.broadcast_to(lanes_ref[2:3, :], (8, 128))], axis=0), copy_ref[...])
    skip = wide[2 * size : 2 * size + 1]
    sides = ((False, actf_ref, smallf_ref, cumtf_ref, basef_ref), (True, actr_ref, smallr_ref, cumtr_ref, baser_ref))
    for c in range(0, size, CHUNK):
        rows = slice(c, c + CHUNK)
        for k, (reverse, act_ref, small_ref, cumt_ref, base_ref) in enumerate(sides):
            small = small_ref[rows, :]
            values = act_ref[rows, :inner].astype(F32)
            weighted = (values * wide[k * size + c : k * size + c + CHUNK]).astype(BF16)
            scores = lax.dot_general(act_ref[rows, inner + STATE :], act_ref[rows, inner : inner + STATE],
                                     (((1,), (1,)), ((), ())), preferred_element_type=F32)
            scores = jnp.where(tri(CHUNK, reverse), scores, 0.0)
            for p in range(inner // 128):
                cols = slice(p * 128, (p + 1) * 128)
                pair = weighted[:, cols]
                mixing, stacked = [], []
                for q in range(per):
                    h = p * per + q
                    gap = jnp.minimum(small[:, heads + h : heads + h + 1] - cumt_ref[h : h + 1, rows], 0.0)
                    mixing.append((scores * jnp.exp(gap)).astype(BF16))
                    stacked.append(jnp.where(group == q, pair, jnp.zeros_like(pair)))
                out = jnp.dot(jnp.concatenate(mixing, axis=1), jnp.concatenate(stacked, axis=0),
                              preferred_element_type=F32)
                base_ref[rows, cols] = (out + skip[:, cols] * values[:, cols]).astype(BF16)


def inside_rows(strands, tile, heads):
    rows_in = []
    for act, small, cumt in strands:
        rows_in += [(act, (tile, act.shape[1]), 0, 0), (small, (tile, 128), 0, 0), (cumt, (heads, tile), 1, 0)]
    return rows_in


def inside(place, strands, lanes, copy, heads, inner, work):
    shape, spec = ordered(place, inner)
    return by_destination(functools.partial(inside_kernel, heads, inner), "inside", place,
                          inside_rows(strands, place[2], heads), [lanes, copy], [], [shape] * 2, [spec] * 2, work)


def finish_kernel(heads, inner, *refs):
    (cf_ref, ef_ref, pf_ref, sf_ref, cr_ref, er_ref, pr_ref, sr_ref, in_ref, copy_ref,
     zf_ref, zr_ref, bf_ref, br_ref, *out_refs) = refs
    width = inner // heads
    size = cf_ref.shape[0]
    row = lax.broadcasted_iota(jnp.int32, (256, 256), 0) // width
    column = lax.broadcasted_iota(jnp.int32, (256, 256), 1) // width
    mean = jnp.where(row == column, 1.0 / width, 0.0).astype(BF16)
    grown = spread(jnp.exp(jnp.minimum(jnp.concatenate([sf_ref[...], sr_ref[...]], axis=0), 0.0)), copy_ref[...])
    both = None
    for k, (c_ref, b_ref, z_ref, e_ref, p_ref) in enumerate(
            ((cf_ref, bf_ref, zf_ref, ef_ref, pf_ref), (cr_ref, br_ref, zr_ref, er_ref, pr_ref))):
        parts = []
        for c in range(e_ref.shape[0]):
            entering = (e_ref[c].astype(F32) + p_ref[c, 1:2, :] * in_ref[k]).astype(BF16)
            parts.append(jnp.dot(c_ref[c * CHUNK : (c + 1) * CHUNK, :], entering, preferred_element_type=F32))
        reads = jnp.concatenate(parts, axis=0)
        out = b_ref[...].astype(F32) + reads * grown[k * size : (k + 1) * size]
        gated = out * silu(z_ref[...].astype(F32))
        squares = (gated * gated).astype(BF16)
        means = jnp.concatenate(
            [jnp.dot(squares[:, g : g + 256], mean, preferred_element_type=F32) for g in range(0, inner, 256)], axis=1)
        result = gated * lax.rsqrt(means + EPS)
        both = result if both is None else both + result
    both = both.astype(BF16)
    step = pl.program_id(0)
    per_piece = out_refs[0].shape[0] // size
    for d, ref in enumerate(out_refs):
        @pl.when(step // per_piece == d)
        def _():
            ref[pl.ds(pl.multiple_of(lax.rem(step, per_piece) * size, size), size), :] = both


def finish_rows(strand, tile, inner):
    enter, prior = strand
    per = tile // CHUNK
    return [(enter, (per, STATE, inner), 0, 0), (prior, (per, 8, inner), 0, 0)]


def finish(place, strands, ends, bases, gated, entering, copy, heads, inner):
    tile = place[2]
    shapes, specs = sent(place, inner)
    rows_in = []
    for (act, small, _), end in zip(strands, ends):
        rows_in += [(act, (tile, STATE), 0, act.shape[1] // STATE - 1)] + finish_rows(end, tile, inner)
        rows_in += [(small, (tile, 128), 0, 0)]
    return by_destination(functools.partial(finish_kernel, heads, inner), "finish", place, rows_in, [entering, copy],
                          [*gated, *bases], shapes, specs, 1e8)


def settle_kernel(heads, inner, *refs):
    (actf_ref, smallf_ref, cumtf_ref, actr_ref, smallr_ref, cumtr_ref, ef_ref, pf_ref, er_ref, pr_ref,
     lanes_ref, first_ref, in_ref, second_ref, zf_ref, zr_ref, *out_refs, basef, baser) = refs
    inside_kernel(heads, inner, actf_ref, smallf_ref, cumtf_ref, actr_ref, smallr_ref, cumtr_ref, lanes_ref, first_ref,
                  basef, baser)
    maps = [ref.at[:, pl.ds(inner + STATE, STATE)] for ref in (actf_ref, actr_ref)]
    finish_kernel(heads, inner, maps[0], ef_ref, pf_ref, smallf_ref, maps[1], er_ref, pr_ref, smallr_ref,
                  in_ref, second_ref, zf_ref, zr_ref, basef, baser, *out_refs)


def settle(place, strands, ends, gated, lanes, first, entering, second, heads, inner):
    tile = place[2]
    shapes, specs = sent(place, inner)
    rows_in = inside_rows(strands, tile, heads) + finish_rows(ends[0], tile, inner) + finish_rows(ends[1], tile, inner)
    return by_destination(functools.partial(settle_kernel, heads, inner), "settle", place, rows_in,
                          [lanes, first, entering, second], list(gated), shapes, specs, 1e8,
                          [pltpu.VMEM((tile, inner), BF16)] * 2)


def read_message(ref, at):
    tail = ref[at + STATE : at + STATE + TAIL, :].astype(F32)
    return ref[at : at + STATE, :].astype(F32), tail[0:1] + tail[1:2] + tail[2:3]


def hop_kernel(first, *refs):
    upper_ref, mine_ref, other_ref = refs[:3]
    into_ref = None if first else refs[3]
    new_ref, msg_ref = refs[-2:]
    upper = upper_ref[0].astype(F32)
    for k in (0, 1):
        later = upper if k == 0 else 1.0 - upper
        at = k * (STATE + TAIL)
        o_state, o_log = read_message(other_ref, at)
        if first:
            new_state, new_log = later * o_state, later * o_log
        else:
            into_log = into_ref[k, STATE : STATE + 1, :]
            new_state = into_ref[k, :STATE, :] + later * jnp.exp(into_log) * o_state
            new_log = into_log + later * o_log
        new_ref[k, :STATE, :] = new_state
        new_ref[k, STATE:, :] = jnp.broadcast_to(new_log, (8, new_log.shape[1]))
        state, log = read_message(mine_ref, at)
        of_other = later * jnp.exp(log) + (1.0 - later)
        of_mine = later + (1.0 - later) * jnp.exp(o_log)
        msg_ref[at : at + STATE, :] = (of_other * o_state + of_mine * state).astype(BF16)
        t = log + o_log
        high = t.astype(BF16).astype(F32)
        mid = (t - high).astype(BF16).astype(F32)
        low = t - high - mid
        row = lax.broadcasted_iota(jnp.int32, (TAIL, t.shape[1]), 0)
        packed = jnp.where(row == 0, high, jnp.where(row == 1, mid, jnp.where(row == 2, low, 0.0)))
        msg_ref[at + STATE : at + STATE + TAIL, :] = packed.astype(BF16)


def local_call(kernel, name, smem, operands, out_shape):
    return pl.pallas_call(
        kernel,
        grid=(1,),
        in_specs=[pl.BlockSpec(memory_space=pltpu.SMEM)] + [whole(x.shape) for x in operands],
        out_specs=[whole(x.shape) for x in out_shape],
        out_shape=out_shape,
        compiler_params=params(10),
        cost_estimate=cost(1e6, 1.5e6),
        name=name,
    )(smem, *operands)


def join_kernel(count, *refs):
    place_ref, into_ref = refs[:2]
    slots, out_ref = refs[2:-1], refs[-1]
    place = place_ref[0]
    groups = [place ^ d for d in range(1, count)]
    read = [read_message(ref, 0) for ref in slots]
    ones = lambda condition: jnp.where(condition, 1.0, 0.0)
    sums = [None, None]
    for j, (state, _) in zip(groups, read):
        lower = ones(j < place)
        log = None
        for i, (_, other) in zip(groups, read):
            between = jnp.logical_or(jnp.logical_and(j < i, i < place), jnp.logical_and(place < i, i < j))
            term = ones(between) * other
            log = term if log is None else log + term
        part = jnp.exp(log) * state
        for k, share in enumerate((lower, 1.0 - lower)):
            sums[k] = share * part if sums[k] is None else sums[k] + share * part
    for k in (0, 1):
        out_ref[k] = into_ref[k, :STATE, :] + jnp.exp(into_ref[k, STATE : STATE + 1, :]) * sums[k]


def incoming(message, axis, beside, before):
    count, index = lax.axis_size(axis), lax.axis_index(axis)
    inner = message.shape[1]
    into = None
    distance = 1
    while count // distance > 4:
        other = lax.ppermute(message, axis, [(i, i ^ distance) for i in range(count)])
        if into is None:
            other, *beside = lax.optimization_barrier((other, *beside))
        upper = ((index // distance) % 2).astype(jnp.int32).reshape(1)
        operands = [message, other] + ([] if into is None else [into])
        out_shape = [jax.ShapeDtypeStruct((2, STATE + 8, inner), F32), jax.ShapeDtypeStruct(message.shape, BF16)]
        into, message = local_call(functools.partial(hop_kernel, into is None), "hop", upper, operands, out_shape)
        distance *= 2
    if into is None:
        into = jnp.zeros((2, STATE + 8, inner), F32)
    message, *before = lax.optimization_barrier((message, *before))
    groups = count // distance
    place = index // distance
    half = STATE + TAIL
    slots = []
    for d in range(1, groups):
        highest = 1 << (d.bit_length() - 1)
        above = (place // highest) % 2
        block = lax.dynamic_slice_in_dim(message, above * half, half, 0)
        slots.append(lax.ppermute(block, axis, [(i, i ^ (d * distance)) for i in range(count)]))
    joined = local_call(functools.partial(join_kernel, groups), "join", place.astype(jnp.int32).reshape(1), [into] + slots,
                        [pltpu.HBM((2, STATE, inner), F32)])[0]
    return joined, beside, before


def shifted(block, axis, distance):
    devices = range(lax.axis_size(axis))
    return lax.ppermute(block, axis, [(i - distance, i) for i in devices if i - distance in devices])


def rotated(block, d, count):
    return lax.ppermute(block, "head", [(i, (i + d) % count) for i in range(count)])


def on_device(
    hidden, norm_gain, w_zx, w_bc, w_dt, dt_bias, decay_rate, skip_gain, conv_x, conv_bc, w_out
):
    rows, depth = hidden.shape
    inner = conv_x.shape[1]
    heads = dt_bias.shape[0]
    width = inner // heads
    n_ctx, n_head = lax.axis_size("ctx"), lax.axis_size("head")
    ctx, head = lax.axis_index("ctx"), lax.axis_index("head")

    rim_f = shifted(hidden[rows - RIM :], "ctx", 1)
    rim_r = shifted(hidden[:RIM], "ctx", -1)

    half = w_out.shape[0] // 2
    parity = ctx % 2
    own_half = lax.dynamic_slice_in_dim(w_out, parity * half, half, 0)
    rim_f, rim_r, own_half = lax.optimization_barrier((rim_f, rim_r, own_half))
    middle = n_head // 2
    early = [d for d in range(1, n_head) if d != middle]
    same = [rotated(own_half, d, n_head) for d in early]

    lanes = jnp.pad(jnp.stack([dt_bias, decay_rate, skip_gain]), [(0, 0), (0, 128 - heads)])
    copy_first = spread_matrix(0, heads, width)
    copy_second = spread_matrix(heads, heads, width)
    (act_f, small_f, cumt_f, enter_f, prior_f, act_r, small_r, cumt_r, enter_r, prior_r,
     message, g_f, g_r) = project(hidden, rim_f, rim_r, (w_zx, w_bc, w_dt.T, norm_gain[None, :]), conv_x, conv_bc, lanes, copy_first, heads, inner)
    share = rows // n_head
    pieces = 2 if share % (2 * CHUNK) == 0 else 1
    size = share // pieces
    tile = min(TILE, size)
    place = lambda k: (k, pieces, tile, rows, head.astype(jnp.int32).reshape(1), n_head)
    strands = ((act_f, small_f, cumt_f), (act_r, small_r, cumt_r))
    ends = ((enter_f, prior_f), (enter_r, prior_r))
    message, own_half, *same = lax.optimization_barrier((message, own_half, *same))
    across = rotated(same[early.index(middle - 1)], 1, n_head) if middle > 1 else rotated(own_half, 1, n_head)
    entering, gated, same = incoming(message, "ctx", gates(place(0), hidden, g_f, g_r, 5e9), same)
    other = lax.ppermute(jnp.concatenate(same, axis=0), "ctx", [(i, i ^ 1) for i in range(n_ctx)])
    entering, other = lax.optimization_barrier((entering, other))
    bases = inside(place(0), strands, lanes, copy_first, heads, inner, 8e9)
    parts = finish(place(0), strands, ends, bases, gated, entering, copy_second, heads, inner)
    (g_f, g_r), parts, across = lax.optimization_barrier(((g_f, g_r), parts, across))
    across_other = lax.ppermute(across, "ctx", [(i, i ^ 1) for i in range(n_ctx)])
    middle_first = sorted(range(1, n_head), key=lambda d: abs(2 * d - n_head))
    arrived = [{0: parts[0], **{d: rotated(parts[d], d, n_head) for d in middle_first}}]
    for k in range(1, pieces):
        gated = gates(place(k), hidden, g_f, g_r, 1e8)
        parts = settle(place(k), strands, ends, gated, lanes, copy_first, entering, copy_second, heads, inner)
        parts, arrived[k - 1], across_other, other, same = lax.optimization_barrier(
            (parts, arrived[k - 1], across_other, other, same))
        arrived.append({0: parts[0], **{d: rotated(parts[d], d, n_head) for d in middle_first}})
    own_rows = lax.dynamic_slice_in_dim(hidden, head * share, share, 0)
    pairs = {d: (one, other[i * half : (i + 1) * half]) for i, (d, one) in enumerate(zip(early, same))}
    pairs[middle] = (across, across_other)
    groups = [w_out]
    for d in range(1, n_head):
        one, two = pairs[d]
        groups.append(jnp.concatenate([jnp.where(parity == 0, one, two), jnp.where(parity == 0, two, one)], axis=0))
    result = None
    order = sorted(range(n_head), key=lambda d: (-abs(2 * d - n_head), -d))
    order = order[:-2] + order[:-3:-1]
    for k in range(pieces):
        total = own_rows[k * size : (k + 1) * size].astype(F32)
        for d in order[:-1]:
            total = total + jnp.dot(arrived[k][d], groups[d], preferred_element_type=F32)
        if k == pieces - 1:
            total = lax.optimization_barrier(total)
        total = (total + jnp.dot(arrived[k][order[-1]], groups[order[-1]], preferred_element_type=F32)).astype(BF16)
        if result is None:
            result = jnp.pad(total, ((0, share - size), (0, 0)))
        else:
            result = lax.dynamic_update_slice(result, total, (k * size, 0))
    return result


def solution(mesh):
    placed = (
        P("ctx", None),
        P(),
        P(None, None, "head"),
        P(),
        P(None, "head"),
        P("head"),
        P("head"),
        P("head"),
        P(None, "head"),
        P(),
        P("head", None),
    )
    return jax.shard_map(
        on_device, mesh=mesh, in_specs=placed, out_specs=P(("ctx", "head"), None), check_vma=False
    )
```
